32 devices in a mesh: replica: 2 (over y), node: 8 (over z, x), shard: 2 (over core).
Axes of the slice: x: 2, y: 2, z: 4, core: 2. Of those that a mesh axis runs over, the one named last changes fastest.
Arguments:
- residual: bfloat16 [192, 6144], P(('replica', 'node'), 'shard'), parts along dimension 0, may hold values from -6 to 6
- queries: bfloat16 [192, 6144], P(('replica', 'node'), 'shard'), parts along dimension 0, may hold values from -110 to 110
- key_cache: bfloat16 [192, 128, 1024], P(('replica', 'node'), None, 'shard'), parts along dimension 0, may hold values from -4 to 4
- value_cache: bfloat16 [192, 128, 1024], P(('replica', 'node'), None, 'shard'), parts along dimension 0, may hold values from -6 to 6
- new_key: bfloat16 [192, 1024], P(('replica', 'node'), 'shard'), parts along dimension 0, may hold values from -4.1 to 4.1
- new_value: bfloat16 [192, 1024], P(('replica', 'node'), 'shard'), parts along dimension 0, may hold values from -6 to 6
- cache_lengths: int32 [192], P(('replica', 'node')), parts along dimension 0, may hold values from 1 to 128, 6144 in all
- norm_gain: float32 [6144], replicated, may hold values from 0.1 to 1.9
- router: bfloat16 [6144, 4], replicated, may hold values from -0.078125 to 0.078125
- routes: int32 [192, 2], P(('replica', 'node')), parts along dimension 0, may hold values from 0 to 3, all different within a row; in each aligned block of 12 rows (0 to 11, 12 to 23, ...) at most 9 rows name the same one
- gate_weight: bfloat16 [6144, 32768], P(None, ('node', 'shard')), may hold values from -0.078125 to 0.078125
- up_weight: bfloat16 [6144, 32768], P(None, ('node', 'shard')), may hold values from -0.078125 to 0.078125
- down_weight: bfloat16 [32768, 6144], P(('node', 'shard')), may hold values from -0.0625 to 0.0625
Outputs:
- mixed: bfloat16 [192, 6144], P(('replica', 'node'), 'shard'), parts along dimension 0
The draws below stay inside these ranges and needn't reach their ends.
There are 2 independent parts, one for each index of `replica`. The reference program is written for one: setup_inputs(seed, part) draws one part's arguments, and reference() takes and returns one part's arrays. A program takes and returns all parts, laid end to end along the dimension named above; an argument that names none is the same for every part. Nothing has to cross between parts.
Inputs may be any that keep to these rules, and one draw needn't show every extreme that they name: `routes`: each row names two different experts; in the 12 rows of one index of node no expert is named more than 9 times, a bound that some block reaches. `cache_lengths`: one request fills all 128 positions.
All inputs are finite; a program needn't handle non-finite values. No bound on the sum of `cache_lengths` on one device may be relied on, other than what follows from the above.
Results may differ from the reference program's by a relative error of at most 0.0049.
Values may be sent and summed in bfloat16 or wider, within the bound.
No kernel may reach another device: no remote copies, remote signals or barrier semaphores. Data moves between devices by JAX's collectives and lax.ppermute only.
A program may use at most 192 MiB of HBM per device.

```python
import math
import jax
import jax.numpy as jnp
import numpy as np
from jax import lax

D = 6144
QUERY_HEADS = 48
KV_HEADS = 8
HEAD_DIM = 128
EXPERTS = 4
FF = 8192
TOK_DEV = 12
CACHE = 128
CAP = 9
TOKENS = 96
N_NODE = 8


def drawn_fields(key, lift):
    cache_key, fresh_key, query_key, pick_key = jax.random.split(key, 4)
    group_size = QUERY_HEADS // KV_HEADS
    cache = jnp.clip(jax.random.normal(cache_key, (TOKENS, CACHE, KV_HEADS, HEAD_DIM), jnp.float32), -4.0, 4.0)
    fresh = jnp.clip(jax.random.normal(fresh_key, (TOKENS, KV_HEADS, HEAD_DIM), jnp.float32), -4.0, 4.0)
    query = jnp.clip(jax.random.normal(query_key, (TOKENS, KV_HEADS, group_size, HEAD_DIM), jnp.float32), -4.0, 4.0)
    chosen = jax.random.bernoulli(pick_key, 0.25, (TOKENS,)).astype(jnp.float32) * lift
    query = (1.0 - chosen[:, None, None, None]) * query
    fresh = (1.0 - chosen[:, None, None]) * fresh
    return (cache, fresh, query)


def draw_queries(key, part):
    lift = 0.0
    cache, fresh, query = drawn_fields(key, lift)
    return query.reshape(TOKENS, QUERY_HEADS * HEAD_DIM).astype(jnp.bfloat16)


def draw_key_cache(key, part):
    lift = 0.0
    cache, fresh, query = drawn_fields(key, lift)
    return cache.reshape(TOKENS, CACHE, KV_HEADS * HEAD_DIM).astype(jnp.bfloat16)


def draw_new_key(key, part):
    lift = 0.0
    cache, fresh, query = drawn_fields(key, lift)
    return fresh.reshape(TOKENS, KV_HEADS * HEAD_DIM).astype(jnp.bfloat16)


def levels(key, shape, pieces, least, high):
    def one(position, shards_of):
        draws = jax.random.uniform(jax.random.fold_in(jax.random.fold_in(key, 6), position), (shards_of,), jnp.float32, least / len(pieces), high / len(pieces))
        return jnp.repeat(jnp.exp(draws), shape[position] // shards_of).reshape((-1,) + (1,) * (len(shape) - position - 1))

    level = one(*pieces[0])
    for cut in pieces[1:]:
        level = level * one(*cut)
    return level


def length_profile(number_of, total, limit, lean):
    loads = [(1 << 20) // math.isqrt(rank ** lean) + 1 for rank in range(2, number_of + 1)]
    surplus, given = total - limit - (number_of - 1), [1] * (number_of - 1)
    while surplus > 0:
        free = [i for i in range(number_of - 1) if given[i] < limit]
        pool, budget = sum([loads[i] for i in free]), surplus
        for i in free:
            more = min(limit - given[i], max(1, budget * loads[i] // pool), surplus)
            given[i] = given[i] + more
            surplus = surplus - more
    return np.array([limit] + given)


def uneven(key, count, total, most, skew):
    if count == 2:
        one = jax.random.randint(key, (), max(1, total - most), min(most, total - 1) + 1)
        return jnp.stack([one, total - one])
    tallies = jnp.asarray(length_profile(count, total, most, skew), jnp.int32)
    twos = (count - 1) // 2
    giver, sink = tallies[1:1 + 2 * twos:2], tallies[2:2 + 2 * twos:2]
    slack = jnp.minimum(giver - 1, most - sink)
    moved = jax.random.randint(jax.random.fold_in(key, 1), (twos,), 0, 1 << 20) % (slack + 1)
    tallies = tallies.at[1:1 + 2 * twos:2].set(giver - moved).at[2:2 + 2 * twos:2].set(sink + moved)
    return tallies[jax.random.permutation(jax.random.fold_in(key, 2), count)]


def deal_out(key, own, number, rows, number_of, top, limit, lean):
    order = jax.random.permutation(key, number_of)
    crowded, ordinary = shares(number_of, rows * top, limit, lean, True), shares(number_of, rows * top, limit, lean, False)
    places = jnp.arange(number_of)

    def named(tallies, turn):
        used = int((tallies > 0).sum())
        fixed = max(1, used // 4)
        shifted = fixed + (places - fixed + turn * (used - fixed)) % max(1, number_of - fixed)
        return jnp.zeros((number_of,), jnp.int32).at[order[jnp.where(places < fixed, places, shifted)]].set(jnp.asarray(tallies, jnp.int32))

    tallies = jnp.where(number % 4 == 0, named(crowded, number // 4), named(ordinary, number - number // 4 - 1))
    mixed = jax.random.permutation(jax.random.fold_in(own, 3), number_of)
    giver, sink = mixed[0:number_of // 2 * 2:2], mixed[1:number_of // 2 * 2:2]
    room = jnp.minimum(tallies[giver] - 1, limit - tallies[sink]) // 2
    room = jnp.where((giver == order[0]) | (sink == order[0]) | (tallies[sink] == 0), 0, jnp.maximum(room, 0))
    shifted = jax.random.randint(jax.random.fold_in(own, 4), (number_of // 2,), 0, 1 << 20) % (room + 1)
    tallies = tallies.at[giver].add(-shifted).at[sink].add(shifted)
    items = jnp.searchsorted(jnp.cumsum(tallies), jnp.arange(rows * top), side="right").astype(jnp.int32)
    table = items.reshape(top, rows).T
    table = table[jax.random.permutation(jax.random.fold_in(own, 1), rows)]
    turn = jax.random.randint(jax.random.fold_in(own, 2), (rows, 1), 0, top)
    return jnp.take_along_axis(table, (jnp.arange(top)[None, :] + turn) % top, axis=1)


def shares(amount, total, limit, skew, full):
    portions = [(1 << 20) // math.isqrt(grade ** skew) + 1 for grade in range(1, amount + 1)]
    largest = limit if full else min(limit, max(-(-total // amount), total * portions[0] // sum(portions)))
    least = 1 if total - largest >= amount - 1 else 0
    holding, rest = [largest] + [least] * (amount - 1), total - largest - least * (amount - 1)
    while rest > 0:
        free = [i for i in range(1, amount) if holding[i] < largest] or [i for i in range(1, amount) if holding[i] < limit]
        mass, budget = sum([portions[i] for i in free]), rest
        for i in free:
            more = min(limit - holding[i], max(1, budget * portions[i] // mass), rest)
            holding[i] = holding[i] + more
            rest = rest - more
    return np.array(holding)


def scatter_about(stream_key, dims, spread, limit, cuts=(), held_as=jnp.bfloat16):
    factor_of = levels(stream_key, dims, cuts, -0.22, 0.18) if cuts else 1.0
    drawn = jax.random.normal(stream_key, dims, jnp.float32) * spread * factor_of
    return jnp.minimum(jnp.maximum(drawn, -limit), limit).astype(held_as)


def setup_inputs(seed: int = 0, part: int = 0) -> dict:
    seeds = jax.random.split(jax.random.key(seed), 14)
    part_splits = jax.random.split(jax.random.fold_in(seeds[13], part), 14)
    residual = scatter_about(part_splits[0], (TOKENS, D), 1.0, 6.0, ((0, 8), (1, 2)))
    queries = draw_queries(jax.random.fold_in(jax.random.fold_in(seeds[13], part), 71), part)
    key_cache = draw_key_cache(jax.random.fold_in(jax.random.fold_in(seeds[13], part), 71), part)
    value_cache = scatter_about(part_splits[3], (TOKENS, CACHE, KV_HEADS * HEAD_DIM), 1.0, 6.0, ((0, 8), (2, 2)))
    new_key = draw_new_key(jax.random.fold_in(jax.random.fold_in(seeds[13], part), 71), part)
    new_value = scatter_about(part_splits[5], (TOKENS, KV_HEADS * HEAD_DIM), 1.0, 6.0, ((0, 8), (1, 2)))
    cache_lengths = uneven(part_splits[6], TOKENS, TOKENS * CACHE // 2, CACHE, 2).astype(jnp.int32)
    norm_gain = jnp.clip(1.0 + 0.18 * jax.random.normal(seeds[7], (D,), jnp.float32), 0.1, 1.9)
    router = scatter_about(seeds[8], (D, EXPERTS), D ** -0.5, 0.078125)
    routes_keys = jax.random.split(jax.random.fold_in(part_splits[9], 1), TOKENS // TOK_DEV)
    routes_turns = jax.random.permutation(jax.random.fold_in(part_splits[9], 3), TOKENS // TOK_DEV)
    routes = jax.vmap(lambda own, number: deal_out(jax.random.fold_in(part_splits[9], 2), own, number, TOK_DEV, EXPERTS, 2, CAP, 2))(routes_keys, routes_turns).reshape((TOKENS, 2))
    gate_weight = scatter_about(seeds[10], (D, EXPERTS * FF), D ** -0.5, 0.078125, ((1, 16),))
    up_weight = scatter_about(seeds[11], (D, EXPERTS * FF), D ** -0.5, 0.078125, ((1, 16),))
    down_weight = scatter_about(seeds[12], (EXPERTS * FF, D), FF ** -0.5, 0.0625, ((0, 16),))
    return dict(residual=residual, queries=queries, key_cache=key_cache, value_cache=value_cache, new_key=new_key, new_value=new_value, cache_lengths=cache_lengths, norm_gain=norm_gain, router=router, routes=routes, gate_weight=gate_weight, up_weight=up_weight, down_weight=down_weight)


def attend_all(queries, key_cache, value_cache, new_key, new_value, cache_lengths):
    tok_count = queries.shape[0]
    group_size = QUERY_HEADS // KV_HEADS
    query_rows = queries.astype(jnp.float32).reshape(tok_count, KV_HEADS, group_size, HEAD_DIM)
    key_rows = key_cache.astype(jnp.float32).reshape(tok_count, CACHE, KV_HEADS, HEAD_DIM)
    value_rows = value_cache.astype(jnp.float32).reshape(tok_count, CACHE, KV_HEADS, HEAD_DIM)
    fresh_key = new_key.astype(jnp.float32).reshape(tok_count, KV_HEADS, HEAD_DIM)
    fresh_value = new_value.astype(jnp.float32).reshape(tok_count, KV_HEADS, HEAD_DIM)
    scaling = 1.0 / math.sqrt(HEAD_DIM)
    cache_scores = jnp.einsum('tgjd,tpgd->tgjp', query_rows, key_rows, precision=lax.Precision.HIGHEST) * scaling
    new_scores = jnp.einsum('tgjd,tgd->tgj', query_rows, fresh_key, precision=lax.Precision.HIGHEST) * scaling
    positions = lax.iota(jnp.int32, CACHE)
    valid = positions[None, :] < cache_lengths.astype(jnp.int32)[:, None]
    cache_scores = jnp.where(valid[:, None, None, :], cache_scores, jnp.float32(-1e+30))
    largest = jnp.maximum(lax.optimization_barrier(jnp.max(cache_scores, axis=-1)), new_scores)
    cache_terms = jnp.exp(cache_scores - largest[..., None])
    new_terms = jnp.exp(new_scores - largest)
    total = lax.optimization_barrier(jnp.sum(cache_terms, axis=-1)) + new_terms
    cache_probs = lax.optimization_barrier(cache_terms.astype(jnp.bfloat16)).astype(jnp.float32)
    new_probs = lax.optimization_barrier(new_terms.astype(jnp.bfloat16)).astype(jnp.float32)
    weighted = jnp.einsum('tgjp,tpgd->tgjd', cache_probs, value_rows, precision=lax.Precision.HIGHEST)
    weighted = weighted + new_probs[..., None] * fresh_value[:, :, None, :]
    return (weighted / total[..., None]).reshape(tok_count, D)

def reference(residual, queries, key_cache, value_cache, new_key, new_value, cache_lengths, norm_gain, router, routes, gate_weight, up_weight, down_weight):
    attention = attend_all(queries, key_cache, value_cache, new_key, new_value, cache_lengths)
    carried = residual.astype(jnp.float32) + attention
    mean_square = lax.optimization_barrier(jnp.mean(carried * carried, axis=-1, keepdims=True))
    normed = (carried * lax.rsqrt(mean_square + 1e-05) * norm_gain.astype(jnp.float32)).astype(jnp.bfloat16)
    normed_f = lax.optimization_barrier(normed).astype(jnp.float32)
    logits = jnp.dot(normed_f, router.astype(jnp.float32), precision=lax.Precision.HIGHEST)
    pair_logits = jnp.take_along_axis(logits, routes.astype(jnp.int32), axis=1)
    first_share = jax.nn.sigmoid(pair_logits[:, 0] - pair_logits[:, 1])
    node_rows = normed_f.reshape(N_NODE, TOK_DEV, D)
    node_routes = routes.astype(jnp.int32).reshape(N_NODE, TOK_DEV, 2)
    node_first = first_share.reshape(N_NODE, TOK_DEV)
    expert_ids = lax.iota(jnp.int32, EXPERTS)
    member = jnp.any(node_routes[:, :, :, None] == expert_ids[None, None, None, :], axis=2)
    slot_index = jnp.cumsum(member.astype(jnp.int32), axis=1) - 1
    slot_ids = lax.iota(jnp.int32, CAP)
    placed = jnp.logical_and(member[..., None], slot_index[..., None] == slot_ids[None, None, None, :]).astype(jnp.float32)
    dispatched = jnp.einsum('ntec,ntd->necd', placed, node_rows, precision=lax.Precision.HIGHEST)
    results = []
    for expert in range(EXPERTS):
        block_rows = dispatched[:, expert].reshape(N_NODE * CAP, D)
        gate_cols = gate_weight[:, expert * FF:(expert + 1) * FF].astype(jnp.float32)
        up_cols = up_weight[:, expert * FF:(expert + 1) * FF].astype(jnp.float32)
        down_rows = down_weight[expert * FF:(expert + 1) * FF, :].astype(jnp.float32)
        gate_val = jnp.dot(block_rows, gate_cols, precision=lax.Precision.HIGHEST)
        up_val = jnp.dot(block_rows, up_cols, precision=lax.Precision.HIGHEST)
        hidden = lax.optimization_barrier((jax.nn.silu(gate_val) * up_val).astype(jnp.bfloat16)).astype(jnp.float32)
        results.append(jnp.dot(hidden, down_rows, precision=lax.Precision.HIGHEST).reshape(N_NODE, CAP, D))
    expert_out = jnp.stack(results, axis=1)
    first_mask = (node_routes[:, :, 0, None] == expert_ids[None, None, :]).astype(jnp.float32)
    second_mask = (node_routes[:, :, 1, None] == expert_ids[None, None, :]).astype(jnp.float32)
    route_share = node_first[..., None] * first_mask + (1.0 - node_first)[..., None] * second_mask
    selection = placed * route_share[..., None]
    moe = jnp.einsum('ntec,necd->ntd', selection, expert_out, precision=lax.Precision.HIGHEST)
    return (carried + moe.reshape(TOKENS, D)).astype(jnp.bfloat16)
```

```python
import functools
import math

import jax
import jax.numpy as jnp
from jax import lax
from jax.experimental import pallas as pl
from jax.experimental.pallas import tpu as pltpu
from jax.sharding import PartitionSpec as P

QUERY_HEADS = 48
KV_HEADS = 8
HEAD_DIM = 128
EXPERTS = 4
GROUP = QUERY_HEADS // KV_HEADS
LANES = 128
FOLD = 2
MIB = 1 << 20
F32 = jnp.float32
BF16 = jnp.bfloat16


def whole_spec(array):
    zeros = (0,) * len(array.shape)
    return pl.BlockSpec(array.shape, lambda *_: zeros)


def attend_kernel(
    place_ref, len_ref, q_ref, k_ref, v_ref, nk_ref, nv_ref, res_ref, gain_ref, rt_ref,
    carried_ref, pay_ref, stat_ref,
    q_scr, o_scr, nk_scr, nv_scr, pay_scr,
):
    tok, width = q_ref.shape
    cache_len, kv_width = k_ref.shape[1], k_ref.shape[2]
    heads = width // HEAD_DIM
    groups = kv_width // HEAD_DIM
    fold_width = width // FOLD
    scaling = 1.0 / math.sqrt(HEAD_DIM)
    half = place_ref[0]
    for h in range(heads):
        q_scr[h * tok:(h + 1) * tok, :] = q_ref[:, h * HEAD_DIM:(h + 1) * HEAD_DIM].astype(F32)
    nk_scr[...] = nk_ref[...].astype(F32)
    nv_scr[...] = nv_ref[...].astype(F32)
    row_group = lax.broadcasted_iota(jnp.int32, (heads, HEAD_DIM), 0) // GROUP
    position = lax.broadcasted_iota(jnp.int32, (heads, cache_len), 1)
    scores, fresh = [], []
    for t in range(tok):
        q_rows = q_scr[pl.ds(t, heads, stride=tok), :]
        q_wide = jnp.concatenate(
            [jnp.where(row_group == g, q_rows, 0.0) for g in range(groups)], axis=1
        )
        scores.append(
            lax.dot_general(
                q_wide.astype(BF16), k_ref[t], (((1,), (1,)), ((), ())),
                preferred_element_type=F32,
            ) * scaling
        )
        fresh.append(
            jnp.sum(q_wide * nk_scr[pl.ds(t, 1), :], axis=1, keepdims=True) * scaling
        )
    terms, fresh_terms, totals = [], [], []
    for t in range(tok):
        score = jnp.where(position < len_ref[t], scores[t], -1e30)
        largest = jnp.maximum(jnp.max(score, axis=1, keepdims=True), fresh[t])
        term = jnp.exp(score - largest)
        fresh_term = jnp.exp(fresh[t] - largest)
        totals.append(jnp.sum(term, axis=1, keepdims=True) + fresh_term)
        terms.append(term.astype(BF16))
        fresh_terms.append(fresh_term.astype(BF16).astype(F32))
    for t in range(tok):
        wide = jnp.dot(terms[t], v_ref[t], preferred_element_type=F32)
        wide = wide + fresh_terms[t] * nv_scr[pl.ds(t, 1), :]
        picked = wide[:, :HEAD_DIM]
        for g in range(1, groups):
            picked = jnp.where(
                row_group == g, wide[:, g * HEAD_DIM:(g + 1) * HEAD_DIM], picked
            )
        o_scr[pl.ds(t, heads, stride=tok), :] = picked / totals[t]
    for h in range(heads):
        cols = slice(h * HEAD_DIM, (h + 1) * HEAD_DIM)
        carried_ref[:, cols] = res_ref[:, cols].astype(F32) + o_scr[h * tok:(h + 1) * tok, :]
    carried = carried_ref[...]
    columns = pl.ds(pl.multiple_of(half * width, LANES), width)
    scaled = carried * gain_ref[:, columns]
    squares = jnp.sum(carried * carried, axis=1, keepdims=True)
    rounded = scaled.astype(BF16).astype(F32)
    router = rt_ref[:, columns].astype(F32)
    lane = lax.broadcasted_iota(jnp.int32, (tok, LANES), 1)
    stat = jnp.where(lane == EXPERTS, squares, 0.0)
    for e in range(EXPERTS):
        logit = jnp.sum(rounded * router[e:e + 1, :], axis=1, keepdims=True)
        stat = jnp.where(lane == e, logit, stat)
    stat_ref[...] = stat
    for f in range(FOLD):
        pay_scr[f * tok:(f + 1) * tok, :fold_width] = scaled[:, f * fold_width:(f + 1) * fold_width]
    first = squares.astype(BF16).astype(F32)
    second = (squares - first).astype(BF16).astype(F32)
    third = squares - first - second
    extra = jnp.where(lane == 0, first, jnp.where(lane == 1, second, jnp.where(lane == 2, third, 0.0)))
    for f in range(FOLD):
        pay_scr[f * tok:(f + 1) * tok, fold_width:] = extra
    pay_ref[...] = pay_scr[...].astype(BF16)


def attend(place, lengths, queries, key_cache, value_cache, new_key, new_value, residual, gain, router_t):
    tok, width = queries.shape
    kv_width = new_key.shape[1]
    heads = width // HEAD_DIM
    smem = pl.BlockSpec(memory_space=pltpu.SMEM)
    vmem = pl.BlockSpec(memory_space=pltpu.VMEM)
    return pl.pallas_call(
        attend_kernel,
        out_shape=(
            jax.ShapeDtypeStruct((tok, width), F32),
            jax.ShapeDtypeStruct((FOLD * tok, width // FOLD + LANES), BF16),
            jax.ShapeDtypeStruct((tok, LANES), F32),
        ),
        in_specs=[smem, smem] + [vmem] * 8,
        out_specs=(vmem, vmem, vmem),
        scratch_shapes=[
            pltpu.VMEM((heads * tok, HEAD_DIM), F32),
            pltpu.VMEM((heads * tok, HEAD_DIM), F32),
            pltpu.VMEM((tok, kv_width), F32),
            pltpu.VMEM((tok, kv_width), F32),
            pltpu.VMEM((FOLD * tok, width // FOLD + LANES), F32),
        ],
        compiler_params=pltpu.CompilerParams(vmem_limit_bytes=16 * MIB),
        cost_estimate=pl.CostEstimate(flops=10**8, bytes_accessed=4 * 10**6, transcendentals=10**5),
        name="attend",
    )(place, lengths, queries, key_cache, value_cache, new_key, new_value, residual, gain, router_t)


def unfold_rows(blocks, x_scr, f_scr, k_block):
    tok = blocks[0].shape[0] // FOLD
    fold_width = blocks[0].shape[1] - LANES
    per_fold = fold_width // k_block
    for f in range(FOLD):
        for i, block in enumerate(blocks):
            f_scr[i * tok:(i + 1) * tok, :] = block[:, :fold_width].astype(F32)[f * tok:(f + 1) * tok, :]
        for p in range(per_fold):
            x_scr[f * per_fold + p] = f_scr[:, p * k_block:(p + 1) * k_block].astype(BF16)


def expand_kernel(count, k_block, last, place_ref, *refs):
    blocks = refs[:count]
    step, steps = pl.program_id(0), pl.num_programs(0)
    if not last:
        gate_ref, up_ref, gate_acc, up_acc, x_scr, f_scr = refs[count:]
    else:
        stats = refs[count:2 * count]
        gate_in, up_in, gate_ref, up_ref, hidden_ref, gate_acc, up_acc, x_scr, f_scr = refs[2 * count:]

    @pl.when(step == 0)
    def _():
        unfold_rows(blocks, x_scr, f_scr, k_block)
        if last:
            gate_acc[...] = gate_in[...]
            up_acc[...] = up_in[...]
        else:
            gate_acc[...] = jnp.zeros_like(gate_acc)
            up_acc[...] = jnp.zeros_like(up_acc)

    rows = x_scr[step]
    gate_acc[...] += jnp.dot(rows, gate_ref[...], preferred_element_type=F32)
    up_acc[...] += jnp.dot(rows, up_ref[...], preferred_element_type=F32)
    if last:
        @pl.when(step == steps - 1)
        def _():
            tok = blocks[0].shape[0] // FOLD
            fold_width = blocks[0].shape[1] - LANES
            for i in range(count):
                both = stats[i][...].astype(F32) + 0.0
                mine = blocks[i][:, fold_width:].astype(F32)
                total = jnp.sum(both, axis=1, keepdims=True) + jnp.sum(mine, axis=1, keepdims=True)
                f_scr[i * tok:(i + 1) * tok, :LANES] = jnp.broadcast_to(total[:tok], (tok, LANES))
            features = 2 * FOLD * fold_width
            scale = lax.rsqrt(f_scr[:, 0:1] * (1.0 / features) + 1e-05)
            gate = gate_acc[...] * scale
            up = up_acc[...] * scale
            hidden_ref[...] = (gate / (1.0 + jnp.exp(-gate)) * up).astype(BF16)


def expand(place, blocks, gate_weight, up_weight, own=None, stat_blocks=()):
    last = own is not None
    count = len(blocks)
    tok = blocks[0].shape[0] // FOLD
    fold_width = blocks[0].shape[1] - LANES
    width = FOLD * fold_width
    hidden = gate_weight.shape[1]
    rows = count * tok
    k_block = math.gcd(512, fold_width)
    steps = width // k_block
    weight_spec = pl.BlockSpec(
        (k_block, hidden),
        (lambda k, place: ((1 - place[0]) * steps + k, 0)) if last
        else (lambda k, place: (place[0] * steps + k, 0)),
    )
    acc = jax.ShapeDtypeStruct((rows, hidden), F32)
    in_specs = [whole_spec(b) for b in blocks]
    operands = list(blocks)
    scratch = [pltpu.VMEM((steps, rows, k_block), BF16), pltpu.VMEM((rows, fold_width), F32)]
    if last:
        tail = fold_width // LANES
        in_specs += [pl.BlockSpec((FOLD * tok, LANES), lambda k, place: (0, tail))] * count
        operands += list(stat_blocks)
        in_specs += [whole_spec(acc)] * 2
        operands += list(own)
        out_shape = jax.ShapeDtypeStruct((rows, hidden), BF16)
        out_specs = whole_spec(out_shape)
        scratch = [pltpu.VMEM((rows, hidden), F32)] * 2 + scratch
    else:
        out_shape = (acc, acc)
        out_specs = (whole_spec(acc), whole_spec(acc))
    return pl.pallas_call(
        functools.partial(expand_kernel, count, k_block, last),
        out_shape=out_shape,
        grid_spec=pltpu.PrefetchScalarGridSpec(
            num_scalar_prefetch=1,
            grid=(steps,),
            in_specs=in_specs + [weight_spec, weight_spec],
            out_specs=out_specs,
            scratch_shapes=scratch,
        ),
        compiler_params=pltpu.CompilerParams(vmem_limit_bytes=40 * MIB),
        cost_estimate=pl.CostEstimate(
            flops=4 * rows * width * hidden, bytes_accessed=4 * width * hidden, transcendentals=0
        ),
        name="expand_last" if last else "expand_first",
    )(place, *operands, gate_weight, up_weight)


def contract_kernel(place_ref, hidden_ref, down_ref, out_ref):
    out_ref[...] = jnp.dot(
        hidden_ref[...], down_ref[...], preferred_element_type=F32
    ).astype(out_ref.dtype)


def contract(place, hidden, down_weight, other, out_type):
    rows, units = hidden.shape
    width = down_weight.shape[1] // 2
    n_block = 512
    steps = width // n_block

    def weight_at(n, place):
        side = 1 - place[0] if other else place[0]
        return (0, side * steps + n)

    return pl.pallas_call(
        contract_kernel,
        out_shape=jax.ShapeDtypeStruct((rows, width), out_type),
        grid_spec=pltpu.PrefetchScalarGridSpec(
            num_scalar_prefetch=1,
            grid=(steps,),
            in_specs=[whole_spec(hidden), pl.BlockSpec((units, n_block), weight_at)],
            out_specs=pl.BlockSpec((rows, n_block), lambda n, place: (0, n)),
        ),
        compiler_params=pltpu.CompilerParams(vmem_limit_bytes=40 * MIB),
        cost_estimate=pl.CostEstimate(
            flops=2 * rows * width * units, bytes_accessed=2 * width * units, transcendentals=0
        ),
        name="contract_other" if other else "contract_own",
    )(place, hidden, down_weight)


def split_kernel(own_ref, got_ref, keep_ref, *send_refs):
    size = keep_ref.shape[0]
    keep_ref[...] = own_ref[:size, :] + got_ref[:size, :].astype(F32)
    for u, send in enumerate(send_refs, 1):
        at = slice(u * size, (u + 1) * size)
        send[...] = (own_ref[at, :] + got_ref[at, :].astype(F32)).astype(BF16)


def split_rows(own, got, parts):
    rows, width = own.shape
    size = rows // parts
    vmem = pl.BlockSpec(memory_space=pltpu.VMEM)
    return pl.pallas_call(
        split_kernel,
        out_shape=(jax.ShapeDtypeStruct((size, width), F32),)
        + (jax.ShapeDtypeStruct((size, width), BF16),) * (parts - 1),
        in_specs=[vmem, vmem],
        out_specs=(vmem,) * parts,
        compiler_params=pltpu.CompilerParams(vmem_limit_bytes=40 * MIB),
        name="split_rows",
    )(own, got)


def planes_kernel(count, own_ref, *refs):
    got, keep_ref, sends, total, folded = (
        refs[:count], refs[count], refs[count + 1:-2], refs[-2], refs[-1]
    )
    value = own_ref[...]
    for ref in got:
        value = value + ref[...].astype(F32)
    total[...] = value
    tok = keep_ref.shape[0]
    fold_width = keep_ref.shape[1] // FOLD
    keep_ref[...] = total[:tok, :]
    for s, send in enumerate(sends, 1):
        for f in range(FOLD):
            folded[f * tok:(f + 1) * tok, :] = total[
                s * tok:(s + 1) * tok, f * fold_width:(f + 1) * fold_width
            ]
        send[...] = folded[...].astype(BF16)


def split_planes(own, got):
    rows, width = own.shape
    tok = rows // EXPERTS
    vmem = pl.BlockSpec(memory_space=pltpu.VMEM)
    return pl.pallas_call(
        functools.partial(planes_kernel, len(got)),
        out_shape=(jax.ShapeDtypeStruct((tok, width), F32),)
        + (jax.ShapeDtypeStruct((FOLD * tok, width // FOLD), BF16),) * (EXPERTS - 1),
        in_specs=[vmem] * (1 + len(got)),
        out_specs=(vmem,) * EXPERTS,
        scratch_shapes=[
            pltpu.VMEM((rows, width), F32),
            pltpu.VMEM((FOLD * tok, width // FOLD), F32),
        ],
        compiler_params=pltpu.CompilerParams(vmem_limit_bytes=40 * MIB),
        name="split_planes",
    )(own, *got)


def finish_kernel(place_ref, carried_ref, routes_ref, stat_ref, stat_got_ref, own_ref, *refs):
    got, out_ref, folded = refs[:-2], refs[-2], refs[-1]
    tok, width = carried_ref.shape
    fold_width = width // FOLD
    stat = stat_ref[...] + stat_got_ref[...]
    lane = lax.broadcasted_iota(jnp.int32, stat.shape, 1)
    scale = lax.rsqrt(stat[:, EXPERTS:EXPERTS + 1] * (1.0 / (2 * width)) + 1e-05)
    first, second = routes_ref[:, 0:1], routes_ref[:, 1:2]
    gap = (
        jnp.sum(jnp.where(lane == second, stat, 0.0), axis=1, keepdims=True)
        - jnp.sum(jnp.where(lane == first, stat, 0.0), axis=1, keepdims=True)
    ) * scale
    share = 1.0 / (1.0 + jnp.exp(gap))

    def weight(s):
        expert = lax.rem(place_ref[1] + s, EXPERTS)
        return jnp.where(first == expert, share, 0.0) + jnp.where(second == expert, 1.0 - share, 0.0)

    for f in range(FOLD):
        at = slice(f * fold_width, (f + 1) * fold_width)
        value = carried_ref[:, at] + weight(0) * own_ref[:, at]
        for s, ref in enumerate(got, 1):
            folded[...] = ref[...].astype(F32)
            value = value + weight(s) * folded[f * tok:(f + 1) * tok, :]
        out_ref[:, at] = value.astype(BF16)


def finish(place, carried, routes, stat, stat_got, own, got):
    tok, width = carried.shape
    smem = pl.BlockSpec(memory_space=pltpu.SMEM)
    vmem = pl.BlockSpec(memory_space=pltpu.VMEM)
    return pl.pallas_call(
        finish_kernel,
        out_shape=jax.ShapeDtypeStruct((tok, width), BF16),
        in_specs=[smem] + [vmem] * (5 + len(got)),
        out_specs=vmem,
        scratch_shapes=[pltpu.VMEM((FOLD * tok, width // FOLD), F32)],
        compiler_params=pltpu.CompilerParams(vmem_limit_bytes=16 * MIB),
        name="finish",
    )(place, carried, routes, stat, stat_got, own, *got)


def on_device(
    residual, queries, key_cache, value_cache, new_key, new_value, cache_lengths,
    norm_gain, router, routes, gate_weight, up_weight, down_weight,
):
    nodes = lax.axis_size("node")
    per_plane = nodes // EXPERTS
    place = jnp.stack(
        [lax.axis_index("shard"), lax.axis_index("node") // per_plane]
    ).astype(jnp.int32)

    def to_plane(array, s):
        perm = [
            (e * per_plane + j, (e + s) % EXPERTS * per_plane + j)
            for e in range(EXPERTS) for j in range(per_plane)
        ]
        return lax.ppermute(array, "node", perm)

    def to_column(array, u):
        perm = [
            (e * per_plane + j, e * per_plane + (j + u) % per_plane)
            for e in range(EXPERTS) for j in range(per_plane)
        ]
        return lax.ppermute(array, "node", perm)

    def to_core(array):
        return lax.ppermute(array, "shard", [(0, 1), (1, 0)])

    carried, payload, stat = attend(
        place, cache_lengths, queries, key_cache, value_cache, new_key, new_value,
        residual, norm_gain.reshape(1, -1), router.T,
    )
    in_column = [payload] + [to_plane(payload, s) for s in range(1, EXPERTS)]
    blocks = list(in_column)
    for u in range(1, per_plane):
        blocks += [to_column(block, u) for block in in_column]
    other_blocks = [to_core(block) for block in blocks]
    stat_got = to_core(stat)
    sums = expand(place, blocks, gate_weight, up_weight)
    hidden = expand(place, other_blocks, gate_weight, up_weight, sums, blocks)
    leaving = contract(place, hidden, down_weight, True, BF16)
    arrived = to_core(leaving)
    staying = contract(place, hidden, down_weight, False, F32)
    parts = split_rows(staying, arrived, per_plane)
    got = [to_column(parts[u], -u) for u in range(1, per_plane)]
    planes = split_planes(parts[0], got)
    returned = [to_plane(planes[s], -s) for s in range(1, EXPERTS)]
    return finish(place, carried, routes, stat, stat_got, planes[0], returned)


def solution(mesh):
    rows = ("replica", "node")
    in_specs = (
        P(rows, "shard"),
        P(rows, "shard"),
        P(rows, None, "shard"),
        P(rows, None, "shard"),
        P(rows, "shard"),
        P(rows, "shard"),
        P(rows),
        P(),
        P(),
        P(rows, None),
        P(None, ("node", "shard")),
        P(None, ("node", "shard")),
        P(("node", "shard"), None),
    )
    return jax.shard_map(
        on_device,
        mesh=mesh,
        in_specs=in_specs,
        out_specs=P(rows, "shard"),
        check_vma=False,
    )
```

```python
import functools
import math

import jax
import jax.numpy as jnp
from jax import lax
from jax.experimental import pallas as pl
from jax.experimental.pallas import tpu as pltpu
from jax.sharding import PartitionSpec as P

QUERY_HEADS = 48
KV_HEADS = 8
HEAD_DIM = 128
EXPERTS = 4
GROUP = QUERY_HEADS // KV_HEADS
LANES = 128
FOLD = 2
MIB = 1 << 20
F32 = jnp.float32
BF16 = jnp.bfloat16


def whole_spec(array):
    zeros = (0,) * len(array.shape)
    return pl.BlockSpec(array.shape, lambda *_: zeros)


def in_vmem(*arrays):
    return [pltpu.with_memory_space_constraint(a, pltpu.VMEM) for a in arrays]


def in_hbm(*arrays):
    return [pltpu.with_memory_space_constraint(a, pltpu.HBM) for a in arrays]


VMEM_SPEC = pl.BlockSpec(memory_space=pltpu.VMEM)
SMEM_SPEC = pl.BlockSpec(memory_space=pltpu.SMEM)
HBM_SPEC = pl.BlockSpec(memory_space=pltpu.HBM)
ROUTE_LANE = 3 + 3 * EXPERTS
GATE_DEPTH = 2
DOWN_DEPTH = 4


def row_block(gate_weight):
    return math.gcd(512, gate_weight.shape[0] // 2)


def weight_copies(pairs, first, count, block, sems, split=2):
    part = block // split
    copies = []
    for i in range(count * split):
        for w, (source, target) in enumerate(pairs):
            copies.append(
                pltpu.make_async_copy(
                    source.at[pl.ds(first * block + i * part, part), :],
                    target.at[pl.ds(i * part, part), :], sems.at[w, i],
                )
            )
    return copies


def load_kernel(first, count, block, dep_ref, g_hbm, u_hbm, g_vmem, u_vmem, token_ref, sems):
    copies = weight_copies([(g_hbm, g_vmem), (u_hbm, u_vmem)], first, count, block, sems)
    for copy in copies:
        copy.start()
    token_ref[...] = jnp.zeros_like(token_ref)
    for copy in copies:
        copy.wait()


def load_blocks(first, count, after, gate_weight, up_weight):
    block = row_block(gate_weight)
    hidden = gate_weight.shape[1]
    piece = pltpu.VMEM((count * block, hidden), BF16)
    return pl.pallas_call(
        functools.partial(load_kernel, first, count, block),
        out_shape=(piece, piece, pltpu.VMEM((8, LANES), F32)),
        in_specs=[pl.BlockSpec(memory_space=pl.ANY), HBM_SPEC, HBM_SPEC],
        out_specs=(VMEM_SPEC,) * 3,
        scratch_shapes=[pltpu.SemaphoreType.DMA((2, 2 * count))],
        compiler_params=pltpu.CompilerParams(vmem_limit_bytes=MIB),
        cost_estimate=pl.CostEstimate(
            flops=0, bytes_accessed=4 * count * block * hidden, transcendentals=0
        ),
        name="load_weights",
    )(*in_vmem(after), *in_hbm(gate_weight, up_weight))


def join_kernel(a_ref, b_ref, token_ref, out_ref):
    out_ref[...] = jnp.concatenate(
        [a_ref[...].astype(F32), b_ref[...].astype(F32)], axis=0
    ).astype(BF16)


def join(a, b, token):
    return pl.pallas_call(
        join_kernel,
        out_shape=pltpu.VMEM((a.shape[0] + b.shape[0], a.shape[1]), BF16),
        in_specs=[VMEM_SPEC] * 3,
        out_specs=VMEM_SPEC,
        compiler_params=pltpu.CompilerParams(vmem_limit_bytes=2 * MIB),
        name="join",
    )(*in_vmem(a, b, token))


def relay_kernel(count, *refs):
    del refs


def relay(arrays, token):
    count = len(arrays)
    return list(pl.pallas_call(
        functools.partial(relay_kernel, count),
        out_shape=tuple(pltpu.VMEM(a.shape, a.dtype) for a in arrays),
        in_specs=[VMEM_SPEC] * (count + 1),
        out_specs=(VMEM_SPEC,) * count,
        input_output_aliases={i: i for i in range(count)},
        compiler_params=pltpu.CompilerParams(vmem_limit_bytes=MIB),
        name="relay",
    )(*in_vmem(*arrays, token)))


def split_three(value):
    first = value.astype(BF16).astype(F32)
    second = (value - first).astype(BF16).astype(F32)
    return first, second, value - first - second


def attend_kernel(
    ahead, block,
    place_ref, len_ref, routes_ref, q_hbm, k_hbm, v_hbm, nk_hbm, nv_hbm, res_hbm, gain_hbm, rt_hbm,
    g_hbm, u_hbm,
    carried_ref, pay_ref, g_vmem, u_vmem,
    q_ref, k_ref, v_ref, nk_ref, nv_ref, res_ref, gain_ref, rt_ref,
    q_scr, o_scr, nk_scr, nv_scr, pay_scr, sems, w_sems,
):
    tok, width = q_ref.shape
    cache_len, kv_width = k_ref.shape[1], k_ref.shape[2]
    heads = width // HEAD_DIM
    groups = kv_width // HEAD_DIM
    fold_width = width // FOLD
    scaling = 1.0 / math.sqrt(HEAD_DIM)
    columns = pl.ds(pl.multiple_of(place_ref[0] * width, LANES), width)
    half = tok // 2
    first, rest = pl.ds(0, half), pl.ds(half, tok - half)
    moves = [
        (q_hbm, q_ref), (nk_hbm, nk_ref),
        (k_hbm.at[first], k_ref.at[first]), (k_hbm.at[rest], k_ref.at[rest]),
        (v_hbm.at[first], v_ref.at[first]), (v_hbm.at[rest], v_ref.at[rest]),
        (nv_hbm, nv_ref), (res_hbm, res_ref),
        (gain_hbm.at[:, columns], gain_ref), (rt_hbm.at[:, columns], rt_ref),
    ]
    copies = [pltpu.make_async_copy(a, b, sems.at[i]) for i, (a, b) in enumerate(moves)]
    for copy in copies:
        copy.start()
    weights = weight_copies([(g_hbm, g_vmem), (u_hbm, u_vmem)], 0, ahead, block, w_sems)
    for copy in weights:
        copy.start()
    copies[0].wait()
    copies[1].wait()
    for h in range(heads):
        q_scr[h * tok:(h + 1) * tok, :] = q_ref[:, h * HEAD_DIM:(h + 1) * HEAD_DIM].astype(F32)
    nk_scr[...] = nk_ref[...].astype(F32)
    row_group = lax.broadcasted_iota(jnp.int32, (heads, HEAD_DIM), 0) // GROUP
    position = lax.broadcasted_iota(jnp.int32, (heads, cache_len), 1)
    scores, fresh = [], []
    for t in range(tok):
        if t == 0:
            copies[2].wait()
        if t == half:
            copies[3].wait()
        q_rows = q_scr[pl.ds(t, heads, stride=tok), :]
        q_wide = jnp.concatenate(
            [jnp.where(row_group == g, q_rows, 0.0) for g in range(groups)], axis=1
        )
        scores.append(
            lax.dot_general(
                q_wide.astype(BF16), k_ref[t], (((1,), (1,)), ((), ())),
                preferred_element_type=F32,
            ) * scaling
        )
        fresh.append(
            jnp.sum(q_wide * nk_scr[pl.ds(t, 1), :], axis=1, keepdims=True) * scaling
        )
    terms, fresh_terms, totals = [], [], []
    for t in range(tok):
        score = jnp.where(position < len_ref[t], scores[t], -1e30)
        largest = jnp.maximum(jnp.max(score, axis=1, keepdims=True), fresh[t])
        term = jnp.exp(score - largest)
        fresh_term = jnp.exp(fresh[t] - largest)
        totals.append(jnp.sum(term, axis=1, keepdims=True) + fresh_term)
        terms.append(term.astype(BF16))
        fresh_terms.append(fresh_term.astype(BF16).astype(F32))
    copies[6].wait()
    nv_scr[...] = nv_ref[...].astype(F32)
    for t in range(tok):
        if t == 0:
            copies[4].wait()
        if t == half:
            copies[5].wait()
        wide = jnp.dot(terms[t], v_ref[t], preferred_element_type=F32)
        wide = wide + fresh_terms[t] * nv_scr[pl.ds(t, 1), :]
        picked = wide[:, :HEAD_DIM]
        for g in range(1, groups):
            picked = jnp.where(
                row_group == g, wide[:, g * HEAD_DIM:(g + 1) * HEAD_DIM], picked
            )
        o_scr[pl.ds(t, heads, stride=tok), :] = picked / totals[t]
    for copy in copies[7:]:
        copy.wait()
    for h in range(heads):
        cols = slice(h * HEAD_DIM, (h + 1) * HEAD_DIM)
        carried_ref[:, cols] = res_ref[:, cols].astype(F32) + o_scr[h * tok:(h + 1) * tok, :]
    carried = carried_ref[...]
    scaled = carried * gain_ref[...]
    rounded = scaled.astype(BF16).astype(F32)
    router = rt_ref[...].astype(F32)
    for f in range(FOLD):
        pay_scr[f * tok:(f + 1) * tok, :fold_width] = scaled[:, f * fold_width:(f + 1) * fold_width]
    lane = lax.broadcasted_iota(jnp.int32, (tok, LANES), 1)
    row = lax.broadcasted_iota(jnp.int32, (tok, LANES), 0)
    sums = [jnp.sum(carried * carried, axis=1, keepdims=True)]
    for e in range(EXPERTS):
        sums.append(jnp.sum(rounded * router[e:e + 1, :], axis=1, keepdims=True))
    extra = jnp.zeros((tok, LANES), F32)
    for i, total in enumerate(sums):
        for j, term in enumerate(split_three(total)):
            extra = jnp.where(lane == 3 * i + j, term, extra)
    for t in range(tok):
        for i in range(2):
            extra = jnp.where(
                jnp.logical_and(row == t, lane == ROUTE_LANE + i),
                routes_ref[i, t].astype(F32), extra,
            )
    for f in range(FOLD):
        pay_scr[f * tok:(f + 1) * tok, fold_width:] = extra
    pay_ref[...] = pay_scr[...].astype(BF16)
    for copy in weights:
        copy.wait()


def attend(
    ahead, place, lengths, routes_t, queries, key_cache, value_cache, new_key, new_value,
    residual, gain, router_t, gate_weight, up_weight,
):
    tok, width = queries.shape
    kv_width = new_key.shape[1]
    heads = width // HEAD_DIM
    wide = width // FOLD + LANES
    piece = pltpu.VMEM((ahead * row_block(gate_weight), gate_weight.shape[1]), BF16)
    here = [
        pltpu.VMEM(a.shape, a.dtype)
        for a in (queries, key_cache, value_cache, new_key, new_value, residual)
    ]
    return pl.pallas_call(
        functools.partial(attend_kernel, ahead, row_block(gate_weight)),
        out_shape=(
            pltpu.VMEM((tok, width), F32),
            pltpu.VMEM((FOLD * tok, wide), BF16),
            piece,
            piece,
        ),
        in_specs=[SMEM_SPEC] * 3 + [HBM_SPEC] * 10,
        out_specs=(VMEM_SPEC,) * 4,
        scratch_shapes=here + [
            pltpu.VMEM((1, width), F32),
            pltpu.VMEM((EXPERTS, width), BF16),
            pltpu.VMEM((heads * tok, HEAD_DIM), F32),
            pltpu.VMEM((heads * tok, HEAD_DIM), F32),
            pltpu.VMEM((tok, kv_width), F32),
            pltpu.VMEM((tok, kv_width), F32),
            pltpu.VMEM((FOLD * tok, wide), F32),
            pltpu.SemaphoreType.DMA((10,)),
            pltpu.SemaphoreType.DMA((2, 2 * ahead)),
        ],
        compiler_params=pltpu.CompilerParams(vmem_limit_bytes=10 * MIB),
        cost_estimate=pl.CostEstimate(flops=10**8, bytes_accessed=8 * 10**6, transcendentals=10**5),
        name="attend",
    )(
        place,
        *in_hbm(
            lengths, routes_t, queries, key_cache, value_cache, new_key, new_value, residual, gain, router_t,
            gate_weight, up_weight,
        ),
    )


def down_copies(d_hbm, ring, sems, column, width, block, k):
    slot = lax.rem(k, ring.shape[0])
    return pltpu.make_async_copy(
        d_hbm.at[pl.ds(pl.multiple_of(k * block, block), block), pl.ds(column, width)],
        ring.at[slot], sems.at[slot],
    )


def down_pass(hidden, d_hbm, ring, sems, column, acc):
    steps, _, block = hidden.shape
    depth, _, width = ring.shape
    acc[...] = jnp.zeros_like(acc)

    def step(k, _):
        slot = lax.rem(k, depth)
        down_copies(d_hbm, ring, sems, column, width, block, k).wait()
        acc[...] += jnp.dot(hidden[k], ring[slot], preferred_element_type=F32)

        @pl.when(k + depth < steps)
        def _():
            down_copies(d_hbm, ring, sems, column, width, block, k + depth).start()

        return 0

    lax.fori_loop(0, steps, step, 0)


def experts_kernel(counts, block, per_plane, place_ref, *refs):
    mine, other = refs[:per_plane], refs[per_plane:2 * per_plane]
    refs = refs[2 * per_plane:]
    pieces = [refs[2 * i:2 * i + 2] for i in range(len(counts))]
    (g_hbm, u_hbm, d_hbm,
     hidden_ref, weight_ref, leaving_ref,
     x_scr, gate_acc, up_acc, gu_ring, ring, acc, g_sems, d_sems) = refs[2 * len(counts):]
    ready = sum(counts)
    rows, units = gate_acc.shape
    slots = EXPERTS
    tok = mine[0].shape[0] // (FOLD * slots)
    fold_width = mine[0].shape[1] - LANES
    width = FOLD * fold_width
    side = place_ref[0]
    steps = g_hbm.shape[0] // block
    per_fold = fold_width // block
    gu_depth = gu_ring.shape[0]

    def gu_copies(k):
        slot = lax.rem(k, gu_depth)
        at = pl.ds(pl.multiple_of(k * block, block), block)
        return [
            pltpu.make_async_copy(w.at[at, :], gu_ring.at[slot, i], g_sems.at[slot, i])
            for i, w in enumerate((g_hbm, u_hbm))
        ]

    for k in range(ready, min(ready + gu_depth, steps)):
        for copy in gu_copies(k):
            copy.start()
    d_steps, _, d_block = hidden_ref.shape
    column = pl.multiple_of((1 - side) * width, LANES)
    for k in range(min(ring.shape[0], d_steps)):
        down_copies(d_hbm, ring, d_sems, column, width, d_block, k).start()

    for arrays, base in ((mine, side * (width // block)), (other, (1 - side) * (width // block))):
        for f in range(FOLD):
            for u, array in enumerate(arrays):
                whole = array[:, :fold_width].astype(F32)
                for i in range(slots):
                    to = (u * slots + i) * tok
                    start = (i * FOLD + f) * tok
                    acc[to:to + tok, :fold_width] = whole[start:start + tok, :]
            for p in range(per_fold):
                x_scr[base + f * per_fold + p] = acc[:, p * block:(p + 1) * block].astype(BF16)

    gate_acc[...] = jnp.zeros_like(gate_acc)
    up_acc[...] = jnp.zeros_like(up_acc)

    first = 0
    for count, (g_ref, u_ref) in zip(counts, pieces):
        def held(k, _, first=first, g_ref=g_ref, u_ref=u_ref):
            at = pl.ds(pl.multiple_of(k * block, block), block)
            gate_acc[...] += jnp.dot(x_scr[first + k], g_ref[at, :], preferred_element_type=F32)
            up_acc[...] += jnp.dot(x_scr[first + k], u_ref[at, :], preferred_element_type=F32)
            return 0

        lax.fori_loop(0, count, held, 0)
        first += count

    def streamed(k, _):
        slot = lax.rem(k, gu_depth)
        for copy in gu_copies(k):
            copy.wait()
        gate_acc[...] += jnp.dot(x_scr[k], gu_ring[slot, 0], preferred_element_type=F32)
        up_acc[...] += jnp.dot(x_scr[k], gu_ring[slot, 1], preferred_element_type=F32)

        @pl.when(k + gu_depth < steps)
        def _():
            for copy in gu_copies(k + gu_depth):
                copy.start()

        return 0

    lax.fori_loop(ready, steps, streamed, 0)

    for u in range(per_plane):
        for i in range(slots):
            to = (u * slots + i) * tok
            start = i * FOLD * tok
            acc[to:to + tok, :LANES] = mine[u][:, fold_width:].astype(F32)[start:start + tok, :]
            acc[to:to + tok, LANES:2 * LANES] = other[u][:, fold_width:].astype(F32)[start:start + tok, :]
    own = acc[:, :LANES]
    both = own + acc[:, LANES:2 * LANES]
    lane = lax.broadcasted_iota(jnp.int32, (rows, LANES), 1)

    def pick(values, mask):
        return jnp.sum(jnp.where(mask, values, 0.0), axis=1, keepdims=True)

    scale = lax.rsqrt(pick(both, lane < 3) * (1.0 / (2 * width)) + 1e-05)
    first, second = pick(own, lane == ROUTE_LANE), pick(own, lane == ROUTE_LANE + 1)
    expert_of = (lane - 3) // 3
    logit_lane = jnp.logical_and(lane >= 3, lane < ROUTE_LANE)

    def logit_at(route):
        return pick(both, jnp.logical_and(logit_lane, expert_of == route.astype(jnp.int32))) * scale

    share = 1.0 / (1.0 + jnp.exp(logit_at(second) - logit_at(first)))
    here = place_ref[1].astype(F32)
    weight = jnp.where(first == here, share, 0.0) + jnp.where(second == here, 1.0 - share, 0.0)
    weight_ref[...] = jnp.broadcast_to(weight, weight_ref.shape)

    gate = gate_acc[...] * scale
    hidden = (gate / (1.0 + jnp.exp(-gate)) * (up_acc[...] * scale)).astype(BF16)
    for k in range(d_steps):
        hidden_ref[k] = hidden[:, k * d_block:(k + 1) * d_block]
    down_pass(hidden_ref, d_hbm, ring, d_sems, column, acc)
    leaving_ref[...] = (acc[...] * weight).astype(BF16)


def experts(place, mine, other, gate_weight, up_weight, down_weight, counts, pieces):
    slots = EXPERTS
    per_plane = len(mine)
    tok = mine[0].shape[0] // (FOLD * slots)
    rows = per_plane * slots * tok
    units = gate_weight.shape[1]
    width = down_weight.shape[1] // 2
    block = row_block(gate_weight)
    steps = gate_weight.shape[0] // block
    d_block = math.gcd(256, units)
    depth = min(DOWN_DEPTH, units // d_block)
    gu_depth = min(GATE_DEPTH, max(1, steps - sum(counts)))
    return pl.pallas_call(
        functools.partial(experts_kernel, counts, block, per_plane),
        out_shape=(
            pltpu.VMEM((units // d_block, rows, d_block), BF16),
            pltpu.VMEM((rows, LANES), F32),
            pltpu.VMEM((rows, width), BF16),
        ),
        in_specs=[SMEM_SPEC] + [VMEM_SPEC] * (2 * per_plane + 2 * len(counts)) + [HBM_SPEC] * 3,
        out_specs=(VMEM_SPEC,) * 3,
        scratch_shapes=[
            pltpu.VMEM((steps, rows, block), BF16),
            pltpu.VMEM((rows, units), F32),
            pltpu.VMEM((rows, units), F32),
            pltpu.VMEM((gu_depth, 2, block, units), BF16),
            pltpu.VMEM((depth, d_block, width), BF16),
            pltpu.VMEM((rows, width), F32),
            pltpu.SemaphoreType.DMA((gu_depth, 2)),
            pltpu.SemaphoreType.DMA((depth,)),
        ],
        compiler_params=pltpu.CompilerParams(vmem_limit_bytes=(25 if rows < 256 else 40) * MIB),
        cost_estimate=pl.CostEstimate(
            flops=6 * rows * 2 * width * units, bytes_accessed=3 * 4 * width * units, transcendentals=0
        ),
        name="experts",
    )(
        place, *in_vmem(*mine, *other, *[p for pair in pieces for p in pair]),
        *in_hbm(gate_weight, up_weight, down_weight),
    )


def own_kernel(place_ref, hidden_ref, weight_ref, d_hbm, out_ref, ring, sems):
    d_steps, _, d_block = hidden_ref.shape
    width = out_ref.shape[1]
    column = pl.multiple_of(place_ref[0] * width, LANES)
    for k in range(min(ring.shape[0], d_steps)):
        down_copies(d_hbm, ring, sems, column, width, d_block, k).start()
    down_pass(hidden_ref, d_hbm, ring, sems, column, out_ref)
    out_ref[...] = out_ref[...] * weight_ref[:, 0:1]


def own_half(place, hidden, weight, down_weight):
    d_steps, rows, d_block = hidden.shape
    width = down_weight.shape[1] // 2
    depth = min(8, d_steps)
    return pl.pallas_call(
        own_kernel,
        out_shape=pltpu.VMEM((rows, width), F32),
        in_specs=[SMEM_SPEC, VMEM_SPEC, VMEM_SPEC, HBM_SPEC],
        out_specs=VMEM_SPEC,
        scratch_shapes=[
            pltpu.VMEM((depth, d_block, width), BF16),
            pltpu.SemaphoreType.DMA((depth,)),
        ],
        compiler_params=pltpu.CompilerParams(vmem_limit_bytes=32 * MIB),
        cost_estimate=pl.CostEstimate(
            flops=2 * rows * width * d_steps * d_block,
            bytes_accessed=2 * width * d_steps * d_block, transcendentals=0,
        ),
        name="own_half",
    )(place, *in_vmem(hidden, weight), *in_hbm(down_weight))


def split_kernel(count, fold, own_ref, *refs):
    got, (keep_ref, *sends), total = refs[:count], refs[count:-1], refs[-1]
    value = own_ref[...]
    for ref in got:
        value = value + ref[...].astype(F32)
    total[...] = value
    size, width = keep_ref.shape
    keep_ref[...] = total[:size, :]
    for u, send in enumerate(sends, 1):
        part = total[u * size:(u + 1) * size, :]
        if fold:
            part = jnp.concatenate(
                [part[:, f * (width // FOLD):(f + 1) * (width // FOLD)] for f in range(FOLD)], axis=0
            )
        send[...] = part.astype(BF16)


def split_rows(own, got, parts, fold=False):
    rows, width = own.shape
    size = rows // parts
    sent = (FOLD * size, width // FOLD) if fold else (size, width)
    return pl.pallas_call(
        functools.partial(split_kernel, len(got), fold),
        out_shape=(pltpu.VMEM((size, width), F32),)
        + (pltpu.VMEM(sent, BF16),) * (parts - 1),
        in_specs=[VMEM_SPEC] * (1 + len(got)),
        out_specs=(VMEM_SPEC,) * parts,
        scratch_shapes=[pltpu.VMEM((rows, width), F32)],
        compiler_params=pltpu.CompilerParams(vmem_limit_bytes=32 * MIB),
        name="split_rows",
    )(*in_vmem(own, *got))


def finish_kernel(carried_ref, own_ref, got_ref, out_ref, folded):
    tok, width = carried_ref.shape
    fold_width = width // FOLD
    folded[...] = got_ref[...].astype(F32)
    for f in range(FOLD):
        at = slice(f * fold_width, (f + 1) * fold_width)
        value = carried_ref[:, at] + own_ref[:, at] + folded[f * tok:(f + 1) * tok, :]
        out_ref[:, at] = value.astype(BF16)


def finish(carried, own, got):
    tok, width = carried.shape
    return pl.pallas_call(
        finish_kernel,
        out_shape=jax.ShapeDtypeStruct((tok, width), BF16),
        in_specs=[VMEM_SPEC] * 3,
        out_specs=VMEM_SPEC,
        scratch_shapes=[pltpu.VMEM((FOLD * tok, width // FOLD), F32)],
        compiler_params=pltpu.CompilerParams(vmem_limit_bytes=8 * MIB),
        name="finish",
    )(*in_vmem(carried, own, got))


def on_device(
    residual, queries, key_cache, value_cache, new_key, new_value, cache_lengths,
    norm_gain, router, routes, gate_weight, up_weight, down_weight,
):
    nodes = lax.axis_size("node")
    per_plane = nodes // EXPERTS
    place = jnp.stack(
        [lax.axis_index("shard"), lax.axis_index("node") // per_plane]
    ).astype(jnp.int32)

    def to_plane(array, s):
        perm = [
            (e * per_plane + j, (e ^ s) * per_plane + j)
            for e in range(EXPERTS) for j in range(per_plane)
        ]
        return lax.ppermute(array, "node", perm)

    def to_column(array, u):
        perm = [
            (e * per_plane + j, e * per_plane + (j + u) % per_plane)
            for e in range(EXPERTS) for j in range(per_plane)
        ]
        return lax.ppermute(array, "node", perm)

    def to_core(array):
        return lax.ppermute(array, "shard", [(0, 1), (1, 0)])

    steps = gate_weight.shape[0] // row_block(gate_weight)
    counts = [n * steps // 12 for n in (1, 2, 2, 3)]

    def load(i, after):
        *piece, token = load_blocks(sum(counts[:i]), counts[i], after, gate_weight, up_weight)
        return piece, token

    carried, payload, *first = attend(
        counts[0], place, cache_lengths, routes.T, queries, key_cache, value_cache, new_key, new_value,
        residual, norm_gain.reshape(1, -1), router.T, gate_weight, up_weight,
    )
    far = to_plane(payload, 2)
    second, token = load(1, payload)
    pair = join(payload, far, token)
    near = to_plane(pair, 1)
    third, token = load(2, pair)
    column = join(pair, near, token)
    mine = [column] + [to_column(column, u) for u in range(1, per_plane)]
    fourth, token = load(3, column)
    mine = [column] + relay(mine[1:], token)
    other = [to_core(array) for array in mine]
    hidden, weight, leaving = experts(
        place, mine, other, gate_weight, up_weight, down_weight, counts,
        [first, second, third, fourth],
    )
    arrived = to_core(leaving)
    staying = own_half(place, hidden, weight, down_weight)
    keep, *sends = split_rows(staying, [arrived], per_plane)
    got = [to_column(sends[u - 1], -u) for u in range(1, per_plane)]
    keep, send = split_rows(keep, got, 2)
    keep, send = split_rows(keep, [to_plane(send, 1)], 2, fold=True)
    return finish(carried, keep, to_plane(send, 2))


def solution(mesh):
    rows = ("replica", "node")
    in_specs = (
        P(rows, "shard"),
        P(rows, "shard"),
        P(rows, None, "shard"),
        P(rows, None, "shard"),
        P(rows, "shard"),
        P(rows, "shard"),
        P(rows),
        P(),
        P(),
        P(rows, None),
        P(None, ("node", "shard")),
        P(None, ("node", "shard")),
        P(("node", "shard"), None),
    )
    return jax.shard_map(
        on_device,
        mesh=mesh,
        in_specs=in_specs,
        out_specs=P(rows, "shard"),
        check_vma=False,
    )
```

```python
import functools
import math

import jax
import jax.numpy as jnp
from jax import lax
from jax.experimental import pallas as pl
from jax.experimental.pallas import tpu as pltpu
from jax.sharding import PartitionSpec as P

QUERY_HEADS = 48
KV_HEADS = 8
HEAD_DIM = 128
EXPERTS = 4
GROUP = QUERY_HEADS // KV_HEADS
LANES = 128
FOLD = 2
MIB = 1 << 20
F32 = jnp.float32
BF16 = jnp.bfloat16


def whole_spec(array):
    zeros = (0,) * len(array.shape)
    return pl.BlockSpec(array.shape, lambda *_: zeros)


def small(shape, dtype):
    return math.prod(shape) * jnp.dtype(dtype).itemsize <= 17 * MIB // 4


def vmem_array(shape, dtype):
    return pltpu.VMEM(shape, dtype) if small(shape, dtype) else jax.ShapeDtypeStruct(shape, dtype)


def in_vmem(*arrays):
    return [
        pltpu.with_memory_space_constraint(a, pltpu.VMEM) if small(a.shape, a.dtype) else a
        for a in arrays
    ]


def in_hbm(*arrays):
    return [pltpu.with_memory_space_constraint(a, pltpu.HBM) for a in arrays]


VMEM_SPEC = pl.BlockSpec(memory_space=pltpu.VMEM)
SMEM_SPEC = pl.BlockSpec(memory_space=pltpu.SMEM)
HBM_SPEC = pl.BlockSpec(memory_space=pltpu.HBM)
ROUTE_LANE = 3 + 3 * EXPERTS
DOWN_DEPTH = 4


def row_unit(gate_weight):
    return gate_weight.shape[0] // 12


def weight_copies(pairs, first, rows, sems):
    parts = sems.shape[1]
    part = rows // parts
    copies = []
    for i in range(parts):
        for w, (source, target) in enumerate(pairs):
            copies.append(
                pltpu.make_async_copy(
                    source.at[pl.ds(pl.multiple_of(first + i * part, 16), part), :],
                    target.at[pl.ds(i * part, part), :], sems.at[w, i],
                )
            )
    return copies


def load_kernel(first, rows, place_ref, dep_ref, g_hbm, u_hbm, g_vmem, u_vmem, token_ref, sems):
    base = place_ref[0] * (g_hbm.shape[0] // 2) + first
    copies = weight_copies([(g_hbm, g_vmem), (u_hbm, u_vmem)], base, rows, sems)
    for copy in copies:
        copy.start()
    token_ref[...] = jnp.zeros_like(token_ref)
    for copy in copies:
        copy.wait()


def load_rows(first, rows, place, after, gate_weight, up_weight):
    hidden = gate_weight.shape[1]
    piece = pltpu.VMEM((rows, hidden), BF16)
    return pl.pallas_call(
        functools.partial(load_kernel, first, rows),
        out_shape=(piece, piece, pltpu.VMEM((8, LANES), F32)),
        in_specs=[SMEM_SPEC, pl.BlockSpec(memory_space=pl.ANY), HBM_SPEC, HBM_SPEC],
        out_specs=(VMEM_SPEC,) * 3,
        scratch_shapes=[pltpu.SemaphoreType.DMA((2, 4))],
        compiler_params=pltpu.CompilerParams(vmem_limit_bytes=MIB),
        cost_estimate=pl.CostEstimate(flops=0, bytes_accessed=4 * rows * hidden, transcendentals=0),
        name="load_weights",
    )(place, *in_vmem(after), *in_hbm(gate_weight, up_weight))


def join_kernel(a_ref, b_ref, token_ref, out_ref):
    out_ref[...] = jnp.concatenate(
        [a_ref[...].astype(F32), b_ref[...].astype(F32)], axis=0
    ).astype(BF16)


def join(a, b, token):
    return pl.pallas_call(
        join_kernel,
        out_shape=vmem_array((a.shape[0] + b.shape[0], a.shape[1]), BF16),
        in_specs=[VMEM_SPEC] * 3,
        out_specs=VMEM_SPEC,
        compiler_params=pltpu.CompilerParams(vmem_limit_bytes=(2 if a.shape[0] < 256 else 24) * MIB),
        name="join",
    )(*in_vmem(a, b, token))


def relay_kernel(count, *refs):
    del refs


def relay(arrays, token):
    count = len(arrays)
    return list(pl.pallas_call(
        functools.partial(relay_kernel, count),
        out_shape=tuple(pltpu.VMEM(a.shape, a.dtype) for a in arrays),
        in_specs=[VMEM_SPEC] * (count + 1),
        out_specs=(VMEM_SPEC,) * count,
        input_output_aliases={i: i for i in range(count)},
        compiler_params=pltpu.CompilerParams(vmem_limit_bytes=MIB),
        name="relay",
    )(*in_vmem(*arrays, token)))


def split_three(value):
    first = value.astype(BF16).astype(F32)
    second = (value - first).astype(BF16).astype(F32)
    return first, second, value - first - second


def attend_kernel(
    ahead,
    place_ref, len_ref, routes_ref, q_hbm, k_hbm, v_hbm, nk_hbm, nv_hbm, res_hbm, gain_hbm, rt_hbm,
    g_hbm, u_hbm,
    carried_ref, pay_ref, g_vmem, u_vmem,
    q_ref, k_ref, v_ref, nk_ref, nv_ref, res_ref, gain_ref, rt_ref,
    q_scr, o_scr, nk_scr, nv_scr, pay_scr, sems, w_sems,
):
    tok, width = q_ref.shape
    cache_len, kv_width = k_ref.shape[1], k_ref.shape[2]
    heads = width // HEAD_DIM
    groups = kv_width // HEAD_DIM
    fold_width = width // FOLD
    scaling = 1.0 / math.sqrt(HEAD_DIM)
    columns = pl.ds(pl.multiple_of(place_ref[0] * width, LANES), width)
    half = tok // 2
    first, rest = pl.ds(0, half), pl.ds(half, tok - half)
    moves = [
        (q_hbm, q_ref), (nk_hbm, nk_ref),
        (k_hbm.at[first], k_ref.at[first]), (k_hbm.at[rest], k_ref.at[rest]),
        (v_hbm.at[first], v_ref.at[first]), (v_hbm.at[rest], v_ref.at[rest]),
        (nv_hbm, nv_ref), (res_hbm, res_ref),
        (gain_hbm.at[:, columns], gain_ref), (rt_hbm.at[:, columns], rt_ref),
    ]
    copies = [pltpu.make_async_copy(a, b, sems.at[i]) for i, (a, b) in enumerate(moves)]
    for copy in copies:
        copy.start()
    weights = weight_copies(
        [(g_hbm, g_vmem), (u_hbm, u_vmem)], place_ref[0] * (g_hbm.shape[0] // 2), ahead, w_sems
    )
    for copy in weights:
        copy.start()
    copies[0].wait()
    copies[1].wait()
    for h in range(heads):
        q_scr[h * tok:(h + 1) * tok, :] = q_ref[:, h * HEAD_DIM:(h + 1) * HEAD_DIM].astype(F32)
    nk_scr[...] = nk_ref[...].astype(F32)
    row_group = lax.broadcasted_iota(jnp.int32, (heads, HEAD_DIM), 0) // GROUP
    position = lax.broadcasted_iota(jnp.int32, (heads, cache_len), 1)
    scores, fresh = [], []
    for t in range(tok):
        if t == 0:
            copies[2].wait()
        if t == half:
            copies[3].wait()
        q_rows = q_scr[pl.ds(t, heads, stride=tok), :]
        q_wide = jnp.concatenate(
            [jnp.where(row_group == g, q_rows, 0.0) for g in range(groups)], axis=1
        )
        scores.append(
            lax.dot_general(
                q_wide.astype(BF16), k_ref[t], (((1,), (1,)), ((), ())),
                preferred_element_type=F32,
            ) * scaling
        )
        fresh.append(
            jnp.sum(q_wide * nk_scr[pl.ds(t, 1), :], axis=1, keepdims=True) * scaling
        )
    terms, fresh_terms, totals = [], [], []
    for t in range(tok):
        score = jnp.where(position < len_ref[t], scores[t], -1e30)
        largest = jnp.maximum(jnp.max(score, axis=1, keepdims=True), fresh[t])
        term = jnp.exp(score - largest)
        fresh_term = jnp.exp(fresh[t] - largest)
        totals.append(jnp.sum(term, axis=1, keepdims=True) + fresh_term)
        terms.append(term.astype(BF16))
        fresh_terms.append(fresh_term.astype(BF16).astype(F32))
    copies[6].wait()
    nv_scr[...] = nv_ref[...].astype(F32)
    for t in range(tok):
        if t == 0:
            copies[4].wait()
        if t == half:
            copies[5].wait()
        wide = jnp.dot(terms[t], v_ref[t], preferred_element_type=F32)
        wide = wide + fresh_terms[t] * nv_scr[pl.ds(t, 1), :]
        picked = wide[:, :HEAD_DIM]
        for g in range(1, groups):
            picked = jnp.where(
                row_group == g, wide[:, g * HEAD_DIM:(g + 1) * HEAD_DIM], picked
            )
        o_scr[pl.ds(t, heads, stride=tok), :] = picked / totals[t]
    for copy in copies[7:]:
        copy.wait()
    for h in range(heads):
        cols = slice(h * HEAD_DIM, (h + 1) * HEAD_DIM)
        carried_ref[:, cols] = res_ref[:, cols].astype(F32) + o_scr[h * tok:(h + 1) * tok, :]
    carried = carried_ref[...]
    scaled = carried * gain_ref[...]
    rounded = scaled.astype(BF16).astype(F32)
    router = rt_ref[...].astype(F32)
    for f in range(FOLD):
        pay_scr[f * tok:(f + 1) * tok, :fold_width] = scaled[:, f * fold_width:(f + 1) * fold_width]
    lane = lax.broadcasted_iota(jnp.int32, (tok, LANES), 1)
    row = lax.broadcasted_iota(jnp.int32, (tok, LANES), 0)
    sums = [jnp.sum(carried * carried, axis=1, keepdims=True)]
    for e in range(EXPERTS):
        sums.append(jnp.sum(rounded * router[e:e + 1, :], axis=1, keepdims=True))
    extra = jnp.zeros((tok, LANES), F32)
    for i, total in enumerate(sums):
        for j, term in enumerate(split_three(total)):
            extra = jnp.where(lane == 3 * i + j, term, extra)
    for t in range(tok):
        for i in range(2):
            extra = jnp.where(
                jnp.logical_and(row == t, lane == ROUTE_LANE + i),
                routes_ref[i, t].astype(F32), extra,
            )
    for f in range(FOLD):
        pay_scr[f * tok:(f + 1) * tok, fold_width:] = extra
    pay_ref[...] = pay_scr[...].astype(BF16)
    for copy in weights:
        copy.wait()


def attend(
    ahead, place, lengths, routes_t, queries, key_cache, value_cache, new_key, new_value,
    residual, gain, router_t, gate_weight, up_weight,
):
    tok, width = queries.shape
    kv_width = new_key.shape[1]
    heads = width // HEAD_DIM
    wide = width // FOLD + LANES
    piece = pltpu.VMEM((ahead, gate_weight.shape[1]), BF16)
    here = [
        pltpu.VMEM(a.shape, a.dtype)
        for a in (queries, key_cache, value_cache, new_key, new_value, residual)
    ]
    return pl.pallas_call(
        functools.partial(attend_kernel, ahead),
        out_shape=(
            pltpu.VMEM((tok, width), F32),
            pltpu.VMEM((FOLD * tok, wide), BF16),
            piece,
            piece,
        ),
        in_specs=[SMEM_SPEC] * 3 + [HBM_SPEC] * 10,
        out_specs=(VMEM_SPEC,) * 4,
        scratch_shapes=here + [
            pltpu.VMEM((1, width), F32),
            pltpu.VMEM((EXPERTS, width), BF16),
            pltpu.VMEM((heads * tok, HEAD_DIM), F32),
            pltpu.VMEM((heads * tok, HEAD_DIM), F32),
            pltpu.VMEM((tok, kv_width), F32),
            pltpu.VMEM((tok, kv_width), F32),
            pltpu.VMEM((FOLD * tok, wide), F32),
            pltpu.SemaphoreType.DMA((10,)),
            pltpu.SemaphoreType.DMA((2, 2)),
        ],
        compiler_params=pltpu.CompilerParams(vmem_limit_bytes=10 * MIB),
        cost_estimate=pl.CostEstimate(flops=10**8, bytes_accessed=8 * 10**6, transcendentals=10**5),
        name="attend",
    )(
        place,
        *in_hbm(
            lengths, routes_t, queries, key_cache, value_cache, new_key, new_value, residual, gain, router_t,
            gate_weight, up_weight,
        ),
    )


def block_rows(arrays, swap, tok):
    per_array = arrays[0].shape[0] // (FOLD * tok)
    places = [(array, i * FOLD * tok) for array in arrays for i in range(per_array)]
    if swap:
        quarter = len(places) // 4
        places = (
            places[:quarter] + places[2 * quarter:3 * quarter]
            + places[quarter:2 * quarter] + places[3 * quarter:]
        )
    return places


def unfold(arrays, swap, tok, x_scr, f_scr):
    fold_width = f_scr.shape[1]
    for f in range(FOLD):
        for i, (array, start) in enumerate(block_rows(arrays, swap, tok)):
            block = array[start:start + FOLD * tok, :fold_width].astype(F32)
            f_scr[i * tok:(i + 1) * tok, :] = block[f * tok:(f + 1) * tok, :]
        x_scr[:, f * fold_width:(f + 1) * fold_width] = f_scr[...].astype(BF16)


def first_half_kernel(
    heights, tok, place_ref, a_ref, b_ref, *refs
):
    pieces = [refs[2 * i:2 * i + 2] for i in range(len(heights))]
    g_hbm, u_hbm, gate_ref, up_ref, *later, x_scr, f_scr, sems = refs[2 * len(heights):]
    half = g_hbm.shape[0] // 2
    copies = []
    for i in range(len(later) // 2):
        height = later[2 * i].shape[0]
        copies += weight_copies(
            [(g_hbm, later[2 * i]), (u_hbm, later[2 * i + 1])],
            (1 - place_ref[0]) * half + i * height, height, sems.at[i],
        )
    for copy in copies:
        copy.start()
    unfold([a_ref, b_ref], False, tok, x_scr, f_scr)
    first = 0
    for i, (height, (g_ref, u_ref)) in enumerate(zip(heights, pieces)):
        rows = x_scr[:, first:first + height]
        for weight, out in ((g_ref, gate_ref), (u_ref, up_ref)):
            part = jnp.dot(rows, weight[...], preferred_element_type=F32)
            out[...] = part if i == 0 else out[...] + part
        first += height
    for copy in copies:
        copy.wait()


def first_half(tok, place, mine, pieces, gate_weight, up_weight):
    heights = tuple(p[0].shape[0] for p in pieces)
    rows = sum(a.shape[0] for a in mine) // FOLD
    width, units = gate_weight.shape
    fold_width = mine[0].shape[1] - LANES
    acc, later = pltpu.VMEM((rows, units), F32), pltpu.VMEM((2 * row_unit(gate_weight), units), BF16)
    return pl.pallas_call(
        functools.partial(first_half_kernel, heights, tok),
        out_shape=(acc, acc, later, later),
        in_specs=[SMEM_SPEC] + [VMEM_SPEC] * (2 + 2 * len(heights)) + [HBM_SPEC] * 2,
        out_specs=(VMEM_SPEC,) * 4,
        scratch_shapes=[
            pltpu.VMEM((rows, width // 2), BF16),
            pltpu.VMEM((rows, fold_width), F32),
            pltpu.SemaphoreType.DMA((1, 2, 4)),
        ],
        compiler_params=pltpu.CompilerParams(vmem_limit_bytes=(6 if rows < 256 else 32) * MIB),
        cost_estimate=pl.CostEstimate(
            flops=2 * rows * width * units, bytes_accessed=width * units, transcendentals=0
        ),
        name="first_half",
    )(
        place, *in_vmem(*mine, *[p for pair in pieces for p in pair]),
        *in_hbm(gate_weight, up_weight),
    )


def second_half_kernel(
    tok, place_ref, a_ref, b_ref, oa_ref, ob_ref, gate_in, up_in, *refs
):
    (g_ref, u_ref, g_hbm, u_hbm, d_hbm, staying_ref, leaving_ref,
     x_scr, f_scr, gate_acc, up_acc, h_scr, gu_scr, ring, gu_sems, sems) = refs
    rows, units = gate_acc.shape
    width = staying_ref.shape[1]
    fold_width = f_scr.shape[1]
    side = place_ref[0]
    depth, d_block, d_wide = ring.shape
    k_steps, n_steps = units // d_block, width // d_wide
    total = 2 * n_steps * k_steps

    def down_copy(i):
        n, k = i // k_steps, i % k_steps
        half = jnp.where(n < n_steps, 1 - side, side)
        column = half * width + lax.rem(n, n_steps) * d_wide
        slot = lax.rem(i, depth)
        return pltpu.make_async_copy(
            d_hbm.at[
                pl.ds(pl.multiple_of(k * d_block, d_block), d_block),
                pl.ds(pl.multiple_of(column, LANES), d_wide),
            ],
            ring.at[slot], sems.at[slot],
        )

    height = g_ref.shape[0]
    blocks = gu_scr.shape[0]
    copies = [
        weight_copies(
            [(g_hbm, gu_scr.at[i, 0]), (u_hbm, gu_scr.at[i, 1])],
            (1 - side) * width + (i + 1) * height, height, gu_sems.at[i],
        )
        for i in range(blocks)
    ]
    for group in copies:
        for copy in group:
            copy.start()
    for i in range(min(depth, total)):
        down_copy(jnp.int32(i)).start()
    unfold([oa_ref, ob_ref], True, tok, x_scr, f_scr)
    part = x_scr[:, :height]
    gate_acc[...] = gate_in[...] + jnp.dot(part, g_ref[...], preferred_element_type=F32)
    up_acc[...] = up_in[...] + jnp.dot(part, u_ref[...], preferred_element_type=F32)
    for i in range(blocks):
        for copy in copies[i]:
            copy.wait()
        part = x_scr[:, (i + 1) * height:(i + 2) * height]
        gate_acc[...] += jnp.dot(part, gu_scr[i, 0], preferred_element_type=F32)
        up_acc[...] += jnp.dot(part, gu_scr[i, 1], preferred_element_type=F32)

    for at, arrays, swap in ((0, [a_ref, b_ref], False), (LANES, [oa_ref, ob_ref], True)):
        for i, (array, start) in enumerate(block_rows(arrays, swap, tok)):
            extra = array[start:start + FOLD * tok, fold_width:].astype(F32)
            f_scr[i * tok:(i + 1) * tok, at:at + LANES] = extra[:tok, :]
    own = f_scr[:, :LANES]
    both = own + f_scr[:, LANES:2 * LANES]
    lane = lax.broadcasted_iota(jnp.int32, (rows, LANES), 1)

    def pick(values, mask):
        return jnp.sum(jnp.where(mask, values, 0.0), axis=1, keepdims=True)

    scale = lax.rsqrt(pick(both, lane < 3) * (1.0 / (2 * width)) + 1e-05)
    first, second = pick(own, lane == ROUTE_LANE), pick(own, lane == ROUTE_LANE + 1)
    expert_of = (lane - 3) // 3
    logit_lane = jnp.logical_and(lane >= 3, lane < ROUTE_LANE)

    def logit_at(route):
        return pick(both, jnp.logical_and(logit_lane, expert_of == route.astype(jnp.int32))) * scale

    share = 1.0 / (1.0 + jnp.exp(logit_at(second) - logit_at(first)))
    here = place_ref[1].astype(F32)
    weight = jnp.where(first == here, share, 0.0) + jnp.where(second == here, 1.0 - share, 0.0)

    gate = gate_acc[...] * scale
    h_scr[...] = (gate / (1.0 + jnp.exp(-gate)) * (up_acc[...] * scale)).astype(BF16)

    def columns(n):
        value = None
        for k in range(k_steps):
            i = n * k_steps + k
            slot = lax.rem(i, depth)
            down_copy(i).wait()
            part = jnp.dot(
                h_scr[:, k * d_block:(k + 1) * d_block], ring[slot], preferred_element_type=F32
            )
            value = part if value is None else value + part

            @pl.when(i + depth < total)
            def _():
                down_copy(i + depth).start()

        return value * weight

    def leave(n, _):
        value = columns(n)
        quarter = rows // 4
        value = jnp.concatenate(
            [value[q * quarter:(q + 1) * quarter, :] for q in (0, 2, 1, 3)], axis=0
        )
        leaving_ref[:, pl.ds(pl.multiple_of(n * d_wide, LANES), d_wide)] = value.astype(BF16)
        return 0

    def stay(n, _):
        staying_ref[:, pl.ds(pl.multiple_of(n * d_wide, LANES), d_wide)] = columns(n + n_steps)
        return 0

    lax.fori_loop(0, n_steps, leave, 0)
    lax.fori_loop(0, n_steps, stay, 0)


def second_half(tok, place, mine, other, sums, weights, gate_weight, up_weight, down_weight):
    rows, units = sums[0].shape
    width = down_weight.shape[1] // 2
    fold_width = mine[0].shape[1] - LANES
    d_block, d_wide = math.gcd(1024, units), math.gcd(1536, width)
    total = 2 * (width // d_wide) * (units // d_block)
    depth = min(DOWN_DEPTH, total)
    height = weights[0].shape[0]
    blocks = width // height - 1
    return pl.pallas_call(
        functools.partial(second_half_kernel, tok),
        out_shape=(vmem_array((rows, width), F32), vmem_array((rows, width), BF16)),
        in_specs=[SMEM_SPEC] + [VMEM_SPEC] * 8 + [HBM_SPEC] * 3,
        out_specs=(VMEM_SPEC,) * 2,
        scratch_shapes=[
            pltpu.VMEM((rows, width), BF16),
            pltpu.VMEM((rows, fold_width), F32),
            pltpu.VMEM((rows, units), F32),
            pltpu.VMEM((rows, units), F32),
            pltpu.VMEM((rows, units), BF16),
            pltpu.VMEM((blocks, 2, height, units), BF16),
            pltpu.VMEM((depth, d_block, d_wide), BF16),
            pltpu.SemaphoreType.DMA((blocks, 2, 4)),
            pltpu.SemaphoreType.DMA((depth,)),
        ],
        compiler_params=pltpu.CompilerParams(vmem_limit_bytes=(38 if rows < 256 else 48) * MIB),
        cost_estimate=pl.CostEstimate(
            flops=6 * rows * width * units, bytes_accessed=4 * width * units, transcendentals=0
        ),
        name="second_half",
    )(
        place, *in_vmem(*mine, *other, *sums, *weights),
        *in_hbm(gate_weight, up_weight, down_weight),
    )


def split_kernel(fold, own_ref, got_ref, keep_ref, send_ref, total):
    total[...] = own_ref[...] + got_ref[...].astype(F32)
    size, width = keep_ref.shape
    keep_ref[...] = total[:size, :]
    part = total[size:, :]
    if fold:
        part = jnp.concatenate(
            [part[:, f * (width // FOLD):(f + 1) * (width // FOLD)] for f in range(FOLD)], axis=0
        )
    send_ref[...] = part.astype(BF16)


def split_rows(own, got, fold=False):
    rows, width = own.shape
    size = rows // 2
    sent = (FOLD * size, width // FOLD) if fold else (size, width)
    return pl.pallas_call(
        functools.partial(split_kernel, fold),
        out_shape=(vmem_array((size, width), F32), vmem_array(sent, BF16)),
        in_specs=[VMEM_SPEC] * 2,
        out_specs=(VMEM_SPEC,) * 2,
        scratch_shapes=[pltpu.VMEM((rows, width), F32)],
        compiler_params=pltpu.CompilerParams(vmem_limit_bytes=(8 if rows < 256 else 32) * MIB),
        name="split_rows",
    )(*in_vmem(own, got))


def finish_kernel(carried_ref, own_ref, got_ref, out_ref, folded):
    tok, width = carried_ref.shape
    fold_width = width // FOLD
    folded[...] = got_ref[...].astype(F32)
    for f in range(FOLD):
        at = slice(f * fold_width, (f + 1) * fold_width)
        value = carried_ref[:, at] + own_ref[:, at] + folded[f * tok:(f + 1) * tok, :]
        out_ref[:, at] = value.astype(BF16)


def finish(carried, own, got):
    tok, width = carried.shape
    return pl.pallas_call(
        finish_kernel,
        out_shape=jax.ShapeDtypeStruct((tok, width), BF16),
        in_specs=[VMEM_SPEC] * 3,
        out_specs=VMEM_SPEC,
        scratch_shapes=[pltpu.VMEM((FOLD * tok, width // FOLD), F32)],
        compiler_params=pltpu.CompilerParams(vmem_limit_bytes=8 * MIB),
        name="finish",
    )(*in_vmem(carried, own, got))


def on_device(
    residual, queries, key_cache, value_cache, new_key, new_value, cache_lengths,
    norm_gain, router, routes, gate_weight, up_weight, down_weight,
):
    nodes = lax.axis_size("node")
    per_plane = nodes // EXPERTS
    place = jnp.stack(
        [lax.axis_index("shard"), lax.axis_index("node") // per_plane]
    ).astype(jnp.int32)

    stages = nodes.bit_length() - 1
    masks = [nodes >> (s + 1) for s in range(stages)]
    routes_of = (masks, masks[:-2] + masks[:-3:-1])

    def exchange(array, stage):
        perm = [
            (2 * n + c, 2 * (n ^ routes_of[c][stage]) + c) for n in range(nodes) for c in range(2)
        ]
        return lax.ppermute(array, ("node", "shard"), perm)

    def to_core(array):
        return lax.ppermute(array, "shard", [(0, 1), (1, 0)])

    unit = row_unit(gate_weight)
    tok = residual.shape[0]
    heights = [unit, 2 * unit, unit, 2 * unit]
    held, payload, *piece = attend(
        heights[0], place, cache_lengths, routes.T, queries, key_cache, value_cache, new_key, new_value,
        residual, norm_gain.reshape(1, -1), router.T, gate_weight, up_weight,
    )
    carried, pieces, first, token = held, [piece], heights[0], None
    for stage in range(stages):
        got = exchange(payload, stage)
        if len(pieces) < len(heights):
            height = heights[len(pieces)]
            *piece, token = load_rows(first, height, place, payload, gate_weight, up_weight)
            pieces.append(piece)
            first += height
        if stage < stages - 1:
            payload = join(payload, got, token)
    mine = [payload, *relay([got], token)]
    other = [to_core(array) for array in mine]
    gate, up, *weights = first_half(tok, place, mine, pieces, gate_weight, up_weight)
    staying, leaving = second_half(
        tok, place, mine, other, (gate, up), weights, gate_weight, up_weight, down_weight
    )
    keep, send = split_rows(staying, to_core(leaving))
    for stage in range(stages - 1, 0, -1):
        keep, send = split_rows(keep, exchange(send, stage), fold=stage == 1)
    return finish(carried, keep, exchange(send, 0))


def solution(mesh):
    rows = ("replica", "node")
    in_specs = (
        P(rows, "shard"),
        P(rows, "shard"),
        P(rows, None, "shard"),
        P(rows, None, "shard"),
        P(rows, "shard"),
        P(rows, "shard"),
        P(rows),
        P(),
        P(),
        P(rows, None),
        P(None, ("node", "shard")),
        P(None, ("node", "shard")),
        P(("node", "shard"), None),
    )
    return jax.shard_map(
        on_device,
        mesh=mesh,
        in_specs=in_specs,
        out_specs=P(rows, "shard"),
        check_vma=False,
    )
```

```python
import functools
import math

import jax
import jax.numpy as jnp
from jax import lax
from jax.experimental import pallas as pl
from jax.experimental.pallas import tpu as pltpu
from jax.sharding import PartitionSpec as P

QUERY_HEADS = 48
KV_HEADS = 8
HEAD_DIM = 128
EXPERTS = 4
GROUP = QUERY_HEADS // KV_HEADS
LANES = 128
FOLD = 2
MIB = 1 << 20
F32 = jnp.float32
BF16 = jnp.bfloat16


def whole_spec(array):
    zeros = (0,) * len(array.shape)
    return pl.BlockSpec(array.shape, lambda *_: zeros)


def small(shape, dtype):
    return math.prod(shape) * jnp.dtype(dtype).itemsize <= 17 * MIB // 4


def vmem_array(shape, dtype):
    return pltpu.VMEM(shape, dtype) if small(shape, dtype) else jax.ShapeDtypeStruct(shape, dtype)


def in_vmem(*arrays):
    return [
        pltpu.with_memory_space_constraint(a, pltpu.VMEM) if small(a.shape, a.dtype) else a
        for a in arrays
    ]


def in_hbm(*arrays):
    return [pltpu.with_memory_space_constraint(a, pltpu.HBM) for a in arrays]


VMEM_SPEC = pl.BlockSpec(memory_space=pltpu.VMEM)
SMEM_SPEC = pl.BlockSpec(memory_space=pltpu.SMEM)
HBM_SPEC = pl.BlockSpec(memory_space=pltpu.HBM)
ROUTE_LANE = 3 + 3 * EXPERTS
GATE_DEPTH = 4
DOWN_DEPTH = 4


def row_unit(gate_weight):
    return gate_weight.shape[0] // 12


def pair_copies(sources, targets, first, rows, sems):
    at = pl.ds(pl.multiple_of(first, 16), rows)
    return [
        pltpu.make_async_copy(source.at[at, :], target, sems.at[i])
        for i, (source, target) in enumerate(zip(sources, targets))
    ]


def split_three(value):
    first = value.astype(BF16).astype(F32)
    second = (value - first).astype(BF16).astype(F32)
    return first, second, value - first - second


def attend_kernel(
    place_ref, len_ref, routes_ref, q_hbm, k_hbm, v_hbm, nk_hbm, nv_hbm, res_hbm, gain_hbm, rt_hbm,
    carried_ref, pay_ref,
    q_ref, k_ref, v_ref, nk_ref, nv_ref, res_ref, gain_ref, rt_ref,
    q_scr, o_scr, nk_scr, nv_scr, pay_scr, sems,
):
    tok, width = q_ref.shape
    cache_len, kv_width = k_ref.shape[1], k_ref.shape[2]
    heads = width // HEAD_DIM
    groups = kv_width // HEAD_DIM
    fold_width = width // FOLD
    scaling = 1.0 / math.sqrt(HEAD_DIM)
    columns = pl.ds(pl.multiple_of(place_ref[0] * width, LANES), width)
    half = tok // 2
    first, rest = pl.ds(0, half), pl.ds(half, tok - half)
    moves = [
        (q_hbm, q_ref), (nk_hbm, nk_ref),
        (k_hbm.at[first], k_ref.at[first]), (k_hbm.at[rest], k_ref.at[rest]),
        (v_hbm.at[first], v_ref.at[first]), (v_hbm.at[rest], v_ref.at[rest]),
        (nv_hbm, nv_ref), (res_hbm, res_ref),
        (gain_hbm.at[:, columns], gain_ref), (rt_hbm.at[:, columns], rt_ref),
    ]
    copies = [pltpu.make_async_copy(a, b, sems.at[i]) for i, (a, b) in enumerate(moves)]
    for copy in copies:
        copy.start()
    copies[0].wait()
    copies[1].wait()
    for h in range(heads):
        q_scr[h * tok:(h + 1) * tok, :] = q_ref[:, h * HEAD_DIM:(h + 1) * HEAD_DIM].astype(F32)
    nk_scr[...] = nk_ref[...].astype(F32)
    row_group = lax.broadcasted_iota(jnp.int32, (heads, HEAD_DIM), 0) // GROUP
    position = lax.broadcasted_iota(jnp.int32, (heads, cache_len), 1)
    scores, fresh = [], []
    for t in range(tok):
        if t == 0:
            copies[2].wait()
        if t == half:
            copies[3].wait()
        q_rows = q_scr[pl.ds(t, heads, stride=tok), :]
        q_wide = jnp.concatenate(
            [jnp.where(row_group == g, q_rows, 0.0) for g in range(groups)], axis=1
        )
        scores.append(
            lax.dot_general(
                q_wide.astype(BF16), k_ref[t], (((1,), (1,)), ((), ())),
                preferred_element_type=F32,
            ) * scaling
        )
        fresh.append(
            jnp.sum(q_wide * nk_scr[pl.ds(t, 1), :], axis=1, keepdims=True) * scaling
        )
    terms, fresh_terms, totals = [], [], []
    for t in range(tok):
        score = jnp.where(position < len_ref[t], scores[t], -1e30)
        largest = jnp.maximum(jnp.max(score, axis=1, keepdims=True), fresh[t])
        term = jnp.exp(score - largest)
        fresh_term = jnp.exp(fresh[t] - largest)
        totals.append(jnp.sum(term, axis=1, keepdims=True) + fresh_term)
        terms.append(term.astype(BF16))
        fresh_terms.append(fresh_term.astype(BF16).astype(F32))
    copies[6].wait()
    nv_scr[...] = nv_ref[...].astype(F32)
    for t in range(tok):
        if t == 0:
            copies[4].wait()
        if t == half:
            copies[5].wait()
        wide = jnp.dot(terms[t], v_ref[t], preferred_element_type=F32)
        wide = wide + fresh_terms[t] * nv_scr[pl.ds(t, 1), :]
        picked = wide[:, :HEAD_DIM]
        for g in range(1, groups):
            picked = jnp.where(
                row_group == g, wide[:, g * HEAD_DIM:(g + 1) * HEAD_DIM], picked
            )
        o_scr[pl.ds(t, heads, stride=tok), :] = picked / totals[t]
    for copy in copies[7:]:
        copy.wait()
    for h in range(heads):
        cols = slice(h * HEAD_DIM, (h + 1) * HEAD_DIM)
        carried_ref[:, cols] = res_ref[:, cols].astype(F32) + o_scr[h * tok:(h + 1) * tok, :]
    carried = carried_ref[...]
    scaled = carried * gain_ref[...]
    rounded = scaled.astype(BF16).astype(F32)
    router = rt_ref[...].astype(F32)
    for f in range(FOLD):
        pay_scr[f * tok:(f + 1) * tok, :fold_width] = scaled[:, f * fold_width:(f + 1) * fold_width]
    lane = lax.broadcasted_iota(jnp.int32, (tok, LANES), 1)
    row = lax.broadcasted_iota(jnp.int32, (tok, LANES), 0)
    sums = [jnp.sum(carried * carried, axis=1, keepdims=True)]
    for e in range(EXPERTS):
        sums.append(jnp.sum(rounded * router[e:e + 1, :], axis=1, keepdims=True))
    extra = jnp.zeros((tok, LANES), F32)
    for i, total in enumerate(sums):
        for j, term in enumerate(split_three(total)):
            extra = jnp.where(lane == 3 * i + j, term, extra)
    for t in range(tok):
        for i in range(2):
            extra = jnp.where(
                jnp.logical_and(row == t, lane == ROUTE_LANE + i),
                routes_ref[i, t].astype(F32), extra,
            )
    for f in range(FOLD):
        pay_scr[f * tok:(f + 1) * tok, fold_width:] = extra
    pay_ref[...] = pay_scr[...].astype(BF16)


def attend(
    place, lengths, routes_t, queries, key_cache, value_cache, new_key, new_value,
    residual, gain, router_t,
):
    tok, width = queries.shape
    kv_width = new_key.shape[1]
    heads = width // HEAD_DIM
    wide = width // FOLD + LANES
    here = [
        pltpu.VMEM(a.shape, a.dtype)
        for a in (queries, key_cache, value_cache, new_key, new_value, residual)
    ]
    return pl.pallas_call(
        attend_kernel,
        out_shape=(
            pltpu.VMEM((tok, width), F32),
            pltpu.VMEM((FOLD * tok, wide), BF16),
        ),
        in_specs=[SMEM_SPEC] * 3 + [HBM_SPEC] * 8,
        out_specs=(VMEM_SPEC,) * 2,
        scratch_shapes=here + [
            pltpu.VMEM((1, width), F32),
            pltpu.VMEM((EXPERTS, width), BF16),
            pltpu.VMEM((heads * tok, HEAD_DIM), F32),
            pltpu.VMEM((heads * tok, HEAD_DIM), F32),
            pltpu.VMEM((tok, kv_width), F32),
            pltpu.VMEM((tok, kv_width), F32),
            pltpu.VMEM((FOLD * tok, wide), F32),
            pltpu.SemaphoreType.DMA((10,)),
        ],
        compiler_params=pltpu.CompilerParams(vmem_limit_bytes=10 * MIB),
        cost_estimate=pl.CostEstimate(flops=10**8, bytes_accessed=8 * 10**6, transcendentals=10**5),
        name="attend",
    )(
        place,
        *in_hbm(
            lengths, routes_t, queries, key_cache, value_cache, new_key, new_value, residual, gain, router_t,
        ),
    )


def sources_of(place_ref, count):
    out = []
    for r in range(count):
        left, right = ((sum(m for t, m in enumerate(side) if r >> t & 1)) for side in stage_masks(count))
        out.append(lax.bitwise_xor(place_ref[2], jnp.where(place_ref[0] == 0, left, right)))
    return out


def unfold(place_ref, array, x_scr, f_scr):
    count = array.shape[0]
    tok = array.shape[1] // FOLD
    fold_width = f_scr.shape[1]
    block = x_scr.shape[2]
    per_fold = fold_width // block
    sources = sources_of(place_ref, count)
    for f in range(FOLD):
        for i, source in enumerate(sources):
            rows = array[source][:, :fold_width].astype(F32)
            f_scr[i * tok:(i + 1) * tok, :] = rows[f * tok:(f + 1) * tok, :]
        for p in range(per_fold):
            x_scr[f * per_fold + p] = f_scr[:, p * block:(p + 1) * block].astype(BF16)


def first_half_kernel(
    place_ref, mine_ref, g_hbm, u_hbm, gate_ref, up_ref, g_next, u_next, x_scr, f_scr, ring, sems, next_sems
):
    width = g_hbm.shape[0] // 2
    depth, _, block, _ = ring.shape
    steps = width // block
    base = place_ref[0] * width

    def copies(k):
        slot = lax.rem(k, depth)
        return pair_copies(
            (g_hbm, u_hbm), (ring.at[slot, 0], ring.at[slot, 1]), base + k * block, block, sems.at[slot]
        )

    for k in range(min(depth, steps)):
        for copy in copies(jnp.int32(k)):
            copy.start()
    following = pair_copies(
        (g_hbm, u_hbm), (g_next, u_next), (1 - place_ref[0]) * width, block, next_sems
    )
    unfold(place_ref, mine_ref, x_scr, f_scr)
    gate_ref[...] = jnp.zeros_like(gate_ref)
    up_ref[...] = jnp.zeros_like(up_ref)

    def step(k, _):
        slot = lax.rem(k, depth)
        for copy in copies(k):
            copy.wait()
        gate_ref[...] += jnp.dot(x_scr[k], ring[slot, 0], preferred_element_type=F32)
        up_ref[...] += jnp.dot(x_scr[k], ring[slot, 1], preferred_element_type=F32)

        @pl.when(k + depth < steps)
        def _():
            for copy in copies(k + depth):
                copy.start()

        @pl.when(k + depth == max(steps, depth))
        def _():
            for copy in following:
                copy.start()

        return 0

    lax.fori_loop(0, steps, step, 0)
    for copy in following:
        copy.wait()


def first_half(place, mine, gate_weight, up_weight):
    count, folded, wide = mine.shape
    rows, fold_width = count * folded // FOLD, wide - LANES
    width, units = gate_weight.shape
    block = math.gcd(512, fold_width)
    steps = width // 2 // block
    depth = min(GATE_DEPTH, steps)
    acc, later = pltpu.VMEM((rows, units), F32), pltpu.VMEM((block, units), BF16)
    return pl.pallas_call(
        first_half_kernel,
        out_shape=(acc, acc, later, later),
        in_specs=[SMEM_SPEC, VMEM_SPEC] + [HBM_SPEC] * 2,
        out_specs=(VMEM_SPEC,) * 4,
        scratch_shapes=[
            pltpu.VMEM((steps, rows, block), BF16),
            pltpu.VMEM((rows, fold_width), F32),
            pltpu.VMEM((depth, 2, block, units), BF16),
            pltpu.SemaphoreType.DMA((depth, 2)),
            pltpu.SemaphoreType.DMA((2,)),
        ],
        compiler_params=pltpu.CompilerParams(vmem_limit_bytes=(24 if rows < 256 else 40) * MIB),
        cost_estimate=pl.CostEstimate(
            flops=2 * rows * width * units, bytes_accessed=2 * width * units, transcendentals=0
        ),
        name="first_half",
    )(place, *in_vmem(mine), *in_hbm(gate_weight, up_weight))


def second_half_kernel(
    place_ref, mine_ref, other_ref, gate_in, up_in, g_ref, u_ref, g_hbm, u_hbm, d_hbm,
    staying_ref, leaving_ref,
    x_scr, f_scr, gate_acc, up_acc, h_scr, gu_ring, ring, gu_sems, sems,
):
    rows, units = gate_acc.shape
    width = staying_ref.shape[1]
    count = mine_ref.shape[0]
    tok = rows // count
    fold_width = f_scr.shape[1]
    side = place_ref[0]
    depth, _, d_wide = ring.shape
    per_side = width // d_wide
    total = 2 * per_side
    gu_depth, _, block, _ = gu_ring.shape
    steps = width // block
    base = (1 - side) * width

    def gu_copies(k):
        slot = lax.rem(k - 1, gu_depth)
        return pair_copies(
            (g_hbm, u_hbm), (gu_ring.at[slot, 0], gu_ring.at[slot, 1]), base + k * block, block,
            gu_sems.at[slot],
        )

    def down_copy(n):
        half = jnp.where(n < per_side, 1 - side, side)
        column = half * width + lax.rem(n, per_side) * d_wide
        slot = lax.rem(n, depth)
        return pltpu.make_async_copy(
            d_hbm.at[:, pl.ds(pl.multiple_of(column, LANES), d_wide)], ring.at[slot], sems.at[slot]
        )

    for k in range(1, 1 + min(gu_depth, steps - 1)):
        for copy in gu_copies(jnp.int32(k)):
            copy.start()
    unfold(place_ref, other_ref, x_scr, f_scr)
    gate_acc[...] = gate_in[...] + jnp.dot(x_scr[0], g_ref[...], preferred_element_type=F32)
    up_acc[...] = up_in[...] + jnp.dot(x_scr[0], u_ref[...], preferred_element_type=F32)

    def step(k, _):
        slot = lax.rem(k - 1, gu_depth)
        for copy in gu_copies(k):
            copy.wait()
        gate_acc[...] += jnp.dot(x_scr[k], gu_ring[slot, 0], preferred_element_type=F32)
        up_acc[...] += jnp.dot(x_scr[k], gu_ring[slot, 1], preferred_element_type=F32)

        @pl.when(k + gu_depth < steps)
        def _():
            for copy in gu_copies(k + gu_depth):
                copy.start()

        ahead = k + gu_depth - steps

        @pl.when(jnp.logical_and(ahead >= 0, ahead < depth))
        def _():
            down_copy(ahead).start()

        return 0

    lax.fori_loop(1, steps, step, 0)
    for n in range(max(0, min(gu_depth, steps - 1)), depth):
        down_copy(jnp.int32(n)).start()

    for i, source in enumerate(sources_of(place_ref, count)):
        for at, array in ((0, mine_ref), (LANES, other_ref)):
            extra = array[source][:, fold_width:].astype(F32)
            f_scr[i * tok:(i + 1) * tok, at:at + LANES] = extra[:tok, :]
    own = f_scr[:, :LANES]
    both = own + f_scr[:, LANES:2 * LANES]
    lane = lax.broadcasted_iota(jnp.int32, (rows, LANES), 1)

    def pick(values, mask):
        return jnp.sum(jnp.where(mask, values, 0.0), axis=1, keepdims=True)

    scale = lax.rsqrt(pick(both, lane < 3) * (1.0 / (2 * width)) + 1e-05)
    first, second = pick(own, lane == ROUTE_LANE), pick(own, lane == ROUTE_LANE + 1)
    expert_of = (lane - 3) // 3
    logit_lane = jnp.logical_and(lane >= 3, lane < ROUTE_LANE)

    def logit_at(route):
        return pick(both, jnp.logical_and(logit_lane, expert_of == route.astype(jnp.int32))) * scale

    share = 1.0 / (1.0 + jnp.exp(logit_at(second) - logit_at(first)))
    here = place_ref[1].astype(F32)
    weight = jnp.where(first == here, share, 0.0) + jnp.where(second == here, 1.0 - share, 0.0)

    gate = gate_acc[...] * scale
    h_scr[...] = (gate / (1.0 + jnp.exp(-gate)) * (up_acc[...] * scale)).astype(BF16)

    def columns(n, _):
        slot = lax.rem(n, depth)
        down_copy(n).wait()
        value = jnp.dot(h_scr[...], ring[slot], preferred_element_type=F32) * weight
        to = pl.ds(pl.multiple_of(lax.rem(n, per_side) * d_wide, LANES), d_wide)

        @pl.when(n + depth < total)
        def _():
            down_copy(n + depth).start()

        @pl.when(n < per_side)
        def _():
            quarter = rows // 4
            leaving_ref[:, to] = jnp.concatenate(
                [value[q * quarter:(q + 1) * quarter, :] for q in (0, 2, 1, 3)], axis=0
            ).astype(BF16)

        @pl.when(n >= per_side)
        def _():
            staying_ref[:, to] = value

        return 0

    lax.fori_loop(0, total, columns, 0)


def second_half(place, mine, other, sums, weights, gate_weight, up_weight, down_weight):
    rows, units = sums[0].shape
    width = down_weight.shape[1] // 2
    fold_width = mine.shape[2] - LANES
    d_wide = math.gcd(768, width)
    depth = min(DOWN_DEPTH, 2 * (width // d_wide))
    block = weights[0].shape[0]
    steps = width // block
    gu_depth = min(GATE_DEPTH, steps - 1)
    return pl.pallas_call(
        second_half_kernel,
        out_shape=(vmem_array((rows, width), F32), vmem_array((rows, width), BF16)),
        in_specs=[SMEM_SPEC] + [VMEM_SPEC] * 6 + [HBM_SPEC] * 3,
        out_specs=(VMEM_SPEC,) * 2,
        scratch_shapes=[
            pltpu.VMEM((steps, rows, block), BF16),
            pltpu.VMEM((rows, fold_width), F32),
            pltpu.VMEM((rows, units), F32),
            pltpu.VMEM((rows, units), F32),
            pltpu.VMEM((rows, units), BF16),
            pltpu.VMEM((gu_depth, 2, block, units), BF16),
            pltpu.VMEM((depth, units, d_wide), BF16),
            pltpu.SemaphoreType.DMA((gu_depth, 2)),
            pltpu.SemaphoreType.DMA((depth,)),
        ],
        compiler_params=pltpu.CompilerParams(vmem_limit_bytes=(38 if rows < 256 else 48) * MIB),
        cost_estimate=pl.CostEstimate(
            flops=6 * rows * width * units, bytes_accessed=4 * width * units, transcendentals=0
        ),
        name="second_half",
    )(
        place, *in_vmem(mine, other, *sums, *weights),
        *in_hbm(gate_weight, up_weight, down_weight),
    )


def split_kernel(fold, own_ref, got_ref, keep_ref, send_ref, total):
    total[...] = own_ref[...] + got_ref[...].astype(F32)
    size, width = keep_ref.shape
    keep_ref[...] = total[:size, :]
    part = total[size:, :]
    if fold:
        part = jnp.concatenate(
            [part[:, f * (width // FOLD):(f + 1) * (width // FOLD)] for f in range(FOLD)], axis=0
        )
    send_ref[...] = part.astype(BF16)


def split_rows(own, got, fold=False):
    rows, width = own.shape
    size = rows // 2
    sent = (FOLD * size, width // FOLD) if fold else (size, width)
    return pl.pallas_call(
        functools.partial(split_kernel, fold),
        out_shape=(vmem_array((size, width), F32), vmem_array(sent, BF16)),
        in_specs=[VMEM_SPEC] * 2,
        out_specs=(VMEM_SPEC,) * 2,
        scratch_shapes=[pltpu.VMEM((rows, width), F32)],
        compiler_params=pltpu.CompilerParams(vmem_limit_bytes=(8 if rows < 256 else 32) * MIB),
        name="split_rows",
    )(*in_vmem(own, got))


def finish_kernel(carried_ref, own_ref, got_ref, out_ref, folded):
    tok, width = carried_ref.shape
    fold_width = width // FOLD
    folded[...] = got_ref[...].astype(F32)
    for f in range(FOLD):
        at = slice(f * fold_width, (f + 1) * fold_width)
        value = carried_ref[:, at] + own_ref[:, at] + folded[f * tok:(f + 1) * tok, :]
        out_ref[:, at] = value.astype(BF16)


def finish(carried, own, got):
    tok, width = carried.shape
    return pl.pallas_call(
        finish_kernel,
        out_shape=jax.ShapeDtypeStruct((tok, width), BF16),
        in_specs=[VMEM_SPEC] * 3,
        out_specs=VMEM_SPEC,
        scratch_shapes=[pltpu.VMEM((FOLD * tok, width // FOLD), F32)],
        compiler_params=pltpu.CompilerParams(vmem_limit_bytes=8 * MIB),
        name="finish",
    )(*in_vmem(carried, own, got))


def stage_masks(nodes):
    masks = [nodes >> (s + 1) for s in range(nodes.bit_length() - 1)]
    return masks, masks[:-2] + masks[:-3:-1]


def on_device(
    residual, queries, key_cache, value_cache, new_key, new_value, cache_lengths,
    norm_gain, router, routes, gate_weight, up_weight, down_weight,
):
    nodes = lax.axis_size("node")
    per_plane = nodes // EXPERTS
    place = jnp.stack(
        [lax.axis_index("shard"), lax.axis_index("node") // per_plane, lax.axis_index("node")]
    ).astype(jnp.int32)

    stages = nodes.bit_length() - 1
    routes_of = stage_masks(nodes)

    def exchange(array, stage):
        perm = [
            (2 * n + c, 2 * (n ^ routes_of[c][stage]) + c) for n in range(nodes) for c in range(2)
        ]
        return lax.ppermute(array, ("node", "shard"), perm)

    def to_core(array):
        return lax.ppermute(array, "shard", [(0, 1), (1, 0)])

    carried, payload = attend(
        place, cache_lengths, routes.T, queries, key_cache, value_cache, new_key, new_value,
        residual, norm_gain.reshape(1, -1), router.T,
    )
    mine = lax.all_gather(payload, "node")
    other = to_core(mine)
    gate, up, *weights = first_half(place, mine, gate_weight, up_weight)
    staying, leaving = second_half(
        place, mine, other, (gate, up), weights, gate_weight, up_weight, down_weight
    )
    keep, send = split_rows(staying, to_core(leaving))
    for stage in range(stages - 1, 0, -1):
        keep, send = split_rows(keep, exchange(send, stage), fold=stage == 1)
    return finish(carried, keep, exchange(send, 0))


def solution(mesh):
    rows = ("replica", "node")
    in_specs = (
        P(rows, "shard"),
        P(rows, "shard"),
        P(rows, None, "shard"),
        P(rows, None, "shard"),
        P(rows, "shard"),
        P(rows, "shard"),
        P(rows),
        P(),
        P(),
        P(rows, None),
        P(None, ("node", "shard")),
        P(None, ("node", "shard")),
        P(("node", "shard"), None),
    )
    return jax.shard_map(
        on_device,
        mesh=mesh,
        in_specs=in_specs,
        out_specs=P(rows, "shard"),
        check_vma=False,
    )
```

```python
import functools
import math

import jax
import jax.numpy as jnp
from jax import lax
from jax.experimental import pallas as pl
from jax.experimental.pallas import tpu as pltpu
from jax.sharding import PartitionSpec as P

QUERY_HEADS = 48
KV_HEADS = 8
HEAD_DIM = 128
EXPERTS = 4
GROUP = QUERY_HEADS // KV_HEADS
LANES = 128
FOLD = 2
MIB = 1 << 20
F32 = jnp.float32
BF16 = jnp.bfloat16


def whole_spec(array):
    zeros = (0,) * len(array.shape)
    return pl.BlockSpec(array.shape, lambda *_: zeros)


def small(shape, dtype):
    return math.prod(shape) * jnp.dtype(dtype).itemsize <= 17 * MIB // 4


def vmem_array(shape, dtype):
    return pltpu.VMEM(shape, dtype) if small(shape, dtype) else jax.ShapeDtypeStruct(shape, dtype)


def in_vmem(*arrays):
    return [
        pltpu.with_memory_space_constraint(a, pltpu.VMEM) if small(a.shape, a.dtype) else a
        for a in arrays
    ]


def in_vmem_always(arrays):
    return [pltpu.with_memory_space_constraint(a, pltpu.VMEM) for a in arrays]


def in_hbm(*arrays):
    return [pltpu.with_memory_space_constraint(a, pltpu.HBM) for a in arrays]


VMEM_SPEC = pl.BlockSpec(memory_space=pltpu.VMEM)
SMEM_SPEC = pl.BlockSpec(memory_space=pltpu.SMEM)
HBM_SPEC = pl.BlockSpec(memory_space=pltpu.HBM)
ROUTE_LANE = 3 + 3 * EXPERTS
READY = 4
DOWN_DEPTH = 4


def row_unit(gate_weight):
    return gate_weight.shape[0] // 12


def own_side():
    return lax.axis_index("shard")


def pair_copies(sources, first, targets, to, rows, sems):
    parts = sems.shape[1]
    part = rows // parts
    return [
        pltpu.make_async_copy(
            source.at[pl.ds(pl.multiple_of(first + p * part, 16), part), :],
            target.at[pl.ds(to + p * part, part), :], sems.at[i, p],
        )
        for p in range(parts) for i, (source, target) in enumerate(zip(sources, targets))
    ]


def load_kernel(first, rows, dep_ref, *refs):
    g_hbm, u_hbm, g_in, u_in, g_vmem, u_vmem, token_ref, sems = refs
    del dep_ref, g_in, u_in
    half = g_hbm.shape[0] // 2
    copies = pair_copies(
        (g_hbm, u_hbm), own_side() * half + first, (g_vmem, u_vmem), first, rows, sems
    )
    for copy in copies:
        copy.start()
    token_ref[...] = jnp.zeros_like(token_ref)
    for copy in copies:
        copy.wait()


def load_rows(first, rows, after, gate_weight, up_weight, held):
    hidden = gate_weight.shape[1]
    return pl.pallas_call(
        lambda *refs: load_kernel(first, rows, *refs),
        out_shape=tuple(pltpu.VMEM(h.shape, BF16) for h in held) + (pltpu.VMEM((8, LANES), F32),),
        in_specs=[pl.BlockSpec(memory_space=pl.ANY), HBM_SPEC, HBM_SPEC, VMEM_SPEC, VMEM_SPEC],
        out_specs=(VMEM_SPEC,) * 3,
        scratch_shapes=[pltpu.SemaphoreType.DMA((2, 4))],
        input_output_aliases={3: 0, 4: 1},
        compiler_params=pltpu.CompilerParams(vmem_limit_bytes=MIB),
        cost_estimate=pl.CostEstimate(flops=0, bytes_accessed=4 * rows * hidden, transcendentals=0),
        name="load_weights",
    )(*in_vmem(after), *in_hbm(gate_weight, up_weight), *in_vmem_always(held))


def join_kernel(a_ref, b_ref, token_ref, out_ref):
    out_ref[...] = jnp.concatenate(
        [a_ref[...].astype(F32), b_ref[...].astype(F32)], axis=0
    ).astype(BF16)


def join(a, b, token):
    return pl.pallas_call(
        join_kernel,
        out_shape=vmem_array((a.shape[0] + b.shape[0], a.shape[1]), BF16),
        in_specs=[VMEM_SPEC] * 3,
        out_specs=VMEM_SPEC,
        compiler_params=pltpu.CompilerParams(vmem_limit_bytes=(2 if a.shape[0] < 256 else 24) * MIB),
        name="join",
    )(*in_vmem(a, b, token))


def relay_kernel(count, *refs):
    del refs


def relay(arrays, token):
    count = len(arrays)
    return list(pl.pallas_call(
        functools.partial(relay_kernel, count),
        out_shape=tuple(pltpu.VMEM(a.shape, a.dtype) for a in arrays),
        in_specs=[VMEM_SPEC] * (count + 1),
        out_specs=(VMEM_SPEC,) * count,
        input_output_aliases={i: i for i in range(count)},
        compiler_params=pltpu.CompilerParams(vmem_limit_bytes=MIB),
        name="relay",
    )(*in_vmem(*arrays, token)))


def split_three(value):
    first = value.astype(BF16).astype(F32)
    second = (value - first).astype(BF16).astype(F32)
    return first, second, value - first - second


def attend_kernel(
    ahead,
    len_hbm, routes_hbm, q_hbm, k_hbm, v_hbm, nk_hbm, nv_hbm, res_hbm, gain_hbm, rt_hbm,
    g_hbm, u_hbm,
    carried_ref, pay_ref, g_vmem, u_vmem,
    q_ref, k_ref, v_ref, nk_ref, nv_ref, res_ref, gain_ref, rt_ref,
    q_scr, o_scr, nk_scr, nv_scr, pay_scr, len_ref, routes_ref, sems, w_sems,
):
    tok, width = q_ref.shape
    cache_len, kv_width = k_ref.shape[1], k_ref.shape[2]
    heads = width // HEAD_DIM
    groups = kv_width // HEAD_DIM
    fold_width = width // FOLD
    scaling = 1.0 / math.sqrt(HEAD_DIM)
    columns = pl.ds(pl.multiple_of(own_side() * width, LANES), width)
    half = tok // 2
    first, rest = pl.ds(0, half), pl.ds(half, tok - half)
    moves = [
        (q_hbm, q_ref), (nk_hbm, nk_ref),
        (k_hbm.at[first], k_ref.at[first]), (k_hbm.at[rest], k_ref.at[rest]),
        (v_hbm.at[first], v_ref.at[first]), (v_hbm.at[rest], v_ref.at[rest]),
        (nv_hbm, nv_ref), (res_hbm, res_ref),
        (gain_hbm.at[:, columns], gain_ref), (rt_hbm.at[:, columns], rt_ref),
        (len_hbm, len_ref), (routes_hbm, routes_ref),
    ]
    copies = [pltpu.make_async_copy(a, b, sems.at[i]) for i, (a, b) in enumerate(moves)]
    for copy in copies:
        copy.start()
    weights = pair_copies(
        (g_hbm, u_hbm), own_side() * (g_hbm.shape[0] // 2), (g_vmem, u_vmem), 0, ahead, w_sems
    )
    for copy in weights:
        copy.start()
    copies[0].wait()
    copies[1].wait()
    for h in range(heads):
        q_scr[h * tok:(h + 1) * tok, :] = q_ref[:, h * HEAD_DIM:(h + 1) * HEAD_DIM].astype(F32)
    nk_scr[...] = nk_ref[...].astype(F32)
    row_group = lax.broadcasted_iota(jnp.int32, (heads, HEAD_DIM), 0) // GROUP
    position = lax.broadcasted_iota(jnp.int32, (heads, cache_len), 1)
    scores, fresh = [], []
    for t in range(tok):
        if t == 0:
            copies[2].wait()
        if t == half:
            copies[3].wait()
        q_rows = q_scr[pl.ds(t, heads, stride=tok), :]
        q_wide = jnp.concatenate(
            [jnp.where(row_group == g, q_rows, 0.0) for g in range(groups)], axis=1
        )
        scores.append(
            lax.dot_general(
                q_wide.astype(BF16), k_ref[t], (((1,), (1,)), ((), ())),
                preferred_element_type=F32,
            ) * scaling
        )
        fresh.append(
            jnp.sum(q_wide * nk_scr[pl.ds(t, 1), :], axis=1, keepdims=True) * scaling
        )
    copies[10].wait()
    terms, fresh_terms, totals = [], [], []
    for t in range(tok):
        score = jnp.where(position < len_ref[t], scores[t], -1e30)
        largest = jnp.maximum(jnp.max(score, axis=1, keepdims=True), fresh[t])
        term = jnp.exp(score - largest)
        fresh_term = jnp.exp(fresh[t] - largest)
        totals.append(jnp.sum(term, axis=1, keepdims=True) + fresh_term)
        terms.append(term.astype(BF16))
        fresh_terms.append(fresh_term.astype(BF16).astype(F32))
    copies[6].wait()
    nv_scr[...] = nv_ref[...].astype(F32)
    for t in range(tok):
        if t == 0:
            copies[4].wait()
        if t == half:
            copies[5].wait()
        wide = jnp.dot(terms[t], v_ref[t], preferred_element_type=F32)
        wide = wide + fresh_terms[t] * nv_scr[pl.ds(t, 1), :]
        picked = wide[:, :HEAD_DIM]
        for g in range(1, groups):
            picked = jnp.where(
                row_group == g, wide[:, g * HEAD_DIM:(g + 1) * HEAD_DIM], picked
            )
        o_scr[pl.ds(t, heads, stride=tok), :] = picked / totals[t]
    for copy in copies[7:10] + copies[11:]:
        copy.wait()
    for h in range(heads):
        cols = slice(h * HEAD_DIM, (h + 1) * HEAD_DIM)
        carried_ref[:, cols] = res_ref[:, cols].astype(F32) + o_scr[h * tok:(h + 1) * tok, :]
    carried = carried_ref[...]
    scaled = carried * gain_ref[...]
    rounded = scaled.astype(BF16).astype(F32)
    router = rt_ref[...].astype(F32)
    for f in range(FOLD):
        pay_scr[f * tok:(f + 1) * tok, :fold_width] = scaled[:, f * fold_width:(f + 1) * fold_width]
    lane = lax.broadcasted_iota(jnp.int32, (tok, LANES), 1)
    row = lax.broadcasted_iota(jnp.int32, (tok, LANES), 0)
    sums = [jnp.sum(carried * carried, axis=1, keepdims=True)]
    for e in range(EXPERTS):
        sums.append(jnp.sum(rounded * router[e:e + 1, :], axis=1, keepdims=True))
    extra = jnp.zeros((tok, LANES), F32)
    for i, total in enumerate(sums):
        for j, term in enumerate(split_three(total)):
            extra = jnp.where(lane == 3 * i + j, term, extra)
    for t in range(tok):
        for i in range(2):
            extra = jnp.where(
                jnp.logical_and(row == t, lane == ROUTE_LANE + i),
                routes_ref[i, t].astype(F32), extra,
            )
    for f in range(FOLD):
        pay_scr[f * tok:(f + 1) * tok, fold_width:] = extra
    pay_ref[...] = pay_scr[...].astype(BF16)
    for copy in weights:
        copy.wait()


def attend(
    ahead, lengths, routes_t, queries, key_cache, value_cache, new_key, new_value,
    residual, gain, router_t, gate_weight, up_weight,
):
    tok, width = queries.shape
    kv_width = new_key.shape[1]
    heads = width // HEAD_DIM
    wide = width // FOLD + LANES
    piece = pltpu.VMEM((gate_weight.shape[0] // 2, gate_weight.shape[1]), BF16)
    here = [
        pltpu.VMEM(a.shape, a.dtype)
        for a in (queries, key_cache, value_cache, new_key, new_value, residual)
    ]
    return pl.pallas_call(
        functools.partial(attend_kernel, ahead),
        out_shape=(
            pltpu.VMEM((tok, width), F32),
            pltpu.VMEM((FOLD * tok, wide), BF16),
            piece,
            piece,
        ),
        in_specs=[HBM_SPEC] * 12,
        out_specs=(VMEM_SPEC,) * 4,
        scratch_shapes=here + [
            pltpu.VMEM((1, width), F32),
            pltpu.VMEM((EXPERTS, width), BF16),
            pltpu.VMEM((heads * tok, HEAD_DIM), F32),
            pltpu.VMEM((heads * tok, HEAD_DIM), F32),
            pltpu.VMEM((tok, kv_width), F32),
            pltpu.VMEM((tok, kv_width), F32),
            pltpu.VMEM((FOLD * tok, wide), F32),
            pltpu.SMEM(lengths.shape, jnp.int32),
            pltpu.SMEM(routes_t.shape, jnp.int32),
            pltpu.SemaphoreType.DMA((12,)),
            pltpu.SemaphoreType.DMA((2, 2)),
        ],
        compiler_params=pltpu.CompilerParams(vmem_limit_bytes=10 * MIB),
        cost_estimate=pl.CostEstimate(flops=10**8, bytes_accessed=8 * 10**6, transcendentals=10**5),
        name="attend",
    )(
        *in_hbm(
            lengths, routes_t, queries, key_cache, value_cache, new_key, new_value, residual, gain, router_t,
            gate_weight, up_weight,
        ),
    )


def block_rows(arrays, swap, tok):
    per_array = arrays[0].shape[0] // (FOLD * tok)
    places = [(array, i * FOLD * tok) for array in arrays for i in range(per_array)]
    if swap:
        quarter = len(places) // 4
        places = (
            places[:quarter] + places[2 * quarter:3 * quarter]
            + places[quarter:2 * quarter] + places[3 * quarter:]
        )
    return places


def unfold(arrays, swap, tok, x_scr, f_scr):
    fold_width = f_scr.shape[1]
    block = x_scr.shape[2]
    per_fold = fold_width // block
    for f in range(FOLD):
        for i, (array, start) in enumerate(block_rows(arrays, swap, tok)):
            rows = array[start:start + FOLD * tok, :fold_width].astype(F32)
            f_scr[i * tok:(i + 1) * tok, :] = rows[f * tok:(f + 1) * tok, :]
        for p in range(per_fold):
            x_scr[f * per_fold + p] = f_scr[:, p * block:(p + 1) * block].astype(BF16)


def add_block(x_scr, k, g_ref, u_ref, at, gate_acc, up_acc):
    gate_acc[...] += jnp.dot(x_scr[k], g_ref[at, :], preferred_element_type=F32)
    up_acc[...] += jnp.dot(x_scr[k], u_ref[at, :], preferred_element_type=F32)


def other_copies(sources, targets, k, block, sems):
    width = targets[0].shape[0]
    at = pl.ds(pl.multiple_of(k * block, block), block)
    first = pl.multiple_of((1 - own_side()) * width + k * block, block)
    return [
        pltpu.make_async_copy(source.at[pl.ds(first, block), :], target.at[at, :], sems.at[i, k])
        for i, (source, target) in enumerate(zip(sources, targets))
    ]


def first_half_kernel(
    tok, ready, a_ref, b_ref, g_hbm, u_hbm, g_in, u_in,
    gate_ref, up_ref, g_ref, u_ref, x_scr, f_scr, sems,
):
    del g_in, u_in
    steps, _, block = x_scr.shape
    unfold([a_ref, b_ref], False, tok, x_scr, f_scr)
    gate_ref[...] = jnp.zeros_like(gate_ref)
    up_ref[...] = jnp.zeros_like(up_ref)

    def step(k, _):
        at = pl.ds(pl.multiple_of(k * block, block), block)
        add_block(x_scr, k, g_ref, u_ref, at, gate_ref, up_ref)

        @pl.when(k < ready)
        def _():
            for copy in other_copies((g_hbm, u_hbm), (g_ref, u_ref), k, block, sems):
                copy.start()

        return 0

    lax.fori_loop(0, steps, step, 0)
    for k in range(ready):
        for copy in other_copies((g_hbm, u_hbm), (g_ref, u_ref), k, block, sems):
            copy.wait()


def first_half(tok, mine, held, gate_weight, up_weight):
    rows = sum(a.shape[0] for a in mine) // FOLD
    width, units = gate_weight.shape
    fold_width = mine[0].shape[1] - LANES
    block = math.gcd(512, fold_width)
    steps = width // 2 // block
    acc = pltpu.VMEM((rows, units), F32)
    return pl.pallas_call(
        functools.partial(first_half_kernel, tok, READY),
        out_shape=(acc, acc) + tuple(pltpu.VMEM(h.shape, BF16) for h in held),
        in_specs=[VMEM_SPEC] * 2 + [HBM_SPEC] * 2 + [VMEM_SPEC] * 2,
        out_specs=(VMEM_SPEC,) * 4,
        scratch_shapes=[
            pltpu.VMEM((steps, rows, block), BF16),
            pltpu.VMEM((rows, fold_width), F32),
            pltpu.SemaphoreType.DMA((2, steps)),
        ],
        input_output_aliases={4: 2, 5: 3},
        compiler_params=pltpu.CompilerParams(vmem_limit_bytes=(5 if rows < 256 else 24) * MIB),
        cost_estimate=pl.CostEstimate(
            flops=2 * rows * width * units, bytes_accessed=width * units, transcendentals=0
        ),
        name="first_half",
    )(*in_vmem(*mine), *in_hbm(gate_weight, up_weight), *in_vmem_always(held))


def second_half_kernel(
    tok, per_plane, ready, a_ref, b_ref, oa_ref, ob_ref, gate_in, up_in, g_hbm, u_hbm, d_hbm, g_in, u_in,
    staying_ref, leaving_ref, g_ref, u_ref,
    x_scr, f_scr, gate_acc, up_acc, h_scr, ring, gu_sems, sems,
):
    del g_in, u_in
    rows, units = gate_acc.shape
    width = staying_ref.shape[1]
    fold_width = f_scr.shape[1]
    side = own_side()
    depth, _, d_wide = ring.shape
    per_side = width // d_wide
    total = 2 * per_side
    steps, _, block = x_scr.shape

    def down_copy(n):
        half = jnp.where(n < per_side, 1 - side, side)
        column = half * width + lax.rem(n, per_side) * d_wide
        slot = lax.rem(n, depth)
        return pltpu.make_async_copy(
            d_hbm.at[:, pl.ds(pl.multiple_of(column, LANES), d_wide)], ring.at[slot], sems.at[slot]
        )

    for k in range(ready, steps):
        for copy in other_copies((g_hbm, u_hbm), (g_ref, u_ref), k, block, gu_sems):
            copy.start()
    unfold([oa_ref, ob_ref], True, tok, x_scr, f_scr)
    gate_acc[...] = gate_in[...]
    up_acc[...] = up_in[...]

    def step(k, _):
        @pl.when(k >= ready)
        def _():
            for copy in other_copies((g_hbm, u_hbm), (g_ref, u_ref), k, block, gu_sems):
                copy.wait()

        at = pl.ds(pl.multiple_of(k * block, block), block)
        add_block(x_scr, k, g_ref, u_ref, at, gate_acc, up_acc)

        @pl.when(k < depth)
        def _():
            down_copy(k).start()

        return 0

    lax.fori_loop(0, steps, step, 0)

    for at, arrays, swap in ((0, [a_ref, b_ref], False), (LANES, [oa_ref, ob_ref], True)):
        for i, (array, start) in enumerate(block_rows(arrays, swap, tok)):
            extra = array[start:start + FOLD * tok, fold_width:].astype(F32)
            f_scr[i * tok:(i + 1) * tok, at:at + LANES] = extra[:tok, :]
    own = f_scr[:, :LANES]
    both = own + f_scr[:, LANES:2 * LANES]
    lane = lax.broadcasted_iota(jnp.int32, (rows, LANES), 1)

    def pick(values, mask):
        return jnp.sum(jnp.where(mask, values, 0.0), axis=1, keepdims=True)

    scale = lax.rsqrt(pick(both, lane < 3) * (1.0 / (2 * width)) + 1e-05)
    first, second = pick(own, lane == ROUTE_LANE), pick(own, lane == ROUTE_LANE + 1)
    expert_of = (lane - 3) // 3
    logit_lane = jnp.logical_and(lane >= 3, lane < ROUTE_LANE)

    def logit_at(route):
        return pick(both, jnp.logical_and(logit_lane, expert_of == route.astype(jnp.int32))) * scale

    share = 1.0 / (1.0 + jnp.exp(logit_at(second) - logit_at(first)))
    here = (lax.axis_index("node") // per_plane).astype(F32)
    weight = jnp.where(first == here, share, 0.0) + jnp.where(second == here, 1.0 - share, 0.0)

    gate = gate_acc[...] * scale
    h_scr[...] = (gate / (1.0 + jnp.exp(-gate)) * (up_acc[...] * scale)).astype(BF16)

    def columns(n, _):
        slot = lax.rem(n, depth)
        down_copy(n).wait()
        value = jnp.dot(h_scr[...], ring[slot], preferred_element_type=F32) * weight
        to = pl.ds(pl.multiple_of(lax.rem(n, per_side) * d_wide, LANES), d_wide)

        @pl.when(n + depth < total)
        def _():
            down_copy(n + depth).start()

        @pl.when(n < per_side)
        def _():
            quarter = rows // 4
            leaving_ref[:, to] = jnp.concatenate(
                [value[q * quarter:(q + 1) * quarter, :] for q in (0, 2, 1, 3)], axis=0
            ).astype(BF16)

        @pl.when(n >= per_side)
        def _():
            staying_ref[:, to] = value

        return 0

    lax.fori_loop(0, total, columns, 0)


def second_half(tok, per_plane, mine, other, sums, held, gate_weight, up_weight, down_weight):
    rows, units = sums[0].shape
    width = down_weight.shape[1] // 2
    fold_width = mine[0].shape[1] - LANES
    d_wide = math.gcd(768, width)
    block = math.gcd(512, fold_width)
    steps = width // block
    depth = min(DOWN_DEPTH, 2 * (width // d_wide), steps)
    return pl.pallas_call(
        functools.partial(second_half_kernel, tok, per_plane, READY),
        out_shape=(vmem_array((rows, width), F32), vmem_array((rows, width), BF16))
        + tuple(pltpu.VMEM(h.shape, BF16) for h in held),
        in_specs=[VMEM_SPEC] * 6 + [HBM_SPEC] * 3 + [VMEM_SPEC] * 2,
        out_specs=(VMEM_SPEC,) * 4,
        scratch_shapes=[
            pltpu.VMEM((steps, rows, block), BF16),
            pltpu.VMEM((rows, fold_width), F32),
            pltpu.VMEM((rows, units), F32),
            pltpu.VMEM((rows, units), F32),
            pltpu.VMEM((rows, units), BF16),
            pltpu.VMEM((depth, units, d_wide), BF16),
            pltpu.SemaphoreType.DMA((2, steps)),
            pltpu.SemaphoreType.DMA((depth,)),
        ],
        input_output_aliases={9: 2, 10: 3},
        compiler_params=pltpu.CompilerParams(vmem_limit_bytes=(22 if rows < 256 else 40) * MIB),
        cost_estimate=pl.CostEstimate(
            flops=6 * rows * width * units, bytes_accessed=4 * width * units, transcendentals=0
        ),
        name="second_half",
    )(
        *in_vmem(*mine, *other, *sums), *in_hbm(gate_weight, up_weight, down_weight),
        *in_vmem_always(held),
    )[:2]


def split_kernel(fold, own_ref, got_ref, keep_ref, send_ref, total):
    total[...] = own_ref[...] + got_ref[...].astype(F32)
    size, width = keep_ref.shape
    keep_ref[...] = total[:size, :]
    part = total[size:, :]
    if fold:
        part = jnp.concatenate(
            [part[:, f * (width // FOLD):(f + 1) * (width // FOLD)] for f in range(FOLD)], axis=0
        )
    send_ref[...] = part.astype(BF16)


def split_rows(own, got, fold=False):
    rows, width = own.shape
    size = rows // 2
    sent = (FOLD * size, width // FOLD) if fold else (size, width)
    return pl.pallas_call(
        functools.partial(split_kernel, fold),
        out_shape=(vmem_array((size, width), F32), vmem_array(sent, BF16)),
        in_specs=[VMEM_SPEC] * 2,
        out_specs=(VMEM_SPEC,) * 2,
        scratch_shapes=[pltpu.VMEM((rows, width), F32)],
        compiler_params=pltpu.CompilerParams(vmem_limit_bytes=(8 if rows < 256 else 32) * MIB),
        name="split_rows",
    )(*in_vmem(own, got))


def finish_kernel(carried_ref, own_ref, got_ref, out_ref, folded):
    tok, width = carried_ref.shape
    fold_width = width // FOLD
    folded[...] = got_ref[...].astype(F32)
    for f in range(FOLD):
        at = slice(f * fold_width, (f + 1) * fold_width)
        value = carried_ref[:, at] + own_ref[:, at] + folded[f * tok:(f + 1) * tok, :]
        out_ref[:, at] = value.astype(BF16)


def finish(carried, own, got):
    tok, width = carried.shape
    return pl.pallas_call(
        finish_kernel,
        out_shape=jax.ShapeDtypeStruct((tok, width), BF16),
        in_specs=[VMEM_SPEC] * 3,
        out_specs=VMEM_SPEC,
        scratch_shapes=[pltpu.VMEM((FOLD * tok, width // FOLD), F32)],
        compiler_params=pltpu.CompilerParams(vmem_limit_bytes=8 * MIB),
        name="finish",
    )(*in_vmem(carried, own, got))


def on_device(
    residual, queries, key_cache, value_cache, new_key, new_value, cache_lengths,
    norm_gain, router, routes, gate_weight, up_weight, down_weight,
):
    nodes = lax.axis_size("node")
    per_plane = nodes // EXPERTS
    stages = nodes.bit_length() - 1
    masks = [nodes >> (s + 1) for s in range(stages)]
    routes_of = (masks, masks[:-2] + masks[:-3:-1])

    def exchange(array, stage):
        perm = [
            (2 * n + c, 2 * (n ^ routes_of[c][stage]) + c) for n in range(nodes) for c in range(2)
        ]
        return lax.ppermute(array, ("node", "shard"), perm)

    def to_core(array):
        return lax.ppermute(array, "shard", [(0, 1), (1, 0)])

    unit = row_unit(gate_weight)
    tok = residual.shape[0]
    heights = [unit, 2 * unit, 2 * unit, unit]
    carried, payload, *held = attend(
        heights[0], cache_lengths, routes.T, queries, key_cache, value_cache, new_key, new_value,
        residual, norm_gain.reshape(1, -1), router.T, gate_weight, up_weight,
    )
    first = heights[0]
    for stage in range(stages):
        got = exchange(payload, stage)
        if stage + 1 < len(heights):
            *held, token = load_rows(first, heights[stage + 1], payload, gate_weight, up_weight, held)
            first += heights[stage + 1]
        if stage < stages - 1:
            payload = join(payload, got, token)
    mine = [payload, *relay([got], token)]
    other = [to_core(array) for array in mine]
    gate, up, *held = first_half(tok, mine, held, gate_weight, up_weight)
    staying, leaving = second_half(
        tok, per_plane, mine, other, (gate, up), held, gate_weight, up_weight, down_weight
    )
    keep, send = split_rows(staying, to_core(leaving))
    for stage in range(stages - 1, 0, -1):
        keep, send = split_rows(keep, exchange(send, stage), fold=stage == 1)
    return finish(carried, keep, exchange(send, 0))


def solution(mesh):
    rows = ("replica", "node")
    in_specs = (
        P(rows, "shard"),
        P(rows, "shard"),
        P(rows, None, "shard"),
        P(rows, None, "shard"),
        P(rows, "shard"),
        P(rows, "shard"),
        P(rows),
        P(),
        P(),
        P(rows, None),
        P(None, ("node", "shard")),
        P(None, ("node", "shard")),
        P(("node", "shard"), None),
    )
    return jax.shard_map(
        on_device,
        mesh=mesh,
        in_specs=in_specs,
        out_specs=P(rows, "shard"),
        check_vma=False,
    )
```

```python
import functools
import math

import jax
import jax.numpy as jnp
from jax import lax
from jax.experimental import pallas as pl
from jax.experimental.pallas import tpu as pltpu
from jax.sharding import PartitionSpec as P

QUERY_HEADS = 48
KV_HEADS = 8
HEAD_DIM = 128
EXPERTS = 4
GROUP = QUERY_HEADS // KV_HEADS
LANES = 128
FOLD = 2
MIB = 1 << 20
F32 = jnp.float32
BF16 = jnp.bfloat16


def small(shape, dtype):
    return math.prod(shape) * jnp.dtype(dtype).itemsize <= 17 * MIB // 4


def vmem_array(shape, dtype):
    return pltpu.VMEM(shape, dtype) if small(shape, dtype) else jax.ShapeDtypeStruct(shape, dtype)


def in_vmem(*arrays):
    return [
        pltpu.with_memory_space_constraint(a, pltpu.VMEM) if small(a.shape, a.dtype) else a
        for a in arrays
    ]


def in_vmem_always(arrays):
    return [pltpu.with_memory_space_constraint(a, pltpu.VMEM) for a in arrays]


def in_hbm(*arrays):
    return [pltpu.with_memory_space_constraint(a, pltpu.HBM) for a in arrays]


VMEM_SPEC = pl.BlockSpec(memory_space=pltpu.VMEM)
SMEM_SPEC = pl.BlockSpec(memory_space=pltpu.SMEM)
HBM_SPEC = pl.BlockSpec(memory_space=pltpu.HBM)
ROUTE_LANE = 3 + 3 * EXPERTS
READY = 4
DOWN_DEPTH = 4


def own_side():
    return lax.axis_index("shard")


def pair_copies(sources, first, targets, to, rows, sems):
    parts = sems.shape[1]
    part = rows // parts
    return [
        pltpu.make_async_copy(
            source.at[pl.ds(pl.multiple_of(first + p * part, 16), part), :],
            target.at[pl.ds(to + p * part, part), :], sems.at[i, p],
        )
        for p in range(parts) for i, (source, target) in enumerate(zip(sources, targets))
    ]


def load_kernel(first, rows, dep_ref, g_hbm, u_hbm, *refs):
    g_vmem, u_vmem, token_ref, sems = refs[-4:]
    half = g_hbm.shape[0] // 2
    copies = pair_copies(
        (g_hbm, u_hbm), own_side() * half + first, (g_vmem, u_vmem), first, rows, sems
    )
    for copy in copies:
        copy.start()
    token_ref[...] = jnp.zeros_like(token_ref)
    for copy in copies:
        copy.wait()


def load_rows(first, rows, after, gate_weight, up_weight, held):
    width, hidden = gate_weight.shape
    return pl.pallas_call(
        functools.partial(load_kernel, first, rows),
        out_shape=(pltpu.VMEM((width // 2, hidden), BF16),) * 2 + (pltpu.VMEM((8, LANES), F32),),
        in_specs=[pl.BlockSpec(memory_space=pl.ANY), HBM_SPEC, HBM_SPEC] + [VMEM_SPEC] * len(held),
        out_specs=(VMEM_SPEC,) * 3,
        scratch_shapes=[pltpu.SemaphoreType.DMA((2, 4))],
        input_output_aliases={3 + i: i for i in range(len(held))},
        compiler_params=pltpu.CompilerParams(vmem_limit_bytes=MIB),
        cost_estimate=pl.CostEstimate(flops=0, bytes_accessed=4 * rows * hidden, transcendentals=0),
        name="load_weights",
    )(*in_vmem(after), *in_hbm(gate_weight, up_weight), *in_vmem_always(held))


def join_kernel(a_ref, b_ref, token_ref, out_ref):
    out_ref[...] = jnp.concatenate(
        [a_ref[...].astype(F32), b_ref[...].astype(F32)], axis=0
    ).astype(BF16)


def join(a, b, token):
    return pl.pallas_call(
        join_kernel,
        out_shape=vmem_array((a.shape[0] + b.shape[0], a.shape[1]), BF16),
        in_specs=[VMEM_SPEC] * 3,
        out_specs=VMEM_SPEC,
        compiler_params=pltpu.CompilerParams(vmem_limit_bytes=(2 if a.shape[0] < 256 else 24) * MIB),
        name="join",
    )(*in_vmem(a, b, token))


def spread_kernel(part, tok, array_ref, *refs):
    x_ref, f_scr = refs[-2:]
    blocks, rows, block = x_ref.shape
    fold_width = f_scr.shape[1] - LANES
    per_fold = fold_width // block
    size = rows // 2
    to = slice(part * size, (part + 1) * size)
    whole = array_ref[...].astype(F32)
    for f in range(FOLD):
        for i in range(size // tok):
            start = (i * FOLD + f) * tok
            f_scr[i * tok:(i + 1) * tok, :] = whole[start:start + tok, :]
        for p in range(per_fold):
            x_ref[f * per_fold + p, to, :] = f_scr[:, p * block:(p + 1) * block].astype(BF16)
        if f == 0:
            x_ref[blocks - 1, to, :LANES] = f_scr[:, fold_width:].astype(BF16)


def spread(part, tok, array, held, token):
    folded, wide = array.shape
    fold_width = wide - LANES
    block = math.gcd(512, fold_width)
    shape = (FOLD * fold_width // block + 1, 2 * folded // FOLD, block)
    return pl.pallas_call(
        functools.partial(spread_kernel, part, tok),
        out_shape=pltpu.VMEM(shape, BF16),
        in_specs=[VMEM_SPEC] * (2 + len(held)),
        out_specs=VMEM_SPEC,
        scratch_shapes=[pltpu.VMEM((folded // FOLD, wide), F32)],
        input_output_aliases={1: 0} if held else {},
        compiler_params=pltpu.CompilerParams(vmem_limit_bytes=(3 if folded < 256 else 24) * MIB),
        name="spread",
    )(*in_vmem(array), *in_vmem_always(held), *in_vmem(token))


def split_three(value):
    first = value.astype(BF16).astype(F32)
    second = (value - first).astype(BF16).astype(F32)
    return first, second, value - first - second


def attend_kernel(
    len_hbm, routes_hbm, q_hbm, k_hbm, v_hbm, nk_hbm, nv_hbm, res_hbm, gain_hbm, rt_hbm,
    carried_ref, pay_ref,
    q_ref, k_ref, v_ref, nk_ref, nv_ref, res_ref, gain_ref, rt_ref,
    q_scr, o_scr, nk_scr, nv_scr, pay_scr, len_ref, routes_ref, sems,
):
    tok, width = q_ref.shape
    cache_len, kv_width = k_ref.shape[1], k_ref.shape[2]
    heads = width // HEAD_DIM
    groups = kv_width // HEAD_DIM
    fold_width = width // FOLD
    scaling = 1.0 / math.sqrt(HEAD_DIM)
    columns = pl.ds(pl.multiple_of(own_side() * width, LANES), width)
    half = tok // 2
    first, rest = pl.ds(0, half), pl.ds(half, tok - half)
    moves = [
        (q_hbm, q_ref), (nk_hbm, nk_ref),
        (k_hbm.at[first], k_ref.at[first]), (k_hbm.at[rest], k_ref.at[rest]),
        (v_hbm.at[first], v_ref.at[first]), (v_hbm.at[rest], v_ref.at[rest]),
        (nv_hbm, nv_ref), (res_hbm, res_ref),
        (gain_hbm.at[:, columns], gain_ref), (rt_hbm.at[:, columns], rt_ref),
        (len_hbm, len_ref), (routes_hbm, routes_ref),
    ]
    copies = [pltpu.make_async_copy(a, b, sems.at[i]) for i, (a, b) in enumerate(moves)]
    for copy in copies:
        copy.start()
    copies[0].wait()
    copies[1].wait()
    for h in range(heads):
        q_scr[h * tok:(h + 1) * tok, :] = q_ref[:, h * HEAD_DIM:(h + 1) * HEAD_DIM].astype(F32)
    nk_scr[...] = nk_ref[...].astype(F32)
    row_group = lax.broadcasted_iota(jnp.int32, (heads, HEAD_DIM), 0) // GROUP
    position = lax.broadcasted_iota(jnp.int32, (heads, cache_len), 1)
    scores, fresh = [], []
    for t in range(tok):
        if t == 0:
            copies[2].wait()
        if t == half:
            copies[3].wait()
        q_rows = q_scr[pl.ds(t, heads, stride=tok), :]
        q_wide = jnp.concatenate(
            [jnp.where(row_group == g, q_rows, 0.0) for g in range(groups)], axis=1
        )
        scores.append(
            lax.dot_general(
                q_wide.astype(BF16), k_ref[t], (((1,), (1,)), ((), ())),
                preferred_element_type=F32,
            ) * scaling
        )
        fresh.append(
            jnp.sum(q_wide * nk_scr[pl.ds(t, 1), :], axis=1, keepdims=True) * scaling
        )
    copies[10].wait()
    terms, fresh_terms, totals = [], [], []
    for t in range(tok):
        score = jnp.where(position < len_ref[t], scores[t], -1e30)
        largest = jnp.maximum(jnp.max(score, axis=1, keepdims=True), fresh[t])
        term = jnp.exp(score - largest)
        fresh_term = jnp.exp(fresh[t] - largest)
        totals.append(jnp.sum(term, axis=1, keepdims=True) + fresh_term)
        terms.append(term.astype(BF16))
        fresh_terms.append(fresh_term.astype(BF16).astype(F32))
    copies[6].wait()
    nv_scr[...] = nv_ref[...].astype(F32)
    for t in range(tok):
        if t == 0:
            copies[4].wait()
        if t == half:
            copies[5].wait()
        wide = jnp.dot(terms[t], v_ref[t], preferred_element_type=F32)
        wide = wide + fresh_terms[t] * nv_scr[pl.ds(t, 1), :]
        picked = wide[:, :HEAD_DIM]
        for g in range(1, groups):
            picked = jnp.where(
                row_group == g, wide[:, g * HEAD_DIM:(g + 1) * HEAD_DIM], picked
            )
        o_scr[pl.ds(t, heads, stride=tok), :] = picked / totals[t]
    for copy in copies[7:10] + copies[11:]:
        copy.wait()
    for h in range(heads):
        cols = slice(h * HEAD_DIM, (h + 1) * HEAD_DIM)
        carried_ref[:, cols] = res_ref[:, cols].astype(F32) + o_scr[h * tok:(h + 1) * tok, :]
    carried = carried_ref[...]
    scaled = carried * gain_ref[...]
    rounded = scaled.astype(BF16).astype(F32)
    router = rt_ref[...].astype(F32)
    for f in range(FOLD):
        pay_scr[f * tok:(f + 1) * tok, :fold_width] = scaled[:, f * fold_width:(f + 1) * fold_width]
    lane = lax.broadcasted_iota(jnp.int32, (tok, LANES), 1)
    row = lax.broadcasted_iota(jnp.int32, (tok, LANES), 0)
    sums = [jnp.sum(carried * carried, axis=1, keepdims=True)]
    for e in range(EXPERTS):
        sums.append(jnp.sum(rounded * router[e:e + 1, :], axis=1, keepdims=True))
    extra = jnp.zeros((tok, LANES), F32)
    for i, total in enumerate(sums):
        for j, term in enumerate(split_three(total)):
            extra = jnp.where(lane == 3 * i + j, term, extra)
    for t in range(tok):
        for i in range(2):
            extra = jnp.where(
                jnp.logical_and(row == t, lane == ROUTE_LANE + i),
                routes_ref[i, t].astype(F32), extra,
            )
    for f in range(FOLD):
        pay_scr[f * tok:(f + 1) * tok, fold_width:] = extra
    pay_ref[...] = pay_scr[...].astype(BF16)


def attend(
    lengths, routes_t, queries, key_cache, value_cache, new_key, new_value,
    residual, gain, router_t,
):
    tok, width = queries.shape
    kv_width = new_key.shape[1]
    heads = width // HEAD_DIM
    wide = width // FOLD + LANES
    here = [
        pltpu.VMEM(a.shape, a.dtype)
        for a in (queries, key_cache, value_cache, new_key, new_value, residual)
    ]
    return pl.pallas_call(
        attend_kernel,
        out_shape=(
            pltpu.VMEM((tok, width), F32),
            pltpu.VMEM((FOLD * tok, wide), BF16),
        ),
        in_specs=[HBM_SPEC] * 10,
        out_specs=(VMEM_SPEC,) * 2,
        scratch_shapes=here + [
            pltpu.VMEM((1, width), F32),
            pltpu.VMEM((EXPERTS, width), BF16),
            pltpu.VMEM((heads * tok, HEAD_DIM), F32),
            pltpu.VMEM((heads * tok, HEAD_DIM), F32),
            pltpu.VMEM((tok, kv_width), F32),
            pltpu.VMEM((tok, kv_width), F32),
            pltpu.VMEM((FOLD * tok, wide), F32),
            pltpu.SMEM(lengths.shape, jnp.int32),
            pltpu.SMEM(routes_t.shape, jnp.int32),
            pltpu.SemaphoreType.DMA((12,)),
        ],
        compiler_params=pltpu.CompilerParams(vmem_limit_bytes=10 * MIB),
        cost_estimate=pl.CostEstimate(flops=10**8, bytes_accessed=8 * 10**6, transcendentals=10**5),
        name="attend",
    )(
        *in_hbm(
            lengths, routes_t, queries, key_cache, value_cache, new_key, new_value, residual, gain, router_t,
        ),
    )


def add_block(x_scr, k, g_ref, u_ref, at, gate_acc, up_acc):
    gate_acc[...] += jnp.dot(x_scr[k], g_ref[at, :], preferred_element_type=F32)
    up_acc[...] += jnp.dot(x_scr[k], u_ref[at, :], preferred_element_type=F32)


def other_copies(sources, targets, k, block, sems):
    width = targets[0].shape[0]
    at = pl.ds(pl.multiple_of(k * block, block), block)
    first = pl.multiple_of((1 - own_side()) * width + k * block, block)
    return [
        pltpu.make_async_copy(source.at[pl.ds(first, block), :], target.at[at, :], sems.at[i, k])
        for i, (source, target) in enumerate(zip(sources, targets))
    ]


def first_half_kernel(
    ready, x_ref, g_hbm, u_hbm, g_in, u_in, gate_ref, up_ref, g_ref, u_ref, sems
):
    del g_in, u_in
    _, _, block = x_ref.shape
    steps = g_ref.shape[0] // block
    gate_ref[...] = jnp.zeros_like(gate_ref)
    up_ref[...] = jnp.zeros_like(up_ref)

    def step(k, _):
        at = pl.ds(pl.multiple_of(k * block, block), block)
        add_block(x_ref, k, g_ref, u_ref, at, gate_ref, up_ref)

        @pl.when(k < ready)
        def _():
            for copy in other_copies((g_hbm, u_hbm), (g_ref, u_ref), k, block, sems):
                copy.start()

        return 0

    lax.fori_loop(0, steps, step, 0)
    for k in range(ready):
        for copy in other_copies((g_hbm, u_hbm), (g_ref, u_ref), k, block, sems):
            copy.wait()


def first_half(rows_in, held, gate_weight, up_weight):
    _, rows, block = rows_in.shape
    width, units = gate_weight.shape
    steps = width // 2 // block
    acc = pltpu.VMEM((rows, units), F32)
    return pl.pallas_call(
        functools.partial(first_half_kernel, READY),
        out_shape=(acc, acc) + tuple(pltpu.VMEM(h.shape, BF16) for h in held),
        in_specs=[VMEM_SPEC] + [HBM_SPEC] * 2 + [VMEM_SPEC] * 2,
        out_specs=(VMEM_SPEC,) * 4,
        scratch_shapes=[pltpu.SemaphoreType.DMA((2, steps))],
        input_output_aliases={3: 2, 4: 3},
        compiler_params=pltpu.CompilerParams(vmem_limit_bytes=(4 if rows < 256 else 16) * MIB),
        cost_estimate=pl.CostEstimate(
            flops=2 * rows * width * units, bytes_accessed=width * units, transcendentals=0
        ),
        name="first_half",
    )(*in_vmem_always([rows_in]), *in_hbm(gate_weight, up_weight), *in_vmem_always(held))


def second_half_kernel(
    per_plane, ready, x_ref, ox_ref, gate_in, up_in, g_hbm, u_hbm, d_hbm, g_in, u_in,
    staying_ref, leaving_ref, g_ref, u_ref,
    x_scr, gate_acc, up_acc, h_scr, ring, gu_sems, sems,
):
    del g_in, u_in
    rows, units = gate_acc.shape
    width = staying_ref.shape[1]
    side = own_side()
    depth, _, d_wide = ring.shape
    per_side = width // d_wide
    total = 2 * per_side
    steps, _, block = x_scr.shape
    free = -(-units // block)
    spare = units // d_wide
    ends = [0, depth, depth + spare, depth + 2 * spare]

    def place(part, n):
        if part == 0:
            return ring.at[n]
        column = (n - ends[part]) * d_wide
        if not isinstance(n, int):
            column = pl.multiple_of(column, LANES)
        return (g_ref, u_ref)[part - 1].at[pl.ds(0, units), pl.ds(column, d_wide)]

    def down_copy(part, n):
        column = jnp.where(n < per_side, 1 - side, side) * width + lax.rem(n, per_side) * d_wide
        return pltpu.make_async_copy(
            d_hbm.at[:, pl.ds(pl.multiple_of(column, LANES), d_wide)], place(part, n), sems.at[n]
        )

    def in_order(values):
        quarter = rows // 4
        return jnp.concatenate(
            [values[q * quarter:(q + 1) * quarter, :] for q in (0, 2, 1, 3)], axis=0
        )

    for k in range(ready, steps):
        for copy in other_copies((g_hbm, u_hbm), (g_ref, u_ref), k, block, gu_sems):
            copy.start()
    for k in range(steps):
        x_scr[k] = in_order(ox_ref[k].astype(F32)).astype(BF16)
    gate_acc[...] = gate_in[...]
    up_acc[...] = up_in[...]

    def step(k, _):
        @pl.when(k >= ready)
        def _():
            for copy in other_copies((g_hbm, u_hbm), (g_ref, u_ref), k, block, gu_sems):
                copy.wait()

        at = pl.ds(pl.multiple_of(k * block, block), block)
        add_block(x_scr, k, g_ref, u_ref, at, gate_acc, up_acc)

        for n in range(total):
            @pl.when(k == (min(n + 1, steps - 2) if n < depth else max(free - 1, steps - 2)))
            def _(n=n):
                down_copy(sum(n >= end for end in ends[1:]), n).start()

        return 0

    lax.fori_loop(0, steps, step, 0)

    own = x_ref[steps, :, :LANES].astype(F32)
    both = own + in_order(ox_ref[steps, :, :LANES].astype(F32))
    lane = lax.broadcasted_iota(jnp.int32, (rows, LANES), 1)

    def pick(values, mask):
        return jnp.sum(jnp.where(mask, values, 0.0), axis=1, keepdims=True)

    scale = lax.rsqrt(pick(both, lane < 3) * (1.0 / (2 * width)) + 1e-05)
    first, second = pick(own, lane == ROUTE_LANE), pick(own, lane == ROUTE_LANE + 1)
    expert_of = (lane - 3) // 3
    logit_lane = jnp.logical_and(lane >= 3, lane < ROUTE_LANE)

    def logit_at(route):
        return pick(both, jnp.logical_and(logit_lane, expert_of == route.astype(jnp.int32))) * scale

    share = 1.0 / (1.0 + jnp.exp(logit_at(second) - logit_at(first)))
    here = (lax.axis_index("node") // per_plane).astype(F32)
    weight = jnp.where(first == here, share, 0.0) + jnp.where(second == here, 1.0 - share, 0.0)

    gate = gate_acc[...] * scale
    h_scr[...] = (gate / (1.0 + jnp.exp(-gate)) * (up_acc[...] * scale)).astype(BF16)

    def columns(part, n, _):
        down_copy(part, n).wait()
        value = jnp.dot(h_scr[...], place(part, n)[...], preferred_element_type=F32) * weight
        to = pl.ds(pl.multiple_of(lax.rem(n, per_side) * d_wide, LANES), d_wide)

        @pl.when(n < per_side)
        def _():
            leaving_ref[:, to] = in_order(value).astype(BF16)

        @pl.when(n >= per_side)
        def _():
            staying_ref[:, to] = value

        return 0

    for part in range(3):
        low, high = min(ends[part], total), min(ends[part + 1], total)
        if low < high:
            lax.fori_loop(low, high, functools.partial(columns, part), 0)


def second_half(per_plane, mine, other, sums, held, gate_weight, up_weight, down_weight):
    rows, units = sums[0].shape
    width = down_weight.shape[1] // 2
    block = mine.shape[2]
    steps = width // block
    d_wide = math.gcd(768, width)
    total = 2 * (width // d_wide)
    depth = max(DOWN_DEPTH, total - 2 * (units // d_wide))
    return pl.pallas_call(
        functools.partial(second_half_kernel, per_plane, READY),
        out_shape=(vmem_array((rows, width), F32), vmem_array((rows, width), BF16))
        + tuple(pltpu.VMEM(h.shape, BF16) for h in held),
        in_specs=[VMEM_SPEC] * 4 + [HBM_SPEC] * 3 + [VMEM_SPEC] * 2,
        out_specs=(VMEM_SPEC,) * 4,
        scratch_shapes=[
            pltpu.VMEM((steps, rows, block), BF16),
            pltpu.VMEM((rows, units), F32),
            pltpu.VMEM((rows, units), F32),
            pltpu.VMEM((rows, units), BF16),
            pltpu.VMEM((depth, units, d_wide), BF16),
            pltpu.SemaphoreType.DMA((2, steps)),
            pltpu.SemaphoreType.DMA((total,)),
        ],
        input_output_aliases={7: 2, 8: 3},
        compiler_params=pltpu.CompilerParams(vmem_limit_bytes=(22 if rows < 256 else 40) * MIB),
        cost_estimate=pl.CostEstimate(
            flops=6 * rows * width * units, bytes_accessed=4 * width * units, transcendentals=0
        ),
        name="second_half",
    )(
        *in_vmem_always([mine, other]), *in_vmem(*sums),
        *in_hbm(gate_weight, up_weight, down_weight), *in_vmem_always(held),
    )[:2]


def split_kernel(fold, own_ref, got_ref, keep_ref, send_ref, total):
    total[...] = own_ref[...] + got_ref[...].astype(F32)
    size, width = keep_ref.shape
    keep_ref[...] = total[:size, :]
    part = total[size:, :]
    if fold:
        part = jnp.concatenate(
            [part[:, f * (width // FOLD):(f + 1) * (width // FOLD)] for f in range(FOLD)], axis=0
        )
    send_ref[...] = part.astype(BF16)


def split_rows(own, got, fold=False):
    rows, width = own.shape
    size = rows // 2
    sent = (FOLD * size, width // FOLD) if fold else (size, width)
    return pl.pallas_call(
        functools.partial(split_kernel, fold),
        out_shape=(vmem_array((size, width), F32), vmem_array(sent, BF16)),
        in_specs=[VMEM_SPEC] * 2,
        out_specs=(VMEM_SPEC,) * 2,
        scratch_shapes=[pltpu.VMEM((rows, width), F32)],
        compiler_params=pltpu.CompilerParams(vmem_limit_bytes=(8 if rows < 256 else 32) * MIB),
        name="split_rows",
    )(*in_vmem(own, got))


def finish_kernel(carried_ref, own_ref, got_ref, out_ref, folded):
    tok, width = carried_ref.shape
    fold_width = width // FOLD
    folded[...] = got_ref[...].astype(F32)
    for f in range(FOLD):
        at = slice(f * fold_width, (f + 1) * fold_width)
        value = carried_ref[:, at] + own_ref[:, at] + folded[f * tok:(f + 1) * tok, :]
        out_ref[:, at] = value.astype(BF16)


def finish(carried, own, got):
    tok, width = carried.shape
    return pl.pallas_call(
        finish_kernel,
        out_shape=jax.ShapeDtypeStruct((tok, width), BF16),
        in_specs=[VMEM_SPEC] * 3,
        out_specs=VMEM_SPEC,
        scratch_shapes=[pltpu.VMEM((FOLD * tok, width // FOLD), F32)],
        compiler_params=pltpu.CompilerParams(vmem_limit_bytes=8 * MIB),
        name="finish",
    )(*in_vmem(carried, own, got))


def on_device(
    residual, queries, key_cache, value_cache, new_key, new_value, cache_lengths,
    norm_gain, router, routes, gate_weight, up_weight, down_weight,
):
    nodes = lax.axis_size("node")
    per_plane = nodes // EXPERTS
    stages = nodes.bit_length() - 1
    masks = [nodes >> (s + 1) for s in range(stages)]
    routes_of = (masks, masks[:-2] + masks[:-3:-1])

    def exchange(array, stage):
        perm = [
            (2 * n + c, 2 * (n ^ routes_of[c][stage]) + c) for n in range(nodes) for c in range(2)
        ]
        return lax.ppermute(array, ("node", "shard"), perm)

    def to_core(array):
        return lax.ppermute(array, "shard", [(0, 1), (1, 0)])

    tok = residual.shape[0]
    half = gate_weight.shape[0] // 2
    heights = [half // 2, half // 4, half // 4]
    carried, payload = attend(
        cache_lengths, routes.T, queries, key_cache, value_cache, new_key, new_value,
        residual, norm_gain.reshape(1, -1), router.T,
    )
    first, held = 0, []
    for stage in range(stages):
        got = exchange(payload, stage)
        if stage < len(heights):
            *held, token = load_rows(first, heights[stage], payload, gate_weight, up_weight, held)
            first += heights[stage]
        if stage < stages - 1:
            payload = join(payload, got, token)
    mine = spread(0, tok, payload, [], token)
    mine = spread(1, tok, got, [mine], token)
    other = to_core(mine)
    gate, up, *held = first_half(mine, held, gate_weight, up_weight)
    staying, leaving = second_half(
        per_plane, mine, other, (gate, up), held, gate_weight, up_weight, down_weight
    )
    keep, send = split_rows(staying, to_core(leaving))
    for stage in range(stages - 1, 0, -1):
        keep, send = split_rows(keep, exchange(send, stage), fold=stage == 1)
    return finish(carried, keep, exchange(send, 0))


def solution(mesh):
    rows = ("replica", "node")
    in_specs = (
        P(rows, "shard"),
        P(rows, "shard"),
        P(rows, None, "shard"),
        P(rows, None, "shard"),
        P(rows, "shard"),
        P(rows, "shard"),
        P(rows),
        P(),
        P(),
        P(rows, None),
        P(None, ("node", "shard")),
        P(None, ("node", "shard")),
        P(("node", "shard"), None),
    )
    return jax.shard_map(
        on_device,
        mesh=mesh,
        in_specs=in_specs,
        out_specs=P(rows, "shard"),
        check_vma=False,
    )
```

```python
import functools
import math

import jax
import jax.numpy as jnp
from jax import lax
from jax.experimental import pallas as pl
from jax.experimental.pallas import tpu as pltpu
from jax.sharding import PartitionSpec as P

MIB = 1 << 20
QUERY_HEADS = 48
KV_HEADS = 8
HEAD_DIM = 128
EXPERTS = 4
GROUP = QUERY_HEADS // KV_HEADS
LANES = 128
FOLD = 2
F32 = jnp.float32
BF16 = jnp.bfloat16


def small(shape, dtype):
    return math.prod(shape) * jnp.dtype(dtype).itemsize <= 17 * MIB // 4


def vmem_array(shape, dtype):
    return pltpu.VMEM(shape, dtype) if small(shape, dtype) else jax.ShapeDtypeStruct(shape, dtype)


def in_vmem(*arrays):
    return [
        pltpu.with_memory_space_constraint(a, pltpu.VMEM) if small(a.shape, a.dtype) else a
        for a in arrays
    ]


def in_vmem_always(arrays):
    return [pltpu.with_memory_space_constraint(a, pltpu.VMEM) for a in arrays]


def in_hbm(*arrays):
    return [pltpu.with_memory_space_constraint(a, pltpu.HBM) for a in arrays]


VMEM_SPEC = pl.BlockSpec(memory_space=pltpu.VMEM)
SMEM_SPEC = pl.BlockSpec(memory_space=pltpu.SMEM)
HBM_SPEC = pl.BlockSpec(memory_space=pltpu.HBM)
ROUTE_LANE = 3 + 3 * EXPERTS
READY = 4
HELD_BELOW = 22 * MIB
DOWN_DEPTH = 4


def own_side():
    return lax.axis_index("shard")


def pair_copies(sources, first, targets, to, rows, sems):
    parts = sems.shape[1]
    part = rows // parts
    return [
        pltpu.make_async_copy(
            source.at[pl.ds(pl.multiple_of(first + p * part, 16), part), :],
            target.at[pl.ds(to + p * part, part), :], sems.at[i, p],
        )
        for p in range(parts) for i, (source, target) in enumerate(zip(sources, targets))
    ]


def load_kernel(first, rows, dep_ref, g_hbm, u_hbm, *refs):
    g_vmem, u_vmem, token_ref, sems = refs[-4:]
    half = g_hbm.shape[0] // 2
    copies = pair_copies(
        (g_hbm, u_hbm), own_side() * half + first, (g_vmem, u_vmem), first, rows, sems
    )
    for copy in copies:
        copy.start()
    token_ref[...] = jnp.zeros_like(token_ref)
    for copy in copies:
        copy.wait()


def load_rows(first, rows, after, gate_weight, up_weight, held):
    width, hidden = gate_weight.shape
    return pl.pallas_call(
        functools.partial(load_kernel, first, rows),
        out_shape=(pltpu.VMEM((width // 2, hidden), BF16),) * 2 + (pltpu.VMEM((8, LANES), F32),),
        in_specs=[pl.BlockSpec(memory_space=pl.ANY), HBM_SPEC, HBM_SPEC] + [VMEM_SPEC] * len(held),
        out_specs=(VMEM_SPEC,) * 3,
        scratch_shapes=[pltpu.SemaphoreType.DMA((2, 4))],
        input_output_aliases={3 + i: i for i in range(len(held))},
        compiler_params=pltpu.CompilerParams(vmem_limit_bytes=HELD_BELOW),
        cost_estimate=pl.CostEstimate(flops=0, bytes_accessed=4 * rows * hidden, transcendentals=0),
        name="load_weights",
    )(*in_vmem(after), *in_hbm(gate_weight, up_weight), *in_vmem_always(held))


def unfold_kernel(tok, *refs):
    *arrays, _, out_ref, scr = refs
    fold_width = arrays[0].shape[1] - LANES
    for i, array in enumerate(arrays):
        rows = array[...].astype(F32)
        to = slice(i * tok, (i + 1) * tok)
        for f in range(FOLD):
            scr[to, f * fold_width:(f + 1) * fold_width] = rows[f * tok:(f + 1) * tok, :fold_width]
        scr[to, FOLD * fold_width:] = rows[:tok, fold_width:]
    out_ref[...] = scr[...].astype(BF16)


def unfold(tok, arrays, token):
    shape = (len(arrays) * tok, FOLD * (arrays[0].shape[1] - LANES) + LANES)
    return pl.pallas_call(
        functools.partial(unfold_kernel, tok),
        out_shape=pltpu.VMEM(shape, BF16),
        in_specs=[VMEM_SPEC] * (len(arrays) + 1),
        out_specs=VMEM_SPEC,
        scratch_shapes=[pltpu.VMEM(shape, F32)],
        compiler_params=pltpu.CompilerParams(vmem_limit_bytes=3 * MIB),
        name="unfold",
    )(*in_vmem_always([*arrays, token]))


def join_kernel(a_ref, b_ref, token_ref, out_ref):
    rows = a_ref.shape[0]
    out_ref[:rows, :] = a_ref[...]
    out_ref[rows:, :] = b_ref[...]


def join(a, b, token):
    return pl.pallas_call(
        join_kernel,
        out_shape=vmem_array((a.shape[0] + b.shape[0], a.shape[1]), BF16),
        in_specs=[VMEM_SPEC] * 3,
        out_specs=VMEM_SPEC,
        compiler_params=pltpu.CompilerParams(vmem_limit_bytes=16 * MIB),
        name="join",
    )(*in_vmem(a, b, token))


def spread_kernel(part, array_ref, *refs):
    x_ref = refs[-1]
    blocks, rows, block = x_ref.shape
    size = rows // 2
    to = slice(part * size, (part + 1) * size)
    for k in range(blocks - 1):
        x_ref[k, to, :] = array_ref[:, k * block:(k + 1) * block]
    x_ref[blocks - 1, to, :LANES] = array_ref[:, (blocks - 1) * block:]


def spread(part, array, held, token):
    size, wide = array.shape
    block = math.gcd(512, wide - LANES)
    return pl.pallas_call(
        functools.partial(spread_kernel, part),
        out_shape=pltpu.VMEM(((wide - LANES) // block + 1, 2 * size, block), BF16),
        in_specs=[VMEM_SPEC] * (2 + len(held)),
        out_specs=VMEM_SPEC,
        input_output_aliases={1: 0} if held else {},
        compiler_params=pltpu.CompilerParams(vmem_limit_bytes=(MIB if size < 128 else 16 * MIB)),
        name="spread",
    )(*in_vmem(array), *in_vmem_always(held), *in_vmem(token))


def split_three(value):
    first = value.astype(BF16).astype(F32)
    second = (value - first).astype(BF16).astype(F32)
    return first, second, value - first - second


def attend_kernel(
    len_hbm, routes_hbm, q_hbm, k_hbm, v_hbm, nk_hbm, nv_hbm, res_hbm, gain_hbm, rt_hbm,
    carried_ref, pay_ref,
    q_ref, k_ref, v_ref, nk_ref, nv_ref, res_ref, gain_ref, rt_ref,
    q_scr, o_scr, nk_scr, nv_scr, pay_scr, len_ref, routes_ref, sems,
):
    tok, width = q_ref.shape
    cache_len, kv_width = k_ref.shape[1], k_ref.shape[2]
    heads = width // HEAD_DIM
    groups = kv_width // HEAD_DIM
    fold_width = width // FOLD
    scaling = 1.0 / math.sqrt(HEAD_DIM)
    columns = pl.ds(pl.multiple_of(own_side() * width, LANES), width)
    parts = math.gcd(4, tok)
    each = tok // parts
    moves = [(q_hbm, q_ref), (nk_hbm, nk_ref), (len_hbm, len_ref)]
    for source, target in ((k_hbm, k_ref), (v_hbm, v_ref)):
        moves += [
            (source.at[pl.ds(p * each, each)], target.at[pl.ds(p * each, each)]) for p in range(parts)
        ]
    moves += [
        (nv_hbm, nv_ref), (res_hbm, res_ref),
        (gain_hbm.at[:, columns], gain_ref), (rt_hbm.at[:, columns], rt_ref),
        (routes_hbm, routes_ref),
    ]
    copies = [pltpu.make_async_copy(a, b, sems.at[i]) for i, (a, b) in enumerate(moves)]
    for copy in copies:
        copy.start()
    copies[0].wait()
    copies[1].wait()
    for h in range(heads):
        q_scr[h * tok:(h + 1) * tok, :] = q_ref[:, h * HEAD_DIM:(h + 1) * HEAD_DIM].astype(F32)
    nk_scr[...] = nk_ref[...].astype(F32)
    row_group = lax.broadcasted_iota(jnp.int32, (heads, HEAD_DIM), 0) // GROUP
    position = lax.broadcasted_iota(jnp.int32, (heads, cache_len), 1)
    scores, fresh = [], []
    for t in range(tok):
        if t % each == 0:
            copies[3 + t // each].wait()
        q_rows = q_scr[pl.ds(t, heads, stride=tok), :]
        q_wide = jnp.concatenate(
            [jnp.where(row_group == g, q_rows, 0.0) for g in range(groups)], axis=1
        )
        scores.append(
            lax.dot_general(
                q_wide.astype(BF16), k_ref[t], (((1,), (1,)), ((), ())),
                preferred_element_type=F32,
            ) * scaling
        )
        fresh.append(
            jnp.sum(q_wide * nk_scr[pl.ds(t, 1), :], axis=1, keepdims=True) * scaling
        )
    copies[2].wait()
    terms, fresh_terms, totals = [], [], []
    for t in range(tok):
        score = jnp.where(position < len_ref[t], scores[t], -1e30)
        largest = jnp.maximum(jnp.max(score, axis=1, keepdims=True), fresh[t])
        term = jnp.exp(score - largest)
        fresh_term = jnp.exp(fresh[t] - largest)
        totals.append(jnp.sum(term, axis=1, keepdims=True) + fresh_term)
        terms.append(term.astype(BF16))
        fresh_terms.append(fresh_term.astype(BF16).astype(F32))
    copies[3 + 2 * parts].wait()
    nv_scr[...] = nv_ref[...].astype(F32)
    for t in range(tok):
        if t % each == 0:
            copies[3 + parts + t // each].wait()
        wide = jnp.dot(terms[t], v_ref[t], preferred_element_type=F32)
        wide = wide + fresh_terms[t] * nv_scr[pl.ds(t, 1), :]
        picked = wide[:, :HEAD_DIM]
        for g in range(1, groups):
            picked = jnp.where(
                row_group == g, wide[:, g * HEAD_DIM:(g + 1) * HEAD_DIM], picked
            )
        o_scr[pl.ds(t, heads, stride=tok), :] = picked / totals[t]
    for copy in copies[4 + 2 * parts:]:
        copy.wait()
    for h in range(heads):
        cols = slice(h * HEAD_DIM, (h + 1) * HEAD_DIM)
        carried_ref[:, cols] = res_ref[:, cols].astype(F32) + o_scr[h * tok:(h + 1) * tok, :]
    carried = carried_ref[...]
    scaled = carried * gain_ref[...]
    rounded = scaled.astype(BF16).astype(F32)
    router = rt_ref[...].astype(F32)
    for f in range(FOLD):
        pay_scr[f * tok:(f + 1) * tok, :fold_width] = scaled[:, f * fold_width:(f + 1) * fold_width]
    lane = lax.broadcasted_iota(jnp.int32, (tok, LANES), 1)
    row = lax.broadcasted_iota(jnp.int32, (tok, LANES), 0)
    sums = [jnp.sum(carried * carried, axis=1, keepdims=True)]
    for e in range(EXPERTS):
        sums.append(jnp.sum(rounded * router[e:e + 1, :], axis=1, keepdims=True))
    extra = jnp.zeros((tok, LANES), F32)
    for i, total in enumerate(sums):
        for j, term in enumerate(split_three(total)):
            extra = jnp.where(lane == 3 * i + j, term, extra)
    for t in range(tok):
        for i in range(2):
            extra = jnp.where(
                jnp.logical_and(row == t, lane == ROUTE_LANE + i),
                routes_ref[i, t].astype(F32), extra,
            )
    for f in range(FOLD):
        pay_scr[f * tok:(f + 1) * tok, fold_width:] = extra
    pay_ref[...] = pay_scr[...].astype(BF16)


def attend(
    lengths, routes_t, queries, key_cache, value_cache, new_key, new_value,
    residual, gain, router_t,
):
    tok, width = queries.shape
    kv_width = new_key.shape[1]
    heads = width // HEAD_DIM
    wide = width // FOLD + LANES
    here = [
        pltpu.VMEM(a.shape, a.dtype)
        for a in (queries, key_cache, value_cache, new_key, new_value, residual)
    ]
    return pl.pallas_call(
        attend_kernel,
        out_shape=(
            pltpu.VMEM((tok, width), F32),
            pltpu.VMEM((FOLD * tok, wide), BF16),
        ),
        in_specs=[HBM_SPEC] * 10,
        out_specs=(VMEM_SPEC,) * 2,
        scratch_shapes=here + [
            pltpu.VMEM((1, width), F32),
            pltpu.VMEM((EXPERTS, width), BF16),
            pltpu.VMEM((heads * tok, HEAD_DIM), F32),
            pltpu.VMEM((heads * tok, HEAD_DIM), F32),
            pltpu.VMEM((tok, kv_width), F32),
            pltpu.VMEM((tok, kv_width), F32),
            pltpu.VMEM((FOLD * tok, wide), F32),
            pltpu.SMEM(lengths.shape, jnp.int32),
            pltpu.SMEM(routes_t.shape, jnp.int32),
            pltpu.SemaphoreType.DMA((8 + 2 * math.gcd(4, tok),)),
        ],
        compiler_params=pltpu.CompilerParams(vmem_limit_bytes=10 * MIB),
        cost_estimate=pl.CostEstimate(flops=10**8, bytes_accessed=8 * 10**6, transcendentals=10**5),
        name="attend",
    )(
        *in_hbm(
            lengths, routes_t, queries, key_cache, value_cache, new_key, new_value, residual, gain, router_t,
        ),
    )


def add_block(x_scr, k, g_ref, u_ref, at, gate_acc, up_acc):
    gate_acc[...] += jnp.dot(x_scr[k], g_ref[at, :], preferred_element_type=F32)
    up_acc[...] += jnp.dot(x_scr[k], u_ref[at, :], preferred_element_type=F32)


def other_copies(sources, targets, k, block, sems):
    width = targets[0].shape[0]
    at = pl.ds(pl.multiple_of(k * block, block), block)
    first = pl.multiple_of((1 - own_side()) * width + k * block, block)
    return [
        pltpu.make_async_copy(source.at[pl.ds(first, block), :], target.at[at, :], sems.at[i, k])
        for i, (source, target) in enumerate(zip(sources, targets))
    ]


def first_half_kernel(
    ready, x_ref, g_hbm, u_hbm, g_in, u_in, gate_ref, up_ref, g_ref, u_ref, sems
):
    del g_in, u_in
    _, _, block = x_ref.shape
    steps = g_ref.shape[0] // block
    gate_ref[...] = jnp.zeros_like(gate_ref)
    up_ref[...] = jnp.zeros_like(up_ref)

    def step(k, _):
        at = pl.ds(pl.multiple_of(k * block, block), block)
        add_block(x_ref, k, g_ref, u_ref, at, gate_ref, up_ref)

        @pl.when(k < ready)
        def _():
            for copy in other_copies((g_hbm, u_hbm), (g_ref, u_ref), k, block, sems):
                copy.start()

        return 0

    lax.fori_loop(0, steps, step, 0)
    for k in range(ready):
        for copy in other_copies((g_hbm, u_hbm), (g_ref, u_ref), k, block, sems):
            copy.wait()


def first_half(rows_in, held, gate_weight, up_weight):
    _, rows, block = rows_in.shape
    width, units = gate_weight.shape
    steps = width // 2 // block
    acc = pltpu.VMEM((rows, units), F32)
    return pl.pallas_call(
        functools.partial(first_half_kernel, READY),
        out_shape=(acc, acc) + tuple(pltpu.VMEM(h.shape, BF16) for h in held),
        in_specs=[VMEM_SPEC] + [HBM_SPEC] * 2 + [VMEM_SPEC] * 2,
        out_specs=(VMEM_SPEC,) * 4,
        scratch_shapes=[pltpu.SemaphoreType.DMA((2, steps))],
        input_output_aliases={3: 2, 4: 3},
        compiler_params=pltpu.CompilerParams(vmem_limit_bytes=HELD_BELOW),
        cost_estimate=pl.CostEstimate(
            flops=2 * rows * width * units, bytes_accessed=width * units, transcendentals=0
        ),
        name="first_half",
    )(*in_vmem_always([rows_in]), *in_hbm(gate_weight, up_weight), *in_vmem_always(held))


def second_half_kernel(
    per_plane, ready, x_ref, ox_ref, gate_in, up_in, g_hbm, u_hbm, d_hbm, g_in, u_in,
    staying_ref, leaving_ref, g_ref, u_ref,
    x_scr, gate_acc, up_acc, h_scr, ring, gu_sems, sems,
):
    del g_in, u_in
    rows, units = gate_acc.shape
    width = staying_ref.shape[1]
    side = own_side()
    depth, _, d_wide = ring.shape
    per_side = width // d_wide
    total = 2 * per_side
    steps, _, block = x_scr.shape
    free = -(-units // block)
    spare = units // d_wide
    ends = [0, depth, depth + spare, depth + 2 * spare]

    def place(part, n):
        if part == 0:
            return ring.at[n]
        column = (n - ends[part]) * d_wide
        if not isinstance(n, int):
            column = pl.multiple_of(column, LANES)
        return (g_ref, u_ref)[part - 1].at[pl.ds(0, units), pl.ds(column, d_wide)]

    def down_copy(part, n):
        column = jnp.where(n < per_side, 1 - side, side) * width + lax.rem(n, per_side) * d_wide
        return pltpu.make_async_copy(
            d_hbm.at[:, pl.ds(pl.multiple_of(column, LANES), d_wide)], place(part, n), sems.at[n]
        )

    def in_order(values):
        quarter = rows // 4
        return jnp.concatenate(
            [values[q * quarter:(q + 1) * quarter, :] for q in (0, 2, 1, 3)], axis=0
        )

    for k in range(ready, steps):
        for copy in other_copies((g_hbm, u_hbm), (g_ref, u_ref), k, block, gu_sems):
            copy.start()
    for k in range(steps):
        x_scr[k] = in_order(ox_ref[k].astype(F32)).astype(BF16)
    gate_acc[...] = gate_in[...]
    up_acc[...] = up_in[...]

    def step(k, _):
        @pl.when(k >= ready)
        def _():
            for copy in other_copies((g_hbm, u_hbm), (g_ref, u_ref), k, block, gu_sems):
                copy.wait()

        at = pl.ds(pl.multiple_of(k * block, block), block)
        add_block(x_scr, k, g_ref, u_ref, at, gate_acc, up_acc)

        for n in range(total):
            @pl.when(k == (min(n + 1, steps - 2) if n < depth else max(free - 1, steps - 2)))
            def _(n=n):
                down_copy(sum(n >= end for end in ends[1:]), n).start()

        return 0

    lax.fori_loop(0, steps, step, 0)

    own = x_ref[steps, :, :LANES].astype(F32)
    both = own + in_order(ox_ref[steps, :, :LANES].astype(F32))
    lane = lax.broadcasted_iota(jnp.int32, (rows, LANES), 1)

    def pick(values, mask):
        return jnp.sum(jnp.where(mask, values, 0.0), axis=1, keepdims=True)

    scale = lax.rsqrt(pick(both, lane < 3) * (1.0 / (2 * width)) + 1e-05)
    first, second = pick(own, lane == ROUTE_LANE), pick(own, lane == ROUTE_LANE + 1)
    expert_of = (lane - 3) // 3
    logit_lane = jnp.logical_and(lane >= 3, lane < ROUTE_LANE)

    def logit_at(route):
        return pick(both, jnp.logical_and(logit_lane, expert_of == route.astype(jnp.int32))) * scale

    share = 1.0 / (1.0 + jnp.exp(logit_at(second) - logit_at(first)))
    here = (lax.axis_index("node") // per_plane).astype(F32)
    weight = jnp.where(first == here, share, 0.0) + jnp.where(second == here, 1.0 - share, 0.0)

    gate = gate_acc[...] * scale
    h_scr[...] = (gate / (1.0 + jnp.exp(-gate)) * (up_acc[...] * scale)).astype(BF16)

    def columns(part, n, _):
        down_copy(part, n).wait()
        value = jnp.dot(h_scr[...], place(part, n)[...], preferred_element_type=F32) * weight
        to = pl.ds(pl.multiple_of(lax.rem(n, per_side) * d_wide, LANES), d_wide)

        @pl.when(n < per_side)
        def _():
            leaving_ref[:, to] = in_order(value).astype(BF16)

        @pl.when(n >= per_side)
        def _():
            staying_ref[:, to] = value

        return 0

    for part in range(3):
        low, high = min(ends[part], total), min(ends[part + 1], total)
        if low < high:
            lax.fori_loop(low, high, functools.partial(columns, part), 0)


def second_half(per_plane, mine, other, sums, held, gate_weight, up_weight, down_weight):
    rows, units = sums[0].shape
    width = down_weight.shape[1] // 2
    block = mine.shape[2]
    steps = width // block
    d_wide = math.gcd(768, width)
    total = 2 * (width // d_wide)
    depth = max(DOWN_DEPTH, total - 2 * (units // d_wide))
    return pl.pallas_call(
        functools.partial(second_half_kernel, per_plane, READY),
        out_shape=(vmem_array((rows, width), F32), vmem_array((rows, width), BF16))
        + tuple(pltpu.VMEM(h.shape, BF16) for h in held),
        in_specs=[VMEM_SPEC] * 4 + [HBM_SPEC] * 3 + [VMEM_SPEC] * 2,
        out_specs=(VMEM_SPEC,) * 4,
        scratch_shapes=[
            pltpu.VMEM((steps, rows, block), BF16),
            pltpu.VMEM((rows, units), F32),
            pltpu.VMEM((rows, units), F32),
            pltpu.VMEM((rows, units), BF16),
            pltpu.VMEM((depth, units, d_wide), BF16),
            pltpu.SemaphoreType.DMA((2, steps)),
            pltpu.SemaphoreType.DMA((total,)),
        ],
        input_output_aliases={7: 2, 8: 3},
        compiler_params=pltpu.CompilerParams(vmem_limit_bytes=HELD_BELOW if rows < 256 else 40 * MIB),
        cost_estimate=pl.CostEstimate(
            flops=6 * rows * width * units, bytes_accessed=4 * width * units, transcendentals=0
        ),
        name="second_half",
    )(
        *in_vmem_always([mine, other]), *in_vmem(*sums),
        *in_hbm(gate_weight, up_weight, down_weight), *in_vmem_always(held),
    )[:2]


def split_kernel(own_ref, got_ref, keep_ref, send_ref):
    size = keep_ref.shape[0]
    keep_ref[...] = own_ref[:size, :] + got_ref[:size, :].astype(F32)
    send_ref[...] = (own_ref[size:, :] + got_ref[size:, :].astype(F32)).astype(BF16)


def split_rows(own, got):
    rows, width = own.shape
    size = rows // 2
    return pl.pallas_call(
        split_kernel,
        out_shape=(vmem_array((size, width), F32), vmem_array((size, width), BF16)),
        in_specs=[VMEM_SPEC] * 2,
        out_specs=(VMEM_SPEC,) * 2,
        compiler_params=pltpu.CompilerParams(vmem_limit_bytes=(8 if rows < 256 else 32) * MIB),
        name="split_rows",
    )(*in_vmem(own, got))


def split_last_kernel(own_ref, got_ref, keep_ref, *refs):
    *sends, total = refs
    total[...] = own_ref[...] + got_ref[...].astype(F32)
    tok, width = keep_ref.shape
    fold_width = width // FOLD
    keep_ref[...] = total[:tok, :]
    for i, send in enumerate(sends, 1):
        rows = total[i * tok:(i + 1) * tok, :]
        send[...] = jnp.concatenate(
            [rows[:, f * fold_width:(f + 1) * fold_width] for f in range(FOLD)], axis=0
        ).astype(BF16)


def split_last(own, got, parts):
    rows, width = own.shape
    tok = rows // parts
    return pl.pallas_call(
        split_last_kernel,
        out_shape=(pltpu.VMEM((tok, width), F32),)
        + (pltpu.VMEM((FOLD * tok, width // FOLD), BF16),) * (parts - 1),
        in_specs=[VMEM_SPEC] * 2,
        out_specs=(VMEM_SPEC,) * parts,
        scratch_shapes=[pltpu.VMEM((rows, width), F32)],
        compiler_params=pltpu.CompilerParams(vmem_limit_bytes=4 * MIB),
        name="split_last",
    )(*in_vmem(own, got))


def finish_kernel(carried_ref, own_ref, *refs):
    *got, out_ref, folded = refs
    tok, width = carried_ref.shape
    fold_width = width // FOLD
    total = got[0][...].astype(F32)
    for ref in got[1:]:
        total = total + ref[...].astype(F32)
    folded[...] = total
    for f in range(FOLD):
        at = slice(f * fold_width, (f + 1) * fold_width)
        value = carried_ref[:, at] + own_ref[:, at] + folded[f * tok:(f + 1) * tok, :]
        out_ref[:, at] = value.astype(BF16)


def finish(carried, own, got):
    tok, width = carried.shape
    return pl.pallas_call(
        finish_kernel,
        out_shape=jax.ShapeDtypeStruct((tok, width), BF16),
        in_specs=[VMEM_SPEC] * (2 + len(got)),
        out_specs=VMEM_SPEC,
        scratch_shapes=[pltpu.VMEM((FOLD * tok, width // FOLD), F32)],
        compiler_params=pltpu.CompilerParams(vmem_limit_bytes=8 * MIB),
        name="finish",
    )(*in_vmem(carried, own, *got))


def on_device(
    residual, queries, key_cache, value_cache, new_key, new_value, cache_lengths,
    norm_gain, router, routes, gate_weight, up_weight, down_weight,
):
    nodes = lax.axis_size("node")
    per_plane = nodes // EXPERTS
    stages = nodes.bit_length() - 1
    masks = [nodes >> (s + 1) for s in range(stages)]
    routes_of = (masks, masks[:-2] + masks[:-3:-1])

    def exchange(array, *flips):
        masks = [sum(side[s] for s in flips) for side in routes_of]
        perm = [(2 * n + c, 2 * (n ^ masks[c]) + c) for n in range(nodes) for c in range(2)]
        return lax.ppermute(array, ("node", "shard"), perm)

    def to_core(array):
        return lax.ppermute(array, "shard", [(0, 1), (1, 0)])

    tok = residual.shape[0]
    half = gate_weight.shape[0] // 2
    carried, payload = attend(
        cache_lengths, routes.T, queries, key_cache, value_cache, new_key, new_value,
        residual, norm_gain.reshape(1, -1), router.T,
    )
    near = ((0,), (1,), (0, 1))
    got = [exchange(payload, *flips) for flips in near]
    *held, token = load_rows(0, half // 2, payload, gate_weight, up_weight, [])
    payload = unfold(tok, [payload, *got], token)
    for stage in range(2, stages):
        got = exchange(payload, stage)
        if stage == 2:
            *held, token = load_rows(half // 2, half - half // 2, payload, gate_weight, up_weight, held)
        if stage < stages - 1:
            payload = join(payload, got, token)
    mine = spread(0, payload, [], token)
    mine = spread(1, got, [mine], token)
    other = to_core(mine)
    gate, up, *held = first_half(mine, held, gate_weight, up_weight)
    staying, leaving = second_half(
        per_plane, mine, other, (gate, up), held, gate_weight, up_weight, down_weight
    )
    keep, got = staying, to_core(leaving)
    for stage in range(stages - 1, 1, -1):
        keep, send = split_rows(keep, got)
        got = exchange(send, stage)
    keep, *sends = split_last(keep, got, 1 + len(near))
    return finish(carried, keep, [exchange(send, *flips) for send, flips in zip(sends, near)])


def solution(mesh):
    rows = ("replica", "node")
    in_specs = (
        P(rows, "shard"),
        P(rows, "shard"),
        P(rows, None, "shard"),
        P(rows, None, "shard"),
        P(rows, "shard"),
        P(rows, "shard"),
        P(rows),
        P(),
        P(),
        P(rows, None),
        P(None, ("node", "shard")),
        P(None, ("node", "shard")),
        P(("node", "shard"), None),
    )
    return jax.shard_map(
        on_device,
        mesh=mesh,
        in_specs=in_specs,
        out_specs=P(rows, "shard"),
        check_vma=False,
    )
```

```python
import functools
import math

import jax
import jax.numpy as jnp
from jax import lax
from jax.experimental import pallas as pl
from jax.experimental.pallas import tpu as pltpu
from jax.sharding import PartitionSpec as P

MIB = 1 << 20
QUERY_HEADS = 48
KV_HEADS = 8
HEAD_DIM = 128
EXPERTS = 4
GROUP = QUERY_HEADS // KV_HEADS
LANES = 128
FOLD = 2
F32 = jnp.float32
BF16 = jnp.bfloat16


def small(shape, dtype):
    return math.prod(shape) * jnp.dtype(dtype).itemsize <= 17 * MIB // 4


def vmem_array(shape, dtype):
    return pltpu.VMEM(shape, dtype) if small(shape, dtype) else jax.ShapeDtypeStruct(shape, dtype)


def in_vmem(*arrays):
    return [
        pltpu.with_memory_space_constraint(a, pltpu.VMEM) if small(a.shape, a.dtype) else a
        for a in arrays
    ]


def in_vmem_always(arrays):
    return [pltpu.with_memory_space_constraint(a, pltpu.VMEM) for a in arrays]


def in_hbm(*arrays):
    return [pltpu.with_memory_space_constraint(a, pltpu.HBM) for a in arrays]


VMEM_SPEC = pl.BlockSpec(memory_space=pltpu.VMEM)
HBM_SPEC = pl.BlockSpec(memory_space=pltpu.HBM)
ROUTE_LANE = 3 + 3 * EXPERTS
HELD_BELOW = 10 * MIB


def own_side():
    return lax.axis_index("shard")


def chunk_of(units):
    return math.gcd(512, units)


def held_shape(gate_weight):
    width, units = gate_weight.shape
    return width // 2, units + chunk_of(units)


def row_copies(sources, targets, first, rows, sems):
    parts = sems.shape[1]
    part = rows // parts
    half, units = sources[0].shape[0] // 2, sources[0].shape[1]
    copies = []
    for p in range(parts):
        at = first + p * part
        for i, (source, target) in enumerate(zip(sources, targets)):
            copies.append(
                pltpu.make_async_copy(
                    source.at[pl.ds(pl.multiple_of(own_side() * half + at, 16), part), :],
                    target.at[pl.ds(at, part), pl.ds(0, units)], sems.at[i, p],
                )
            )
    return copies


def slot_at(q, chunk, slots):
    start = lax.rem(q, slots) * chunk
    return pl.ds(start if isinstance(q, int) else pl.multiple_of(start, LANES), chunk)


def other_copy(source, target, c, chunk, sem):
    half, units = target.shape[0], source.shape[1]
    chunks = units // chunk
    first = pl.multiple_of((1 - own_side()) * half, 16)
    column = c * chunk if isinstance(c, int) else pl.multiple_of(c * chunk, LANES)
    return pltpu.make_async_copy(
        source.at[pl.ds(first, half), pl.ds(column, chunk)],
        target.at[:, slot_at(chunks + c, chunk, chunks + 1)], sem,
    )


def load_kernel(first, rows, ahead, dep_ref, g_hbm, u_hbm, g_in, u_in, g_vmem, u_vmem, token_ref, sems, sem):
    del g_in, u_in
    copies = row_copies((g_hbm, u_hbm), (g_vmem, u_vmem), first, rows, sems)
    if ahead:
        copies.append(other_copy(g_hbm, g_vmem, 0, chunk_of(g_hbm.shape[1]), sem))
    for copy in copies:
        copy.start()
    token_ref[...] = jnp.zeros_like(token_ref)
    for copy in copies:
        copy.wait()


def load_rows(first, rows, ahead, after, gate_weight, up_weight, held):
    hidden = gate_weight.shape[1]
    return pl.pallas_call(
        functools.partial(load_kernel, first, rows, ahead),
        out_shape=tuple(pltpu.VMEM(h.shape, BF16) for h in held) + (pltpu.VMEM((8, LANES), F32),),
        in_specs=[pl.BlockSpec(memory_space=pl.ANY), HBM_SPEC, HBM_SPEC, VMEM_SPEC, VMEM_SPEC],
        out_specs=(VMEM_SPEC,) * 3,
        scratch_shapes=[pltpu.SemaphoreType.DMA((2, 4)), pltpu.SemaphoreType.DMA],
        input_output_aliases={3: 0, 4: 1},
        compiler_params=pltpu.CompilerParams(vmem_limit_bytes=HELD_BELOW),
        cost_estimate=pl.CostEstimate(flops=0, bytes_accessed=4 * rows * hidden, transcendentals=0),
        name="load_weights",
    )(*in_vmem(after), *in_hbm(gate_weight, up_weight), *in_vmem_always(held))


def unfold_kernel(tok, *refs):
    *arrays, _, out_ref, scr = refs
    fold_width = arrays[0].shape[1] - LANES
    for i, array in enumerate(arrays):
        rows = array[...].astype(F32)
        to = slice(i * tok, (i + 1) * tok)
        for f in range(FOLD):
            scr[to, f * fold_width:(f + 1) * fold_width] = rows[f * tok:(f + 1) * tok, :fold_width]
        scr[to, FOLD * fold_width:] = rows[:tok, fold_width:]
    out_ref[...] = scr[...].astype(BF16)


def unfold(tok, arrays, token):
    shape = (len(arrays) * tok, FOLD * (arrays[0].shape[1] - LANES) + LANES)
    return pl.pallas_call(
        functools.partial(unfold_kernel, tok),
        out_shape=pltpu.VMEM(shape, BF16),
        in_specs=[VMEM_SPEC] * (len(arrays) + 1),
        out_specs=VMEM_SPEC,
        scratch_shapes=[pltpu.VMEM(shape, F32)],
        compiler_params=pltpu.CompilerParams(vmem_limit_bytes=3 * MIB),
        name="unfold",
    )(*in_vmem_always([*arrays, token]))


def join_kernel(a_ref, b_ref, token_ref, out_ref):
    rows = a_ref.shape[0]
    out_ref[:rows, :] = a_ref[...]
    out_ref[rows:, :] = b_ref[...]


def join(a, b, token):
    return pl.pallas_call(
        join_kernel,
        out_shape=vmem_array((a.shape[0] + b.shape[0], a.shape[1]), BF16),
        in_specs=[VMEM_SPEC] * 3,
        out_specs=VMEM_SPEC,
        compiler_params=pltpu.CompilerParams(vmem_limit_bytes=HELD_BELOW),
        name="join",
    )(*in_vmem(a, b, token))


def split_three(value):
    first = value.astype(BF16).astype(F32)
    second = (value - first).astype(BF16).astype(F32)
    return first, second, value - first - second


def attend_kernel(
    ahead, len_hbm, routes_hbm, q_hbm, k_hbm, v_hbm, nk_hbm, nv_hbm, res_hbm, gain_hbm, rt_hbm,
    g_hbm, u_hbm, carried_ref, pay_ref, g_vmem, u_vmem,
    q_ref, k_ref, v_ref, nk_ref, nv_ref, res_ref, gain_ref, rt_ref,
    q_scr, o_scr, nk_scr, nv_scr, pay_scr, len_ref, routes_ref, sems, w_sems,
):
    tok, width = q_ref.shape
    cache_len, kv_width = k_ref.shape[1], k_ref.shape[2]
    heads = width // HEAD_DIM
    groups = kv_width // HEAD_DIM
    fold_width = width // FOLD
    scaling = 1.0 / math.sqrt(HEAD_DIM)
    columns = pl.ds(pl.multiple_of(own_side() * width, LANES), width)
    moves = [
        (q_hbm, q_ref), (k_hbm, k_ref), (nk_hbm, nk_ref), (len_hbm, len_ref), (v_hbm, v_ref),
        (nv_hbm, nv_ref), (res_hbm, res_ref),
        (gain_hbm.at[:, columns], gain_ref), (rt_hbm.at[:, columns], rt_ref),
        (routes_hbm, routes_ref),
    ]
    copies = [pltpu.make_async_copy(a, b, sems.at[i]) for i, (a, b) in enumerate(moves)]
    weights = row_copies((g_hbm, u_hbm), (g_vmem, u_vmem), 0, ahead, w_sems)
    for copy in copies:
        copy.start()
    copies[0].wait()
    for h in range(heads):
        q_scr[h * tok:(h + 1) * tok, :] = q_ref[:, h * HEAD_DIM:(h + 1) * HEAD_DIM].astype(F32)
    copies[2].wait()
    nk_scr[...] = nk_ref[...].astype(F32)
    row_group = lax.broadcasted_iota(jnp.int32, (heads, HEAD_DIM), 0) // GROUP
    position = lax.broadcasted_iota(jnp.int32, (heads, cache_len), 1)
    scores, fresh = [], []
    for t in range(tok):
        if t == 0:
            copies[1].wait()
            for copy in weights:
                copy.start()
        q_rows = q_scr[pl.ds(t, heads, stride=tok), :]
        q_wide = jnp.concatenate(
            [jnp.where(row_group == g, q_rows, 0.0) for g in range(groups)], axis=1
        )
        scores.append(
            lax.dot_general(
                q_wide.astype(BF16), k_ref[t], (((1,), (1,)), ((), ())),
                preferred_element_type=F32,
            ) * scaling
        )
        fresh.append(
            jnp.sum(q_wide * nk_scr[pl.ds(t, 1), :], axis=1, keepdims=True) * scaling
        )
    copies[3].wait()
    terms, fresh_terms, totals = [], [], []
    for t in range(tok):
        score = jnp.where(position < len_ref[t], scores[t], -1e30)
        largest = jnp.maximum(jnp.max(score, axis=1, keepdims=True), fresh[t])
        term = jnp.exp(score - largest)
        fresh_term = jnp.exp(fresh[t] - largest)
        totals.append(jnp.sum(term, axis=1, keepdims=True) + fresh_term)
        terms.append(term.astype(BF16))
        fresh_terms.append(fresh_term.astype(BF16).astype(F32))
    copies[5].wait()
    nv_scr[...] = nv_ref[...].astype(F32)
    for t in range(tok):
        if t == 0:
            copies[4].wait()
        wide = jnp.dot(terms[t], v_ref[t], preferred_element_type=F32)
        wide = wide + fresh_terms[t] * nv_scr[pl.ds(t, 1), :]
        picked = wide[:, :HEAD_DIM]
        for g in range(1, groups):
            picked = jnp.where(
                row_group == g, wide[:, g * HEAD_DIM:(g + 1) * HEAD_DIM], picked
            )
        o_scr[pl.ds(t, heads, stride=tok), :] = picked / totals[t]
    for copy in copies[6:]:
        copy.wait()
    for h in range(heads):
        cols = slice(h * HEAD_DIM, (h + 1) * HEAD_DIM)
        carried_ref[:, cols] = res_ref[:, cols].astype(F32) + o_scr[h * tok:(h + 1) * tok, :]
    carried = carried_ref[...]
    scaled = carried * gain_ref[...]
    rounded = scaled.astype(BF16).astype(F32)
    router = rt_ref[...].astype(F32)
    for f in range(FOLD):
        pay_scr[f * tok:(f + 1) * tok, :fold_width] = scaled[:, f * fold_width:(f + 1) * fold_width]
    lane = lax.broadcasted_iota(jnp.int32, (tok, LANES), 1)
    row = lax.broadcasted_iota(jnp.int32, (tok, LANES), 0)
    sums = [jnp.sum(carried * carried, axis=1, keepdims=True)]
    for e in range(EXPERTS):
        sums.append(jnp.sum(rounded * router[e:e + 1, :], axis=1, keepdims=True))
    extra = jnp.zeros((tok, LANES), F32)
    for i, total in enumerate(sums):
        for j, term in enumerate(split_three(total)):
            extra = jnp.where(lane == 3 * i + j, term, extra)
    for t in range(tok):
        for i in range(2):
            extra = jnp.where(
                jnp.logical_and(row == t, lane == ROUTE_LANE + i),
                routes_ref[i, t].astype(F32), extra,
            )
    for f in range(FOLD):
        pay_scr[f * tok:(f + 1) * tok, fold_width:] = extra
    pay_ref[...] = pay_scr[...].astype(BF16)
    for copy in weights:
        copy.wait()


def attend(
    ahead, lengths, routes_t, queries, key_cache, value_cache, new_key, new_value,
    residual, gain, router_t, gate_weight, up_weight,
):
    tok, width = queries.shape
    kv_width = new_key.shape[1]
    heads = width // HEAD_DIM
    wide = width // FOLD + LANES
    here = [
        pltpu.VMEM(a.shape, a.dtype)
        for a in (queries, key_cache, value_cache, new_key, new_value, residual)
    ]
    return pl.pallas_call(
        functools.partial(attend_kernel, ahead),
        out_shape=(
            pltpu.VMEM((tok, width), F32),
            pltpu.VMEM((FOLD * tok, wide), BF16),
            pltpu.VMEM(held_shape(gate_weight), BF16),
            pltpu.VMEM(held_shape(gate_weight), BF16),
        ),
        in_specs=[HBM_SPEC] * 12,
        out_specs=(VMEM_SPEC,) * 4,
        scratch_shapes=here + [
            pltpu.VMEM((1, width), F32),
            pltpu.VMEM((EXPERTS, width), BF16),
            pltpu.VMEM((heads * tok, HEAD_DIM), F32),
            pltpu.VMEM((heads * tok, HEAD_DIM), F32),
            pltpu.VMEM((tok, kv_width), F32),
            pltpu.VMEM((tok, kv_width), F32),
            pltpu.VMEM((FOLD * tok, wide), F32),
            pltpu.SMEM(lengths.shape, jnp.int32),
            pltpu.SMEM(routes_t.shape, jnp.int32),
            pltpu.SemaphoreType.DMA((10,)),
            pltpu.SemaphoreType.DMA((2, 1)),
        ],
        compiler_params=pltpu.CompilerParams(vmem_limit_bytes=HELD_BELOW),
        cost_estimate=pl.CostEstimate(flops=10**8, bytes_accessed=8 * 10**6, transcendentals=10**5),
        name="attend",
    )(
        *in_hbm(
            lengths, routes_t, queries, key_cache, value_cache, new_key, new_value, residual, gain, router_t,
            gate_weight, up_weight,
        ),
    )


def first_half_kernel(x_ref, g_hbm, u_hbm, g_in, u_in, gate_ref, up_ref, g_ref, u_ref, sems):
    del g_in, u_in
    half, units = g_ref.shape[0], gate_ref.shape[1]
    chunk = chunk_of(units)
    chunks = units // chunk
    ready = [(1, 0)] + [(0, 1), (1, 1), (0, 2)][:2 * (chunks - 1)]
    ready = [(i, c) for i, c in ready if c < chunks]

    def copy(i, c):
        return other_copy((g_hbm, u_hbm)[i], (g_ref, u_ref)[i], c, chunk, sems.at[i, c])

    copy(1, 0).start()

    def step(n, _):
        at = pl.ds(pl.multiple_of(n * chunk, LANES), chunk)
        rows = x_ref[:, :half]
        gate_ref[:, at] = jnp.dot(rows, g_ref[:, at], preferred_element_type=F32)
        up_ref[:, at] = jnp.dot(rows, u_ref[:, at], preferred_element_type=F32)
        for i, c in ready[1:]:
            @pl.when(n == c - 1)
            def _(i=i, c=c):
                copy(i, c).start()

        return 0

    lax.fori_loop(0, chunks, step, 0)
    for i, c in ready:
        copy(i, c).wait()


def first_half(mine, held, gate_weight, up_weight):
    rows = mine.shape[0]
    width, units = gate_weight.shape
    acc = pltpu.VMEM((rows, units), F32)
    return pl.pallas_call(
        first_half_kernel,
        out_shape=(acc, acc) + tuple(pltpu.VMEM(h.shape, BF16) for h in held),
        in_specs=[VMEM_SPEC] + [HBM_SPEC] * 2 + [VMEM_SPEC] * 2,
        out_specs=(VMEM_SPEC,) * 4,
        scratch_shapes=[pltpu.SemaphoreType.DMA((2, units // chunk_of(units)))],
        input_output_aliases={3: 2, 4: 3},
        compiler_params=pltpu.CompilerParams(vmem_limit_bytes=HELD_BELOW),
        cost_estimate=pl.CostEstimate(
            flops=2 * rows * width * units, bytes_accessed=width * units, transcendentals=0
        ),
        name="first_half",
    )(*in_vmem_always([mine]), *in_hbm(gate_weight, up_weight), *in_vmem_always(held))


def second_half_kernel(
    per_plane, x_ref, ox_ref, gate_ref, up_ref, g_hbm, u_hbm, d_hbm, g_in, u_in,
    staying_ref, leaving_ref, g_ref, u_ref, x_scr, h_scr, gu_sems, sems,
):
    del g_in, u_in
    rows, units = h_scr.shape
    width = staying_ref.shape[1]
    side = own_side()
    chunk = chunk_of(units)
    chunks = units // chunk
    slots = chunks + 1
    per_side = width // chunk
    pairs = per_side

    def gu_copy(i, c):
        return other_copy((g_hbm, u_hbm)[i], (g_ref, u_ref)[i], c, chunk, gu_sems.at[i, c])

    def down_copy(i, p):
        n = 2 * p + i
        column = jnp.where(n < per_side, 1 - side, side) * width + lax.rem(n, per_side) * chunk
        return pltpu.make_async_copy(
            d_hbm.at[:, pl.ds(pl.multiple_of(column, LANES), chunk)],
            (g_ref, u_ref)[i].at[pl.ds(0, units), slot_at(2 * chunks + p, chunk, slots)],
            sems.at[i, p],
        )

    def in_order(values):
        quarter = rows // 4
        return jnp.concatenate(
            [values[q * quarter:(q + 1) * quarter, :] for q in (0, 2, 1, 3)], axis=0
        )

    later = [(1, 2)] if chunks > 2 else []
    later += [(i, c) for c in range(3, chunks) for i in range(2)]
    for i, c in later:
        gu_copy(i, c).start()
    for i in range(2):
        down_copy(i, 0).start()
    x_scr[...] = in_order(ox_ref[:, :width].astype(F32)).astype(BF16)

    own = x_ref[:, width:].astype(F32)
    both = own + in_order(ox_ref[:, width:].astype(F32))
    lane = lax.broadcasted_iota(jnp.int32, (rows, LANES), 1)

    def pick(values, mask):
        return jnp.sum(jnp.where(mask, values, 0.0), axis=1, keepdims=True)

    scale = lax.rsqrt(pick(both, lane < 3) * (1.0 / (2 * width)) + 1e-05)
    first, second = pick(own, lane == ROUTE_LANE), pick(own, lane == ROUTE_LANE + 1)
    expert_of = (lane - 3) // 3
    logit_lane = jnp.logical_and(lane >= 3, lane < ROUTE_LANE)

    def logit_at(route):
        return pick(both, jnp.logical_and(logit_lane, expert_of == route.astype(jnp.int32))) * scale

    share = 1.0 / (1.0 + jnp.exp(logit_at(second) - logit_at(first)))
    here = (lax.axis_index("node") // per_plane).astype(F32)
    weight = jnp.where(first == here, share, 0.0) + jnp.where(second == here, 1.0 - share, 0.0)

    def hidden_step(c, _):
        for i, late in later:
            @pl.when(c == late)
            def _(i=i, late=late):
                gu_copy(i, late).wait()

        slot = slot_at(chunks + c, chunk, slots)
        at = pl.ds(pl.multiple_of(c * chunk, LANES), chunk)
        gate = gate_ref[:, at] + jnp.dot(x_scr[...], g_ref[:, slot], preferred_element_type=F32)
        up = up_ref[:, at] + jnp.dot(x_scr[...], u_ref[:, slot], preferred_element_type=F32)
        gate = gate * scale
        h_scr[:, at] = (gate / (1.0 + jnp.exp(-gate)) * (up * scale)).astype(BF16)

        @pl.when(c + 1 < pairs)
        def _():
            for i in range(2):
                down_copy(i, c + 1).start()

        return 0

    lax.fori_loop(0, chunks, hidden_step, 0)

    def down_step(p, _):
        slot = slot_at(2 * chunks + p, chunk, slots)
        for i, ref in enumerate((g_ref, u_ref)):
            n = 2 * p + i
            down_copy(i, p).wait()
            value = jnp.dot(h_scr[...], ref[:units, slot], preferred_element_type=F32) * weight
            to = pl.ds(pl.multiple_of(lax.rem(n, per_side) * chunk, LANES), chunk)

            @pl.when(n < per_side)
            def _(value=value, to=to):
                leaving_ref[:, to] = in_order(value).astype(BF16)

            @pl.when(n >= per_side)
            def _(value=value, to=to):
                staying_ref[:, to] = value

        @pl.when(p + slots < pairs)
        def _():
            for i in range(2):
                down_copy(i, p + slots).start()

        return 0

    lax.fori_loop(0, pairs, down_step, 0)


def second_half(per_plane, mine, other, sums, held, gate_weight, up_weight, down_weight):
    rows, units = sums[0].shape
    width = down_weight.shape[1] // 2
    chunk = chunk_of(units)
    return pl.pallas_call(
        functools.partial(second_half_kernel, per_plane),
        out_shape=(vmem_array((rows, width), F32), vmem_array((rows, width), BF16))
        + tuple(pltpu.VMEM(h.shape, BF16) for h in held),
        in_specs=[VMEM_SPEC] * 4 + [HBM_SPEC] * 3 + [VMEM_SPEC] * 2,
        out_specs=(VMEM_SPEC,) * 4,
        scratch_shapes=[
            pltpu.VMEM((rows, width), BF16),
            pltpu.VMEM((rows, units), BF16),
            pltpu.SemaphoreType.DMA((2, units // chunk)),
            pltpu.SemaphoreType.DMA((2, width // chunk)),
        ],
        input_output_aliases={7: 2, 8: 3},
        compiler_params=pltpu.CompilerParams(
            vmem_limit_bytes=HELD_BELOW if rows < 256 else 40 * MIB
        ),
        cost_estimate=pl.CostEstimate(
            flops=6 * rows * width * units, bytes_accessed=4 * width * units, transcendentals=0
        ),
        name="second_half",
    )(
        *in_vmem_always([mine, other]), *in_vmem(*sums),
        *in_hbm(gate_weight, up_weight, down_weight), *in_vmem_always(held),
    )[:2]


def split_kernel(own_ref, got_ref, keep_ref, send_ref):
    size = keep_ref.shape[0]
    keep_ref[...] = own_ref[:size, :] + got_ref[:size, :].astype(F32)
    send_ref[...] = (own_ref[size:, :] + got_ref[size:, :].astype(F32)).astype(BF16)


def split_rows(own, got):
    rows, width = own.shape
    size = rows // 2
    return pl.pallas_call(
        split_kernel,
        out_shape=(vmem_array((size, width), F32), vmem_array((size, width), BF16)),
        in_specs=[VMEM_SPEC] * 2,
        out_specs=(VMEM_SPEC,) * 2,
        compiler_params=pltpu.CompilerParams(vmem_limit_bytes=(8 if rows < 256 else 32) * MIB),
        name="split_rows",
    )(*in_vmem(own, got))


def split_last_kernel(own_ref, got_ref, keep_ref, *refs):
    *sends, total = refs
    total[...] = own_ref[...] + got_ref[...].astype(F32)
    tok, width = keep_ref.shape
    fold_width = width // FOLD
    keep_ref[...] = total[:tok, :]
    for i, send in enumerate(sends, 1):
        rows = total[i * tok:(i + 1) * tok, :]
        send[...] = jnp.concatenate(
            [rows[:, f * fold_width:(f + 1) * fold_width] for f in range(FOLD)], axis=0
        ).astype(BF16)


def split_last(own, got, parts):
    rows, width = own.shape
    tok = rows // parts
    return pl.pallas_call(
        split_last_kernel,
        out_shape=(pltpu.VMEM((tok, width), F32),)
        + (pltpu.VMEM((FOLD * tok, width // FOLD), BF16),) * (parts - 1),
        in_specs=[VMEM_SPEC] * 2,
        out_specs=(VMEM_SPEC,) * parts,
        scratch_shapes=[pltpu.VMEM((rows, width), F32)],
        compiler_params=pltpu.CompilerParams(vmem_limit_bytes=4 * MIB),
        name="split_last",
    )(*in_vmem(own, got))


def finish_kernel(carried_ref, own_ref, *refs):
    *got, out_ref, folded = refs
    tok, width = carried_ref.shape
    fold_width = width // FOLD
    total = got[0][...].astype(F32)
    for ref in got[1:]:
        total = total + ref[...].astype(F32)
    folded[...] = total
    for f in range(FOLD):
        at = slice(f * fold_width, (f + 1) * fold_width)
        value = carried_ref[:, at] + own_ref[:, at] + folded[f * tok:(f + 1) * tok, :]
        out_ref[:, at] = value.astype(BF16)


def finish(carried, own, got):
    tok, width = carried.shape
    return pl.pallas_call(
        finish_kernel,
        out_shape=jax.ShapeDtypeStruct((tok, width), BF16),
        in_specs=[VMEM_SPEC] * (2 + len(got)),
        out_specs=VMEM_SPEC,
        scratch_shapes=[pltpu.VMEM((FOLD * tok, width // FOLD), F32)],
        compiler_params=pltpu.CompilerParams(vmem_limit_bytes=8 * MIB),
        name="finish",
    )(*in_vmem(carried, own, *got))


def on_device(
    residual, queries, key_cache, value_cache, new_key, new_value, cache_lengths,
    norm_gain, router, routes, gate_weight, up_weight, down_weight,
):
    nodes = lax.axis_size("node")
    per_plane = nodes // EXPERTS
    stages = nodes.bit_length() - 1
    masks = [nodes >> (s + 1) for s in range(stages)]
    routes_of = (masks, masks[:-2] + masks[:-3:-1])

    def exchange(array, *flips):
        masks = [sum(side[s] for s in flips) for side in routes_of]
        perm = [(2 * n + c, 2 * (n ^ masks[c]) + c) for n in range(nodes) for c in range(2)]
        return lax.ppermute(array, ("node", "shard"), perm)

    def to_core(array):
        return lax.ppermute(array, "shard", [(0, 1), (1, 0)])

    tok = residual.shape[0]
    half = gate_weight.shape[0] // 2
    heights = [half // 6, half // 2, half // 3]
    carried, payload, *held = attend(
        heights[0], cache_lengths, routes.T, queries, key_cache, value_cache, new_key, new_value,
        residual, norm_gain.reshape(1, -1), router.T, gate_weight, up_weight,
    )
    near = ((0,), (1,), (0, 1))
    got = [exchange(payload, *flips) for flips in near]
    *held, token = load_rows(
        heights[0], heights[1], False, payload, gate_weight, up_weight, held
    )
    payload = unfold(tok, [payload, *got], token)
    for stage in range(2, stages):
        got = exchange(payload, stage)
        if stage == 2:
            *held, token = load_rows(
                heights[0] + heights[1], heights[2], True, payload, gate_weight, up_weight, held
            )
        payload = join(payload, got, token)
    mine = payload
    other = to_core(mine)
    gate, up, *held = first_half(mine, held, gate_weight, up_weight)
    staying, leaving = second_half(
        per_plane, mine, other, (gate, up), held, gate_weight, up_weight, down_weight
    )
    keep, got = staying, to_core(leaving)
    for stage in range(stages - 1, 1, -1):
        keep, send = split_rows(keep, got)
        got = exchange(send, stage)
    keep, *sends = split_last(keep, got, 1 + len(near))
    return finish(carried, keep, [exchange(send, *flips) for send, flips in zip(sends, near)])


def solution(mesh):
    rows = ("replica", "node")
    in_specs = (
        P(rows, "shard"),
        P(rows, "shard"),
        P(rows, None, "shard"),
        P(rows, None, "shard"),
        P(rows, "shard"),
        P(rows, "shard"),
        P(rows),
        P(),
        P(),
        P(rows, None),
        P(None, ("node", "shard")),
        P(None, ("node", "shard")),
        P(("node", "shard"), None),
    )
    return jax.shard_map(
        on_device,
        mesh=mesh,
        in_specs=in_specs,
        out_specs=P(rows, "shard"),
        check_vma=False,
    )
```

```python
import functools
import math

import jax
import jax.numpy as jnp
from jax import lax
from jax.experimental import pallas as pl
from jax.experimental.pallas import tpu as pltpu
from jax.sharding import PartitionSpec as P

MIB = 1 << 20
QUERY_HEADS = 48
KV_HEADS = 8
HEAD_DIM = 128
EXPERTS = 4
GROUP = QUERY_HEADS // KV_HEADS
LANES = 128
FOLD = 2
F32 = jnp.float32
BF16 = jnp.bfloat16


def small(shape, dtype):
    return math.prod(shape) * jnp.dtype(dtype).itemsize <= 17 * MIB // 4


def vmem_array(shape, dtype):
    return pltpu.VMEM(shape, dtype) if small(shape, dtype) else jax.ShapeDtypeStruct(shape, dtype)


def in_vmem(*arrays):
    return [
        pltpu.with_memory_space_constraint(a, pltpu.VMEM) if small(a.shape, a.dtype) else a
        for a in arrays
    ]


def in_vmem_always(arrays):
    return [pltpu.with_memory_space_constraint(a, pltpu.VMEM) for a in arrays]


def in_hbm(*arrays):
    return [pltpu.with_memory_space_constraint(a, pltpu.HBM) for a in arrays]


VMEM_SPEC = pl.BlockSpec(memory_space=pltpu.VMEM)
HBM_SPEC = pl.BlockSpec(memory_space=pltpu.HBM)
ROUTE_LANE = 3 + 3 * EXPERTS
HELD_BELOW = 10 * MIB
LOADED_BELOW = 12 * MIB


def own_side():
    return lax.axis_index("shard")


def chunk_of(units):
    return math.gcd(512, units)


def held_shape(gate_weight):
    width, units = gate_weight.shape
    return width // 2, units


def spare_shape(gate_weight):
    width, units = gate_weight.shape
    return 2, width // 2, chunk_of(units)


def row_copies(sources, targets, first, rows, sems):
    parts = sems.shape[1]
    part = rows // parts
    half, units = sources[0].shape[0] // 2, sources[0].shape[1]
    copies = []
    for p in range(parts):
        at = first + p * part
        for i, (source, target) in enumerate(zip(sources, targets)):
            copies.append(
                pltpu.make_async_copy(
                    source.at[pl.ds(pl.multiple_of(own_side() * half + at, 16), part), :],
                    target.at[pl.ds(at, part), pl.ds(0, units)], sems.at[i, p],
                )
            )
    return copies


def chunk_at(n, chunk):
    return pl.ds(n * chunk if isinstance(n, int) else pl.multiple_of(n * chunk, LANES), chunk)


def other_copy(source, held, spare, c, chunk, sem):
    half = source.shape[0] // 2
    first = pl.multiple_of((1 - own_side()) * half, 16)
    target = spare if isinstance(c, int) and c == 0 else held.at[:, chunk_at(c - 1, chunk)]
    return pltpu.make_async_copy(source.at[pl.ds(first, half), chunk_at(c, chunk)], target, sem)


def load_kernel(first, rows, ahead, dep_ref, g_hbm, u_hbm, g_in, u_in, g_vmem, u_vmem, *refs):
    del dep_ref, g_in, u_in
    *spare, token_ref, sems, sem = refs
    copies = row_copies((g_hbm, u_hbm), (g_vmem, u_vmem), first, rows, sems)
    if ahead:
        copies.append(other_copy(g_hbm, None, spare[0].at[0], 0, spare[0].shape[2], sem))
    for copy in copies:
        copy.start()
    token_ref[...] = jnp.zeros_like(token_ref)
    for copy in copies:
        copy.wait()


def load_rows(first, rows, ahead, after, gate_weight, up_weight, held):
    hidden = gate_weight.shape[1]
    spare = (pltpu.VMEM(spare_shape(gate_weight), BF16),) if ahead else ()
    return pl.pallas_call(
        functools.partial(load_kernel, first, rows, ahead),
        out_shape=tuple(pltpu.VMEM(h.shape, BF16) for h in held) + spare
        + (pltpu.VMEM((8, LANES), F32),),
        in_specs=[pl.BlockSpec(memory_space=pl.ANY), HBM_SPEC, HBM_SPEC, VMEM_SPEC, VMEM_SPEC],
        out_specs=(VMEM_SPEC,) * (3 + len(spare)),
        scratch_shapes=[pltpu.SemaphoreType.DMA((2, 4)), pltpu.SemaphoreType.DMA],
        input_output_aliases={3: 0, 4: 1},
        compiler_params=pltpu.CompilerParams(vmem_limit_bytes=LOADED_BELOW),
        cost_estimate=pl.CostEstimate(flops=0, bytes_accessed=4 * rows * hidden, transcendentals=0),
        name="load_weights",
    )(*in_vmem(after), *in_hbm(gate_weight, up_weight), *in_vmem_always(held))


def unfold_kernel(tok, *refs):
    *arrays, _, out_ref, scr = refs
    fold_width = arrays[0].shape[1] - LANES
    for i, array in enumerate(arrays):
        rows = array[...].astype(F32)
        to = slice(i * tok, (i + 1) * tok)
        for f in range(FOLD):
            scr[to, f * fold_width:(f + 1) * fold_width] = rows[f * tok:(f + 1) * tok, :fold_width]
        scr[to, FOLD * fold_width:] = rows[:tok, fold_width:]
    out_ref[...] = scr[...].astype(BF16)


def unfold(tok, arrays, token):
    shape = (len(arrays) * tok, FOLD * (arrays[0].shape[1] - LANES) + LANES)
    return pl.pallas_call(
        functools.partial(unfold_kernel, tok),
        out_shape=pltpu.VMEM(shape, BF16),
        in_specs=[VMEM_SPEC] * (len(arrays) + 1),
        out_specs=VMEM_SPEC,
        scratch_shapes=[pltpu.VMEM(shape, F32)],
        compiler_params=pltpu.CompilerParams(vmem_limit_bytes=3 * MIB),
        name="unfold",
    )(*in_vmem_always([*arrays, token]))


def join_kernel(a_ref, b_ref, token_ref, out_ref):
    rows = a_ref.shape[0]
    out_ref[:rows, :] = a_ref[...]
    out_ref[rows:, :] = b_ref[...]


def join(a, b, token):
    return pl.pallas_call(
        join_kernel,
        out_shape=vmem_array((a.shape[0] + b.shape[0], a.shape[1]), BF16),
        in_specs=[VMEM_SPEC] * 3,
        out_specs=VMEM_SPEC,
        compiler_params=pltpu.CompilerParams(vmem_limit_bytes=HELD_BELOW),
        name="join",
    )(*in_vmem(a, b, token))


def split_three(value):
    first = value.astype(BF16).astype(F32)
    second = (value - first).astype(BF16).astype(F32)
    return first, second, value - first - second


def attend_kernel(
    ahead, len_hbm, routes_hbm, q_hbm, k_hbm, v_hbm, nk_hbm, nv_hbm, res_hbm, gain_hbm, rt_hbm,
    g_hbm, u_hbm, carried_ref, pay_ref, g_vmem, u_vmem,
    q_ref, k_ref, v_ref, nk_ref, nv_ref, res_ref, gain_ref, rt_ref,
    q_scr, o_scr, nk_scr, nv_scr, pay_scr, len_ref, routes_ref, sems, w_sems,
):
    tok, width = q_ref.shape
    cache_len, kv_width = k_ref.shape[1], k_ref.shape[2]
    heads = width // HEAD_DIM
    groups = kv_width // HEAD_DIM
    fold_width = width // FOLD
    scaling = 1.0 / math.sqrt(HEAD_DIM)
    columns = pl.ds(pl.multiple_of(own_side() * width, LANES), width)
    moves = [
        (q_hbm, q_ref), (k_hbm, k_ref), (nk_hbm, nk_ref), (len_hbm, len_ref), (v_hbm, v_ref),
        (nv_hbm, nv_ref), (res_hbm, res_ref),
        (gain_hbm.at[:, columns], gain_ref), (rt_hbm.at[:, columns], rt_ref),
        (routes_hbm, routes_ref),
    ]
    copies = [pltpu.make_async_copy(a, b, sems.at[i]) for i, (a, b) in enumerate(moves)]
    weights = row_copies((g_hbm, u_hbm), (g_vmem, u_vmem), 0, ahead, w_sems)
    for copy in copies + weights:
        copy.start()
    copies[0].wait()
    for h in range(heads):
        q_scr[h * tok:(h + 1) * tok, :] = q_ref[:, h * HEAD_DIM:(h + 1) * HEAD_DIM].astype(F32)
    copies[2].wait()
    nk_scr[...] = nk_ref[...].astype(F32)
    row_group = lax.broadcasted_iota(jnp.int32, (heads, HEAD_DIM), 0) // GROUP
    position = lax.broadcasted_iota(jnp.int32, (heads, cache_len), 1)
    scores, fresh = [], []
    for t in range(tok):
        if t == 0:
            copies[1].wait()
        q_rows = q_scr[pl.ds(t, heads, stride=tok), :]
        q_wide = jnp.concatenate(
            [jnp.where(row_group == g, q_rows, 0.0) for g in range(groups)], axis=1
        )
        scores.append(
            lax.dot_general(
                q_wide.astype(BF16), k_ref[t], (((1,), (1,)), ((), ())),
                preferred_element_type=F32,
            ) * scaling
        )
        fresh.append(
            jnp.sum(q_wide * nk_scr[pl.ds(t, 1), :], axis=1, keepdims=True) * scaling
        )
    copies[3].wait()
    terms, fresh_terms, totals = [], [], []
    for t in range(tok):
        score = jnp.where(position < len_ref[t], scores[t], -1e30)
        largest = jnp.maximum(jnp.max(score, axis=1, keepdims=True), fresh[t])
        term = jnp.exp(score - largest)
        fresh_term = jnp.exp(fresh[t] - largest)
        totals.append(jnp.sum(term, axis=1, keepdims=True) + fresh_term)
        terms.append(term.astype(BF16))
        fresh_terms.append(fresh_term.astype(BF16).astype(F32))
    copies[5].wait()
    nv_scr[...] = nv_ref[...].astype(F32)
    for t in range(tok):
        if t == 0:
            copies[4].wait()
        wide = jnp.dot(terms[t], v_ref[t], preferred_element_type=F32)
        wide = wide + fresh_terms[t] * nv_scr[pl.ds(t, 1), :]
        picked = wide[:, :HEAD_DIM]
        for g in range(1, groups):
            picked = jnp.where(
                row_group == g, wide[:, g * HEAD_DIM:(g + 1) * HEAD_DIM], picked
            )
        o_scr[pl.ds(t, heads, stride=tok), :] = picked / totals[t]
    for copy in copies[6:]:
        copy.wait()
    for h in range(heads):
        cols = slice(h * HEAD_DIM, (h + 1) * HEAD_DIM)
        carried_ref[:, cols] = res_ref[:, cols].astype(F32) + o_scr[h * tok:(h + 1) * tok, :]
    carried = carried_ref[...]
    scaled = carried * gain_ref[...]
    rounded = scaled.astype(BF16).astype(F32)
    router = rt_ref[...].astype(F32)
    for f in range(FOLD):
        pay_scr[f * tok:(f + 1) * tok, :fold_width] = scaled[:, f * fold_width:(f + 1) * fold_width]
    lane = lax.broadcasted_iota(jnp.int32, (tok, LANES), 1)
    row = lax.broadcasted_iota(jnp.int32, (tok, LANES), 0)
    sums = [jnp.sum(carried * carried, axis=1, keepdims=True)]
    for e in range(EXPERTS):
        sums.append(jnp.sum(rounded * router[e:e + 1, :], axis=1, keepdims=True))
    extra = jnp.zeros((tok, LANES), F32)
    for i, total in enumerate(sums):
        for j, term in enumerate(split_three(total)):
            extra = jnp.where(lane == 3 * i + j, term, extra)
    for t in range(tok):
        for i in range(2):
            extra = jnp.where(
                jnp.logical_and(row == t, lane == ROUTE_LANE + i),
                routes_ref[i, t].astype(F32), extra,
            )
    for f in range(FOLD):
        pay_scr[f * tok:(f + 1) * tok, fold_width:] = extra
    pay_ref[...] = pay_scr[...].astype(BF16)
    for copy in weights:
        copy.wait()


def attend(
    ahead, lengths, routes_t, queries, key_cache, value_cache, new_key, new_value,
    residual, gain, router_t, gate_weight, up_weight,
):
    tok, width = queries.shape
    kv_width = new_key.shape[1]
    heads = width // HEAD_DIM
    wide = width // FOLD + LANES
    here = [
        pltpu.VMEM(a.shape, a.dtype)
        for a in (queries, key_cache, value_cache, new_key, new_value, residual)
    ]
    return pl.pallas_call(
        functools.partial(attend_kernel, ahead),
        out_shape=(
            pltpu.VMEM((tok, width), F32),
            pltpu.VMEM((FOLD * tok, wide), BF16),
            pltpu.VMEM(held_shape(gate_weight), BF16),
            pltpu.VMEM(held_shape(gate_weight), BF16),
        ),
        in_specs=[HBM_SPEC] * 12,
        out_specs=(VMEM_SPEC,) * 4,
        scratch_shapes=here + [
            pltpu.VMEM((1, width), F32),
            pltpu.VMEM((EXPERTS, width), BF16),
            pltpu.VMEM((heads * tok, HEAD_DIM), F32),
            pltpu.VMEM((heads * tok, HEAD_DIM), F32),
            pltpu.VMEM((tok, kv_width), F32),
            pltpu.VMEM((tok, kv_width), F32),
            pltpu.VMEM((FOLD * tok, wide), F32),
            pltpu.SMEM(lengths.shape, jnp.int32),
            pltpu.SMEM(routes_t.shape, jnp.int32),
            pltpu.SemaphoreType.DMA((10,)),
            pltpu.SemaphoreType.DMA((2, 1)),
        ],
        compiler_params=pltpu.CompilerParams(vmem_limit_bytes=LOADED_BELOW),
        cost_estimate=pl.CostEstimate(flops=10**8, bytes_accessed=8 * 10**6, transcendentals=10**5),
        name="attend",
    )(
        *in_hbm(
            lengths, routes_t, queries, key_cache, value_cache, new_key, new_value, residual, gain, router_t,
            gate_weight, up_weight,
        ),
    )


def first_half_kernel(
    x_ref, g_hbm, u_hbm, g_in, u_in, spare_in, gate_ref, up_ref, g_ref, u_ref, spare_ref, sems
):
    del g_in, u_in, spare_in
    half, units = g_ref.shape[0], gate_ref.shape[1]
    chunk = chunk_of(units)
    chunks = units // chunk
    ready = [(1, 0)] + [(0, 1), (1, 1), (0, 2)][:2 * (chunks - 1)]
    ready = [(i, c) for i, c in ready if c < chunks]

    def copy(i, c):
        return other_copy(
            (g_hbm, u_hbm)[i], (g_ref, u_ref)[i], spare_ref.at[i], c, chunk, sems.at[i, c]
        )

    copy(1, 0).start()

    def step(n, _):
        at = chunk_at(n, chunk)
        rows = x_ref[:, :half]
        gate_ref[:, at] = jnp.dot(rows, g_ref[:, at], preferred_element_type=F32)
        up_ref[:, at] = jnp.dot(rows, u_ref[:, at], preferred_element_type=F32)
        for i, c in ready[1:]:
            @pl.when(n == c - 1)
            def _(i=i, c=c):
                copy(i, c).start()

        return 0

    lax.fori_loop(0, chunks, step, 0)
    for i, c in ready:
        copy(i, c).wait()


def first_half(mine, held, spare, gate_weight, up_weight):
    rows = mine.shape[0]
    width, units = gate_weight.shape
    acc = pltpu.VMEM((rows, units), F32)
    return pl.pallas_call(
        first_half_kernel,
        out_shape=(acc, acc) + tuple(pltpu.VMEM(h.shape, BF16) for h in (*held, spare)),
        in_specs=[VMEM_SPEC] + [HBM_SPEC] * 2 + [VMEM_SPEC] * 3,
        out_specs=(VMEM_SPEC,) * 5,
        scratch_shapes=[pltpu.SemaphoreType.DMA((2, units // chunk_of(units)))],
        input_output_aliases={3: 2, 4: 3, 5: 4},
        compiler_params=pltpu.CompilerParams(vmem_limit_bytes=HELD_BELOW),
        cost_estimate=pl.CostEstimate(
            flops=2 * rows * width * units, bytes_accessed=width * units, transcendentals=0
        ),
        name="first_half",
    )(*in_vmem_always([mine]), *in_hbm(gate_weight, up_weight), *in_vmem_always([*held, spare]))


def second_half_kernel(
    per_plane, x_ref, ox_ref, gate_ref, up_ref, spare_ref, g_hbm, u_hbm, d_hbm, g_in, u_in,
    staying_ref, leaving_ref, g_ref, u_ref, x_scr, h_scr, gu_sems, sems,
):
    del g_in, u_in
    rows, units = h_scr.shape
    width = staying_ref.shape[1]
    side = own_side()
    chunk = chunk_of(units)
    chunks = units // chunk
    per_side = width // chunk
    pairs = per_side

    def gu_copy(i, c):
        return other_copy((g_hbm, u_hbm)[i], (g_ref, u_ref)[i], None, c, chunk, gu_sems.at[i, c])

    def down_slot(p):
        return chunk_at(lax.rem(p + chunks - 1, chunks), chunk)

    def down_copy(i, p):
        n = 2 * p + i
        column = jnp.where(n < per_side, 1 - side, side) * width + lax.rem(n, per_side) * chunk
        return pltpu.make_async_copy(
            d_hbm.at[:, pl.ds(pl.multiple_of(column, LANES), chunk)],
            (g_ref, u_ref)[i].at[pl.ds(0, units), down_slot(p)],
            sems.at[i, p],
        )

    def in_order(values):
        quarter = rows // 4
        return jnp.concatenate(
            [values[q * quarter:(q + 1) * quarter, :] for q in (0, 2, 1, 3)], axis=0
        )

    later = [(1, 2)] if chunks > 2 else []
    later += [(i, c) for c in range(3, chunks) for i in range(2)]
    for i, c in later:
        gu_copy(i, c).start()
    for i in range(2):
        down_copy(i, 0).start()
    x_scr[...] = in_order(ox_ref[:, :width].astype(F32)).astype(BF16)

    own = x_ref[:, width:].astype(F32)
    both = own + in_order(ox_ref[:, width:].astype(F32))
    lane = lax.broadcasted_iota(jnp.int32, (rows, LANES), 1)

    def pick(values, mask):
        return jnp.sum(jnp.where(mask, values, 0.0), axis=1, keepdims=True)

    scale = lax.rsqrt(pick(both, lane < 3) * (1.0 / (2 * width)) + 1e-05)
    first, second = pick(own, lane == ROUTE_LANE), pick(own, lane == ROUTE_LANE + 1)
    expert_of = (lane - 3) // 3
    logit_lane = jnp.logical_and(lane >= 3, lane < ROUTE_LANE)

    def logit_at(route):
        return pick(both, jnp.logical_and(logit_lane, expert_of == route.astype(jnp.int32))) * scale

    share = 1.0 / (1.0 + jnp.exp(logit_at(second) - logit_at(first)))
    here = (lax.axis_index("node") // per_plane).astype(F32)
    weight = jnp.where(first == here, share, 0.0) + jnp.where(second == here, 1.0 - share, 0.0)

    def hidden_chunk(c, g_part, u_part):
        at = chunk_at(c, chunk)
        gate = gate_ref[:, at] + jnp.dot(x_scr[...], g_part, preferred_element_type=F32)
        up = up_ref[:, at] + jnp.dot(x_scr[...], u_part, preferred_element_type=F32)
        gate = gate * scale
        h_scr[:, at] = (gate / (1.0 + jnp.exp(-gate)) * (up * scale)).astype(BF16)

    hidden_chunk(0, spare_ref[0], spare_ref[1])

    def hidden_step(c, _):
        for i, late in later:
            @pl.when(c == late)
            def _(i=i, late=late):
                gu_copy(i, late).wait()

        slot = chunk_at(c - 1, chunk)
        hidden_chunk(c, g_ref[:, slot], u_ref[:, slot])

        @pl.when(c < pairs)
        def _():
            for i in range(2):
                down_copy(i, c).start()

        return 0

    lax.fori_loop(1, chunks, hidden_step, 0)

    def down_step(p, _):
        slot = down_slot(p)
        for i, ref in enumerate((g_ref, u_ref)):
            n = 2 * p + i
            down_copy(i, p).wait()
            value = jnp.dot(h_scr[...], ref[:units, slot], preferred_element_type=F32) * weight
            to = pl.ds(pl.multiple_of(lax.rem(n, per_side) * chunk, LANES), chunk)

            @pl.when(n < per_side)
            def _(value=value, to=to):
                leaving_ref[:, to] = in_order(value).astype(BF16)

            @pl.when(n >= per_side)
            def _(value=value, to=to):
                staying_ref[:, to] = value

        @pl.when(p + chunks < pairs)
        def _():
            for i in range(2):
                down_copy(i, p + chunks).start()

        return 0

    lax.fori_loop(0, pairs, down_step, 0)


def second_half(per_plane, mine, other, sums, held, spare, gate_weight, up_weight, down_weight):
    rows, units = sums[0].shape
    width = down_weight.shape[1] // 2
    chunk = chunk_of(units)
    return pl.pallas_call(
        functools.partial(second_half_kernel, per_plane),
        out_shape=(vmem_array((rows, width), F32), vmem_array((rows, width), BF16))
        + tuple(pltpu.VMEM(h.shape, BF16) for h in held),
        in_specs=[VMEM_SPEC] * 5 + [HBM_SPEC] * 3 + [VMEM_SPEC] * 2,
        out_specs=(VMEM_SPEC,) * 4,
        scratch_shapes=[
            pltpu.VMEM((rows, width), BF16),
            pltpu.VMEM((rows, units), BF16),
            pltpu.SemaphoreType.DMA((2, units // chunk)),
            pltpu.SemaphoreType.DMA((2, width // chunk)),
        ],
        input_output_aliases={8: 2, 9: 3},
        compiler_params=pltpu.CompilerParams(
            vmem_limit_bytes=HELD_BELOW if rows < 256 else 40 * MIB
        ),
        cost_estimate=pl.CostEstimate(
            flops=6 * rows * width * units, bytes_accessed=4 * width * units, transcendentals=0
        ),
        name="second_half",
    )(
        *in_vmem_always([mine, other]), *in_vmem(*sums), *in_vmem_always([spare]),
        *in_hbm(gate_weight, up_weight, down_weight), *in_vmem_always(held),
    )[:2]


def split_kernel(own_ref, got_ref, keep_ref, send_ref):
    size = keep_ref.shape[0]
    keep_ref[...] = own_ref[:size, :] + got_ref[:size, :].astype(F32)
    send_ref[...] = (own_ref[size:, :] + got_ref[size:, :].astype(F32)).astype(BF16)


def split_rows(own, got):
    rows, width = own.shape
    size = rows // 2
    return pl.pallas_call(
        split_kernel,
        out_shape=(vmem_array((size, width), F32), vmem_array((size, width), BF16)),
        in_specs=[VMEM_SPEC] * 2,
        out_specs=(VMEM_SPEC,) * 2,
        compiler_params=pltpu.CompilerParams(vmem_limit_bytes=(8 if rows < 256 else 32) * MIB),
        name="split_rows",
    )(*in_vmem(own, got))


def split_last_kernel(own_ref, got_ref, keep_ref, *refs):
    *sends, total = refs
    total[...] = own_ref[...] + got_ref[...].astype(F32)
    tok, width = keep_ref.shape
    fold_width = width // FOLD
    keep_ref[...] = total[:tok, :]
    for i, send in enumerate(sends, 1):
        rows = total[i * tok:(i + 1) * tok, :]
        send[...] = jnp.concatenate(
            [rows[:, f * fold_width:(f + 1) * fold_width] for f in range(FOLD)], axis=0
        ).astype(BF16)


def split_last(own, got, parts):
    rows, width = own.shape
    tok = rows // parts
    return pl.pallas_call(
        split_last_kernel,
        out_shape=(pltpu.VMEM((tok, width), F32),)
        + (pltpu.VMEM((FOLD * tok, width // FOLD), BF16),) * (parts - 1),
        in_specs=[VMEM_SPEC] * 2,
        out_specs=(VMEM_SPEC,) * parts,
        scratch_shapes=[pltpu.VMEM((rows, width), F32)],
        compiler_params=pltpu.CompilerParams(vmem_limit_bytes=4 * MIB),
        name="split_last",
    )(*in_vmem(own, got))


def finish_kernel(carried_ref, own_ref, *refs):
    *got, out_ref, folded = refs
    tok, width = carried_ref.shape
    fold_width = width // FOLD
    total = got[0][...].astype(F32)
    for ref in got[1:]:
        total = total + ref[...].astype(F32)
    folded[...] = total
    for f in range(FOLD):
        at = slice(f * fold_width, (f + 1) * fold_width)
        value = carried_ref[:, at] + own_ref[:, at] + folded[f * tok:(f + 1) * tok, :]
        out_ref[:, at] = value.astype(BF16)


def finish(carried, own, got):
    tok, width = carried.shape
    return pl.pallas_call(
        finish_kernel,
        out_shape=jax.ShapeDtypeStruct((tok, width), BF16),
        in_specs=[VMEM_SPEC] * (2 + len(got)),
        out_specs=VMEM_SPEC,
        scratch_shapes=[pltpu.VMEM((FOLD * tok, width // FOLD), F32)],
        compiler_params=pltpu.CompilerParams(vmem_limit_bytes=8 * MIB),
        name="finish",
    )(*in_vmem(carried, own, *got))


def on_device(
    residual, queries, key_cache, value_cache, new_key, new_value, cache_lengths,
    norm_gain, router, routes, gate_weight, up_weight, down_weight,
):
    nodes = lax.axis_size("node")
    per_plane = nodes // EXPERTS
    stages = nodes.bit_length() - 1
    masks = [nodes >> (s + 1) for s in range(stages)]
    routes_of = (masks, masks[:-2] + masks[:-3:-1])

    def exchange(array, *flips):
        masks = [sum(side[s] for s in flips) for side in routes_of]
        perm = [(2 * n + c, 2 * (n ^ masks[c]) + c) for n in range(nodes) for c in range(2)]
        return lax.ppermute(array, ("node", "shard"), perm)

    def to_core(array):
        return lax.ppermute(array, "shard", [(0, 1), (1, 0)])

    tok = residual.shape[0]
    half = gate_weight.shape[0] // 2
    heights = [half // 6, half // 2, half // 3]
    carried, payload, *held = attend(
        heights[0], cache_lengths, routes.T, queries, key_cache, value_cache, new_key, new_value,
        residual, norm_gain.reshape(1, -1), router.T, gate_weight, up_weight,
    )
    near = ((0,), (1,), (0, 1))
    got = [exchange(payload, *flips) for flips in near]
    *held, token = load_rows(
        heights[0], heights[1], False, payload, gate_weight, up_weight, held
    )
    payload = unfold(tok, [payload, *got], token)
    for stage in range(2, stages):
        got = exchange(payload, stage)
        if stage == 2:
            *held, spare, token = load_rows(
                heights[0] + heights[1], heights[2], True, payload, gate_weight, up_weight, held
            )
        payload = join(payload, got, token)
    mine = payload
    other = to_core(mine)
    gate, up, *held, spare = first_half(mine, held, spare, gate_weight, up_weight)
    staying, leaving = second_half(
        per_plane, mine, other, (gate, up), held, spare, gate_weight, up_weight, down_weight
    )
    keep, got = staying, to_core(leaving)
    for stage in range(stages - 1, 1, -1):
        keep, send = split_rows(keep, got)
        got = exchange(send, stage)
    keep, *sends = split_last(keep, got, 1 + len(near))
    return finish(carried, keep, [exchange(send, *flips) for send, flips in zip(sends, near)])


def solution(mesh):
    rows = ("replica", "node")
    in_specs = (
        P(rows, "shard"),
        P(rows, "shard"),
        P(rows, None, "shard"),
        P(rows, None, "shard"),
        P(rows, "shard"),
        P(rows, "shard"),
        P(rows),
        P(),
        P(),
        P(rows, None),
        P(None, ("node", "shard")),
        P(None, ("node", "shard")),
        P(("node", "shard"), None),
    )
    return jax.shard_map(
        on_device,
        mesh=mesh,
        in_specs=in_specs,
        out_specs=P(rows, "shard"),
        check_vma=False,
    )
```

```python
import functools
import math

import jax
import jax.numpy as jnp
from jax import lax
from jax.experimental import pallas as pl
from jax.experimental.pallas import tpu as pltpu
from jax.sharding import PartitionSpec as P

MIB = 1 << 20
QUERY_HEADS = 48
KV_HEADS = 8
HEAD_DIM = 128
EXPERTS = 4
GROUP = QUERY_HEADS // KV_HEADS
LANES = 128
FOLD = 2
F32 = jnp.float32
BF16 = jnp.bfloat16


def small(shape, dtype):
    return math.prod(shape) * jnp.dtype(dtype).itemsize <= 17 * MIB // 4


def vmem_array(shape, dtype):
    return pltpu.VMEM(shape, dtype) if small(shape, dtype) else jax.ShapeDtypeStruct(shape, dtype)


def in_vmem(*arrays):
    return [
        pltpu.with_memory_space_constraint(a, pltpu.VMEM) if small(a.shape, a.dtype) else a
        for a in arrays
    ]


def in_vmem_always(arrays):
    return [pltpu.with_memory_space_constraint(a, pltpu.VMEM) for a in arrays]


def in_hbm(*arrays):
    return [pltpu.with_memory_space_constraint(a, pltpu.HBM) for a in arrays]


VMEM_SPEC = pl.BlockSpec(memory_space=pltpu.VMEM)
HBM_SPEC = pl.BlockSpec(memory_space=pltpu.HBM)
ROUTE_LANE = 3 + 3 * EXPERTS
HELD_BELOW = 8 * MIB
LOADED_BELOW = 10 * MIB


def own_side():
    return lax.axis_index("shard")


def chunk_of(units):
    return math.gcd(512, units)


def held_shape(gate_weight):
    width, units = gate_weight.shape
    return width // 2, units


def spare_shape(gate_weight):
    width, units = gate_weight.shape
    return min(2, units // chunk_of(units)), 2, width // 2, chunk_of(units)


def row_copies(sources, targets, first, rows, sems):
    parts = sems.shape[1]
    part = rows // parts
    half, units = sources[0].shape[0] // 2, sources[0].shape[1]
    copies = []
    for p in range(parts):
        at = first + p * part
        for i, (source, target) in enumerate(zip(sources, targets)):
            copies.append(
                pltpu.make_async_copy(
                    source.at[pl.ds(pl.multiple_of(own_side() * half + at, 16), part), :],
                    target.at[pl.ds(at, part), pl.ds(0, units)], sems.at[i, p],
                )
            )
    return copies


def chunk_at(n, chunk):
    return pl.ds(n * chunk if isinstance(n, int) else pl.multiple_of(n * chunk, LANES), chunk)


def other_copy(source, held, spare, i, c, chunk, sem):
    half = source.shape[0] // 2
    first = pl.multiple_of((1 - own_side()) * half, 16)
    count = spare.shape[0]
    target = spare.at[c, i] if c < count else held.at[:, chunk_at(c - count, chunk)]
    return pltpu.make_async_copy(source.at[pl.ds(first, half), chunk_at(c, chunk)], target, sem)


def load_kernel(first, rows, ahead, dep_ref, g_hbm, u_hbm, *refs):
    g_vmem, u_vmem, spare, token_ref, sems, sem = refs[3:]
    copies = row_copies((g_hbm, u_hbm), (g_vmem, u_vmem), first, rows, sems)
    if ahead:
        for i, source in enumerate((g_hbm, u_hbm)):
            copies.append(other_copy(source, None, spare, i, 0, spare.shape[3], sem.at[i]))
    for copy in copies:
        copy.start()
    token_ref[...] = jnp.zeros_like(token_ref)
    for copy in copies:
        copy.wait()


def load_rows(first, rows, ahead, after, gate_weight, up_weight, held):
    hidden = gate_weight.shape[1]
    return pl.pallas_call(
        functools.partial(load_kernel, first, rows, ahead),
        out_shape=tuple(pltpu.VMEM(h.shape, BF16) for h in held) + (pltpu.VMEM((8, LANES), F32),),
        in_specs=[pl.BlockSpec(memory_space=pl.ANY), HBM_SPEC, HBM_SPEC] + [VMEM_SPEC] * 3,
        out_specs=(VMEM_SPEC,) * 4,
        scratch_shapes=[pltpu.SemaphoreType.DMA((2, 4)), pltpu.SemaphoreType.DMA((2,))],
        input_output_aliases={3: 0, 4: 1, 5: 2},
        compiler_params=pltpu.CompilerParams(vmem_limit_bytes=LOADED_BELOW),
        cost_estimate=pl.CostEstimate(flops=0, bytes_accessed=4 * rows * hidden, transcendentals=0),
        name="load_weights",
    )(*in_vmem(after), *in_hbm(gate_weight, up_weight), *in_vmem_always(held))


def unfold_kernel(tok, *refs):
    *arrays, _, out_ref, scr = refs
    fold_width = arrays[0].shape[1] - LANES
    for i, array in enumerate(arrays):
        rows = array[...].astype(F32)
        to = slice(i * tok, (i + 1) * tok)
        for f in range(FOLD):
            scr[to, f * fold_width:(f + 1) * fold_width] = rows[f * tok:(f + 1) * tok, :fold_width]
        scr[to, FOLD * fold_width:] = rows[:tok, fold_width:]
    out_ref[...] = scr[...].astype(BF16)


def unfold(tok, arrays, token):
    shape = (len(arrays) * tok, FOLD * (arrays[0].shape[1] - LANES) + LANES)
    return pl.pallas_call(
        functools.partial(unfold_kernel, tok),
        out_shape=pltpu.VMEM(shape, BF16),
        in_specs=[VMEM_SPEC] * (len(arrays) + 1),
        out_specs=VMEM_SPEC,
        scratch_shapes=[pltpu.VMEM(shape, F32)],
        compiler_params=pltpu.CompilerParams(vmem_limit_bytes=3 * MIB),
        name="unfold",
    )(*in_vmem_always([*arrays, token]))


def join_kernel(a_ref, b_ref, token_ref, out_ref):
    rows = a_ref.shape[0]
    out_ref[:rows, :] = a_ref[...]
    out_ref[rows:, :] = b_ref[...]


def join(a, b, token):
    return pl.pallas_call(
        join_kernel,
        out_shape=vmem_array((a.shape[0] + b.shape[0], a.shape[1]), BF16),
        in_specs=[VMEM_SPEC] * 3,
        out_specs=VMEM_SPEC,
        compiler_params=pltpu.CompilerParams(vmem_limit_bytes=HELD_BELOW),
        name="join",
    )(*in_vmem(a, b, token))


def split_three(value):
    first = value.astype(BF16).astype(F32)
    second = (value - first).astype(BF16).astype(F32)
    return first, second, value - first - second


def attend_kernel(
    ahead, len_hbm, routes_hbm, q_hbm, k_hbm, v_hbm, nk_hbm, nv_hbm, res_hbm, gain_hbm, rt_hbm,
    g_hbm, u_hbm, carried_ref, pay_ref, g_vmem, u_vmem, spare_ref,
    q_ref, k_ref, v_ref, nk_ref, nv_ref, res_ref, gain_ref, rt_ref,
    q_scr, o_scr, nk_scr, nv_scr, pay_scr, len_ref, routes_ref, sems, w_sems,
):
    tok, width = q_ref.shape
    cache_len, kv_width = k_ref.shape[1], k_ref.shape[2]
    heads = width // HEAD_DIM
    groups = kv_width // HEAD_DIM
    fold_width = width // FOLD
    scaling = 1.0 / math.sqrt(HEAD_DIM)
    columns = pl.ds(pl.multiple_of(own_side() * width, LANES), width)
    moves = [
        (q_hbm, q_ref), (k_hbm, k_ref), (nk_hbm, nk_ref), (len_hbm, len_ref), (v_hbm, v_ref),
        (nv_hbm, nv_ref), (res_hbm, res_ref),
        (gain_hbm.at[:, columns], gain_ref), (rt_hbm.at[:, columns], rt_ref),
        (routes_hbm, routes_ref),
    ]
    copies = [pltpu.make_async_copy(a, b, sems.at[i]) for i, (a, b) in enumerate(moves)]
    weights = row_copies((g_hbm, u_hbm), (g_vmem, u_vmem), 0, ahead, w_sems)
    for copy in copies + weights:
        copy.start()
    copies[0].wait()
    for h in range(heads):
        q_scr[h * tok:(h + 1) * tok, :] = q_ref[:, h * HEAD_DIM:(h + 1) * HEAD_DIM].astype(F32)
    copies[2].wait()
    nk_scr[...] = nk_ref[...].astype(F32)
    row_group = lax.broadcasted_iota(jnp.int32, (heads, HEAD_DIM), 0) // GROUP
    position = lax.broadcasted_iota(jnp.int32, (heads, cache_len), 1)
    scores, fresh = [], []
    for t in range(tok):
        if t == 0:
            copies[1].wait()
        q_rows = q_scr[pl.ds(t, heads, stride=tok), :]
        q_wide = jnp.concatenate(
            [jnp.where(row_group == g, q_rows, 0.0) for g in range(groups)], axis=1
        )
        scores.append(
            lax.dot_general(
                q_wide.astype(BF16), k_ref[t], (((1,), (1,)), ((), ())),
                preferred_element_type=F32,
            ) * scaling
        )
        fresh.append(
            jnp.sum(q_wide * nk_scr[pl.ds(t, 1), :], axis=1, keepdims=True) * scaling
        )
    copies[3].wait()
    terms, fresh_terms, totals = [], [], []
    for t in range(tok):
        score = jnp.where(position < len_ref[t], scores[t], -1e30)
        largest = jnp.maximum(jnp.max(score, axis=1, keepdims=True), fresh[t])
        term = jnp.exp(score - largest)
        fresh_term = jnp.exp(fresh[t] - largest)
        totals.append(jnp.sum(term, axis=1, keepdims=True) + fresh_term)
        terms.append(term.astype(BF16))
        fresh_terms.append(fresh_term.astype(BF16).astype(F32))
    copies[5].wait()
    nv_scr[...] = nv_ref[...].astype(F32)
    for t in range(tok):
        if t == 0:
            copies[4].wait()
        wide = jnp.dot(terms[t], v_ref[t], preferred_element_type=F32)
        wide = wide + fresh_terms[t] * nv_scr[pl.ds(t, 1), :]
        picked = wide[:, :HEAD_DIM]
        for g in range(1, groups):
            picked = jnp.where(
                row_group == g, wide[:, g * HEAD_DIM:(g + 1) * HEAD_DIM], picked
            )
        o_scr[pl.ds(t, heads, stride=tok), :] = picked / totals[t]
    for copy in copies[6:]:
        copy.wait()
    for h in range(heads):
        cols = slice(h * HEAD_DIM, (h + 1) * HEAD_DIM)
        carried_ref[:, cols] = res_ref[:, cols].astype(F32) + o_scr[h * tok:(h + 1) * tok, :]
    carried = carried_ref[...]
    scaled = carried * gain_ref[...]
    rounded = scaled.astype(BF16).astype(F32)
    router = rt_ref[...].astype(F32)
    for f in range(FOLD):
        pay_scr[f * tok:(f + 1) * tok, :fold_width] = scaled[:, f * fold_width:(f + 1) * fold_width]
    lane = lax.broadcasted_iota(jnp.int32, (tok, LANES), 1)
    row = lax.broadcasted_iota(jnp.int32, (tok, LANES), 0)
    sums = [jnp.sum(carried * carried, axis=1, keepdims=True)]
    for e in range(EXPERTS):
        sums.append(jnp.sum(rounded * router[e:e + 1, :], axis=1, keepdims=True))
    extra = jnp.zeros((tok, LANES), F32)
    for i, total in enumerate(sums):
        for j, term in enumerate(split_three(total)):
            extra = jnp.where(lane == 3 * i + j, term, extra)
    for t in range(tok):
        for i in range(2):
            extra = jnp.where(
                jnp.logical_and(row == t, lane == ROUTE_LANE + i),
                routes_ref[i, t].astype(F32), extra,
            )
    for f in range(FOLD):
        pay_scr[f * tok:(f + 1) * tok, fold_width:] = extra
    pay_ref[...] = pay_scr[...].astype(BF16)
    for copy in weights:
        copy.wait()


def attend(
    ahead, lengths, routes_t, queries, key_cache, value_cache, new_key, new_value,
    residual, gain, router_t, gate_weight, up_weight,
):
    tok, width = queries.shape
    kv_width = new_key.shape[1]
    heads = width // HEAD_DIM
    wide = width // FOLD + LANES
    here = [
        pltpu.VMEM(a.shape, a.dtype)
        for a in (queries, key_cache, value_cache, new_key, new_value, residual)
    ]
    return pl.pallas_call(
        functools.partial(attend_kernel, ahead),
        out_shape=(
            pltpu.VMEM((tok, width), F32),
            pltpu.VMEM((FOLD * tok, wide), BF16),
            pltpu.VMEM(held_shape(gate_weight), BF16),
            pltpu.VMEM(held_shape(gate_weight), BF16),
            pltpu.VMEM(spare_shape(gate_weight), BF16),
        ),
        in_specs=[HBM_SPEC] * 12,
        out_specs=(VMEM_SPEC,) * 5,
        scratch_shapes=here + [
            pltpu.VMEM((1, width), F32),
            pltpu.VMEM((EXPERTS, width), BF16),
            pltpu.VMEM((heads * tok, HEAD_DIM), F32),
            pltpu.VMEM((heads * tok, HEAD_DIM), F32),
            pltpu.VMEM((tok, kv_width), F32),
            pltpu.VMEM((tok, kv_width), F32),
            pltpu.VMEM((FOLD * tok, wide), F32),
            pltpu.SMEM(lengths.shape, jnp.int32),
            pltpu.SMEM(routes_t.shape, jnp.int32),
            pltpu.SemaphoreType.DMA((10,)),
            pltpu.SemaphoreType.DMA((2, 1)),
        ],
        compiler_params=pltpu.CompilerParams(vmem_limit_bytes=LOADED_BELOW),
        cost_estimate=pl.CostEstimate(flops=10**8, bytes_accessed=8 * 10**6, transcendentals=10**5),
        name="attend",
    )(
        *in_hbm(
            lengths, routes_t, queries, key_cache, value_cache, new_key, new_value, residual, gain, router_t,
            gate_weight, up_weight,
        ),
    )


def first_half_kernel(
    x_ref, g_hbm, u_hbm, g_in, u_in, spare_in, gate_ref, up_ref, g_ref, u_ref, spare_ref, sems
):
    del g_in, u_in, spare_in
    half, units = g_ref.shape[0], gate_ref.shape[1]
    chunk = chunk_of(units)
    chunks = units // chunk
    count = spare_ref.shape[0]
    ready = [(i, c) for c in range(1, min(count + 1, chunks)) for i in range(2)]

    def copy(i, c):
        return other_copy(
            (g_hbm, u_hbm)[i], (g_ref, u_ref)[i], spare_ref, i, c, chunk, sems.at[i, c]
        )

    for i, c in ready:
        if c < count:
            copy(i, c).start()

    def step(n, _):
        at = chunk_at(n, chunk)
        rows = x_ref[:, :half]
        gate_ref[:, at] = jnp.dot(rows, g_ref[:, at], preferred_element_type=F32)
        up_ref[:, at] = jnp.dot(rows, u_ref[:, at], preferred_element_type=F32)
        for i, c in ready:
            if c >= count:
                @pl.when(n == c - count)
                def _(i=i, c=c):
                    copy(i, c).start()

        return 0

    lax.fori_loop(0, chunks, step, 0)
    for i, c in ready:
        copy(i, c).wait()


def first_half(mine, held, gate_weight, up_weight):
    rows = mine.shape[0]
    width, units = gate_weight.shape
    acc = pltpu.VMEM((rows, units), F32)
    return pl.pallas_call(
        first_half_kernel,
        out_shape=(acc, acc) + tuple(pltpu.VMEM(h.shape, BF16) for h in held),
        in_specs=[VMEM_SPEC] + [HBM_SPEC] * 2 + [VMEM_SPEC] * 3,
        out_specs=(VMEM_SPEC,) * 5,
        scratch_shapes=[pltpu.SemaphoreType.DMA((2, units // chunk_of(units)))],
        input_output_aliases={3: 2, 4: 3, 5: 4},
        compiler_params=pltpu.CompilerParams(vmem_limit_bytes=HELD_BELOW),
        cost_estimate=pl.CostEstimate(
            flops=2 * rows * width * units, bytes_accessed=width * units, transcendentals=0
        ),
        name="first_half",
    )(*in_vmem_always([mine]), *in_hbm(gate_weight, up_weight), *in_vmem_always(held))


def second_half_kernel(
    per_plane, x_ref, ox_ref, gate_ref, up_ref, g_hbm, u_hbm, d_hbm, g_in, u_in, spare_in,
    staying_ref, leaving_ref, g_ref, u_ref, spare_ref, h_scr, gu_sems, sems,
):
    del g_in, u_in, spare_in
    rows, units = h_scr.shape
    width = staying_ref.shape[1]
    side = own_side()
    chunk = chunk_of(units)
    chunks = units // chunk
    per_side = width // chunk
    pairs = per_side

    count = spare_ref.shape[0]
    places = count + chunks

    def gu_copy(i, c):
        return other_copy(
            (g_hbm, u_hbm)[i], (g_ref, u_ref)[i], spare_ref, i, c, chunk, gu_sems.at[i, c]
        )

    def down_place(i, part, r):
        if part == 1:
            return spare_ref.at[r - count, i, pl.ds(0, units)]
        start = r + chunks - count if part == 0 else r - 2 * count
        return (g_ref, u_ref)[i].at[pl.ds(0, units), chunk_at(start, chunk)]

    def part_of(r):
        return 0 if r < count else 1 if r < 2 * count else 2

    def down_copy(i, p, part, r):
        n = 2 * p + i
        column = jnp.where(n < per_side, 1 - side, side) * width + lax.rem(n, per_side) * chunk
        return pltpu.make_async_copy(
            d_hbm.at[:, pl.ds(pl.multiple_of(column, LANES), chunk)], down_place(i, part, r),
            sems.at[i, p],
        )

    def start_down(p):
        for i in range(2):
            down_copy(i, p, part_of(p % places), p % places).start()

    def in_order(values):
        quarter = rows // 4
        return jnp.concatenate(
            [values[q * quarter:(q + 1) * quarter, :] for q in (0, 2, 1, 3)], axis=0
        )

    later = [(i, c) for c in range(count + 1, chunks) for i in range(2)]
    for i, c in later:
        gu_copy(i, c).start()
    for p in range(min(count, pairs)):
        start_down(p)

    own = x_ref[:, width:].astype(F32)
    both = own + in_order(ox_ref[:, width:].astype(F32))
    lane = lax.broadcasted_iota(jnp.int32, (rows, LANES), 1)

    def pick(values, mask):
        return jnp.sum(jnp.where(mask, values, 0.0), axis=1, keepdims=True)

    scale = lax.rsqrt(pick(both, lane < 3) * (1.0 / (2 * width)) + 1e-05)
    first, second = pick(own, lane == ROUTE_LANE), pick(own, lane == ROUTE_LANE + 1)
    expert_of = (lane - 3) // 3
    logit_lane = jnp.logical_and(lane >= 3, lane < ROUTE_LANE)

    def logit_at(route):
        return pick(both, jnp.logical_and(logit_lane, expert_of == route.astype(jnp.int32))) * scale

    share = 1.0 / (1.0 + jnp.exp(logit_at(second) - logit_at(first)))
    here = (lax.axis_index("node") // per_plane).astype(F32)
    weight = jnp.where(first == here, share, 0.0) + jnp.where(second == here, 1.0 - share, 0.0)

    def hidden_chunk(c, g_part, u_part):
        at = chunk_at(c, chunk)
        rows_in = ox_ref[:, :width]
        gate = gate_ref[:, at] + in_order(jnp.dot(rows_in, g_part, preferred_element_type=F32))
        up = up_ref[:, at] + in_order(jnp.dot(rows_in, u_part, preferred_element_type=F32))
        gate = gate * scale
        h_scr[:, at] = (gate / (1.0 + jnp.exp(-gate)) * (up * scale)).astype(BF16)
        for late in range(chunks):
            if count + late < pairs:
                @pl.when(c == late)
                def _(late=late):
                    start_down(count + late)

    def spare_step(c, _):
        hidden_chunk(c, spare_ref[c, 0], spare_ref[c, 1])
        return 0

    def held_step(c, _):
        for i, late in later:
            @pl.when(c == late)
            def _(i=i, late=late):
                gu_copy(i, late).wait()

        slot = chunk_at(c - count, chunk)
        hidden_chunk(c, g_ref[:, slot], u_ref[:, slot])
        return 0

    lax.fori_loop(0, count, spare_step, 0)
    lax.fori_loop(count, chunks, held_step, 0)

    def down_step(turn, part, r, _):
        p = turn * places + r
        for i in range(2):
            n = 2 * p + i
            down_copy(i, p, part, r).wait()
            value = jnp.dot(
                h_scr[...], down_place(i, part, r)[...], preferred_element_type=F32
            ) * weight
            to = chunk_at(lax.rem(n, per_side), chunk)

            @pl.when(n < per_side)
            def _(value=value, to=to):
                leaving_ref[:, to] = in_order(value).astype(BF16)

            @pl.when(n >= per_side)
            def _(value=value, to=to):
                staying_ref[:, to] = value

        return 0

    for turn in range(-(-pairs // places)):
        for part, (low, high) in enumerate(((0, count), (count, 2 * count), (2 * count, places))):
            high = min(high, pairs - turn * places)
            if low < high:
                lax.fori_loop(low, high, functools.partial(down_step, turn, part), 0)
            for r in range(low, high):
                if (turn + 1) * places + r < pairs:
                    start_down((turn + 1) * places + r)


def second_half(per_plane, mine, other, sums, held, gate_weight, up_weight, down_weight):
    rows, units = sums[0].shape
    width = down_weight.shape[1] // 2
    chunk = chunk_of(units)
    return pl.pallas_call(
        functools.partial(second_half_kernel, per_plane),
        out_shape=(vmem_array((rows, width), F32), vmem_array((rows, width), BF16))
        + tuple(pltpu.VMEM(h.shape, BF16) for h in held),
        in_specs=[VMEM_SPEC] * 4 + [HBM_SPEC] * 3 + [VMEM_SPEC] * 3,
        out_specs=(VMEM_SPEC,) * 5,
        scratch_shapes=[
            pltpu.VMEM((rows, units), BF16),
            pltpu.SemaphoreType.DMA((2, units // chunk)),
            pltpu.SemaphoreType.DMA((2, width // chunk)),
        ],
        input_output_aliases={7: 2, 8: 3, 9: 4},
        compiler_params=pltpu.CompilerParams(
            vmem_limit_bytes=HELD_BELOW if rows < 256 else 40 * MIB
        ),
        cost_estimate=pl.CostEstimate(
            flops=6 * rows * width * units, bytes_accessed=4 * width * units, transcendentals=0
        ),
        name="second_half",
    )(
        *in_vmem_always([mine, other]), *in_vmem(*sums),
        *in_hbm(gate_weight, up_weight, down_weight), *in_vmem_always(held),
    )[:2]


def split_kernel(own_ref, got_ref, keep_ref, send_ref):
    size = keep_ref.shape[0]
    keep_ref[...] = own_ref[:size, :] + got_ref[:size, :].astype(F32)
    send_ref[...] = (own_ref[size:, :] + got_ref[size:, :].astype(F32)).astype(BF16)


def split_rows(own, got):
    rows, width = own.shape
    size = rows // 2
    return pl.pallas_call(
        split_kernel,
        out_shape=(vmem_array((size, width), F32), vmem_array((size, width), BF16)),
        in_specs=[VMEM_SPEC] * 2,
        out_specs=(VMEM_SPEC,) * 2,
        compiler_params=pltpu.CompilerParams(vmem_limit_bytes=(8 if rows < 256 else 32) * MIB),
        name="split_rows",
    )(*in_vmem(own, got))


def split_last_kernel(own_ref, got_ref, keep_ref, *refs):
    *sends, total = refs
    total[...] = own_ref[...] + got_ref[...].astype(F32)
    tok, width = keep_ref.shape
    fold_width = width // FOLD
    keep_ref[...] = total[:tok, :]
    for i, send in enumerate(sends, 1):
        rows = total[i * tok:(i + 1) * tok, :]
        send[...] = jnp.concatenate(
            [rows[:, f * fold_width:(f + 1) * fold_width] for f in range(FOLD)], axis=0
        ).astype(BF16)


def split_last(own, got, parts):
    rows, width = own.shape
    tok = rows // parts
    return pl.pallas_call(
        split_last_kernel,
        out_shape=(pltpu.VMEM((tok, width), F32),)
        + (pltpu.VMEM((FOLD * tok, width // FOLD), BF16),) * (parts - 1),
        in_specs=[VMEM_SPEC] * 2,
        out_specs=(VMEM_SPEC,) * parts,
        scratch_shapes=[pltpu.VMEM((rows, width), F32)],
        compiler_params=pltpu.CompilerParams(vmem_limit_bytes=4 * MIB),
        name="split_last",
    )(*in_vmem(own, got))


def finish_kernel(carried_ref, own_ref, *refs):
    *got, out_ref, folded = refs
    tok, width = carried_ref.shape
    fold_width = width // FOLD
    total = got[0][...].astype(F32)
    for ref in got[1:]:
        total = total + ref[...].astype(F32)
    folded[...] = total
    for f in range(FOLD):
        at = slice(f * fold_width, (f + 1) * fold_width)
        value = carried_ref[:, at] + own_ref[:, at] + folded[f * tok:(f + 1) * tok, :]
        out_ref[:, at] = value.astype(BF16)


def finish(carried, own, got):
    tok, width = carried.shape
    return pl.pallas_call(
        finish_kernel,
        out_shape=jax.ShapeDtypeStruct((tok, width), BF16),
        in_specs=[VMEM_SPEC] * (2 + len(got)),
        out_specs=VMEM_SPEC,
        scratch_shapes=[pltpu.VMEM((FOLD * tok, width // FOLD), F32)],
        compiler_params=pltpu.CompilerParams(vmem_limit_bytes=8 * MIB),
        name="finish",
    )(*in_vmem(carried, own, *got))


def on_device(
    residual, queries, key_cache, value_cache, new_key, new_value, cache_lengths,
    norm_gain, router, routes, gate_weight, up_weight, down_weight,
):
    nodes = lax.axis_size("node")
    per_plane = nodes // EXPERTS
    stages = nodes.bit_length() - 1
    masks = [nodes >> (s + 1) for s in range(stages)]
    routes_of = (masks, masks[:-2] + masks[:-3:-1])

    def exchange(array, *flips):
        masks = [sum(side[s] for s in flips) for side in routes_of]
        perm = [(2 * n + c, 2 * (n ^ masks[c]) + c) for n in range(nodes) for c in range(2)]
        return lax.ppermute(array, ("node", "shard"), perm)

    def to_core(array):
        return lax.ppermute(array, "shard", [(0, 1), (1, 0)])

    tok = residual.shape[0]
    half = gate_weight.shape[0] // 2
    heights = [half // 6, half // 2, half // 3]
    carried, payload, *held = attend(
        heights[0], cache_lengths, routes.T, queries, key_cache, value_cache, new_key, new_value,
        residual, norm_gain.reshape(1, -1), router.T, gate_weight, up_weight,
    )
    near = ((0,), (1,), (0, 1))
    got = [exchange(payload, *flips) for flips in near]
    *held, token = load_rows(
        heights[0], heights[1], False, payload, gate_weight, up_weight, held
    )
    payload = unfold(tok, [payload, *got], token)
    for stage in range(2, stages):
        got = exchange(payload, stage)
        if stage == 2:
            *held, token = load_rows(
                heights[0] + heights[1], heights[2], True, payload, gate_weight, up_weight, held
            )
        payload = join(payload, got, token)
    mine = payload
    other = to_core(mine)
    gate, up, *held = first_half(mine, held, gate_weight, up_weight)
    staying, leaving = second_half(
        per_plane, mine, other, (gate, up), held, gate_weight, up_weight, down_weight
    )
    keep, got = staying, to_core(leaving)
    for stage in range(stages - 1, 1, -1):
        keep, send = split_rows(keep, got)
        got = exchange(send, stage)
    keep, *sends = split_last(keep, got, 1 + len(near))
    return finish(carried, keep, [exchange(send, *flips) for send, flips in zip(sends, near)])


def solution(mesh):
    rows = ("replica", "node")
    in_specs = (
        P(rows, "shard"),
        P(rows, "shard"),
        P(rows, None, "shard"),
        P(rows, None, "shard"),
        P(rows, "shard"),
        P(rows, "shard"),
        P(rows),
        P(),
        P(),
        P(rows, None),
        P(None, ("node", "shard")),
        P(None, ("node", "shard")),
        P(("node", "shard"), None),
    )
    return jax.shard_map(
        on_device,
        mesh=mesh,
        in_specs=in_specs,
        out_specs=P(rows, "shard"),
        check_vma=False,
    )
```

```python
import functools
import math

import jax
import jax.numpy as jnp
from jax import lax
from jax.experimental import pallas as pl
from jax.experimental.pallas import tpu as pltpu
from jax.sharding import PartitionSpec as P

MIB = 1 << 20
QUERY_HEADS = 48
KV_HEADS = 8
HEAD_DIM = 128
EXPERTS = 4
GROUP = QUERY_HEADS // KV_HEADS
LANES = 128
FOLD = 2
F32 = jnp.float32
BF16 = jnp.bfloat16


def small(shape, dtype):
    return math.prod(shape) * jnp.dtype(dtype).itemsize <= 17 * MIB // 4


def vmem_array(shape, dtype):
    return pltpu.VMEM(shape, dtype) if small(shape, dtype) else jax.ShapeDtypeStruct(shape, dtype)


def in_vmem(*arrays):
    return [
        pltpu.with_memory_space_constraint(a, pltpu.VMEM) if small(a.shape, a.dtype) else a
        for a in arrays
    ]


def in_vmem_always(arrays):
    return [pltpu.with_memory_space_constraint(a, pltpu.VMEM) for a in arrays]


def in_hbm(*arrays):
    return [pltpu.with_memory_space_constraint(a, pltpu.HBM) for a in arrays]


VMEM_SPEC = pl.BlockSpec(memory_space=pltpu.VMEM)
HBM_SPEC = pl.BlockSpec(memory_space=pltpu.HBM)
ROUTE_LANE = 3 + 3 * EXPERTS
HELD_BELOW = 8 * MIB
LOADED_BELOW = 10 * MIB


def own_side():
    return lax.axis_index("shard")


def chunk_of(units):
    return math.gcd(512, units)


def held_shape(gate_weight):
    width, units = gate_weight.shape
    return width // 2, units


def spare_shape(gate_weight):
    width, units = gate_weight.shape
    return min(2, units // chunk_of(units)), 2, width // 2, chunk_of(units)


def row_copies(sources, targets, first, rows, sems):
    parts = sems.shape[1]
    part = rows // parts
    half, units = sources[0].shape[0] // 2, sources[0].shape[1]
    copies = []
    for p in range(parts):
        at = first + p * part
        for i, (source, target) in enumerate(zip(sources, targets)):
            copies.append(
                pltpu.make_async_copy(
                    source.at[pl.ds(pl.multiple_of(own_side() * half + at, 16), part), :],
                    target.at[pl.ds(at, part), pl.ds(0, units)], sems.at[i, p],
                )
            )
    return copies


def chunk_at(n, chunk):
    return pl.ds(n * chunk if isinstance(n, int) else pl.multiple_of(n * chunk, LANES), chunk)


def other_copy(source, held, spare, i, c, chunk, sem):
    half = source.shape[0] // 2
    first = pl.multiple_of((1 - own_side()) * half, 16)
    count = spare.shape[0]
    target = spare.at[c, i] if c < count else held.at[:, chunk_at(c - count, chunk)]
    return pltpu.make_async_copy(source.at[pl.ds(first, half), chunk_at(c, chunk)], target, sem)


def load_kernel(first, rows, ahead, dep_ref, g_hbm, u_hbm, *refs):
    g_vmem, u_vmem, spare, token_ref, sems, sem = refs[3:]
    copies = row_copies((g_hbm, u_hbm), (g_vmem, u_vmem), first, rows, sems)
    if ahead:
        for i, source in enumerate((g_hbm, u_hbm)):
            copies.append(other_copy(source, None, spare, i, 0, spare.shape[3], sem.at[i]))
    for copy in copies:
        copy.start()
    token_ref[...] = jnp.zeros_like(token_ref)
    for copy in copies:
        copy.wait()


def load_rows(first, rows, ahead, after, gate_weight, up_weight, held):
    hidden = gate_weight.shape[1]
    return pl.pallas_call(
        functools.partial(load_kernel, first, rows, ahead),
        out_shape=tuple(pltpu.VMEM(h.shape, BF16) for h in held) + (pltpu.VMEM((8, LANES), F32),),
        in_specs=[pl.BlockSpec(memory_space=pl.ANY), HBM_SPEC, HBM_SPEC] + [VMEM_SPEC] * 3,
        out_specs=(VMEM_SPEC,) * 4,
        scratch_shapes=[pltpu.SemaphoreType.DMA((2, 4)), pltpu.SemaphoreType.DMA((2,))],
        input_output_aliases={3: 0, 4: 1, 5: 2},
        compiler_params=pltpu.CompilerParams(vmem_limit_bytes=LOADED_BELOW),
        cost_estimate=pl.CostEstimate(flops=0, bytes_accessed=4 * rows * hidden, transcendentals=0),
        name="load_weights",
    )(*in_vmem(after), *in_hbm(gate_weight, up_weight), *in_vmem_always(held))


def unfold_kernel(tok, *refs):
    *arrays, _, out_ref, scr = refs
    fold_width = arrays[0].shape[1] - LANES
    for i, array in enumerate(arrays):
        rows = array[...].astype(F32)
        to = slice(i * tok, (i + 1) * tok)
        for f in range(FOLD):
            scr[to, f * fold_width:(f + 1) * fold_width] = rows[f * tok:(f + 1) * tok, :fold_width]
        scr[to, FOLD * fold_width:] = rows[:tok, fold_width:]
    out_ref[...] = scr[...].astype(BF16)


def unfold(tok, arrays, token):
    shape = (len(arrays) * tok, FOLD * (arrays[0].shape[1] - LANES) + LANES)
    return pl.pallas_call(
        functools.partial(unfold_kernel, tok),
        out_shape=pltpu.VMEM(shape, BF16),
        in_specs=[VMEM_SPEC] * (len(arrays) + 1),
        out_specs=VMEM_SPEC,
        scratch_shapes=[pltpu.VMEM(shape, F32)],
        compiler_params=pltpu.CompilerParams(vmem_limit_bytes=3 * MIB),
        name="unfold",
    )(*in_vmem_always([*arrays, token]))


def join_kernel(a_ref, b_ref, token_ref, out_ref):
    rows = a_ref.shape[0]
    out_ref[:rows, :] = a_ref[...]
    out_ref[rows:, :] = b_ref[...]


def join(a, b, token):
    return pl.pallas_call(
        join_kernel,
        out_shape=vmem_array((a.shape[0] + b.shape[0], a.shape[1]), BF16),
        in_specs=[VMEM_SPEC] * 3,
        out_specs=VMEM_SPEC,
        compiler_params=pltpu.CompilerParams(vmem_limit_bytes=HELD_BELOW),
        name="join",
    )(*in_vmem(a, b, token))


def split_three(value):
    first = value.astype(BF16).astype(F32)
    second = (value - first).astype(BF16).astype(F32)
    return first, second, value - first - second


def attend_kernel(
    ahead, len_hbm, routes_hbm, q_hbm, k_hbm, v_hbm, nk_hbm, nv_hbm, res_hbm, gain_hbm, rt_hbm,
    g_hbm, u_hbm, carried_ref, pay_ref, g_vmem, u_vmem, spare_ref,
    q_ref, k_ref, v_ref, nk_ref, nv_ref, res_ref, gain_ref, rt_ref,
    q_scr, o_scr, nk_scr, nv_scr, pay_scr, len_ref, routes_ref, sems, w_sems,
):
    tok, width = q_ref.shape
    cache_len, kv_width = k_ref.shape[1], k_ref.shape[2]
    heads = width // HEAD_DIM
    groups = kv_width // HEAD_DIM
    fold_width = width // FOLD
    scaling = 1.0 / math.sqrt(HEAD_DIM)
    columns = pl.ds(pl.multiple_of(own_side() * width, LANES), width)
    moves = [
        (q_hbm, q_ref), (k_hbm, k_ref), (nk_hbm, nk_ref), (len_hbm, len_ref), (v_hbm, v_ref),
        (nv_hbm, nv_ref), (res_hbm, res_ref),
        (gain_hbm.at[:, columns], gain_ref), (rt_hbm.at[:, columns], rt_ref),
        (routes_hbm, routes_ref),
    ]
    copies = [pltpu.make_async_copy(a, b, sems.at[i]) for i, (a, b) in enumerate(moves)]
    weights = row_copies((g_hbm, u_hbm), (g_vmem, u_vmem), 0, ahead, w_sems)
    for copy in copies + weights:
        copy.start()
    copies[0].wait()
    for h in range(heads):
        q_scr[h * tok:(h + 1) * tok, :] = q_ref[:, h * HEAD_DIM:(h + 1) * HEAD_DIM].astype(F32)
    copies[2].wait()
    nk_scr[...] = nk_ref[...].astype(F32)
    row_group = lax.broadcasted_iota(jnp.int32, (heads, HEAD_DIM), 0) // GROUP
    position = lax.broadcasted_iota(jnp.int32, (heads, cache_len), 1)
    scores, fresh = [], []
    for t in range(tok):
        if t == 0:
            copies[1].wait()
        q_rows = q_scr[pl.ds(t, heads, stride=tok), :]
        q_wide = jnp.concatenate(
            [jnp.where(row_group == g, q_rows, 0.0) for g in range(groups)], axis=1
        )
        scores.append(
            lax.dot_general(
                q_wide.astype(BF16), k_ref[t], (((1,), (1,)), ((), ())),
                preferred_element_type=F32,
            ) * scaling
        )
        fresh.append(
            jnp.sum(q_wide * nk_scr[pl.ds(t, 1), :], axis=1, keepdims=True) * scaling
        )
    copies[3].wait()
    terms, fresh_terms, totals = [], [], []
    for t in range(tok):
        score = jnp.where(position < len_ref[t], scores[t], -1e30)
        largest = jnp.maximum(jnp.max(score, axis=1, keepdims=True), fresh[t])
        term = jnp.exp(score - largest)
        fresh_term = jnp.exp(fresh[t] - largest)
        totals.append(jnp.sum(term, axis=1, keepdims=True) + fresh_term)
        terms.append(term.astype(BF16))
        fresh_terms.append(fresh_term.astype(BF16).astype(F32))
    copies[5].wait()
    nv_scr[...] = nv_ref[...].astype(F32)
    for t in range(tok):
        if t == 0:
            copies[4].wait()
        wide = jnp.dot(terms[t], v_ref[t], preferred_element_type=F32)
        wide = wide + fresh_terms[t] * nv_scr[pl.ds(t, 1), :]
        picked = wide[:, :HEAD_DIM]
        for g in range(1, groups):
            picked = jnp.where(
                row_group == g, wide[:, g * HEAD_DIM:(g + 1) * HEAD_DIM], picked
            )
        o_scr[pl.ds(t, heads, stride=tok), :] = picked / totals[t]
    for copy in copies[6:]:
        copy.wait()
    for h in range(heads):
        cols = slice(h * HEAD_DIM, (h + 1) * HEAD_DIM)
        carried_ref[:, cols] = res_ref[:, cols].astype(F32) + o_scr[h * tok:(h + 1) * tok, :]
    carried = carried_ref[...]
    scaled = carried * gain_ref[...]
    rounded = scaled.astype(BF16).astype(F32)
    router = rt_ref[...].astype(F32)
    for f in range(FOLD):
        pay_scr[f * tok:(f + 1) * tok, :fold_width] = scaled[:, f * fold_width:(f + 1) * fold_width]
    lane = lax.broadcasted_iota(jnp.int32, (tok, LANES), 1)
    row = lax.broadcasted_iota(jnp.int32, (tok, LANES), 0)
    sums = [jnp.sum(carried * carried, axis=1, keepdims=True)]
    for e in range(EXPERTS):
        sums.append(jnp.sum(rounded * router[e:e + 1, :], axis=1, keepdims=True))
    extra = jnp.zeros((tok, LANES), F32)
    for i, total in enumerate(sums):
        for j, term in enumerate(split_three(total)):
            extra = jnp.where(lane == 3 * i + j, term, extra)
    for t in range(tok):
        for i in range(2):
            extra = jnp.where(
                jnp.logical_and(row == t, lane == ROUTE_LANE + i),
                routes_ref[i, t].astype(F32), extra,
            )
    for f in range(FOLD):
        pay_scr[f * tok:(f + 1) * tok, fold_width:] = extra
    pay_ref[...] = pay_scr[...].astype(BF16)
    for copy in weights:
        copy.wait()


def attend(
    ahead, lengths, routes_t, queries, key_cache, value_cache, new_key, new_value,
    residual, gain, router_t, gate_weight, up_weight,
):
    tok, width = queries.shape
    kv_width = new_key.shape[1]
    heads = width // HEAD_DIM
    wide = width // FOLD + LANES
    here = [
        pltpu.VMEM(a.shape, a.dtype)
        for a in (queries, key_cache, value_cache, new_key, new_value, residual)
    ]
    return pl.pallas_call(
        functools.partial(attend_kernel, ahead),
        out_shape=(
            pltpu.VMEM((tok, width), F32),
            pltpu.VMEM((FOLD * tok, wide), BF16),
            pltpu.VMEM(held_shape(gate_weight), BF16),
            pltpu.VMEM(held_shape(gate_weight), BF16),
            pltpu.VMEM(spare_shape(gate_weight), BF16),
        ),
        in_specs=[HBM_SPEC] * 12,
        out_specs=(VMEM_SPEC,) * 5,
        scratch_shapes=here + [
            pltpu.VMEM((1, width), F32),
            pltpu.VMEM((EXPERTS, width), BF16),
            pltpu.VMEM((heads * tok, HEAD_DIM), F32),
            pltpu.VMEM((heads * tok, HEAD_DIM), F32),
            pltpu.VMEM((tok, kv_width), F32),
            pltpu.VMEM((tok, kv_width), F32),
            pltpu.VMEM((FOLD * tok, wide), F32),
            pltpu.SMEM(lengths.shape, jnp.int32),
            pltpu.SMEM(routes_t.shape, jnp.int32),
            pltpu.SemaphoreType.DMA((10,)),
            pltpu.SemaphoreType.DMA((2, 1)),
        ],
        compiler_params=pltpu.CompilerParams(vmem_limit_bytes=LOADED_BELOW),
        cost_estimate=pl.CostEstimate(flops=10**8, bytes_accessed=8 * 10**6, transcendentals=10**5),
        name="attend",
    )(
        *in_hbm(
            lengths, routes_t, queries, key_cache, value_cache, new_key, new_value, residual, gain, router_t,
            gate_weight, up_weight,
        ),
    )


def first_half_kernel(
    x_ref, g_hbm, u_hbm, g_in, u_in, spare_in, gate_ref, up_ref, g_ref, u_ref, spare_ref, sems
):
    del g_in, u_in, spare_in
    half, units = g_ref.shape[0], gate_ref.shape[1]
    chunk = chunk_of(units)
    chunks = units // chunk
    count = spare_ref.shape[0]
    ready = [(i, c) for c in range(1, min(count + 1, chunks)) for i in range(2)]

    def copy(i, c):
        return other_copy(
            (g_hbm, u_hbm)[i], (g_ref, u_ref)[i], spare_ref, i, c, chunk, sems.at[i, c]
        )

    for i, c in ready:
        if c < count:
            copy(i, c).start()

    def step(n, _):
        at = chunk_at(n, chunk)
        rows = x_ref[:, :half]
        gate_ref[:, at] = jnp.dot(rows, g_ref[:, at], preferred_element_type=F32)
        up_ref[:, at] = jnp.dot(rows, u_ref[:, at], preferred_element_type=F32)
        for i, c in ready:
            if c >= count:
                @pl.when(n == c - count)
                def _(i=i, c=c):
                    copy(i, c).start()

        return 0

    lax.fori_loop(0, chunks, step, 0)
    for i, c in ready:
        copy(i, c).wait()


def first_half(mine, held, gate_weight, up_weight):
    rows = mine.shape[0]
    width, units = gate_weight.shape
    acc = pltpu.VMEM((rows, units), F32)
    return pl.pallas_call(
        first_half_kernel,
        out_shape=(acc, acc) + tuple(pltpu.VMEM(h.shape, BF16) for h in held),
        in_specs=[VMEM_SPEC] + [HBM_SPEC] * 2 + [VMEM_SPEC] * 3,
        out_specs=(VMEM_SPEC,) * 5,
        scratch_shapes=[pltpu.SemaphoreType.DMA((2, units // chunk_of(units)))],
        input_output_aliases={3: 2, 4: 3, 5: 4},
        compiler_params=pltpu.CompilerParams(vmem_limit_bytes=HELD_BELOW),
        cost_estimate=pl.CostEstimate(
            flops=2 * rows * width * units, bytes_accessed=width * units, transcendentals=0
        ),
        name="first_half",
    )(*in_vmem_always([mine]), *in_hbm(gate_weight, up_weight), *in_vmem_always(held))


def down_tools(d_hbm, g_ref, u_ref, spare_ref, h_ref, sems, width):
    units = h_ref.shape[1]
    chunk = chunk_of(units)
    chunks, count = units // chunk, spare_ref.shape[0]
    per_side = width // chunk
    places = count + chunks
    side = own_side()

    def place(i, part, r):
        if part == 1:
            return spare_ref.at[r - count, i, pl.ds(0, units)]
        start = r + chunks - count if part == 0 else r - 2 * count
        return (g_ref, u_ref)[i].at[pl.ds(0, units), chunk_at(start, chunk)]

    def copy(i, p, part, r):
        n = 2 * p + i
        column = jnp.where(n < per_side, 1 - side, side) * width + lax.rem(n, per_side) * chunk
        return pltpu.make_async_copy(
            d_hbm.at[:, pl.ds(pl.multiple_of(column, LANES), chunk)], place(i, part, r), sems.at[i, p]
        )

    def copies(p):
        r = p % places
        part = 0 if r < count else 1 if r < 2 * count else 2
        return [copy(i, p, part, r) for i in range(2)]

    def run(low, high, limit, put, ready=0):
        def step(turn, part, r, _):
            p = turn * places + r
            for i in range(2):
                @pl.when(p >= ready)
                def _(i=i):
                    copy(i, p, part, r).wait()

                value = jnp.dot(h_ref[...], place(i, part, r)[...], preferred_element_type=F32)
                put(chunk_at(lax.rem(2 * p + i, per_side), chunk), value)
            return 0

        for turn in range(low // places, -(-high // places)):
            for part, (start, end) in enumerate(((0, count), (count, 2 * count), (2 * count, places))):
                start = max(start, low - turn * places)
                end = min(end, high - turn * places)
                if start < end:
                    lax.fori_loop(start, end, functools.partial(step, turn, part), 0)
                for r in range(start, end):
                    if (turn + 1) * places + r < limit:
                        for item in copies((turn + 1) * places + r):
                            item.start()

    return copies, run, places


def pairs_ahead(places, leaving):
    return max(0, min(2, places - leaving))


def second_half_kernel(
    per_plane, x_ref, ox_ref, gate_ref, up_ref, g_hbm, u_hbm, d_hbm, g_in, u_in, spare_in,
    leaving_ref, h_scr, weight_ref, g_ref, u_ref, spare_ref, gu_sems, sems,
):
    del g_in, u_in, spare_in
    rows, units = h_scr.shape
    width = leaving_ref.shape[1]
    chunk = chunk_of(units)
    chunks = units // chunk
    count = spare_ref.shape[0]
    leaving = width // chunk // 2
    copies, run, places = down_tools(d_hbm, g_ref, u_ref, spare_ref, h_scr, sems, width)
    ahead = pairs_ahead(places, leaving)

    def gu_copy(i, c):
        return other_copy(
            (g_hbm, u_hbm)[i], (g_ref, u_ref)[i], spare_ref, i, c, chunk, gu_sems.at[i, c]
        )

    def start_down(p):
        for item in copies(p):
            item.start()

    def in_order(values):
        quarter = rows // 4
        return jnp.concatenate(
            [values[q * quarter:(q + 1) * quarter, :] for q in (0, 2, 1, 3)], axis=0
        )

    later = [(i, c) for c in range(count + 1, chunks) for i in range(2)]
    for i, c in later:
        gu_copy(i, c).start()
    for p in range(min(count, leaving + ahead)):
        start_down(p)

    own = x_ref[:, width:].astype(F32)
    both = own + in_order(ox_ref[:, width:].astype(F32))
    lane = lax.broadcasted_iota(jnp.int32, (rows, LANES), 1)

    def pick(values, mask):
        return jnp.sum(jnp.where(mask, values, 0.0), axis=1, keepdims=True)

    scale = lax.rsqrt(pick(both, lane < 3) * (1.0 / (2 * width)) + 1e-05)
    first, second = pick(own, lane == ROUTE_LANE), pick(own, lane == ROUTE_LANE + 1)
    expert_of = (lane - 3) // 3
    logit_lane = jnp.logical_and(lane >= 3, lane < ROUTE_LANE)

    def logit_at(route):
        return pick(both, jnp.logical_and(logit_lane, expert_of == route.astype(jnp.int32))) * scale

    share = 1.0 / (1.0 + jnp.exp(logit_at(second) - logit_at(first)))
    here = (lax.axis_index("node") // per_plane).astype(F32)
    weight = jnp.where(first == here, share, 0.0) + jnp.where(second == here, 1.0 - share, 0.0)

    def hidden_chunk(c, g_part, u_part):
        at = chunk_at(c, chunk)
        rows_in = ox_ref[:, :width]
        gate = gate_ref[:, at] + in_order(jnp.dot(rows_in, g_part, preferred_element_type=F32))
        up = up_ref[:, at] + in_order(jnp.dot(rows_in, u_part, preferred_element_type=F32))
        gate = gate * scale
        h_scr[:, at] = (gate / (1.0 + jnp.exp(-gate)) * (up * scale)).astype(BF16)
        for late in range(chunks):
            if count + late < leaving + ahead:
                @pl.when(c == late)
                def _(late=late):
                    start_down(count + late)

    def spare_step(c, _):
        hidden_chunk(c, spare_ref[c, 0], spare_ref[c, 1])
        return 0

    def held_step(c, _):
        for i, late in later:
            @pl.when(c == late)
            def _(i=i, late=late):
                gu_copy(i, late).wait()

        slot = chunk_at(c - count, chunk)
        hidden_chunk(c, g_ref[:, slot], u_ref[:, slot])
        return 0

    lax.fori_loop(0, count, spare_step, 0)
    lax.fori_loop(count, chunks, held_step, 0)

    def leave(to, value):
        leaving_ref[:, to] = in_order(value * weight).astype(BF16)

    run(0, leaving, leaving + ahead, leave)
    weight_ref[...] = jnp.broadcast_to(weight, weight_ref.shape)
    for p in range(leaving, leaving + ahead):
        for item in copies(p):
            item.wait()


def second_half(per_plane, mine, other, sums, held, gate_weight, up_weight, down_weight):
    rows, units = sums[0].shape
    width = down_weight.shape[1] // 2
    chunk = chunk_of(units)
    return pl.pallas_call(
        functools.partial(second_half_kernel, per_plane),
        out_shape=(vmem_array((rows, width), BF16), pltpu.VMEM((rows, units), BF16))
        + (pltpu.VMEM((rows, LANES), F32),) + tuple(pltpu.VMEM(h.shape, BF16) for h in held),
        in_specs=[VMEM_SPEC] * 4 + [HBM_SPEC] * 3 + [VMEM_SPEC] * 3,
        out_specs=(VMEM_SPEC,) * 6,
        scratch_shapes=[
            pltpu.SemaphoreType.DMA((2, units // chunk)),
            pltpu.SemaphoreType.DMA((2, width // chunk)),
        ],
        input_output_aliases={7: 3, 8: 4, 9: 5},
        compiler_params=pltpu.CompilerParams(
            vmem_limit_bytes=HELD_BELOW if rows < 256 else 40 * MIB
        ),
        cost_estimate=pl.CostEstimate(
            flops=6 * rows * width * units, bytes_accessed=4 * width * units, transcendentals=0
        ),
        name="second_half",
    )(
        *in_vmem_always([mine, other]), *in_vmem(*sums),
        *in_hbm(gate_weight, up_weight, down_weight), *in_vmem_always(held),
    )


def staying_kernel(
    h_ref, weight_ref, d_hbm, g_in, u_in, spare_in, out_ref, g_ref, u_ref, spare_ref, sems
):
    del g_in, u_in, spare_in
    width = out_ref.shape[1]
    pairs = sems.shape[1]
    leaving = pairs // 2
    copies, run, places = down_tools(d_hbm, g_ref, u_ref, spare_ref, h_ref, sems, width)
    ahead = pairs_ahead(places, leaving)
    for p in range(leaving + ahead, min(leaving + places, pairs)):
        for item in copies(p):
            item.start()
    weight = weight_ref[:, 0:1]

    def stay(to, value):
        out_ref[:, to] = value * weight

    run(leaving, pairs, pairs, stay, leaving + ahead)


def staying_half(hidden, weight, held, down_weight):
    rows, units = hidden.shape
    width = down_weight.shape[1] // 2
    return pl.pallas_call(
        staying_kernel,
        out_shape=(vmem_array((rows, width), F32),)
        + tuple(pltpu.VMEM(h.shape, BF16) for h in held),
        in_specs=[VMEM_SPEC] * 2 + [HBM_SPEC] + [VMEM_SPEC] * 3,
        out_specs=(VMEM_SPEC,) * 4,
        scratch_shapes=[pltpu.SemaphoreType.DMA((2, width // chunk_of(units)))],
        input_output_aliases={3: 1, 4: 2, 5: 3},
        compiler_params=pltpu.CompilerParams(
            vmem_limit_bytes=HELD_BELOW if rows < 256 else 40 * MIB
        ),
        cost_estimate=pl.CostEstimate(
            flops=2 * rows * width * units, bytes_accessed=width * units, transcendentals=0
        ),
        name="staying_half",
    )(*in_vmem_always([hidden, weight]), *in_hbm(down_weight), *in_vmem_always(held))[0]


def split_kernel(own_ref, got_ref, keep_ref, send_ref):
    size = keep_ref.shape[0]
    keep_ref[...] = own_ref[:size, :] + got_ref[:size, :].astype(F32)
    send_ref[...] = (own_ref[size:, :] + got_ref[size:, :].astype(F32)).astype(BF16)


def split_rows(own, got):
    rows, width = own.shape
    size = rows // 2
    return pl.pallas_call(
        split_kernel,
        out_shape=(vmem_array((size, width), F32), vmem_array((size, width), BF16)),
        in_specs=[VMEM_SPEC] * 2,
        out_specs=(VMEM_SPEC,) * 2,
        compiler_params=pltpu.CompilerParams(vmem_limit_bytes=(8 if rows < 256 else 32) * MIB),
        name="split_rows",
    )(*in_vmem(own, got))


def split_last_kernel(own_ref, got_ref, keep_ref, *refs):
    *sends, total = refs
    total[...] = own_ref[...] + got_ref[...].astype(F32)
    tok, width = keep_ref.shape
    fold_width = width // FOLD
    keep_ref[...] = total[:tok, :]
    for i, send in enumerate(sends, 1):
        rows = total[i * tok:(i + 1) * tok, :]
        send[...] = jnp.concatenate(
            [rows[:, f * fold_width:(f + 1) * fold_width] for f in range(FOLD)], axis=0
        ).astype(BF16)


def split_last(own, got, parts):
    rows, width = own.shape
    tok = rows // parts
    return pl.pallas_call(
        split_last_kernel,
        out_shape=(pltpu.VMEM((tok, width), F32),)
        + (pltpu.VMEM((FOLD * tok, width // FOLD), BF16),) * (parts - 1),
        in_specs=[VMEM_SPEC] * 2,
        out_specs=(VMEM_SPEC,) * parts,
        scratch_shapes=[pltpu.VMEM((rows, width), F32)],
        compiler_params=pltpu.CompilerParams(vmem_limit_bytes=4 * MIB),
        name="split_last",
    )(*in_vmem(own, got))


def finish_kernel(carried_ref, own_ref, *refs):
    *got, out_ref, folded = refs
    tok, width = carried_ref.shape
    fold_width = width // FOLD
    total = got[0][...].astype(F32)
    for ref in got[1:]:
        total = total + ref[...].astype(F32)
    folded[...] = total
    for f in range(FOLD):
        at = slice(f * fold_width, (f + 1) * fold_width)
        value = carried_ref[:, at] + own_ref[:, at] + folded[f * tok:(f + 1) * tok, :]
        out_ref[:, at] = value.astype(BF16)


def finish(carried, own, got):
    tok, width = carried.shape
    return pl.pallas_call(
        finish_kernel,
        out_shape=jax.ShapeDtypeStruct((tok, width), BF16),
        in_specs=[VMEM_SPEC] * (2 + len(got)),
        out_specs=VMEM_SPEC,
        scratch_shapes=[pltpu.VMEM((FOLD * tok, width // FOLD), F32)],
        compiler_params=pltpu.CompilerParams(vmem_limit_bytes=8 * MIB),
        name="finish",
    )(*in_vmem(carried, own, *got))


def on_device(
    residual, queries, key_cache, value_cache, new_key, new_value, cache_lengths,
    norm_gain, router, routes, gate_weight, up_weight, down_weight,
):
    nodes = lax.axis_size("node")
    per_plane = nodes // EXPERTS
    stages = nodes.bit_length() - 1
    masks = [nodes >> (s + 1) for s in range(stages)]
    routes_of = (masks, masks[:-2] + masks[:-3:-1])

    def exchange(array, *flips):
        masks = [sum(side[s] for s in flips) for side in routes_of]
        perm = [(2 * n + c, 2 * (n ^ masks[c]) + c) for n in range(nodes) for c in range(2)]
        return lax.ppermute(array, ("node", "shard"), perm)

    def to_core(array):
        return lax.ppermute(array, "shard", [(0, 1), (1, 0)])

    tok = residual.shape[0]
    half = gate_weight.shape[0] // 2
    heights = [half // 6, half // 2, half // 3]
    carried, payload, *held = attend(
        heights[0], cache_lengths, routes.T, queries, key_cache, value_cache, new_key, new_value,
        residual, norm_gain.reshape(1, -1), router.T, gate_weight, up_weight,
    )
    near = ((0,), (1,), (0, 1))
    got = [exchange(payload, *flips) for flips in near]
    *held, token = load_rows(
        heights[0], heights[1], False, payload, gate_weight, up_weight, held
    )
    payload = unfold(tok, [payload, *got], token)
    for stage in range(2, stages):
        got = exchange(payload, stage)
        if stage == 2:
            *held, token = load_rows(
                heights[0] + heights[1], heights[2], True, payload, gate_weight, up_weight, held
            )
        payload = join(payload, got, token)
    mine = payload
    other = to_core(mine)
    gate, up, *held = first_half(mine, held, gate_weight, up_weight)
    leaving, hidden, weight, *held = second_half(
        per_plane, mine, other, (gate, up), held, gate_weight, up_weight, down_weight
    )
    got = to_core(leaving)
    keep = staying_half(hidden, weight, held, down_weight)
    for stage in range(stages - 1, 1, -1):
        keep, send = split_rows(keep, got)
        got = exchange(send, stage)
    keep, *sends = split_last(keep, got, 1 + len(near))
    return finish(carried, keep, [exchange(send, *flips) for send, flips in zip(sends, near)])


def solution(mesh):
    rows = ("replica", "node")
    in_specs = (
        P(rows, "shard"),
        P(rows, "shard"),
        P(rows, None, "shard"),
        P(rows, None, "shard"),
        P(rows, "shard"),
        P(rows, "shard"),
        P(rows),
        P(),
        P(),
        P(rows, None),
        P(None, ("node", "shard")),
        P(None, ("node", "shard")),
        P(("node", "shard"), None),
    )
    return jax.shard_map(
        on_device,
        mesh=mesh,
        in_specs=in_specs,
        out_specs=P(rows, "shard"),
        check_vma=False,
    )
```

```python
import functools
import math

import jax
import jax.numpy as jnp
from jax import lax
from jax.experimental import pallas as pl
from jax.experimental.pallas import tpu as pltpu
from jax.sharding import PartitionSpec as P

MIB = 1 << 20
QUERY_HEADS = 48
KV_HEADS = 8
HEAD_DIM = 128
EXPERTS = 4
GROUP = QUERY_HEADS // KV_HEADS
LANES = 128
FOLD = 2
F32 = jnp.float32
BF16 = jnp.bfloat16


def small(shape, dtype):
    return math.prod(shape) * jnp.dtype(dtype).itemsize <= 17 * MIB // 4


def vmem_array(shape, dtype):
    return pltpu.VMEM(shape, dtype) if small(shape, dtype) else jax.ShapeDtypeStruct(shape, dtype)


def in_vmem(*arrays):
    return [
        pltpu.with_memory_space_constraint(a, pltpu.VMEM) if small(a.shape, a.dtype) else a
        for a in arrays
    ]


def in_vmem_always(arrays):
    return [pltpu.with_memory_space_constraint(a, pltpu.VMEM) for a in arrays]


def in_hbm(*arrays):
    return [pltpu.with_memory_space_constraint(a, pltpu.HBM) for a in arrays]


VMEM_SPEC = pl.BlockSpec(memory_space=pltpu.VMEM)
HBM_SPEC = pl.BlockSpec(memory_space=pltpu.HBM)
ROUTE_LANE = 3 + 3 * EXPERTS
HELD_BELOW = 8 * MIB
LOADED_BELOW = 10 * MIB


def own_side():
    return lax.axis_index("shard")


def chunk_of(units):
    return math.gcd(512, units)


def held_shape(gate_weight):
    width, units = gate_weight.shape
    return width // 2, units


def spare_shape(gate_weight):
    width, units = gate_weight.shape
    return min(2, units // chunk_of(units)), 2, width // 2, chunk_of(units)


def row_copies(sources, targets, first, rows, sems):
    parts = sems.shape[1]
    part = rows // parts
    half, units = sources[0].shape[0] // 2, sources[0].shape[1]
    copies = []
    for p in range(parts):
        at = first + p * part
        for i, (source, target) in enumerate(zip(sources, targets)):
            copies.append(
                pltpu.make_async_copy(
                    source.at[pl.ds(pl.multiple_of(own_side() * half + at, 16), part), :],
                    target.at[pl.ds(at, part), pl.ds(0, units)], sems.at[i, p],
                )
            )
    return copies


def chunk_at(n, chunk):
    return pl.ds(n * chunk if isinstance(n, int) else pl.multiple_of(n * chunk, LANES), chunk)


def other_copy(source, held, spare, i, c, chunk, sem):
    half = source.shape[0] // 2
    first = pl.multiple_of((1 - own_side()) * half, 16)
    count = spare.shape[0]
    target = spare.at[c, i] if c < count else held.at[:, chunk_at(c - count, chunk)]
    return pltpu.make_async_copy(source.at[pl.ds(first, half), chunk_at(c, chunk)], target, sem)


def load_kernel(first, rows, ahead, dep_ref, g_hbm, u_hbm, *refs):
    g_vmem, u_vmem, spare, token_ref, sems, sem = refs[3:]
    copies = row_copies((g_hbm, u_hbm), (g_vmem, u_vmem), first, rows, sems)
    if ahead:
        for i, source in enumerate((g_hbm, u_hbm)):
            copies.append(other_copy(source, None, spare, i, 0, spare.shape[3], sem.at[i]))
    for copy in copies:
        copy.start()
    token_ref[...] = jnp.zeros_like(token_ref)
    for copy in copies:
        copy.wait()


def load_rows(first, rows, ahead, after, gate_weight, up_weight, held):
    hidden = gate_weight.shape[1]
    return pl.pallas_call(
        functools.partial(load_kernel, first, rows, ahead),
        out_shape=tuple(pltpu.VMEM(h.shape, BF16) for h in held) + (pltpu.VMEM((8, LANES), F32),),
        in_specs=[pl.BlockSpec(memory_space=pl.ANY), HBM_SPEC, HBM_SPEC] + [VMEM_SPEC] * 3,
        out_specs=(VMEM_SPEC,) * 4,
        scratch_shapes=[pltpu.SemaphoreType.DMA((2, 4)), pltpu.SemaphoreType.DMA((2,))],
        input_output_aliases={3: 0, 4: 1, 5: 2},
        compiler_params=pltpu.CompilerParams(vmem_limit_bytes=LOADED_BELOW),
        cost_estimate=pl.CostEstimate(flops=0, bytes_accessed=4 * rows * hidden, transcendentals=0),
        name="load_weights",
    )(*in_vmem(after), *in_hbm(gate_weight, up_weight), *in_vmem_always(held))


def unfold_kernel(tok, *refs):
    *arrays, _, out_ref, scr = refs
    fold_width = arrays[0].shape[1] - LANES
    for i, array in enumerate([arrays[0], *reversed(arrays[1:])]):
        rows = array[...].astype(F32)
        to = slice(i * tok, (i + 1) * tok)
        for f in range(FOLD):
            scr[to, f * fold_width:(f + 1) * fold_width] = rows[f * tok:(f + 1) * tok, :fold_width]
        scr[to, FOLD * fold_width:] = rows[:tok, fold_width:]
    out_ref[...] = scr[...].astype(BF16)


def unfold(tok, arrays, token):
    shape = (len(arrays) * tok, FOLD * (arrays[0].shape[1] - LANES) + LANES)
    return pl.pallas_call(
        functools.partial(unfold_kernel, tok),
        out_shape=pltpu.VMEM(shape, BF16),
        in_specs=[VMEM_SPEC] * (len(arrays) + 1),
        out_specs=VMEM_SPEC,
        scratch_shapes=[pltpu.VMEM(shape, F32)],
        compiler_params=pltpu.CompilerParams(vmem_limit_bytes=3 * MIB),
        name="unfold",
    )(*in_vmem_always([*arrays, token]))


def join_kernel(a_ref, b_ref, token_ref, out_ref):
    rows = a_ref.shape[0]
    out_ref[:rows, :] = a_ref[...]
    out_ref[rows:, :] = b_ref[...]


def join(a, b, token):
    return pl.pallas_call(
        join_kernel,
        out_shape=vmem_array((a.shape[0] + b.shape[0], a.shape[1]), BF16),
        in_specs=[VMEM_SPEC] * 3,
        out_specs=VMEM_SPEC,
        compiler_params=pltpu.CompilerParams(vmem_limit_bytes=HELD_BELOW),
        name="join",
    )(*in_vmem(a, b, token))


def split_three(value):
    first = value.astype(BF16).astype(F32)
    second = (value - first).astype(BF16).astype(F32)
    return first, second, value - first - second


def attend_kernel(
    ahead, len_hbm, routes_hbm, q_hbm, k_hbm, v_hbm, nk_hbm, nv_hbm, res_hbm, gain_hbm, rt_hbm,
    g_hbm, u_hbm, carried_ref, pay_ref, g_vmem, u_vmem, spare_ref,
    q_ref, k_ref, v_ref, nk_ref, nv_ref, res_ref, gain_ref, rt_ref,
    q_scr, o_scr, nk_scr, nv_scr, pay_scr, len_ref, routes_ref, sems, w_sems,
):
    tok, width = q_ref.shape
    cache_len, kv_width = k_ref.shape[1], k_ref.shape[2]
    heads = width // HEAD_DIM
    groups = kv_width // HEAD_DIM
    fold_width = width // FOLD
    scaling = 1.0 / math.sqrt(HEAD_DIM)
    columns = pl.ds(pl.multiple_of(own_side() * width, LANES), width)
    moves = [
        (q_hbm, q_ref), (k_hbm, k_ref), (nk_hbm, nk_ref), (len_hbm, len_ref), (v_hbm, v_ref),
        (nv_hbm, nv_ref), (res_hbm, res_ref),
        (gain_hbm.at[:, columns], gain_ref), (rt_hbm.at[:, columns], rt_ref),
        (routes_hbm, routes_ref),
    ]
    copies = [pltpu.make_async_copy(a, b, sems.at[i]) for i, (a, b) in enumerate(moves)]
    weights = row_copies((g_hbm, u_hbm), (g_vmem, u_vmem), 0, ahead, w_sems)
    for copy in copies + weights:
        copy.start()
    copies[0].wait()
    for h in range(heads):
        q_scr[h * tok:(h + 1) * tok, :] = q_ref[:, h * HEAD_DIM:(h + 1) * HEAD_DIM].astype(F32)
    copies[2].wait()
    nk_scr[...] = nk_ref[...].astype(F32)
    row_group = lax.broadcasted_iota(jnp.int32, (heads, HEAD_DIM), 0) // GROUP
    position = lax.broadcasted_iota(jnp.int32, (heads, cache_len), 1)
    scores, fresh = [], []
    for t in range(tok):
        if t == 0:
            copies[1].wait()
        q_rows = q_scr[pl.ds(t, heads, stride=tok), :]
        q_wide = jnp.concatenate(
            [jnp.where(row_group == g, q_rows, 0.0) for g in range(groups)], axis=1
        )
        scores.append(
            lax.dot_general(
                q_wide.astype(BF16), k_ref[t], (((1,), (1,)), ((), ())),
                preferred_element_type=F32,
            ) * scaling
        )
        fresh.append(
            jnp.sum(q_wide * nk_scr[pl.ds(t, 1), :], axis=1, keepdims=True) * scaling
        )
    copies[3].wait()
    terms, fresh_terms, totals = [], [], []
    for t in range(tok):
        score = jnp.where(position < len_ref[t], scores[t], -1e30)
        largest = jnp.maximum(jnp.max(score, axis=1, keepdims=True), fresh[t])
        term = jnp.exp(score - largest)
        fresh_term = jnp.exp(fresh[t] - largest)
        totals.append(jnp.sum(term, axis=1, keepdims=True) + fresh_term)
        terms.append(term.astype(BF16))
        fresh_terms.append(fresh_term.astype(BF16).astype(F32))
    copies[5].wait()
    nv_scr[...] = nv_ref[...].astype(F32)
    for t in range(tok):
        if t == 0:
            copies[4].wait()
        wide = jnp.dot(terms[t], v_ref[t], preferred_element_type=F32)
        wide = wide + fresh_terms[t] * nv_scr[pl.ds(t, 1), :]
        picked = wide[:, :HEAD_DIM]
        for g in range(1, groups):
            picked = jnp.where(
                row_group == g, wide[:, g * HEAD_DIM:(g + 1) * HEAD_DIM], picked
            )
        o_scr[pl.ds(t, heads, stride=tok), :] = picked / totals[t]
    for copy in copies[6:]:
        copy.wait()
    for h in range(heads):
        cols = slice(h * HEAD_DIM, (h + 1) * HEAD_DIM)
        carried_ref[:, cols] = res_ref[:, cols].astype(F32) + o_scr[h * tok:(h + 1) * tok, :]
    carried = carried_ref[...]
    scaled = carried * gain_ref[...]
    rounded = scaled.astype(BF16).astype(F32)
    router = rt_ref[...].astype(F32)
    for f in range(FOLD):
        pay_scr[f * tok:(f + 1) * tok, :fold_width] = scaled[:, f * fold_width:(f + 1) * fold_width]
    lane = lax.broadcasted_iota(jnp.int32, (tok, LANES), 1)
    row = lax.broadcasted_iota(jnp.int32, (tok, LANES), 0)
    sums = [jnp.sum(carried * carried, axis=1, keepdims=True)]
    for e in range(EXPERTS):
        sums.append(jnp.sum(rounded * router[e:e + 1, :], axis=1, keepdims=True))
    extra = jnp.zeros((tok, LANES), F32)
    for i, total in enumerate(sums):
        for j, term in enumerate(split_three(total)):
            extra = jnp.where(lane == 3 * i + j, term, extra)
    for t in range(tok):
        for i in range(2):
            extra = jnp.where(
                jnp.logical_and(row == t, lane == ROUTE_LANE + i),
                routes_ref[i, t].astype(F32), extra,
            )
    for f in range(FOLD):
        pay_scr[f * tok:(f + 1) * tok, fold_width:] = extra
    pay_ref[...] = pay_scr[...].astype(BF16)
    for copy in weights:
        copy.wait()


def attend(
    ahead, lengths, routes_t, queries, key_cache, value_cache, new_key, new_value,
    residual, gain, router_t, gate_weight, up_weight,
):
    tok, width = queries.shape
    kv_width = new_key.shape[1]
    heads = width // HEAD_DIM
    wide = width // FOLD + LANES
    here = [
        pltpu.VMEM(a.shape, a.dtype)
        for a in (queries, key_cache, value_cache, new_key, new_value, residual)
    ]
    return pl.pallas_call(
        functools.partial(attend_kernel, ahead),
        out_shape=(
            pltpu.VMEM((tok, width), F32),
            pltpu.VMEM((FOLD * tok, wide), BF16),
            pltpu.VMEM(held_shape(gate_weight), BF16),
            pltpu.VMEM(held_shape(gate_weight), BF16),
            pltpu.VMEM(spare_shape(gate_weight), BF16),
        ),
        in_specs=[HBM_SPEC] * 12,
        out_specs=(VMEM_SPEC,) * 5,
        scratch_shapes=here + [
            pltpu.VMEM((1, width), F32),
            pltpu.VMEM((EXPERTS, width), BF16),
            pltpu.VMEM((heads * tok, HEAD_DIM), F32),
            pltpu.VMEM((heads * tok, HEAD_DIM), F32),
            pltpu.VMEM((tok, kv_width), F32),
            pltpu.VMEM((tok, kv_width), F32),
            pltpu.VMEM((FOLD * tok, wide), F32),
            pltpu.SMEM(lengths.shape, jnp.int32),
            pltpu.SMEM(routes_t.shape, jnp.int32),
            pltpu.SemaphoreType.DMA((10,)),
            pltpu.SemaphoreType.DMA((2, 1)),
        ],
        compiler_params=pltpu.CompilerParams(vmem_limit_bytes=LOADED_BELOW),
        cost_estimate=pl.CostEstimate(flops=10**8, bytes_accessed=8 * 10**6, transcendentals=10**5),
        name="attend",
    )(
        *in_hbm(
            lengths, routes_t, queries, key_cache, value_cache, new_key, new_value, residual, gain, router_t,
            gate_weight, up_weight,
        ),
    )


def ready_parts(count, chunks):
    parts = [(i, c) for c in range(1, chunks) for i in range(2)]
    return parts[:2 * count + 1]


def first_half_kernel(
    x_ref, g_hbm, u_hbm, g_in, u_in, spare_in, gate_ref, up_ref, g_ref, u_ref, spare_ref, sems
):
    del g_in, u_in, spare_in
    half, units = g_ref.shape[0], gate_ref.shape[1]
    chunk = chunk_of(units)
    chunks = units // chunk
    count = spare_ref.shape[0]
    ready = ready_parts(count, chunks)

    def copy(i, c):
        return other_copy(
            (g_hbm, u_hbm)[i], (g_ref, u_ref)[i], spare_ref, i, c, chunk, sems.at[i, c]
        )

    for i, c in ready:
        if c < count:
            copy(i, c).start()

    def step(n, _):
        at = chunk_at(n, chunk)
        rows = x_ref[:, :half]
        gate_ref[:, at] = jnp.dot(rows, g_ref[:, at], preferred_element_type=F32)
        up_ref[:, at] = jnp.dot(rows, u_ref[:, at], preferred_element_type=F32)
        for i, c in ready:
            if c >= count:
                @pl.when(n == c - count)
                def _(i=i, c=c):
                    copy(i, c).start()

        return 0

    lax.fori_loop(0, chunks, step, 0)
    for i, c in ready:
        copy(i, c).wait()


def first_half(mine, held, gate_weight, up_weight):
    rows = mine.shape[0]
    width, units = gate_weight.shape
    acc = pltpu.VMEM((rows, units), F32)
    return pl.pallas_call(
        first_half_kernel,
        out_shape=(acc, acc) + tuple(pltpu.VMEM(h.shape, BF16) for h in held),
        in_specs=[VMEM_SPEC] + [HBM_SPEC] * 2 + [VMEM_SPEC] * 3,
        out_specs=(VMEM_SPEC,) * 5,
        scratch_shapes=[pltpu.SemaphoreType.DMA((2, units // chunk_of(units)))],
        input_output_aliases={3: 2, 4: 3, 5: 4},
        compiler_params=pltpu.CompilerParams(vmem_limit_bytes=HELD_BELOW),
        cost_estimate=pl.CostEstimate(
            flops=2 * rows * width * units, bytes_accessed=width * units, transcendentals=0
        ),
        name="first_half",
    )(*in_vmem_always([mine]), *in_hbm(gate_weight, up_weight), *in_vmem_always(held))


def down_tools(d_hbm, g_ref, u_ref, spare_ref, h_ref, sems, width):
    units = h_ref.shape[1]
    chunk = chunk_of(units)
    chunks, count = units // chunk, spare_ref.shape[0]
    per_side = width // chunk
    places = count + chunks
    side = own_side()

    def place(i, part, r):
        if part == 1:
            return spare_ref.at[r - count, i, pl.ds(0, units)]
        start = r + chunks - count if part == 0 else r - 2 * count
        return (g_ref, u_ref)[i].at[pl.ds(0, units), chunk_at(start, chunk)]

    def copy(i, p, part, r):
        n = 2 * p + i
        column = jnp.where(n < per_side, 1 - side, side) * width + lax.rem(n, per_side) * chunk
        return pltpu.make_async_copy(
            d_hbm.at[:, pl.ds(pl.multiple_of(column, LANES), chunk)], place(i, part, r), sems.at[i, p]
        )

    def copies(p):
        r = p % places
        part = 0 if r < count else 1 if r < 2 * count else 2
        return [copy(i, p, part, r) for i in range(2)]

    def run(low, high, limit, put, ready=0):
        def step(turn, part, r, _):
            p = turn * places + r
            for i in range(2):
                @pl.when(p >= ready)
                def _(i=i):
                    copy(i, p, part, r).wait()

                value = jnp.dot(h_ref[...], place(i, part, r)[...], preferred_element_type=F32)
                put(chunk_at(lax.rem(2 * p + i, per_side), chunk), value)
            return 0

        for turn in range(low // places, -(-high // places)):
            for part, (start, end) in enumerate(((0, count), (count, 2 * count), (2 * count, places))):
                start = max(start, low - turn * places)
                end = min(end, high - turn * places)
                if start < end:
                    lax.fori_loop(start, end, functools.partial(step, turn, part), 0)
                for r in range(start, end):
                    if (turn + 1) * places + r < limit:
                        for item in copies((turn + 1) * places + r):
                            item.start()

    return copies, run, places


def pairs_ahead(places, leaving):
    return max(0, min(2, places - leaving))


def second_half_kernel(
    per_plane, x_ref, ox_ref, gate_ref, up_ref, g_hbm, u_hbm, d_hbm, g_in, u_in, spare_in,
    leaving_ref, h_scr, weight_ref, g_ref, u_ref, spare_ref, gu_sems, sems,
):
    del g_in, u_in, spare_in
    rows, units = h_scr.shape
    width = leaving_ref.shape[1]
    chunk = chunk_of(units)
    chunks = units // chunk
    count = spare_ref.shape[0]
    leaving = width // chunk // 2
    copies, run, places = down_tools(d_hbm, g_ref, u_ref, spare_ref, h_scr, sems, width)
    ahead = pairs_ahead(places, leaving)

    def gu_copy(i, c):
        return other_copy(
            (g_hbm, u_hbm)[i], (g_ref, u_ref)[i], spare_ref, i, c, chunk, gu_sems.at[i, c]
        )

    def start_down(p):
        for item in copies(p):
            item.start()

    def in_order(values):
        quarter = rows // 4
        return jnp.concatenate(
            [values[q * quarter:(q + 1) * quarter, :] for q in (0, 2, 1, 3)], axis=0
        )

    there = ready_parts(count, chunks)
    later = [(i, c) for c in range(1, chunks) for i in range(2) if (i, c) not in there]
    for i, c in later:
        gu_copy(i, c).start()
    for p in range(min(count, leaving + ahead)):
        start_down(p)

    own = x_ref[:, width:].astype(F32)
    both = own + in_order(ox_ref[:, width:].astype(F32))
    lane = lax.broadcasted_iota(jnp.int32, (rows, LANES), 1)

    def pick(values, mask):
        return jnp.sum(jnp.where(mask, values, 0.0), axis=1, keepdims=True)

    scale = lax.rsqrt(pick(both, lane < 3) * (1.0 / (2 * width)) + 1e-05)
    first, second = pick(own, lane == ROUTE_LANE), pick(own, lane == ROUTE_LANE + 1)
    expert_of = (lane - 3) // 3
    logit_lane = jnp.logical_and(lane >= 3, lane < ROUTE_LANE)

    def logit_at(route):
        return pick(both, jnp.logical_and(logit_lane, expert_of == route.astype(jnp.int32))) * scale

    share = 1.0 / (1.0 + jnp.exp(logit_at(second) - logit_at(first)))
    here = (lax.axis_index("node") // per_plane).astype(F32)
    weight = jnp.where(first == here, share, 0.0) + jnp.where(second == here, 1.0 - share, 0.0)

    def hidden_chunk(c, g_part, u_part):
        at = chunk_at(c, chunk)
        rows_in = ox_ref[:, :width]
        gate = gate_ref[:, at] + in_order(jnp.dot(rows_in, g_part, preferred_element_type=F32))
        up = up_ref[:, at] + in_order(jnp.dot(rows_in, u_part, preferred_element_type=F32))
        gate = gate * scale
        h_scr[:, at] = (gate / (1.0 + jnp.exp(-gate)) * (up * scale)).astype(BF16)
        for late in range(chunks):
            if count + late < leaving + ahead:
                @pl.when(c == late)
                def _(late=late):
                    start_down(count + late)

    def spare_step(c, _):
        hidden_chunk(c, spare_ref[c, 0], spare_ref[c, 1])
        return 0

    def held_step(c, _):
        for i, late in later:
            @pl.when(c == late)
            def _(i=i, late=late):
                gu_copy(i, late).wait()

        slot = chunk_at(c - count, chunk)
        hidden_chunk(c, g_ref[:, slot], u_ref[:, slot])
        return 0

    lax.fori_loop(0, count, spare_step, 0)
    lax.fori_loop(count, chunks, held_step, 0)

    def leave(to, value):
        leaving_ref[:, to] = in_order(value * weight).astype(BF16)

    run(0, leaving, leaving + ahead, leave)
    weight_ref[...] = jnp.broadcast_to(weight, weight_ref.shape)
    for p in range(leaving, leaving + ahead):
        for item in copies(p):
            item.wait()


def second_half(per_plane, mine, other, sums, held, gate_weight, up_weight, down_weight):
    rows, units = sums[0].shape
    width = down_weight.shape[1] // 2
    chunk = chunk_of(units)
    return pl.pallas_call(
        functools.partial(second_half_kernel, per_plane),
        out_shape=(vmem_array((rows, width), BF16), pltpu.VMEM((rows, units), BF16))
        + (pltpu.VMEM((rows, LANES), F32),) + tuple(pltpu.VMEM(h.shape, BF16) for h in held),
        in_specs=[VMEM_SPEC] * 4 + [HBM_SPEC] * 3 + [VMEM_SPEC] * 3,
        out_specs=(VMEM_SPEC,) * 6,
        scratch_shapes=[
            pltpu.SemaphoreType.DMA((2, units // chunk)),
            pltpu.SemaphoreType.DMA((2, width // chunk)),
        ],
        input_output_aliases={7: 3, 8: 4, 9: 5},
        compiler_params=pltpu.CompilerParams(
            vmem_limit_bytes=HELD_BELOW if rows < 256 else 40 * MIB
        ),
        cost_estimate=pl.CostEstimate(
            flops=6 * rows * width * units, bytes_accessed=4 * width * units, transcendentals=0
        ),
        name="second_half",
    )(
        *in_vmem_always([mine, other]), *in_vmem(*sums),
        *in_hbm(gate_weight, up_weight, down_weight), *in_vmem_always(held),
    )


def staying_kernel(
    h_ref, weight_ref, d_hbm, g_in, u_in, spare_in, out_ref, g_ref, u_ref, spare_ref, sems
):
    del g_in, u_in, spare_in
    width = out_ref.shape[1]
    pairs = sems.shape[1]
    leaving = pairs // 2
    copies, run, places = down_tools(d_hbm, g_ref, u_ref, spare_ref, h_ref, sems, width)
    ahead = pairs_ahead(places, leaving)
    for p in range(leaving + ahead, min(leaving + places, pairs)):
        for item in copies(p):
            item.start()
    weight = weight_ref[:, 0:1]

    def stay(to, value):
        out_ref[:, to] = value * weight

    run(leaving, pairs, pairs, stay, leaving + ahead)


def staying_half(hidden, weight, held, down_weight):
    rows, units = hidden.shape
    width = down_weight.shape[1] // 2
    return pl.pallas_call(
        staying_kernel,
        out_shape=(vmem_array((rows, width), F32),)
        + tuple(pltpu.VMEM(h.shape, BF16) for h in held),
        in_specs=[VMEM_SPEC] * 2 + [HBM_SPEC] + [VMEM_SPEC] * 3,
        out_specs=(VMEM_SPEC,) * 4,
        scratch_shapes=[pltpu.SemaphoreType.DMA((2, width // chunk_of(units)))],
        input_output_aliases={3: 1, 4: 2, 5: 3},
        compiler_params=pltpu.CompilerParams(
            vmem_limit_bytes=HELD_BELOW if rows < 256 else 40 * MIB
        ),
        cost_estimate=pl.CostEstimate(
            flops=2 * rows * width * units, bytes_accessed=width * units, transcendentals=0
        ),
        name="staying_half",
    )(*in_vmem_always([hidden, weight]), *in_hbm(down_weight), *in_vmem_always(held))[0]


def split_kernel(own_ref, got_ref, keep_ref, send_ref):
    size = keep_ref.shape[0]
    keep_ref[...] = own_ref[:size, :] + got_ref[:size, :].astype(F32)
    send_ref[...] = (own_ref[size:, :] + got_ref[size:, :].astype(F32)).astype(BF16)


def split_rows(own, got):
    rows, width = own.shape
    size = rows // 2
    return pl.pallas_call(
        split_kernel,
        out_shape=(vmem_array((size, width), F32), vmem_array((size, width), BF16)),
        in_specs=[VMEM_SPEC] * 2,
        out_specs=(VMEM_SPEC,) * 2,
        compiler_params=pltpu.CompilerParams(vmem_limit_bytes=(8 if rows < 256 else 32) * MIB),
        name="split_rows",
    )(*in_vmem(own, got))


def split_last_kernel(own_ref, got_ref, keep_ref, *refs):
    *sends, total = refs
    total[...] = own_ref[...] + got_ref[...].astype(F32)
    tok, width = keep_ref.shape
    fold_width = width // FOLD
    keep_ref[...] = total[:tok, :]
    for i, send in enumerate(sends, 1):
        rows = total[i * tok:(i + 1) * tok, :]
        send[...] = jnp.concatenate(
            [rows[:, f * fold_width:(f + 1) * fold_width] for f in range(FOLD)], axis=0
        ).astype(BF16)


def split_last(own, got, parts):
    rows, width = own.shape
    tok = rows // parts
    return pl.pallas_call(
        split_last_kernel,
        out_shape=(pltpu.VMEM((tok, width), F32),)
        + (pltpu.VMEM((FOLD * tok, width // FOLD), BF16),) * (parts - 1),
        in_specs=[VMEM_SPEC] * 2,
        out_specs=(VMEM_SPEC,) * parts,
        scratch_shapes=[pltpu.VMEM((rows, width), F32)],
        compiler_params=pltpu.CompilerParams(vmem_limit_bytes=4 * MIB),
        name="split_last",
    )(*in_vmem(own, got))


def finish_kernel(carried_ref, own_ref, *refs):
    *got, out_ref, folded = refs
    tok, width = carried_ref.shape
    fold_width = width // FOLD
    total = got[0][...].astype(F32)
    for ref in got[1:]:
        total = total + ref[...].astype(F32)
    folded[...] = total
    for f in range(FOLD):
        at = slice(f * fold_width, (f + 1) * fold_width)
        value = carried_ref[:, at] + own_ref[:, at] + folded[f * tok:(f + 1) * tok, :]
        out_ref[:, at] = value.astype(BF16)


def finish(carried, own, got):
    tok, width = carried.shape
    return pl.pallas_call(
        finish_kernel,
        out_shape=jax.ShapeDtypeStruct((tok, width), BF16),
        in_specs=[VMEM_SPEC] * (2 + len(got)),
        out_specs=VMEM_SPEC,
        scratch_shapes=[pltpu.VMEM((FOLD * tok, width // FOLD), F32)],
        compiler_params=pltpu.CompilerParams(vmem_limit_bytes=8 * MIB),
        name="finish",
    )(*in_vmem(carried, own, *got))


def on_device(
    residual, queries, key_cache, value_cache, new_key, new_value, cache_lengths,
    norm_gain, router, routes, gate_weight, up_weight, down_weight,
):
    nodes = lax.axis_size("node")
    per_plane = nodes // EXPERTS
    stages = nodes.bit_length() - 1
    masks = [nodes >> (s + 1) for s in range(stages)]
    routes_of = (masks, masks[:-2] + masks[:-3:-1])

    def exchange(array, *flips):
        masks = [sum(side[s] for s in flips) for side in routes_of]
        perm = [(2 * n + c, 2 * (n ^ masks[c]) + c) for n in range(nodes) for c in range(2)]
        return lax.ppermute(array, ("node", "shard"), perm)

    def to_core(array):
        return lax.ppermute(array, "shard", [(0, 1), (1, 0)])

    tok = residual.shape[0]
    half = gate_weight.shape[0] // 2
    heights = [half // 6, half // 2, half // 3]
    carried, payload, *held = attend(
        heights[0], cache_lengths, routes.T, queries, key_cache, value_cache, new_key, new_value,
        residual, norm_gain.reshape(1, -1), router.T, gate_weight, up_weight,
    )
    near = ((0,), (1,), (0, 1))
    got = [exchange(payload, *flips) for flips in near]
    *held, token = load_rows(
        heights[0], heights[1], False, payload, gate_weight, up_weight, held
    )
    payload = unfold(tok, [payload, *reversed(got)], token)
    for stage in range(2, stages):
        got = exchange(payload, stage)
        if stage == 2:
            *held, token = load_rows(
                heights[0] + heights[1], heights[2], True, payload, gate_weight, up_weight, held
            )
        payload = join(payload, got, token)
    mine = payload
    other = to_core(mine)
    gate, up, *held = first_half(mine, held, gate_weight, up_weight)
    leaving, hidden, weight, *held = second_half(
        per_plane, mine, other, (gate, up), held, gate_weight, up_weight, down_weight
    )
    got = to_core(leaving)
    keep = staying_half(hidden, weight, held, down_weight)
    for stage in range(stages - 1, 1, -1):
        keep, send = split_rows(keep, got)
        got = exchange(send, stage)
    keep, *sends = split_last(keep, got, 1 + len(near))
    return finish(carried, keep, [exchange(send, *flips) for send, flips in zip(sends, near)])


def solution(mesh):
    rows = ("replica", "node")
    in_specs = (
        P(rows, "shard"),
        P(rows, "shard"),
        P(rows, None, "shard"),
        P(rows, None, "shard"),
        P(rows, "shard"),
        P(rows, "shard"),
        P(rows),
        P(),
        P(),
        P(rows, None),
        P(None, ("node", "shard")),
        P(None, ("node", "shard")),
        P(("node", "shard"), None),
    )
    return jax.shard_map(
        on_device,
        mesh=mesh,
        in_specs=in_specs,
        out_specs=P(rows, "shard"),
        check_vma=False,
    )
```

```python
import functools
import math

import jax
import jax.numpy as jnp
from jax import lax
from jax.experimental import pallas as pl
from jax.experimental.pallas import tpu as pltpu
from jax.sharding import PartitionSpec as P

MIB = 1 << 20
QUERY_HEADS = 48
KV_HEADS = 8
HEAD_DIM = 128
EXPERTS = 4
GROUP = QUERY_HEADS // KV_HEADS
LANES = 128
FOLD = 2
F32 = jnp.float32
BF16 = jnp.bfloat16


def small(shape, dtype):
    return math.prod(shape) * jnp.dtype(dtype).itemsize <= 17 * MIB // 4


def vmem_array(shape, dtype):
    return pltpu.VMEM(shape, dtype) if small(shape, dtype) else jax.ShapeDtypeStruct(shape, dtype)


def in_vmem(*arrays):
    return [
        pltpu.with_memory_space_constraint(a, pltpu.VMEM) if small(a.shape, a.dtype) else a
        for a in arrays
    ]


def in_vmem_always(arrays):
    return [pltpu.with_memory_space_constraint(a, pltpu.VMEM) for a in arrays]


def in_hbm(*arrays):
    return [pltpu.with_memory_space_constraint(a, pltpu.HBM) for a in arrays]


VMEM_SPEC = pl.BlockSpec(memory_space=pltpu.VMEM)
HBM_SPEC = pl.BlockSpec(memory_space=pltpu.HBM)
ROUTE_LANE = 3 + 3 * EXPERTS
HELD_BELOW = 8 * MIB
LOADED_BELOW = 10 * MIB


def own_side():
    return lax.axis_index("shard")


def chunk_of(units):
    return math.gcd(512, units)


def held_shape(gate_weight):
    width, units = gate_weight.shape
    return width // 2, units


def spare_shape(gate_weight):
    width, units = gate_weight.shape
    return min(2, units // chunk_of(units)), 2, width // 2, chunk_of(units)


def row_copies(sources, targets, first, rows, sems):
    parts = sems.shape[1]
    part = rows // parts
    half, units = sources[0].shape[0] // 2, sources[0].shape[1]
    copies = []
    for p in range(parts):
        at = first + p * part
        for i, (source, target) in enumerate(zip(sources, targets)):
            copies.append(
                pltpu.make_async_copy(
                    source.at[pl.ds(pl.multiple_of(own_side() * half + at, 16), part), :],
                    target.at[pl.ds(at, part), pl.ds(0, units)], sems.at[i, p],
                )
            )
    return copies


def chunk_at(n, chunk):
    return pl.ds(n * chunk if isinstance(n, int) else pl.multiple_of(n * chunk, LANES), chunk)


def other_copy(source, held, spare, i, c, chunk, sem):
    half = source.shape[0] // 2
    first = pl.multiple_of((1 - own_side()) * half, 16)
    count = spare.shape[0]
    target = spare.at[c, i] if c < count else held.at[:, chunk_at(c - count, chunk)]
    return pltpu.make_async_copy(source.at[pl.ds(first, half), chunk_at(c, chunk)], target, sem)


def load_kernel(first, rows, ahead, dep_ref, g_hbm, u_hbm, *refs):
    g_vmem, u_vmem, spare, token_ref, sems, sem = refs[3:]
    copies = row_copies((g_hbm, u_hbm), (g_vmem, u_vmem), first, rows, sems)
    if ahead:
        for i, source in enumerate((g_hbm, u_hbm)):
            copies.append(other_copy(source, None, spare, i, 0, spare.shape[3], sem.at[i]))
    for copy in copies:
        copy.start()
    token_ref[...] = jnp.zeros_like(token_ref)
    for copy in copies:
        copy.wait()


def load_rows(first, rows, ahead, after, gate_weight, up_weight, held):
    hidden = gate_weight.shape[1]
    return pl.pallas_call(
        functools.partial(load_kernel, first, rows, ahead),
        out_shape=tuple(pltpu.VMEM(h.shape, BF16) for h in held) + (pltpu.VMEM((8, LANES), F32),),
        in_specs=[pl.BlockSpec(memory_space=pl.ANY), HBM_SPEC, HBM_SPEC] + [VMEM_SPEC] * 3,
        out_specs=(VMEM_SPEC,) * 4,
        scratch_shapes=[pltpu.SemaphoreType.DMA((2, 4)), pltpu.SemaphoreType.DMA((2,))],
        input_output_aliases={3: 0, 4: 1, 5: 2},
        compiler_params=pltpu.CompilerParams(vmem_limit_bytes=LOADED_BELOW),
        cost_estimate=pl.CostEstimate(flops=0, bytes_accessed=4 * rows * hidden, transcendentals=0),
        name="load_weights",
    )(*in_vmem(after), *in_hbm(gate_weight, up_weight), *in_vmem_always(held))


def unfold_kernel(tok, *refs):
    *arrays, _, out_ref, scr = refs
    fold_width = arrays[0].shape[1] - LANES
    for i, array in enumerate([arrays[0], *reversed(arrays[1:])]):
        rows = array[...].astype(F32)
        to = slice(i * tok, (i + 1) * tok)
        for f in range(FOLD):
            scr[to, f * fold_width:(f + 1) * fold_width] = rows[f * tok:(f + 1) * tok, :fold_width]
        scr[to, FOLD * fold_width:] = rows[:tok, fold_width:]
    out_ref[...] = scr[...].astype(BF16)


def unfold(tok, arrays, token):
    shape = (len(arrays) * tok, FOLD * (arrays[0].shape[1] - LANES) + LANES)
    return pl.pallas_call(
        functools.partial(unfold_kernel, tok),
        out_shape=pltpu.VMEM(shape, BF16),
        in_specs=[VMEM_SPEC] * (len(arrays) + 1),
        out_specs=VMEM_SPEC,
        scratch_shapes=[pltpu.VMEM(shape, F32)],
        compiler_params=pltpu.CompilerParams(vmem_limit_bytes=3 * MIB),
        name="unfold",
    )(*in_vmem_always([*arrays, token]))


def join_kernel(a_ref, b_ref, token_ref, out_ref):
    rows = a_ref.shape[0]
    out_ref[:rows, :] = a_ref[...]
    out_ref[rows:, :] = b_ref[...]


def join(a, b, token):
    return pl.pallas_call(
        join_kernel,
        out_shape=vmem_array((a.shape[0] + b.shape[0], a.shape[1]), BF16),
        in_specs=[VMEM_SPEC] * 3,
        out_specs=VMEM_SPEC,
        compiler_params=pltpu.CompilerParams(vmem_limit_bytes=HELD_BELOW),
        name="join",
    )(*in_vmem(a, b, token))


def split_three(value):
    first = value.astype(BF16).astype(F32)
    second = (value - first).astype(BF16).astype(F32)
    return first, second, value - first - second


def attend_kernel(
    ahead, len_hbm, routes_hbm, q_hbm, k_hbm, v_hbm, nk_hbm, nv_hbm, res_hbm, gain_hbm, rt_hbm,
    g_hbm, u_hbm, carried_ref, pay_ref, g_vmem, u_vmem, spare_ref,
    q_ref, k_ref, v_ref, nk_ref, nv_ref, res_ref, gain_ref, rt_ref,
    q_scr, o_scr, nk_scr, nv_scr, pay_scr, len_ref, routes_ref, sems, w_sems,
):
    tok, width = q_ref.shape
    cache_len, kv_width = k_ref.shape[1], k_ref.shape[2]
    heads = width // HEAD_DIM
    groups = kv_width // HEAD_DIM
    fold_width = width // FOLD
    scaling = 1.0 / math.sqrt(HEAD_DIM)
    columns = pl.ds(pl.multiple_of(own_side() * width, LANES), width)
    moves = [
        (q_hbm, q_ref), (k_hbm, k_ref), (nk_hbm, nk_ref), (len_hbm, len_ref), (v_hbm, v_ref),
        (nv_hbm, nv_ref), (res_hbm, res_ref),
        (gain_hbm.at[:, columns], gain_ref), (rt_hbm.at[:, columns], rt_ref),
        (routes_hbm, routes_ref),
    ]
    copies = [pltpu.make_async_copy(a, b, sems.at[i]) for i, (a, b) in enumerate(moves)]
    weights = row_copies((g_hbm, u_hbm), (g_vmem, u_vmem), 0, ahead, w_sems)
    for copy in copies[:5] + weights + copies[5:]:
        copy.start()
    copies[0].wait()
    for h in range(heads):
        q_scr[h * tok:(h + 1) * tok, :] = q_ref[:, h * HEAD_DIM:(h + 1) * HEAD_DIM].astype(F32)
    copies[2].wait()
    nk_scr[...] = nk_ref[...].astype(F32)
    row_group = lax.broadcasted_iota(jnp.int32, (heads, HEAD_DIM), 0) // GROUP
    position = lax.broadcasted_iota(jnp.int32, (heads, cache_len), 1)
    scores, fresh = [], []
    for t in range(tok):
        if t == 0:
            copies[1].wait()
        q_rows = q_scr[pl.ds(t, heads, stride=tok), :]
        q_wide = jnp.concatenate(
            [jnp.where(row_group == g, q_rows, 0.0) for g in range(groups)], axis=1
        )
        scores.append(
            lax.dot_general(
                q_wide.astype(BF16), k_ref[t], (((1,), (1,)), ((), ())),
                preferred_element_type=F32,
            ) * scaling
        )
        fresh.append(
            jnp.sum(q_wide * nk_scr[pl.ds(t, 1), :], axis=1, keepdims=True) * scaling
        )
    copies[3].wait()
    terms, fresh_terms, totals = [], [], []
    for t in range(tok):
        score = jnp.where(position < len_ref[t], scores[t], -1e30)
        largest = jnp.maximum(jnp.max(score, axis=1, keepdims=True), fresh[t])
        term = jnp.exp(score - largest)
        fresh_term = jnp.exp(fresh[t] - largest)
        totals.append(jnp.sum(term, axis=1, keepdims=True) + fresh_term)
        terms.append(term.astype(BF16))
        fresh_terms.append(fresh_term.astype(BF16).astype(F32))
    copies[5].wait()
    nv_scr[...] = nv_ref[...].astype(F32)
    for t in range(tok):
        if t == 0:
            copies[4].wait()
        wide = jnp.dot(terms[t], v_ref[t], preferred_element_type=F32)
        wide = wide + fresh_terms[t] * nv_scr[pl.ds(t, 1), :]
        picked = wide[:, :HEAD_DIM]
        for g in range(1, groups):
            picked = jnp.where(
                row_group == g, wide[:, g * HEAD_DIM:(g + 1) * HEAD_DIM], picked
            )
        o_scr[pl.ds(t, heads, stride=tok), :] = picked / totals[t]
    for copy in copies[6:]:
        copy.wait()
    for h in range(heads):
        cols = slice(h * HEAD_DIM, (h + 1) * HEAD_DIM)
        carried_ref[:, cols] = res_ref[:, cols].astype(F32) + o_scr[h * tok:(h + 1) * tok, :]
    carried = carried_ref[...]
    scaled = carried * gain_ref[...]
    rounded = scaled.astype(BF16).astype(F32)
    router = rt_ref[...].astype(F32)
    for f in range(FOLD):
        pay_scr[f * tok:(f + 1) * tok, :fold_width] = scaled[:, f * fold_width:(f + 1) * fold_width]
    lane = lax.broadcasted_iota(jnp.int32, (tok, LANES), 1)
    row = lax.broadcasted_iota(jnp.int32, (tok, LANES), 0)
    sums = [jnp.sum(carried * carried, axis=1, keepdims=True)]
    for e in range(EXPERTS):
        sums.append(jnp.sum(rounded * router[e:e + 1, :], axis=1, keepdims=True))
    extra = jnp.zeros((tok, LANES), F32)
    for i, total in enumerate(sums):
        for j, term in enumerate(split_three(total)):
            extra = jnp.where(lane == 3 * i + j, term, extra)
    for t in range(tok):
        for i in range(2):
            extra = jnp.where(
                jnp.logical_and(row == t, lane == ROUTE_LANE + i),
                routes_ref[i, t].astype(F32), extra,
            )
    for f in range(FOLD):
        pay_scr[f * tok:(f + 1) * tok, fold_width:] = extra
    pay_ref[...] = pay_scr[...].astype(BF16)
    for copy in weights:
        copy.wait()


def attend(
    ahead, lengths, routes_t, queries, key_cache, value_cache, new_key, new_value,
    residual, gain, router_t, gate_weight, up_weight,
):
    tok, width = queries.shape
    kv_width = new_key.shape[1]
    heads = width // HEAD_DIM
    wide = width // FOLD + LANES
    here = [
        pltpu.VMEM(a.shape, a.dtype)
        for a in (queries, key_cache, value_cache, new_key, new_value, residual)
    ]
    return pl.pallas_call(
        functools.partial(attend_kernel, ahead),
        out_shape=(
            pltpu.VMEM((tok, width), F32),
            pltpu.VMEM((FOLD * tok, wide), BF16),
            pltpu.VMEM(held_shape(gate_weight), BF16),
            pltpu.VMEM(held_shape(gate_weight), BF16),
            pltpu.VMEM(spare_shape(gate_weight), BF16),
        ),
        in_specs=[HBM_SPEC] * 12,
        out_specs=(VMEM_SPEC,) * 5,
        scratch_shapes=here + [
            pltpu.VMEM((1, width), F32),
            pltpu.VMEM((EXPERTS, width), BF16),
            pltpu.VMEM((heads * tok, HEAD_DIM), F32),
            pltpu.VMEM((heads * tok, HEAD_DIM), F32),
            pltpu.VMEM((tok, kv_width), F32),
            pltpu.VMEM((tok, kv_width), F32),
            pltpu.VMEM((FOLD * tok, wide), F32),
            pltpu.SMEM(lengths.shape, jnp.int32),
            pltpu.SMEM(routes_t.shape, jnp.int32),
            pltpu.SemaphoreType.DMA((10,)),
            pltpu.SemaphoreType.DMA((2, 1)),
        ],
        compiler_params=pltpu.CompilerParams(vmem_limit_bytes=LOADED_BELOW),
        cost_estimate=pl.CostEstimate(flops=10**8, bytes_accessed=8 * 10**6, transcendentals=10**5),
        name="attend",
    )(
        *in_hbm(
            lengths, routes_t, queries, key_cache, value_cache, new_key, new_value, residual, gain, router_t,
            gate_weight, up_weight,
        ),
    )


def ready_parts(count, chunks):
    parts = [(i, c) for c in range(1, chunks) for i in range(2)]
    return parts[:2 * count + 1]


def first_half_kernel(
    x_ref, g_hbm, u_hbm, g_in, u_in, spare_in, gate_ref, up_ref, g_ref, u_ref, spare_ref, sems
):
    del g_in, u_in, spare_in
    half, units = g_ref.shape[0], gate_ref.shape[1]
    chunk = chunk_of(units)
    chunks = units // chunk
    count = spare_ref.shape[0]
    ready = ready_parts(count, chunks)

    def copy(i, c):
        return other_copy(
            (g_hbm, u_hbm)[i], (g_ref, u_ref)[i], spare_ref, i, c, chunk, sems.at[i, c]
        )

    for i, c in ready:
        if c < count:
            copy(i, c).start()

    def step(n, _):
        at = chunk_at(n, chunk)
        rows = x_ref[:, :half]
        gate_ref[:, at] = jnp.dot(rows, g_ref[:, at], preferred_element_type=F32)
        up_ref[:, at] = jnp.dot(rows, u_ref[:, at], preferred_element_type=F32)
        for i, c in ready:
            if c >= count:
                @pl.when(n == c - count)
                def _(i=i, c=c):
                    copy(i, c).start()

        return 0

    lax.fori_loop(0, chunks, step, 0)
    for i, c in ready:
        copy(i, c).wait()


def first_half(mine, held, gate_weight, up_weight):
    rows = mine.shape[0]
    width, units = gate_weight.shape
    acc = pltpu.VMEM((rows, units), F32)
    return pl.pallas_call(
        first_half_kernel,
        out_shape=(acc, acc) + tuple(pltpu.VMEM(h.shape, BF16) for h in held),
        in_specs=[VMEM_SPEC] + [HBM_SPEC] * 2 + [VMEM_SPEC] * 3,
        out_specs=(VMEM_SPEC,) * 5,
        scratch_shapes=[pltpu.SemaphoreType.DMA((2, units // chunk_of(units)))],
        input_output_aliases={3: 2, 4: 3, 5: 4},
        compiler_params=pltpu.CompilerParams(vmem_limit_bytes=HELD_BELOW),
        cost_estimate=pl.CostEstimate(
            flops=2 * rows * width * units, bytes_accessed=width * units, transcendentals=0
        ),
        name="first_half",
    )(*in_vmem_always([mine]), *in_hbm(gate_weight, up_weight), *in_vmem_always(held))


def down_tools(d_hbm, g_ref, u_ref, spare_ref, h_ref, sems, width):
    units = h_ref.shape[1]
    chunk = chunk_of(units)
    chunks, count = units // chunk, spare_ref.shape[0]
    per_side = width // chunk
    places = count + chunks
    side = own_side()

    def place(i, part, r):
        if part == 1:
            return spare_ref.at[r - count, i, pl.ds(0, units)]
        start = r + chunks - count if part == 0 else r - 2 * count
        return (g_ref, u_ref)[i].at[pl.ds(0, units), chunk_at(start, chunk)]

    def copy(i, p, part, r):
        n = 2 * p + i
        column = jnp.where(n < per_side, 1 - side, side) * width + lax.rem(n, per_side) * chunk
        return pltpu.make_async_copy(
            d_hbm.at[:, pl.ds(pl.multiple_of(column, LANES), chunk)], place(i, part, r), sems.at[i, p]
        )

    def copies(p):
        r = p % places
        part = 0 if r < count else 1 if r < 2 * count else 2
        return [copy(i, p, part, r) for i in range(2)]

    def run(low, high, limit, put, ready=0):
        def step(turn, part, r, _):
            p = turn * places + r
            for i in range(2):
                @pl.when(p >= ready)
                def _(i=i):
                    copy(i, p, part, r).wait()

                value = jnp.dot(h_ref[...], place(i, part, r)[...], preferred_element_type=F32)
                put(chunk_at(lax.rem(2 * p + i, per_side), chunk), value)
            return 0

        for turn in range(low // places, -(-high // places)):
            for part, (start, end) in enumerate(((0, count), (count, 2 * count), (2 * count, places))):
                start = max(start, low - turn * places)
                end = min(end, high - turn * places)
                if start < end:
                    lax.fori_loop(start, end, functools.partial(step, turn, part), 0)
                for r in range(start, end):
                    if (turn + 1) * places + r < limit:
                        for item in copies((turn + 1) * places + r):
                            item.start()

    return copies, run, places


def pairs_ahead(places, leaving):
    return max(0, min(2, places - leaving))


def second_half_kernel(
    per_plane, x_ref, ox_ref, gate_ref, up_ref, g_hbm, u_hbm, d_hbm, g_in, u_in, spare_in,
    leaving_ref, h_scr, weight_ref, g_ref, u_ref, spare_ref, gu_sems, sems,
):
    del g_in, u_in, spare_in
    rows, units = h_scr.shape
    width = leaving_ref.shape[1]
    chunk = chunk_of(units)
    chunks = units // chunk
    count = spare_ref.shape[0]
    leaving = width // chunk // 2
    copies, run, places = down_tools(d_hbm, g_ref, u_ref, spare_ref, h_scr, sems, width)
    ahead = pairs_ahead(places, leaving)

    def gu_copy(i, c):
        return other_copy(
            (g_hbm, u_hbm)[i], (g_ref, u_ref)[i], spare_ref, i, c, chunk, gu_sems.at[i, c]
        )

    def start_down(p):
        for item in copies(p):
            item.start()

    def in_order(values):
        quarter = rows // 4
        return jnp.concatenate(
            [values[q * quarter:(q + 1) * quarter, :] for q in (0, 2, 1, 3)], axis=0
        )

    there = ready_parts(count, chunks)
    later = [(i, c) for c in range(1, chunks) for i in range(2) if (i, c) not in there]
    for i, c in later:
        gu_copy(i, c).start()
    for p in range(min(count, leaving + ahead)):
        start_down(p)

    own = x_ref[:, width:].astype(F32)
    both = own + in_order(ox_ref[:, width:].astype(F32))
    lane = lax.broadcasted_iota(jnp.int32, (rows, LANES), 1)

    def pick(values, mask):
        return jnp.sum(jnp.where(mask, values, 0.0), axis=1, keepdims=True)

    scale = lax.rsqrt(pick(both, lane < 3) * (1.0 / (2 * width)) + 1e-05)
    first, second = pick(own, lane == ROUTE_LANE), pick(own, lane == ROUTE_LANE + 1)
    expert_of = (lane - 3) // 3
    logit_lane = jnp.logical_and(lane >= 3, lane < ROUTE_LANE)

    def logit_at(route):
        return pick(both, jnp.logical_and(logit_lane, expert_of == route.astype(jnp.int32))) * scale

    share = 1.0 / (1.0 + jnp.exp(logit_at(second) - logit_at(first)))
    here = (lax.axis_index("node") // per_plane).astype(F32)
    weight = jnp.where(first == here, share, 0.0) + jnp.where(second == here, 1.0 - share, 0.0)

    def hidden_chunk(c, g_part, u_part):
        at = chunk_at(c, chunk)
        rows_in = ox_ref[:, :width]
        gate = gate_ref[:, at] + in_order(jnp.dot(rows_in, g_part, preferred_element_type=F32))
        up = up_ref[:, at] + in_order(jnp.dot(rows_in, u_part, preferred_element_type=F32))
        gate = gate * scale
        h_scr[:, at] = (gate / (1.0 + jnp.exp(-gate)) * (up * scale)).astype(BF16)
        for late in range(chunks):
            if count + late < leaving + ahead:
                @pl.when(c == late)
                def _(late=late):
                    start_down(count + late)

    def spare_step(c, _):
        hidden_chunk(c, spare_ref[c, 0], spare_ref[c, 1])
        return 0

    def held_step(c, _):
        for i, late in later:
            @pl.when(c == late)
            def _(i=i, late=late):
                gu_copy(i, late).wait()

        slot = chunk_at(c - count, chunk)
        hidden_chunk(c, g_ref[:, slot], u_ref[:, slot])
        return 0

    lax.fori_loop(0, count, spare_step, 0)
    lax.fori_loop(count, chunks, held_step, 0)

    def leave(to, value):
        leaving_ref[:, to] = in_order(value * weight).astype(BF16)

    run(0, leaving, leaving + ahead, leave)
    weight_ref[...] = jnp.broadcast_to(weight, weight_ref.shape)
    for p in range(leaving, leaving + ahead):
        for item in copies(p):
            item.wait()


def second_half(per_plane, mine, other, sums, held, gate_weight, up_weight, down_weight):
    rows, units = sums[0].shape
    width = down_weight.shape[1] // 2
    chunk = chunk_of(units)
    return pl.pallas_call(
        functools.partial(second_half_kernel, per_plane),
        out_shape=(vmem_array((rows, width), BF16), pltpu.VMEM((rows, units), BF16))
        + (pltpu.VMEM((rows, LANES), F32),) + tuple(pltpu.VMEM(h.shape, BF16) for h in held),
        in_specs=[VMEM_SPEC] * 4 + [HBM_SPEC] * 3 + [VMEM_SPEC] * 3,
        out_specs=(VMEM_SPEC,) * 6,
        scratch_shapes=[
            pltpu.SemaphoreType.DMA((2, units // chunk)),
            pltpu.SemaphoreType.DMA((2, width // chunk)),
        ],
        input_output_aliases={7: 3, 8: 4, 9: 5},
        compiler_params=pltpu.CompilerParams(
            vmem_limit_bytes=HELD_BELOW if rows < 256 else 40 * MIB
        ),
        cost_estimate=pl.CostEstimate(
            flops=6 * rows * width * units, bytes_accessed=4 * width * units, transcendentals=0
        ),
        name="second_half",
    )(
        *in_vmem_always([mine, other]), *in_vmem(*sums),
        *in_hbm(gate_weight, up_weight, down_weight), *in_vmem_always(held),
    )


def staying_kernel(
    h_ref, weight_ref, d_hbm, g_in, u_in, spare_in, out_ref, g_ref, u_ref, spare_ref, sems
):
    del g_in, u_in, spare_in
    width = out_ref.shape[1]
    pairs = sems.shape[1]
    leaving = pairs // 2
    copies, run, places = down_tools(d_hbm, g_ref, u_ref, spare_ref, h_ref, sems, width)
    ahead = pairs_ahead(places, leaving)
    for p in range(leaving + ahead, min(leaving + places, pairs)):
        for item in copies(p):
            item.start()
    weight = weight_ref[:, 0:1]

    def stay(to, value):
        out_ref[:, to] = value * weight

    run(leaving, pairs, pairs, stay, leaving + ahead)


def staying_half(hidden, weight, held, down_weight):
    rows, units = hidden.shape
    width = down_weight.shape[1] // 2
    return pl.pallas_call(
        staying_kernel,
        out_shape=(vmem_array((rows, width), F32),)
        + tuple(pltpu.VMEM(h.shape, BF16) for h in held),
        in_specs=[VMEM_SPEC] * 2 + [HBM_SPEC] + [VMEM_SPEC] * 3,
        out_specs=(VMEM_SPEC,) * 4,
        scratch_shapes=[pltpu.SemaphoreType.DMA((2, width // chunk_of(units)))],
        input_output_aliases={3: 1, 4: 2, 5: 3},
        compiler_params=pltpu.CompilerParams(
            vmem_limit_bytes=HELD_BELOW if rows < 256 else 40 * MIB
        ),
        cost_estimate=pl.CostEstimate(
            flops=2 * rows * width * units, bytes_accessed=width * units, transcendentals=0
        ),
        name="staying_half",
    )(*in_vmem_always([hidden, weight]), *in_hbm(down_weight), *in_vmem_always(held))[0]


def split_kernel(own_ref, got_ref, keep_ref, send_ref):
    size = keep_ref.shape[0]
    keep_ref[...] = own_ref[:size, :] + got_ref[:size, :].astype(F32)
    send_ref[...] = (own_ref[size:, :] + got_ref[size:, :].astype(F32)).astype(BF16)


def split_rows(own, got):
    rows, width = own.shape
    size = rows // 2
    return pl.pallas_call(
        split_kernel,
        out_shape=(vmem_array((size, width), F32), vmem_array((size, width), BF16)),
        in_specs=[VMEM_SPEC] * 2,
        out_specs=(VMEM_SPEC,) * 2,
        compiler_params=pltpu.CompilerParams(vmem_limit_bytes=(8 if rows < 256 else 32) * MIB),
        name="split_rows",
    )(*in_vmem(own, got))


def split_last_kernel(own_ref, got_ref, keep_ref, *refs):
    *sends, total = refs
    total[...] = own_ref[...] + got_ref[...].astype(F32)
    tok, width = keep_ref.shape
    fold_width = width // FOLD
    keep_ref[...] = total[:tok, :]
    for i, send in enumerate(sends, 1):
        rows = total[i * tok:(i + 1) * tok, :]
        send[...] = jnp.concatenate(
            [rows[:, f * fold_width:(f + 1) * fold_width] for f in range(FOLD)], axis=0
        ).astype(BF16)


def split_last(own, got, parts):
    rows, width = own.shape
    tok = rows // parts
    return pl.pallas_call(
        split_last_kernel,
        out_shape=(pltpu.VMEM((tok, width), F32),)
        + (pltpu.VMEM((FOLD * tok, width // FOLD), BF16),) * (parts - 1),
        in_specs=[VMEM_SPEC] * 2,
        out_specs=(VMEM_SPEC,) * parts,
        scratch_shapes=[pltpu.VMEM((rows, width), F32)],
        compiler_params=pltpu.CompilerParams(vmem_limit_bytes=4 * MIB),
        name="split_last",
    )(*in_vmem(own, got))


def finish_kernel(carried_ref, own_ref, *refs):
    *got, out_ref, folded = refs
    tok, width = carried_ref.shape
    fold_width = width // FOLD
    total = got[0][...].astype(F32)
    for ref in got[1:]:
        total = total + ref[...].astype(F32)
    folded[...] = total
    for f in range(FOLD):
        at = slice(f * fold_width, (f + 1) * fold_width)
        value = carried_ref[:, at] + own_ref[:, at] + folded[f * tok:(f + 1) * tok, :]
        out_ref[:, at] = value.astype(BF16)


def finish(carried, own, got):
    tok, width = carried.shape
    return pl.pallas_call(
        finish_kernel,
        out_shape=jax.ShapeDtypeStruct((tok, width), BF16),
        in_specs=[VMEM_SPEC] * (2 + len(got)),
        out_specs=VMEM_SPEC,
        scratch_shapes=[pltpu.VMEM((FOLD * tok, width // FOLD), F32)],
        compiler_params=pltpu.CompilerParams(vmem_limit_bytes=8 * MIB),
        name="finish",
    )(*in_vmem(carried, own, *got))


def on_device(
    residual, queries, key_cache, value_cache, new_key, new_value, cache_lengths,
    norm_gain, router, routes, gate_weight, up_weight, down_weight,
):
    nodes = lax.axis_size("node")
    per_plane = nodes // EXPERTS
    stages = nodes.bit_length() - 1
    masks = [nodes >> (s + 1) for s in range(stages)]
    routes_of = (masks, masks[:-2] + masks[:-3:-1])

    def exchange(array, *flips):
        masks = [sum(side[s] for s in flips) for side in routes_of]
        perm = [(2 * n + c, 2 * (n ^ masks[c]) + c) for n in range(nodes) for c in range(2)]
        return lax.ppermute(array, ("node", "shard"), perm)

    def to_core(array):
        return lax.ppermute(array, "shard", [(0, 1), (1, 0)])

    tok = residual.shape[0]
    half = gate_weight.shape[0] // 2
    heights = [half // 6, half // 2, half // 3]
    carried, payload, *held = attend(
        heights[0], cache_lengths, routes.T, queries, key_cache, value_cache, new_key, new_value,
        residual, norm_gain.reshape(1, -1), router.T, gate_weight, up_weight,
    )
    near = ((0,), (1,), (0, 1))
    got = [exchange(payload, *flips) for flips in near]
    *held, token = load_rows(
        heights[0], heights[1], False, payload, gate_weight, up_weight, held
    )
    payload = unfold(tok, [payload, *reversed(got)], token)
    for stage in range(2, stages):
        got = exchange(payload, stage)
        if stage == 2:
            *held, token = load_rows(
                heights[0] + heights[1], heights[2], True, payload, gate_weight, up_weight, held
            )
        payload = join(payload, got, token)
    mine = payload
    other = to_core(mine)
    gate, up, *held = first_half(mine, held, gate_weight, up_weight)
    leaving, hidden, weight, *held = second_half(
        per_plane, mine, other, (gate, up), held, gate_weight, up_weight, down_weight
    )
    got = to_core(leaving)
    keep = staying_half(hidden, weight, held, down_weight)
    for stage in range(stages - 1, 1, -1):
        keep, send = split_rows(keep, got)
        got = exchange(send, stage)
    keep, *sends = split_last(keep, got, 1 + len(near))
    return finish(carried, keep, [exchange(send, *flips) for send, flips in zip(sends, near)])


def solution(mesh):
    rows = ("replica", "node")
    in_specs = (
        P(rows, "shard"),
        P(rows, "shard"),
        P(rows, None, "shard"),
        P(rows, None, "shard"),
        P(rows, "shard"),
        P(rows, "shard"),
        P(rows),
        P(),
        P(),
        P(rows, None),
        P(None, ("node", "shard")),
        P(None, ("node", "shard")),
        P(("node", "shard"), None),
    )
    return jax.shard_map(
        on_device,
        mesh=mesh,
        in_specs=in_specs,
        out_specs=P(rows, "shard"),
        check_vma=False,
    )
```

```python
import functools
import math

import jax
import jax.numpy as jnp
from jax import lax
from jax.experimental import pallas as pl
from jax.experimental.pallas import tpu as pltpu
from jax.sharding import PartitionSpec as P

MIB = 1 << 20
QUERY_HEADS = 48
KV_HEADS = 8
HEAD_DIM = 128
EXPERTS = 4
GROUP = QUERY_HEADS // KV_HEADS
LANES = 128
FOLD = 2
F32 = jnp.float32
BF16 = jnp.bfloat16


def small(shape, dtype):
    return math.prod(shape) * jnp.dtype(dtype).itemsize <= 17 * MIB // 4


def vmem_array(shape, dtype):
    return pltpu.VMEM(shape, dtype) if small(shape, dtype) else jax.ShapeDtypeStruct(shape, dtype)


def in_vmem(*arrays):
    return [
        pltpu.with_memory_space_constraint(a, pltpu.VMEM) if small(a.shape, a.dtype) else a
        for a in arrays
    ]


def in_vmem_always(arrays):
    return [pltpu.with_memory_space_constraint(a, pltpu.VMEM) for a in arrays]


def in_hbm(*arrays):
    return [pltpu.with_memory_space_constraint(a, pltpu.HBM) for a in arrays]


VMEM_SPEC = pl.BlockSpec(memory_space=pltpu.VMEM)
HBM_SPEC = pl.BlockSpec(memory_space=pltpu.HBM)
ROUTE_LANE = 3 + 3 * EXPERTS
HELD_BELOW = 8 * MIB
LOADED_BELOW = 10 * MIB


def own_side():
    return lax.axis_index("shard")


def chunk_of(units):
    return math.gcd(512, units)


def held_shape(gate_weight):
    width, units = gate_weight.shape
    return width // 2, units


def spare_shape(gate_weight):
    width, units = gate_weight.shape
    return min(2, units // chunk_of(units)), 2, width // 2, chunk_of(units)


def row_copies(sources, targets, first, rows, sems):
    parts = sems.shape[1]
    part = rows // parts
    half, units = sources[0].shape[0] // 2, sources[0].shape[1]
    copies = []
    for p in range(parts):
        at = first + p * part
        for i, (source, target) in enumerate(zip(sources, targets)):
            copies.append(
                pltpu.make_async_copy(
                    source.at[pl.ds(pl.multiple_of(own_side() * half + at, 16), part), :],
                    target.at[pl.ds(at, part), pl.ds(0, units)], sems.at[i, p],
                )
            )
    return copies


def chunk_at(n, chunk):
    return pl.ds(n * chunk if isinstance(n, int) else pl.multiple_of(n * chunk, LANES), chunk)


def other_copy(source, held, spare, i, c, chunk, sem):
    half = source.shape[0] // 2
    first = pl.multiple_of((1 - own_side()) * half, 16)
    count = spare.shape[0]
    target = spare.at[c, i] if c < count else held.at[:, chunk_at(c - count, chunk)]
    return pltpu.make_async_copy(source.at[pl.ds(first, half), chunk_at(c, chunk)], target, sem)


def load_kernel(first, rows, ahead, dep_ref, g_hbm, u_hbm, *refs):
    g_vmem, u_vmem, spare, token_ref, sems, sem = refs[3:]
    copies = row_copies((g_hbm, u_hbm), (g_vmem, u_vmem), first, rows, sems)
    if ahead:
        for i, source in enumerate((g_hbm, u_hbm)):
            copies.append(other_copy(source, None, spare, i, 0, spare.shape[3], sem.at[i]))
    for copy in copies:
        copy.start()
    token_ref[...] = jnp.zeros_like(token_ref)
    for copy in copies:
        copy.wait()


def load_rows(first, rows, ahead, after, gate_weight, up_weight, held):
    hidden = gate_weight.shape[1]
    return pl.pallas_call(
        functools.partial(load_kernel, first, rows, ahead),
        out_shape=tuple(pltpu.VMEM(h.shape, BF16) for h in held) + (pltpu.VMEM((8, LANES), F32),),
        in_specs=[pl.BlockSpec(memory_space=pl.ANY), HBM_SPEC, HBM_SPEC] + [VMEM_SPEC] * 3,
        out_specs=(VMEM_SPEC,) * 4,
        scratch_shapes=[pltpu.SemaphoreType.DMA((2, 4)), pltpu.SemaphoreType.DMA((2,))],
        input_output_aliases={3: 0, 4: 1, 5: 2},
        compiler_params=pltpu.CompilerParams(vmem_limit_bytes=LOADED_BELOW),
        cost_estimate=pl.CostEstimate(flops=0, bytes_accessed=4 * rows * hidden, transcendentals=0),
        name="load_weights",
    )(*in_vmem(after), *in_hbm(gate_weight, up_weight), *in_vmem_always(held))


def unfold_kernel(tok, *refs):
    *arrays, _, out_ref, scr = refs
    fold_width = arrays[0].shape[1] - LANES
    first, near, both, far = arrays
    for i, array in enumerate((first, far, near, both)):
        rows = array[...].astype(F32)
        to = slice(i * tok, (i + 1) * tok)
        for f in range(FOLD):
            scr[to, f * fold_width:(f + 1) * fold_width] = rows[f * tok:(f + 1) * tok, :fold_width]
        scr[to, FOLD * fold_width:] = rows[:tok, fold_width:]
    out_ref[...] = scr[...].astype(BF16)


def unfold(tok, arrays, token):
    shape = (len(arrays) * tok, FOLD * (arrays[0].shape[1] - LANES) + LANES)
    return pl.pallas_call(
        functools.partial(unfold_kernel, tok),
        out_shape=pltpu.VMEM(shape, BF16),
        in_specs=[VMEM_SPEC] * (len(arrays) + 1),
        out_specs=VMEM_SPEC,
        scratch_shapes=[pltpu.VMEM(shape, F32)],
        compiler_params=pltpu.CompilerParams(vmem_limit_bytes=3 * MIB),
        name="unfold",
    )(*in_vmem_always([*arrays, token]))


def join_kernel(a_ref, b_ref, token_ref, out_ref):
    rows = a_ref.shape[0]
    out_ref[:rows, :] = a_ref[...]
    out_ref[rows:, :] = b_ref[...]


def join(a, b, token):
    return pl.pallas_call(
        join_kernel,
        out_shape=vmem_array((a.shape[0] + b.shape[0], a.shape[1]), BF16),
        in_specs=[VMEM_SPEC] * 3,
        out_specs=VMEM_SPEC,
        compiler_params=pltpu.CompilerParams(vmem_limit_bytes=HELD_BELOW),
        name="join",
    )(*in_vmem(a, b, token))


def split_three(value):
    first = value.astype(BF16).astype(F32)
    second = (value - first).astype(BF16).astype(F32)
    return first, second, value - first - second


def attend_kernel(
    ahead, len_hbm, routes_hbm, q_hbm, k_hbm, v_hbm, nk_hbm, nv_hbm, res_hbm, gain_hbm, rt_hbm,
    g_hbm, u_hbm, carried_ref, pay_ref, g_vmem, u_vmem, spare_ref,
    q_ref, k_ref, v_ref, nk_ref, nv_ref, res_ref, gain_ref, rt_ref,
    q_scr, o_scr, nk_scr, nv_scr, pay_scr, len_ref, routes_ref, sems, w_sems,
):
    tok, width = q_ref.shape
    cache_len, kv_width = k_ref.shape[1], k_ref.shape[2]
    heads = width // HEAD_DIM
    groups = kv_width // HEAD_DIM
    fold_width = width // FOLD
    scaling = 1.0 / math.sqrt(HEAD_DIM)
    columns = pl.ds(pl.multiple_of(own_side() * width, LANES), width)
    moves = [
        (q_hbm, q_ref), (k_hbm, k_ref), (nk_hbm, nk_ref), (len_hbm, len_ref), (v_hbm, v_ref),
        (nv_hbm, nv_ref), (res_hbm, res_ref),
        (gain_hbm.at[:, columns], gain_ref), (rt_hbm.at[:, columns], rt_ref),
        (routes_hbm, routes_ref),
    ]
    copies = [pltpu.make_async_copy(a, b, sems.at[i]) for i, (a, b) in enumerate(moves)]
    weights = row_copies((g_hbm, u_hbm), (g_vmem, u_vmem), 0, ahead, w_sems)
    for copy in copies[:5] + weights + copies[5:]:
        copy.start()
    copies[0].wait()
    for h in range(heads):
        q_scr[h * tok:(h + 1) * tok, :] = q_ref[:, h * HEAD_DIM:(h + 1) * HEAD_DIM].astype(F32)
    copies[2].wait()
    nk_scr[...] = nk_ref[...].astype(F32)
    row_group = lax.broadcasted_iota(jnp.int32, (heads, HEAD_DIM), 0) // GROUP
    position = lax.broadcasted_iota(jnp.int32, (heads, cache_len), 1)
    scores, fresh = [], []
    for t in range(tok):
        if t == 0:
            copies[1].wait()
        q_rows = q_scr[pl.ds(t, heads, stride=tok), :]
        q_wide = jnp.concatenate(
            [jnp.where(row_group == g, q_rows, 0.0) for g in range(groups)], axis=1
        )
        scores.append(
            lax.dot_general(
                q_wide.astype(BF16), k_ref[t], (((1,), (1,)), ((), ())),
                preferred_element_type=F32,
            ) * scaling
        )
        fresh.append(
            jnp.sum(q_wide * nk_scr[pl.ds(t, 1), :], axis=1, keepdims=True) * scaling
        )
    copies[3].wait()
    terms, fresh_terms, totals = [], [], []
    for t in range(tok):
        score = jnp.where(position < len_ref[t], scores[t], -1e30)
        largest = jnp.maximum(jnp.max(score, axis=1, keepdims=True), fresh[t])
        term = jnp.exp(score - largest)
        fresh_term = jnp.exp(fresh[t] - largest)
        totals.append(jnp.sum(term, axis=1, keepdims=True) + fresh_term)
        terms.append(term.astype(BF16))
        fresh_terms.append(fresh_term.astype(BF16).astype(F32))
    copies[5].wait()
    nv_scr[...] = nv_ref[...].astype(F32)
    for t in range(tok):
        if t == 0:
            copies[4].wait()
        wide = jnp.dot(terms[t], v_ref[t], preferred_element_type=F32)
        wide = wide + fresh_terms[t] * nv_scr[pl.ds(t, 1), :]
        picked = wide[:, :HEAD_DIM]
        for g in range(1, groups):
            picked = jnp.where(
                row_group == g, wide[:, g * HEAD_DIM:(g + 1) * HEAD_DIM], picked
            )
        o_scr[pl.ds(t, heads, stride=tok), :] = picked / totals[t]
    for copy in copies[6:]:
        copy.wait()
    for h in range(heads):
        cols = slice(h * HEAD_DIM, (h + 1) * HEAD_DIM)
        carried_ref[:, cols] = res_ref[:, cols].astype(F32) + o_scr[h * tok:(h + 1) * tok, :]
    carried = carried_ref[...]
    scaled = carried * gain_ref[...]
    rounded = scaled.astype(BF16).astype(F32)
    router = rt_ref[...].astype(F32)
    for f in range(FOLD):
        pay_scr[f * tok:(f + 1) * tok, :fold_width] = scaled[:, f * fold_width:(f + 1) * fold_width]
    lane = lax.broadcasted_iota(jnp.int32, (tok, LANES), 1)
    row = lax.broadcasted_iota(jnp.int32, (tok, LANES), 0)
    sums = [jnp.sum(carried * carried, axis=1, keepdims=True)]
    for e in range(EXPERTS):
        sums.append(jnp.sum(rounded * router[e:e + 1, :], axis=1, keepdims=True))
    extra = jnp.zeros((tok, LANES), F32)
    for i, total in enumerate(sums):
        for j, term in enumerate(split_three(total)):
            extra = jnp.where(lane == 3 * i + j, term, extra)
    for t in range(tok):
        for i in range(2):
            extra = jnp.where(
                jnp.logical_and(row == t, lane == ROUTE_LANE + i),
                routes_ref[i, t].astype(F32), extra,
            )
    for f in range(FOLD):
        pay_scr[f * tok:(f + 1) * tok, fold_width:] = extra
    pay_ref[...] = pay_scr[...].astype(BF16)
    for copy in weights:
        copy.wait()


def attend(
    ahead, lengths, routes_t, queries, key_cache, value_cache, new_key, new_value,
    residual, gain, router_t, gate_weight, up_weight,
):
    tok, width = queries.shape
    kv_width = new_key.shape[1]
    heads = width // HEAD_DIM
    wide = width // FOLD + LANES
    here = [
        pltpu.VMEM(a.shape, a.dtype)
        for a in (queries, key_cache, value_cache, new_key, new_value, residual)
    ]
    return pl.pallas_call(
        functools.partial(attend_kernel, ahead),
        out_shape=(
            pltpu.VMEM((tok, width), F32),
            pltpu.VMEM((FOLD * tok, wide), BF16),
            pltpu.VMEM(held_shape(gate_weight), BF16),
            pltpu.VMEM(held_shape(gate_weight), BF16),
            pltpu.VMEM(spare_shape(gate_weight), BF16),
        ),
        in_specs=[HBM_SPEC] * 12,
        out_specs=(VMEM_SPEC,) * 5,
        scratch_shapes=here + [
            pltpu.VMEM((1, width), F32),
            pltpu.VMEM((EXPERTS, width), BF16),
            pltpu.VMEM((heads * tok, HEAD_DIM), F32),
            pltpu.VMEM((heads * tok, HEAD_DIM), F32),
            pltpu.VMEM((tok, kv_width), F32),
            pltpu.VMEM((tok, kv_width), F32),
            pltpu.VMEM((FOLD * tok, wide), F32),
            pltpu.SMEM(lengths.shape, jnp.int32),
            pltpu.SMEM(routes_t.shape, jnp.int32),
            pltpu.SemaphoreType.DMA((10,)),
            pltpu.SemaphoreType.DMA((2, 1)),
        ],
        compiler_params=pltpu.CompilerParams(vmem_limit_bytes=LOADED_BELOW),
        cost_estimate=pl.CostEstimate(flops=10**8, bytes_accessed=8 * 10**6, transcendentals=10**5),
        name="attend",
    )(
        *in_hbm(
            lengths, routes_t, queries, key_cache, value_cache, new_key, new_value, residual, gain, router_t,
            gate_weight, up_weight,
        ),
    )


def ready_parts(count, chunks):
    parts = [(i, c) for c in range(1, chunks) for i in range(2)]
    return parts[:2 * count + 1]


def first_half_kernel(
    x_ref, g_hbm, u_hbm, g_in, u_in, spare_in, gate_ref, up_ref, g_ref, u_ref, spare_ref, sems
):
    del g_in, u_in, spare_in
    half, units = g_ref.shape[0], gate_ref.shape[1]
    chunk = chunk_of(units)
    chunks = units // chunk
    count = spare_ref.shape[0]
    ready = ready_parts(count, chunks)

    def copy(i, c):
        return other_copy(
            (g_hbm, u_hbm)[i], (g_ref, u_ref)[i], spare_ref, i, c, chunk, sems.at[i, c]
        )

    for i, c in ready:
        if c < count:
            copy(i, c).start()

    def step(n, _):
        at = chunk_at(n, chunk)
        rows = x_ref[:, :half]
        gate_ref[:, at] = jnp.dot(rows, g_ref[:, at], preferred_element_type=F32)
        up_ref[:, at] = jnp.dot(rows, u_ref[:, at], preferred_element_type=F32)
        for i, c in ready:
            if c >= count:
                @pl.when(n == c - count)
                def _(i=i, c=c):
                    copy(i, c).start()

        return 0

    lax.fori_loop(0, chunks, step, 0)
    for i, c in ready:
        copy(i, c).wait()


def first_half(mine, held, gate_weight, up_weight):
    rows = mine.shape[0]
    width, units = gate_weight.shape
    acc = pltpu.VMEM((rows, units), F32)
    return pl.pallas_call(
        first_half_kernel,
        out_shape=(acc, acc) + tuple(pltpu.VMEM(h.shape, BF16) for h in held),
        in_specs=[VMEM_SPEC] + [HBM_SPEC] * 2 + [VMEM_SPEC] * 3,
        out_specs=(VMEM_SPEC,) * 5,
        scratch_shapes=[pltpu.SemaphoreType.DMA((2, units // chunk_of(units)))],
        input_output_aliases={3: 2, 4: 3, 5: 4},
        compiler_params=pltpu.CompilerParams(vmem_limit_bytes=HELD_BELOW),
        cost_estimate=pl.CostEstimate(
            flops=2 * rows * width * units, bytes_accessed=width * units, transcendentals=0
        ),
        name="first_half",
    )(*in_vmem_always([mine]), *in_hbm(gate_weight, up_weight), *in_vmem_always(held))


def down_tools(d_hbm, g_ref, u_ref, spare_ref, h_ref, sems, width):
    units = h_ref.shape[1]
    chunk = chunk_of(units)
    chunks, count = units // chunk, spare_ref.shape[0]
    per_side = width // chunk
    places = count + chunks
    side = own_side()

    def place(i, part, r):
        if part == 1:
            return spare_ref.at[r - count, i, pl.ds(0, units)]
        start = r + chunks - count if part == 0 else r - 2 * count
        return (g_ref, u_ref)[i].at[pl.ds(0, units), chunk_at(start, chunk)]

    def copy(i, p, part, r):
        n = 2 * p + i
        column = jnp.where(n < per_side, 1 - side, side) * width + lax.rem(n, per_side) * chunk
        return pltpu.make_async_copy(
            d_hbm.at[:, pl.ds(pl.multiple_of(column, LANES), chunk)], place(i, part, r), sems.at[i, p]
        )

    def copies(p):
        r = p % places
        part = 0 if r < count else 1 if r < 2 * count else 2
        return [copy(i, p, part, r) for i in range(2)]

    def run(low, high, limit, put, ready=0):
        def step(turn, part, r, _):
            p = turn * places + r
            for i in range(2):
                @pl.when(p >= ready)
                def _(i=i):
                    copy(i, p, part, r).wait()

                value = jnp.dot(h_ref[...], place(i, part, r)[...], preferred_element_type=F32)
                put(chunk_at(lax.rem(2 * p + i, per_side), chunk), value)
            return 0

        for turn in range(low // places, -(-high // places)):
            for part, (start, end) in enumerate(((0, count), (count, 2 * count), (2 * count, places))):
                start = max(start, low - turn * places)
                end = min(end, high - turn * places)
                if start < end:
                    lax.fori_loop(start, end, functools.partial(step, turn, part), 0)
                for r in range(start, end):
                    if (turn + 1) * places + r < limit:
                        for item in copies((turn + 1) * places + r):
                            item.start()

    return copies, run, places


def pairs_ahead(places, leaving):
    return max(0, min(2, places - leaving))


def second_half_kernel(
    per_plane, x_ref, ox_ref, gate_ref, up_ref, g_hbm, u_hbm, d_hbm, g_in, u_in, spare_in,
    leaving_ref, h_scr, weight_ref, g_ref, u_ref, spare_ref, gu_sems, sems,
):
    del g_in, u_in, spare_in
    rows, units = h_scr.shape
    width = leaving_ref.shape[1]
    chunk = chunk_of(units)
    chunks = units // chunk
    count = spare_ref.shape[0]
    leaving = width // chunk // 2
    copies, run, places = down_tools(d_hbm, g_ref, u_ref, spare_ref, h_scr, sems, width)
    ahead = pairs_ahead(places, leaving)

    def gu_copy(i, c):
        return other_copy(
            (g_hbm, u_hbm)[i], (g_ref, u_ref)[i], spare_ref, i, c, chunk, gu_sems.at[i, c]
        )

    def start_down(p):
        for item in copies(p):
            item.start()

    def in_order(values):
        quarter = rows // 4
        return jnp.concatenate(
            [values[q * quarter:(q + 1) * quarter, :] for q in (0, 2, 1, 3)], axis=0
        )

    there = ready_parts(count, chunks)
    later = [(i, c) for c in range(1, chunks) for i in range(2) if (i, c) not in there]
    for i, c in later:
        gu_copy(i, c).start()
    for p in range(min(count, leaving + ahead)):
        start_down(p)

    own = x_ref[:, width:].astype(F32)
    both = own + in_order(ox_ref[:, width:].astype(F32))
    lane = lax.broadcasted_iota(jnp.int32, (rows, LANES), 1)

    def pick(values, mask):
        return jnp.sum(jnp.where(mask, values, 0.0), axis=1, keepdims=True)

    scale = lax.rsqrt(pick(both, lane < 3) * (1.0 / (2 * width)) + 1e-05)
    first, second = pick(own, lane == ROUTE_LANE), pick(own, lane == ROUTE_LANE + 1)
    expert_of = (lane - 3) // 3
    logit_lane = jnp.logical_and(lane >= 3, lane < ROUTE_LANE)

    def logit_at(route):
        return pick(both, jnp.logical_and(logit_lane, expert_of == route.astype(jnp.int32))) * scale

    share = 1.0 / (1.0 + jnp.exp(logit_at(second) - logit_at(first)))
    here = (lax.axis_index("node") // per_plane).astype(F32)
    weight = jnp.where(first == here, share, 0.0) + jnp.where(second == here, 1.0 - share, 0.0)

    def hidden_chunk(c, g_part, u_part):
        at = chunk_at(c, chunk)
        rows_in = ox_ref[:, :width]
        gate = gate_ref[:, at] + in_order(jnp.dot(rows_in, g_part, preferred_element_type=F32))
        up = up_ref[:, at] + in_order(jnp.dot(rows_in, u_part, preferred_element_type=F32))
        gate = gate * scale
        h_scr[:, at] = (gate / (1.0 + jnp.exp(-gate)) * (up * scale)).astype(BF16)
        for late in range(chunks):
            if count + late < leaving + ahead:
                @pl.when(c == late)
                def _(late=late):
                    start_down(count + late)

    def spare_step(c, _):
        hidden_chunk(c, spare_ref[c, 0], spare_ref[c, 1])
        return 0

    def held_step(c, _):
        for i, late in later:
            @pl.when(c == late)
            def _(i=i, late=late):
                gu_copy(i, late).wait()

        slot = chunk_at(c - count, chunk)
        hidden_chunk(c, g_ref[:, slot], u_ref[:, slot])
        return 0

    lax.fori_loop(0, count, spare_step, 0)
    lax.fori_loop(count, chunks, held_step, 0)

    def leave(to, value):
        leaving_ref[:, to] = in_order(value * weight).astype(BF16)

    run(0, leaving, leaving + ahead, leave)
    weight_ref[...] = jnp.broadcast_to(weight, weight_ref.shape)
    for p in range(leaving, leaving + ahead):
        for item in copies(p):
            item.wait()


def second_half(per_plane, mine, other, sums, held, gate_weight, up_weight, down_weight):
    rows, units = sums[0].shape
    width = down_weight.shape[1] // 2
    chunk = chunk_of(units)
    return pl.pallas_call(
        functools.partial(second_half_kernel, per_plane),
        out_shape=(vmem_array((rows, width), BF16), pltpu.VMEM((rows, units), BF16))
        + (pltpu.VMEM((rows, LANES), F32),) + tuple(pltpu.VMEM(h.shape, BF16) for h in held),
        in_specs=[VMEM_SPEC] * 4 + [HBM_SPEC] * 3 + [VMEM_SPEC] * 3,
        out_specs=(VMEM_SPEC,) * 6,
        scratch_shapes=[
            pltpu.SemaphoreType.DMA((2, units // chunk)),
            pltpu.SemaphoreType.DMA((2, width // chunk)),
        ],
        input_output_aliases={7: 3, 8: 4, 9: 5},
        compiler_params=pltpu.CompilerParams(
            vmem_limit_bytes=HELD_BELOW if rows < 256 else 40 * MIB
        ),
        cost_estimate=pl.CostEstimate(
            flops=6 * rows * width * units, bytes_accessed=4 * width * units, transcendentals=0
        ),
        name="second_half",
    )(
        *in_vmem_always([mine, other]), *in_vmem(*sums),
        *in_hbm(gate_weight, up_weight, down_weight), *in_vmem_always(held),
    )


def staying_kernel(
    h_ref, weight_ref, d_hbm, g_in, u_in, spare_in, out_ref, g_ref, u_ref, spare_ref, sems
):
    del g_in, u_in, spare_in
    width = out_ref.shape[1]
    pairs = sems.shape[1]
    leaving = pairs // 2
    copies, run, places = down_tools(d_hbm, g_ref, u_ref, spare_ref, h_ref, sems, width)
    ahead = pairs_ahead(places, leaving)
    for p in range(leaving + ahead, min(leaving + places, pairs)):
        for item in copies(p):
            item.start()
    weight = weight_ref[:, 0:1]

    def stay(to, value):
        out_ref[:, to] = value * weight

    run(leaving, pairs, pairs, stay, leaving + ahead)


def staying_half(hidden, weight, held, down_weight):
    rows, units = hidden.shape
    width = down_weight.shape[1] // 2
    return pl.pallas_call(
        staying_kernel,
        out_shape=(vmem_array((rows, width), F32),)
        + tuple(pltpu.VMEM(h.shape, BF16) for h in held),
        in_specs=[VMEM_SPEC] * 2 + [HBM_SPEC] + [VMEM_SPEC] * 3,
        out_specs=(VMEM_SPEC,) * 4,
        scratch_shapes=[pltpu.SemaphoreType.DMA((2, width // chunk_of(units)))],
        input_output_aliases={3: 1, 4: 2, 5: 3},
        compiler_params=pltpu.CompilerParams(
            vmem_limit_bytes=HELD_BELOW if rows < 256 else 40 * MIB
        ),
        cost_estimate=pl.CostEstimate(
            flops=2 * rows * width * units, bytes_accessed=width * units, transcendentals=0
        ),
        name="staying_half",
    )(*in_vmem_always([hidden, weight]), *in_hbm(down_weight), *in_vmem_always(held))[0]


def split_kernel(own_ref, got_ref, keep_ref, send_ref):
    size = keep_ref.shape[0]
    keep_ref[...] = own_ref[:size, :] + got_ref[:size, :].astype(F32)
    send_ref[...] = (own_ref[size:, :] + got_ref[size:, :].astype(F32)).astype(BF16)


def split_rows(own, got):
    rows, width = own.shape
    size = rows // 2
    return pl.pallas_call(
        split_kernel,
        out_shape=(vmem_array((size, width), F32), vmem_array((size, width), BF16)),
        in_specs=[VMEM_SPEC] * 2,
        out_specs=(VMEM_SPEC,) * 2,
        compiler_params=pltpu.CompilerParams(vmem_limit_bytes=(8 if rows < 256 else 32) * MIB),
        name="split_rows",
    )(*in_vmem(own, got))


def split_last_kernel(own_ref, got_ref, keep_ref, *refs):
    *sends, total = refs
    total[...] = own_ref[...] + got_ref[...].astype(F32)
    tok, width = keep_ref.shape
    fold_width = width // FOLD
    keep_ref[...] = total[:tok, :]
    for i, send in enumerate(sends, 1):
        rows = total[i * tok:(i + 1) * tok, :]
        send[...] = jnp.concatenate(
            [rows[:, f * fold_width:(f + 1) * fold_width] for f in range(FOLD)], axis=0
        ).astype(BF16)


def split_last(own, got, parts):
    rows, width = own.shape
    tok = rows // parts
    return pl.pallas_call(
        split_last_kernel,
        out_shape=(pltpu.VMEM((tok, width), F32),)
        + (pltpu.VMEM((FOLD * tok, width // FOLD), BF16),) * (parts - 1),
        in_specs=[VMEM_SPEC] * 2,
        out_specs=(VMEM_SPEC,) * parts,
        scratch_shapes=[pltpu.VMEM((rows, width), F32)],
        compiler_params=pltpu.CompilerParams(vmem_limit_bytes=4 * MIB),
        name="split_last",
    )(*in_vmem(own, got))


def finish_kernel(carried_ref, own_ref, *refs):
    *got, out_ref, folded = refs
    tok, width = carried_ref.shape
    fold_width = width // FOLD
    total = got[0][...].astype(F32)
    for ref in got[1:]:
        total = total + ref[...].astype(F32)
    folded[...] = total
    for f in range(FOLD):
        at = slice(f * fold_width, (f + 1) * fold_width)
        value = carried_ref[:, at] + own_ref[:, at] + folded[f * tok:(f + 1) * tok, :]
        out_ref[:, at] = value.astype(BF16)


def finish(carried, own, got):
    tok, width = carried.shape
    return pl.pallas_call(
        finish_kernel,
        out_shape=jax.ShapeDtypeStruct((tok, width), BF16),
        in_specs=[VMEM_SPEC] * (2 + len(got)),
        out_specs=VMEM_SPEC,
        scratch_shapes=[pltpu.VMEM((FOLD * tok, width // FOLD), F32)],
        compiler_params=pltpu.CompilerParams(vmem_limit_bytes=8 * MIB),
        name="finish",
    )(*in_vmem(carried, own, *got))


def on_device(
    residual, queries, key_cache, value_cache, new_key, new_value, cache_lengths,
    norm_gain, router, routes, gate_weight, up_weight, down_weight,
):
    nodes = lax.axis_size("node")
    per_plane = nodes // EXPERTS
    stages = nodes.bit_length() - 1
    masks = [nodes >> (s + 1) for s in range(stages)]
    routes_of = (masks, masks[:-2] + masks[:-3:-1])

    def exchange(array, *flips):
        masks = [sum(side[s] for s in flips) for side in routes_of]
        perm = [(2 * n + c, 2 * (n ^ masks[c]) + c) for n in range(nodes) for c in range(2)]
        return lax.ppermute(array, ("node", "shard"), perm)

    def to_core(array):
        return lax.ppermute(array, "shard", [(0, 1), (1, 0)])

    tok = residual.shape[0]
    half = gate_weight.shape[0] // 2
    heights = [half // 6, half // 2, half // 3]
    carried, payload, *held = attend(
        heights[0], cache_lengths, routes.T, queries, key_cache, value_cache, new_key, new_value,
        residual, norm_gain.reshape(1, -1), router.T, gate_weight, up_weight,
    )
    near = ((0,), (1,), (0, 1))
    got = [exchange(payload, *flips) for flips in near]
    *held, token = load_rows(
        heights[0], heights[1], False, payload, gate_weight, up_weight, held
    )
    payload = unfold(tok, [payload, got[1], got[2], got[0]], token)
    for stage in range(2, stages):
        got = exchange(payload, stage)
        if stage == 2:
            *held, token = load_rows(
                heights[0] + heights[1], heights[2], True, payload, gate_weight, up_weight, held
            )
        payload = join(payload, got, token)
    mine = payload
    other = to_core(mine)
    gate, up, *held = first_half(mine, held, gate_weight, up_weight)
    leaving, hidden, weight, *held = second_half(
        per_plane, mine, other, (gate, up), held, gate_weight, up_weight, down_weight
    )
    got = to_core(leaving)
    keep = staying_half(hidden, weight, held, down_weight)
    for stage in range(stages - 1, 1, -1):
        keep, send = split_rows(keep, got)
        got = exchange(send, stage)
    keep, *sends = split_last(keep, got, 1 + len(near))
    got = [exchange(send, *flips) for send, flips in zip(sends, near)]
    return finish(carried, keep, [got[0], got[2], got[1]])


def solution(mesh):
    rows = ("replica", "node")
    in_specs = (
        P(rows, "shard"),
        P(rows, "shard"),
        P(rows, None, "shard"),
        P(rows, None, "shard"),
        P(rows, "shard"),
        P(rows, "shard"),
        P(rows),
        P(),
        P(),
        P(rows, None),
        P(None, ("node", "shard")),
        P(None, ("node", "shard")),
        P(("node", "shard"), None),
    )
    return jax.shard_map(
        on_device,
        mesh=mesh,
        in_specs=in_specs,
        out_specs=P(rows, "shard"),
        check_vma=False,
    )
```

```python
import functools
import math

import jax
import jax.numpy as jnp
from jax import lax
from jax.experimental import pallas as pl
from jax.experimental.pallas import tpu as pltpu
from jax.sharding import PartitionSpec as P

MIB = 1 << 20
QUERY_HEADS = 48
KV_HEADS = 8
HEAD_DIM = 128
EXPERTS = 4
GROUP = QUERY_HEADS // KV_HEADS
LANES = 128
FOLD = 2
F32 = jnp.float32
BF16 = jnp.bfloat16


def small(shape, dtype):
    return math.prod(shape) * jnp.dtype(dtype).itemsize <= 17 * MIB // 4


def vmem_array(shape, dtype):
    return pltpu.VMEM(shape, dtype) if small(shape, dtype) else jax.ShapeDtypeStruct(shape, dtype)


def in_vmem(*arrays):
    return [
        pltpu.with_memory_space_constraint(a, pltpu.VMEM) if small(a.shape, a.dtype) else a
        for a in arrays
    ]


def in_vmem_always(arrays):
    return [pltpu.with_memory_space_constraint(a, pltpu.VMEM) for a in arrays]


def in_hbm(*arrays):
    return [pltpu.with_memory_space_constraint(a, pltpu.HBM) for a in arrays]


VMEM_SPEC = pl.BlockSpec(memory_space=pltpu.VMEM)
HBM_SPEC = pl.BlockSpec(memory_space=pltpu.HBM)
ROUTE_LANE = 3 + 3 * EXPERTS
HELD_BELOW = 8 * MIB
LOADED_BELOW = 10 * MIB


def own_side():
    return lax.axis_index("shard")


def chunk_of(units):
    return math.gcd(512, units)


def held_shape(gate_weight):
    width, units = gate_weight.shape
    return width // 2, units


def spare_shape(gate_weight):
    width, units = gate_weight.shape
    return min(2, units // chunk_of(units)), 2, width // 2, chunk_of(units)


def row_copies(sources, targets, first, rows, sems):
    parts = sems.shape[1]
    part = rows // parts
    half, units = sources[0].shape[0] // 2, sources[0].shape[1]
    copies = []
    for p in range(parts):
        at = first + p * part
        for i, (source, target) in enumerate(zip(sources, targets)):
            copies.append(
                pltpu.make_async_copy(
                    source.at[pl.ds(pl.multiple_of(own_side() * half + at, 16), part), :],
                    target.at[pl.ds(at, part), pl.ds(0, units)], sems.at[i, p],
                )
            )
    return copies


def chunk_at(n, chunk):
    return pl.ds(n * chunk if isinstance(n, int) else pl.multiple_of(n * chunk, LANES), chunk)


def other_copy(source, held, spare, i, c, chunk, sem):
    half = source.shape[0] // 2
    first = pl.multiple_of((1 - own_side()) * half, 16)
    count = spare.shape[0]
    target = spare.at[c, i] if c < count else held.at[:, chunk_at(c - count, chunk)]
    return pltpu.make_async_copy(source.at[pl.ds(first, half), chunk_at(c, chunk)], target, sem)


def load_kernel(first, rows, ahead, dep_ref, g_hbm, u_hbm, *refs):
    g_vmem, u_vmem, spare, token_ref, sems, sem = refs[3:]
    copies = row_copies((g_hbm, u_hbm), (g_vmem, u_vmem), first, rows, sems)
    if ahead:
        for i, source in enumerate((g_hbm, u_hbm)):
            copies.append(other_copy(source, None, spare, i, 0, spare.shape[3], sem.at[i]))
    for copy in copies:
        copy.start()
    token_ref[...] = jnp.zeros_like(token_ref)
    for copy in copies:
        copy.wait()


def load_rows(first, rows, ahead, after, gate_weight, up_weight, held):
    hidden = gate_weight.shape[1]
    return pl.pallas_call(
        functools.partial(load_kernel, first, rows, ahead),
        out_shape=tuple(pltpu.VMEM(h.shape, BF16) for h in held) + (pltpu.VMEM((8, LANES), F32),),
        in_specs=[pl.BlockSpec(memory_space=pl.ANY), HBM_SPEC, HBM_SPEC] + [VMEM_SPEC] * 3,
        out_specs=(VMEM_SPEC,) * 4,
        scratch_shapes=[pltpu.SemaphoreType.DMA((2, 4)), pltpu.SemaphoreType.DMA((2,))],
        input_output_aliases={3: 0, 4: 1, 5: 2},
        compiler_params=pltpu.CompilerParams(vmem_limit_bytes=LOADED_BELOW),
        cost_estimate=pl.CostEstimate(flops=0, bytes_accessed=4 * rows * hidden, transcendentals=0),
        name="load_weights",
    )(*in_vmem(after), *in_hbm(gate_weight, up_weight), *in_vmem_always(held))


def unfold_kernel(tok, *refs):
    *arrays, _, out_ref, scr = refs
    fold_width = arrays[0].shape[1] - LANES
    for i, array in enumerate([arrays[0], *reversed(arrays[1:])]):
        rows = array[...].astype(F32)
        to = slice(i * tok, (i + 1) * tok)
        for f in range(FOLD):
            scr[to, f * fold_width:(f + 1) * fold_width] = rows[f * tok:(f + 1) * tok, :fold_width]
        scr[to, FOLD * fold_width:] = rows[:tok, fold_width:]
    out_ref[...] = scr[...].astype(BF16)


def unfold(tok, arrays, token):
    shape = (len(arrays) * tok, FOLD * (arrays[0].shape[1] - LANES) + LANES)
    return pl.pallas_call(
        functools.partial(unfold_kernel, tok),
        out_shape=pltpu.VMEM(shape, BF16),
        in_specs=[VMEM_SPEC] * (len(arrays) + 1),
        out_specs=VMEM_SPEC,
        scratch_shapes=[pltpu.VMEM(shape, F32)],
        compiler_params=pltpu.CompilerParams(vmem_limit_bytes=3 * MIB),
        name="unfold",
    )(*in_vmem_always([*arrays, token]))


def join_kernel(a_ref, b_ref, token_ref, out_ref):
    rows = a_ref.shape[0]
    out_ref[:rows, :] = a_ref[...]
    out_ref[rows:, :] = b_ref[...]


def join(a, b, token):
    return pl.pallas_call(
        join_kernel,
        out_shape=vmem_array((a.shape[0] + b.shape[0], a.shape[1]), BF16),
        in_specs=[VMEM_SPEC] * 3,
        out_specs=VMEM_SPEC,
        compiler_params=pltpu.CompilerParams(vmem_limit_bytes=HELD_BELOW),
        name="join",
    )(*in_vmem(a, b, token))


def split_three(value):
    first = value.astype(BF16).astype(F32)
    second = (value - first).astype(BF16).astype(F32)
    return first, second, value - first - second


def attend_kernel(
    ahead, len_hbm, routes_hbm, q_hbm, k_hbm, v_hbm, nk_hbm, nv_hbm, res_hbm, gain_hbm, rt_hbm,
    g_hbm, u_hbm, carried_ref, pay_ref, g_vmem, u_vmem, spare_ref,
    q_ref, k_ref, v_ref, nk_ref, nv_ref, res_ref, gain_ref, rt_ref,
    q_scr, o_scr, nk_scr, nv_scr, pay_scr, len_ref, routes_ref, sems, w_sems,
):
    tok, width = q_ref.shape
    cache_len, kv_width = k_ref.shape[1], k_ref.shape[2]
    heads = width // HEAD_DIM
    groups = kv_width // HEAD_DIM
    fold_width = width // FOLD
    scaling = 1.0 / math.sqrt(HEAD_DIM)
    columns = pl.ds(pl.multiple_of(own_side() * width, LANES), width)
    moves = [
        (q_hbm, q_ref), (k_hbm, k_ref), (nk_hbm, nk_ref), (len_hbm, len_ref), (v_hbm, v_ref),
        (nv_hbm, nv_ref), (res_hbm, res_ref),
        (gain_hbm.at[:, columns], gain_ref), (rt_hbm.at[:, columns], rt_ref),
        (routes_hbm, routes_ref),
    ]
    copies = [pltpu.make_async_copy(a, b, sems.at[i]) for i, (a, b) in enumerate(moves)]
    weights = row_copies((g_hbm, u_hbm), (g_vmem, u_vmem), 0, ahead, w_sems)
    for copy in copies[:5] + weights + copies[5:]:
        copy.start()
    copies[0].wait()
    for h in range(heads):
        q_scr[h * tok:(h + 1) * tok, :] = q_ref[:, h * HEAD_DIM:(h + 1) * HEAD_DIM].astype(F32)
    copies[2].wait()
    nk_scr[...] = nk_ref[...].astype(F32)
    row_group = lax.broadcasted_iota(jnp.int32, (heads, HEAD_DIM), 0) // GROUP
    position = lax.broadcasted_iota(jnp.int32, (heads, cache_len), 1)
    scores, fresh = [], []
    for t in range(tok):
        if t == 0:
            copies[1].wait()
        q_rows = q_scr[pl.ds(t, heads, stride=tok), :]
        q_wide = jnp.concatenate(
            [jnp.where(row_group == g, q_rows, 0.0) for g in range(groups)], axis=1
        )
        scores.append(
            lax.dot_general(
                q_wide.astype(BF16), k_ref[t], (((1,), (1,)), ((), ())),
                preferred_element_type=F32,
            ) * scaling
        )
        fresh.append(
            jnp.sum(q_wide * nk_scr[pl.ds(t, 1), :], axis=1, keepdims=True) * scaling
        )
    copies[3].wait()
    terms, fresh_terms, totals = [], [], []
    for t in range(tok):
        score = jnp.where(position < len_ref[t], scores[t], -1e30)
        largest = jnp.maximum(jnp.max(score, axis=1, keepdims=True), fresh[t])
        term = jnp.exp(score - largest)
        fresh_term = jnp.exp(fresh[t] - largest)
        totals.append(jnp.sum(term, axis=1, keepdims=True) + fresh_term)
        terms.append(term.astype(BF16))
        fresh_terms.append(fresh_term.astype(BF16).astype(F32))
    copies[5].wait()
    nv_scr[...] = nv_ref[...].astype(F32)
    for t in range(tok):
        if t == 0:
            copies[4].wait()
        wide = jnp.dot(terms[t], v_ref[t], preferred_element_type=F32)
        wide = wide + fresh_terms[t] * nv_scr[pl.ds(t, 1), :]
        picked = wide[:, :HEAD_DIM]
        for g in range(1, groups):
            picked = jnp.where(
                row_group == g, wide[:, g * HEAD_DIM:(g + 1) * HEAD_DIM], picked
            )
        o_scr[pl.ds(t, heads, stride=tok), :] = picked / totals[t]
    for copy in copies[6:]:
        copy.wait()
    for h in range(heads):
        cols = slice(h * HEAD_DIM, (h + 1) * HEAD_DIM)
        carried_ref[:, cols] = res_ref[:, cols].astype(F32) + o_scr[h * tok:(h + 1) * tok, :]
    carried = carried_ref[...]
    scaled = carried * gain_ref[...]
    rounded = scaled.astype(BF16).astype(F32)
    router = rt_ref[...].astype(F32)
    for f in range(FOLD):
        pay_scr[f * tok:(f + 1) * tok, :fold_width] = scaled[:, f * fold_width:(f + 1) * fold_width]
    lane = lax.broadcasted_iota(jnp.int32, (tok, LANES), 1)
    row = lax.broadcasted_iota(jnp.int32, (tok, LANES), 0)
    sums = [jnp.sum(carried * carried, axis=1, keepdims=True)]
    for e in range(EXPERTS):
        sums.append(jnp.sum(rounded * router[e:e + 1, :], axis=1, keepdims=True))
    extra = jnp.zeros((tok, LANES), F32)
    for i, total in enumerate(sums):
        for j, term in enumerate(split_three(total)):
            extra = jnp.where(lane == 3 * i + j, term, extra)
    for t in range(tok):
        for i in range(2):
            extra = jnp.where(
                jnp.logical_and(row == t, lane == ROUTE_LANE + i),
                routes_ref[i, t].astype(F32), extra,
            )
    for f in range(FOLD):
        pay_scr[f * tok:(f + 1) * tok, fold_width:] = extra
    pay_ref[...] = pay_scr[...].astype(BF16)
    for copy in weights:
        copy.wait()


def attend(
    ahead, lengths, routes_t, queries, key_cache, value_cache, new_key, new_value,
    residual, gain, router_t, gate_weight, up_weight,
):
    tok, width = queries.shape
    kv_width = new_key.shape[1]
    heads = width // HEAD_DIM
    wide = width // FOLD + LANES
    here = [
        pltpu.VMEM(a.shape, a.dtype)
        for a in (queries, key_cache, value_cache, new_key, new_value, residual)
    ]
    return pl.pallas_call(
        functools.partial(attend_kernel, ahead),
        out_shape=(
            pltpu.VMEM((tok, width), F32),
            pltpu.VMEM((FOLD * tok, wide), BF16),
            pltpu.VMEM(held_shape(gate_weight), BF16),
            pltpu.VMEM(held_shape(gate_weight), BF16),
            pltpu.VMEM(spare_shape(gate_weight), BF16),
        ),
        in_specs=[HBM_SPEC] * 12,
        out_specs=(VMEM_SPEC,) * 5,
        scratch_shapes=here + [
            pltpu.VMEM((1, width), F32),
            pltpu.VMEM((EXPERTS, width), BF16),
            pltpu.VMEM((heads * tok + 16, HEAD_DIM), F32),
            pltpu.VMEM((heads * tok + 16, HEAD_DIM), F32),
            pltpu.VMEM((tok, kv_width), F32),
            pltpu.VMEM((tok, kv_width), F32),
            pltpu.VMEM((FOLD * tok, wide), F32),
            pltpu.SMEM(lengths.shape, jnp.int32),
            pltpu.SMEM(routes_t.shape, jnp.int32),
            pltpu.SemaphoreType.DMA((10,)),
            pltpu.SemaphoreType.DMA((2, 1)),
        ],
        compiler_params=pltpu.CompilerParams(vmem_limit_bytes=LOADED_BELOW),
        cost_estimate=pl.CostEstimate(flops=10**8, bytes_accessed=8 * 10**6, transcendentals=10**5),
        name="attend",
    )(
        *in_hbm(
            lengths, routes_t, queries, key_cache, value_cache, new_key, new_value, residual, gain, router_t,
            gate_weight, up_weight,
        ),
    )


def ready_parts(count, chunks):
    parts = [(i, c) for c in range(1, chunks) for i in range(2)]
    return parts[:2 * count + 1]


def first_half_kernel(
    x_ref, g_hbm, u_hbm, g_in, u_in, spare_in, gate_ref, up_ref, g_ref, u_ref, spare_ref, sems
):
    del g_in, u_in, spare_in
    half, units = g_ref.shape[0], gate_ref.shape[1]
    chunk = chunk_of(units)
    chunks = units // chunk
    count = spare_ref.shape[0]
    ready = ready_parts(count, chunks)

    def copy(i, c):
        return other_copy(
            (g_hbm, u_hbm)[i], (g_ref, u_ref)[i], spare_ref, i, c, chunk, sems.at[i, c]
        )

    for i, c in ready:
        if c < count:
            copy(i, c).start()

    def step(n, _):
        at = chunk_at(n, chunk)
        rows = x_ref[:, :half]
        gate_ref[:, at] = jnp.dot(rows, g_ref[:, at], preferred_element_type=F32)
        up_ref[:, at] = jnp.dot(rows, u_ref[:, at], preferred_element_type=F32)
        for i, c in ready:
            if c >= count:
                @pl.when(n == c - count)
                def _(i=i, c=c):
                    copy(i, c).start()

        return 0

    lax.fori_loop(0, chunks, step, 0)
    for i, c in ready:
        copy(i, c).wait()


def first_half(mine, held, gate_weight, up_weight):
    rows = mine.shape[0]
    width, units = gate_weight.shape
    acc = pltpu.VMEM((rows, units), F32)
    return pl.pallas_call(
        first_half_kernel,
        out_shape=(acc, acc) + tuple(pltpu.VMEM(h.shape, BF16) for h in held),
        in_specs=[VMEM_SPEC] + [HBM_SPEC] * 2 + [VMEM_SPEC] * 3,
        out_specs=(VMEM_SPEC,) * 5,
        scratch_shapes=[pltpu.SemaphoreType.DMA((2, units // chunk_of(units)))],
        input_output_aliases={3: 2, 4: 3, 5: 4},
        compiler_params=pltpu.CompilerParams(vmem_limit_bytes=HELD_BELOW),
        cost_estimate=pl.CostEstimate(
            flops=2 * rows * width * units, bytes_accessed=width * units, transcendentals=0
        ),
        name="first_half",
    )(*in_vmem_always([mine]), *in_hbm(gate_weight, up_weight), *in_vmem_always(held))


def down_tools(d_hbm, g_ref, u_ref, spare_ref, h_ref, sems, width):
    units = h_ref.shape[1]
    chunk = chunk_of(units)
    chunks, count = units // chunk, spare_ref.shape[0]
    per_side = width // chunk
    places = count + chunks
    side = own_side()

    def place(i, part, r):
        if part == 1:
            return spare_ref.at[r - count, i, pl.ds(0, units)]
        start = r + chunks - count if part == 0 else r - 2 * count
        return (g_ref, u_ref)[i].at[pl.ds(0, units), chunk_at(start, chunk)]

    def copy(i, p, part, r):
        n = 2 * p + i
        column = jnp.where(n < per_side, 1 - side, side) * width + lax.rem(n, per_side) * chunk
        return pltpu.make_async_copy(
            d_hbm.at[:, pl.ds(pl.multiple_of(column, LANES), chunk)], place(i, part, r), sems.at[i, p]
        )

    def copies(p):
        r = p % places
        part = 0 if r < count else 1 if r < 2 * count else 2
        return [copy(i, p, part, r) for i in range(2)]

    def run(low, high, limit, put, ready=0):
        def step(turn, part, r, _):
            p = turn * places + r
            for i in range(2):
                @pl.when(p >= ready)
                def _(i=i):
                    copy(i, p, part, r).wait()

                value = jnp.dot(h_ref[...], place(i, part, r)[...], preferred_element_type=F32)
                put(chunk_at(lax.rem(2 * p + i, per_side), chunk), value)
            return 0

        for turn in range(low // places, -(-high // places)):
            for part, (start, end) in enumerate(((0, count), (count, 2 * count), (2 * count, places))):
                start = max(start, low - turn * places)
                end = min(end, high - turn * places)
                if start < end:
                    lax.fori_loop(start, end, functools.partial(step, turn, part), 0)
                for r in range(start, end):
                    if (turn + 1) * places + r < limit:
                        for item in copies((turn + 1) * places + r):
                            item.start()

    return copies, run, places


def pairs_ahead(places, leaving):
    return max(0, min(2, places - leaving))


def second_half_kernel(
    per_plane, x_ref, ox_ref, gate_ref, up_ref, g_hbm, u_hbm, d_hbm, g_in, u_in, spare_in,
    leaving_ref, h_scr, weight_ref, g_ref, u_ref, spare_ref, gu_sems, sems,
):
    del g_in, u_in, spare_in
    rows, units = h_scr.shape
    width = leaving_ref.shape[1]
    chunk = chunk_of(units)
    chunks = units // chunk
    count = spare_ref.shape[0]
    leaving = width // chunk // 2
    copies, run, places = down_tools(d_hbm, g_ref, u_ref, spare_ref, h_scr, sems, width)
    ahead = pairs_ahead(places, leaving)

    def gu_copy(i, c):
        return other_copy(
            (g_hbm, u_hbm)[i], (g_ref, u_ref)[i], spare_ref, i, c, chunk, gu_sems.at[i, c]
        )

    def start_down(p):
        for item in copies(p):
            item.start()

    def in_order(values):
        quarter = rows // 4
        return jnp.concatenate(
            [values[q * quarter:(q + 1) * quarter, :] for q in (0, 2, 1, 3)], axis=0
        )

    there = ready_parts(count, chunks)
    later = [(i, c) for c in range(1, chunks) for i in range(2) if (i, c) not in there]
    for i, c in later:
        gu_copy(i, c).start()
    for p in range(min(count, leaving + ahead)):
        start_down(p)

    own = x_ref[:, width:].astype(F32)
    both = own + in_order(ox_ref[:, width:].astype(F32))
    lane = lax.broadcasted_iota(jnp.int32, (rows, LANES), 1)

    def pick(values, mask):
        return jnp.sum(jnp.where(mask, values, 0.0), axis=1, keepdims=True)

    scale = lax.rsqrt(pick(both, lane < 3) * (1.0 / (2 * width)) + 1e-05)
    first, second = pick(own, lane == ROUTE_LANE), pick(own, lane == ROUTE_LANE + 1)
    expert_of = (lane - 3) // 3
    logit_lane = jnp.logical_and(lane >= 3, lane < ROUTE_LANE)

    def logit_at(route):
        return pick(both, jnp.logical_and(logit_lane, expert_of == route.astype(jnp.int32))) * scale

    share = 1.0 / (1.0 + jnp.exp(logit_at(second) - logit_at(first)))
    here = (lax.axis_index("node") // per_plane).astype(F32)
    weight = jnp.where(first == here, share, 0.0) + jnp.where(second == here, 1.0 - share, 0.0)

    def hidden_chunk(c, g_part, u_part):
        at = chunk_at(c, chunk)
        rows_in = ox_ref[:, :width]
        gate = gate_ref[:, at] + in_order(jnp.dot(rows_in, g_part, preferred_element_type=F32))
        up = up_ref[:, at] + in_order(jnp.dot(rows_in, u_part, preferred_element_type=F32))
        gate = gate * scale
        h_scr[:, at] = (gate / (1.0 + jnp.exp(-gate)) * (up * scale)).astype(BF16)
        for late in range(chunks):
            if count + late < leaving + ahead:
                @pl.when(c == late)
                def _(late=late):
                    start_down(count + late)

    def spare_step(c, _):
        hidden_chunk(c, spare_ref[c, 0], spare_ref[c, 1])
        return 0

    def held_step(c, _):
        for i, late in later:
            @pl.when(c == late)
            def _(i=i, late=late):
                gu_copy(i, late).wait()

        slot = chunk_at(c - count, chunk)
        hidden_chunk(c, g_ref[:, slot], u_ref[:, slot])
        return 0

    lax.fori_loop(0, count, spare_step, 0)
    lax.fori_loop(count, chunks, held_step, 0)

    def leave(to, value):
        leaving_ref[:, to] = in_order(value * weight).astype(BF16)

    run(0, leaving, leaving + ahead, leave)
    weight_ref[...] = jnp.broadcast_to(weight, weight_ref.shape)
    for p in range(leaving, leaving + ahead):
        for item in copies(p):
            item.wait()


def second_half(per_plane, mine, other, sums, held, gate_weight, up_weight, down_weight):
    rows, units = sums[0].shape
    width = down_weight.shape[1] // 2
    chunk = chunk_of(units)
    return pl.pallas_call(
        functools.partial(second_half_kernel, per_plane),
        out_shape=(vmem_array((rows, width), BF16), pltpu.VMEM((rows, units), BF16))
        + (pltpu.VMEM((rows, LANES), F32),) + tuple(pltpu.VMEM(h.shape, BF16) for h in held),
        in_specs=[VMEM_SPEC] * 4 + [HBM_SPEC] * 3 + [VMEM_SPEC] * 3,
        out_specs=(VMEM_SPEC,) * 6,
        scratch_shapes=[
            pltpu.SemaphoreType.DMA((2, units // chunk)),
            pltpu.SemaphoreType.DMA((2, width // chunk)),
        ],
        input_output_aliases={7: 3, 8: 4, 9: 5},
        compiler_params=pltpu.CompilerParams(
            vmem_limit_bytes=HELD_BELOW if rows < 256 else 40 * MIB
        ),
        cost_estimate=pl.CostEstimate(
            flops=6 * rows * width * units, bytes_accessed=4 * width * units, transcendentals=0
        ),
        name="second_half",
    )(
        *in_vmem_always([mine, other]), *in_vmem(*sums),
        *in_hbm(gate_weight, up_weight, down_weight), *in_vmem_always(held),
    )


def staying_kernel(
    h_ref, weight_ref, d_hbm, g_in, u_in, spare_in, out_ref, g_ref, u_ref, spare_ref, sems
):
    del g_in, u_in, spare_in
    width = out_ref.shape[1]
    pairs = sems.shape[1]
    leaving = pairs // 2
    copies, run, places = down_tools(d_hbm, g_ref, u_ref, spare_ref, h_ref, sems, width)
    ahead = pairs_ahead(places, leaving)
    for p in range(leaving + ahead, min(leaving + places, pairs)):
        for item in copies(p):
            item.start()
    weight = weight_ref[:, 0:1]

    def stay(to, value):
        out_ref[:, to] = value * weight

    run(leaving, pairs, pairs, stay, leaving + ahead)


def staying_half(hidden, weight, held, down_weight):
    rows, units = hidden.shape
    width = down_weight.shape[1] // 2
    return pl.pallas_call(
        staying_kernel,
        out_shape=(vmem_array((rows, width), F32),)
        + tuple(pltpu.VMEM(h.shape, BF16) for h in held),
        in_specs=[VMEM_SPEC] * 2 + [HBM_SPEC] + [VMEM_SPEC] * 3,
        out_specs=(VMEM_SPEC,) * 4,
        scratch_shapes=[pltpu.SemaphoreType.DMA((2, width // chunk_of(units)))],
        input_output_aliases={3: 1, 4: 2, 5: 3},
        compiler_params=pltpu.CompilerParams(
            vmem_limit_bytes=HELD_BELOW if rows < 256 else 40 * MIB
        ),
        cost_estimate=pl.CostEstimate(
            flops=2 * rows * width * units, bytes_accessed=width * units, transcendentals=0
        ),
        name="staying_half",
    )(*in_vmem_always([hidden, weight]), *in_hbm(down_weight), *in_vmem_always(held))[0]


def split_kernel(own_ref, got_ref, keep_ref, send_ref):
    size = keep_ref.shape[0]
    keep_ref[...] = own_ref[:size, :] + got_ref[:size, :].astype(F32)
    send_ref[...] = (own_ref[size:, :] + got_ref[size:, :].astype(F32)).astype(BF16)


def split_rows(own, got):
    rows, width = own.shape
    size = rows // 2
    return pl.pallas_call(
        split_kernel,
        out_shape=(vmem_array((size, width), F32), vmem_array((size, width), BF16)),
        in_specs=[VMEM_SPEC] * 2,
        out_specs=(VMEM_SPEC,) * 2,
        compiler_params=pltpu.CompilerParams(vmem_limit_bytes=(8 if rows < 256 else 32) * MIB),
        name="split_rows",
    )(*in_vmem(own, got))


def split_last_kernel(own_ref, got_ref, keep_ref, *refs):
    *sends, total = refs
    total[...] = own_ref[...] + got_ref[...].astype(F32)
    tok, width = keep_ref.shape
    fold_width = width // FOLD
    keep_ref[...] = total[:tok, :]
    for i, send in enumerate(sends, 1):
        rows = total[i * tok:(i + 1) * tok, :]
        send[...] = jnp.concatenate(
            [rows[:, f * fold_width:(f + 1) * fold_width] for f in range(FOLD)], axis=0
        ).astype(BF16)


def split_last(own, got, parts):
    rows, width = own.shape
    tok = rows // parts
    return pl.pallas_call(
        split_last_kernel,
        out_shape=(pltpu.VMEM((tok, width), F32),)
        + (pltpu.VMEM((FOLD * tok, width // FOLD), BF16),) * (parts - 1),
        in_specs=[VMEM_SPEC] * 2,
        out_specs=(VMEM_SPEC,) * parts,
        scratch_shapes=[pltpu.VMEM((rows, width), F32)],
        compiler_params=pltpu.CompilerParams(vmem_limit_bytes=4 * MIB),
        name="split_last",
    )(*in_vmem(own, got))


def finish_kernel(carried_ref, own_ref, *refs):
    *got, out_ref, folded = refs
    tok, width = carried_ref.shape
    fold_width = width // FOLD
    total = got[0][...].astype(F32)
    for ref in got[1:]:
        total = total + ref[...].astype(F32)
    folded[...] = total
    for f in range(FOLD):
        at = slice(f * fold_width, (f + 1) * fold_width)
        value = carried_ref[:, at] + own_ref[:, at] + folded[f * tok:(f + 1) * tok, :]
        out_ref[:, at] = value.astype(BF16)


def finish(carried, own, got):
    tok, width = carried.shape
    return pl.pallas_call(
        finish_kernel,
        out_shape=jax.ShapeDtypeStruct((tok, width), BF16),
        in_specs=[VMEM_SPEC] * (2 + len(got)),
        out_specs=VMEM_SPEC,
        scratch_shapes=[pltpu.VMEM((FOLD * tok, width // FOLD), F32)],
        compiler_params=pltpu.CompilerParams(vmem_limit_bytes=8 * MIB),
        name="finish",
    )(*in_vmem(carried, own, *got))


def on_device(
    residual, queries, key_cache, value_cache, new_key, new_value, cache_lengths,
    norm_gain, router, routes, gate_weight, up_weight, down_weight,
):
    nodes = lax.axis_size("node")
    per_plane = nodes // EXPERTS
    stages = nodes.bit_length() - 1
    masks = [nodes >> (s + 1) for s in range(stages)]
    routes_of = (masks, masks[:-2] + masks[:-3:-1])

    def exchange(array, *flips):
        masks = [sum(side[s] for s in flips) for side in routes_of]
        perm = [(2 * n + c, 2 * (n ^ masks[c]) + c) for n in range(nodes) for c in range(2)]
        return lax.ppermute(array, ("node", "shard"), perm)

    def to_core(array):
        return lax.ppermute(array, "shard", [(0, 1), (1, 0)])

    tok = residual.shape[0]
    half = gate_weight.shape[0] // 2
    heights = [half // 6, half // 2, half // 3]
    carried, payload, *held = attend(
        heights[0], cache_lengths, routes.T, queries, key_cache, value_cache, new_key, new_value,
        residual, norm_gain.reshape(1, -1), router.T, gate_weight, up_weight,
    )
    near = ((0,), (1,), (0, 1))
    got = [exchange(payload, *flips) for flips in near]
    *held, token = load_rows(
        heights[0], heights[1], False, payload, gate_weight, up_weight, held
    )
    payload = unfold(tok, [payload, *reversed(got)], token)
    for stage in range(2, stages):
        got = exchange(payload, stage)
        if stage == 2:
            *held, token = load_rows(
                heights[0] + heights[1], heights[2], True, payload, gate_weight, up_weight, held
            )
        payload = join(payload, got, token)
    mine = payload
    other = to_core(mine)
    gate, up, *held = first_half(mine, held, gate_weight, up_weight)
    leaving, hidden, weight, *held = second_half(
        per_plane, mine, other, (gate, up), held, gate_weight, up_weight, down_weight
    )
    got = to_core(leaving)
    keep = staying_half(hidden, weight, held, down_weight)
    for stage in range(stages - 1, 1, -1):
        keep, send = split_rows(keep, got)
        got = exchange(send, stage)
    keep, *sends = split_last(keep, got, 1 + len(near))
    return finish(carried, keep, [exchange(send, *flips) for send, flips in zip(sends, near)])


def solution(mesh):
    rows = ("replica", "node")
    in_specs = (
        P(rows, "shard"),
        P(rows, "shard"),
        P(rows, None, "shard"),
        P(rows, None, "shard"),
        P(rows, "shard"),
        P(rows, "shard"),
        P(rows),
        P(),
        P(),
        P(rows, None),
        P(None, ("node", "shard")),
        P(None, ("node", "shard")),
        P(("node", "shard"), None),
    )
    return jax.shard_map(
        on_device,
        mesh=mesh,
        in_specs=in_specs,
        out_specs=P(rows, "shard"),
        check_vma=False,
    )
```

```python
import functools
import math

import jax
import jax.numpy as jnp
from jax import lax
from jax.experimental import pallas as pl
from jax.experimental.pallas import tpu as pltpu
from jax.sharding import PartitionSpec as P

MIB = 1 << 20
QUERY_HEADS = 48
KV_HEADS = 8
HEAD_DIM = 128
EXPERTS = 4
GROUP = QUERY_HEADS // KV_HEADS
LANES = 128
FOLD = 2
F32 = jnp.float32
BF16 = jnp.bfloat16


def small(shape, dtype):
    return math.prod(shape) * jnp.dtype(dtype).itemsize <= 17 * MIB // 4


def vmem_array(shape, dtype):
    return pltpu.VMEM(shape, dtype) if small(shape, dtype) else jax.ShapeDtypeStruct(shape, dtype)


def in_vmem(*arrays):
    return [
        pltpu.with_memory_space_constraint(a, pltpu.VMEM) if small(a.shape, a.dtype) else a
        for a in arrays
    ]


def in_vmem_always(arrays):
    return [pltpu.with_memory_space_constraint(a, pltpu.VMEM) for a in arrays]


def in_hbm(*arrays):
    return [pltpu.with_memory_space_constraint(a, pltpu.HBM) for a in arrays]


VMEM_SPEC = pl.BlockSpec(memory_space=pltpu.VMEM)
HBM_SPEC = pl.BlockSpec(memory_space=pltpu.HBM)
ROUTE_LANE = 3 + 3 * EXPERTS
HELD_BELOW = 8 * MIB
LOADED_BELOW = 10 * MIB


def own_side():
    return lax.axis_index("shard")


def chunk_of(units):
    return math.gcd(512, units)


def held_shape(gate_weight):
    width, units = gate_weight.shape
    return width // 2, units


def spare_shape(gate_weight):
    width, units = gate_weight.shape
    return min(2, units // chunk_of(units)), 2, width // 2, chunk_of(units)


def row_copies(sources, targets, first, rows, sems):
    parts = sems.shape[1]
    part = rows // parts
    half, units = sources[0].shape[0] // 2, sources[0].shape[1]
    copies = []
    for p in range(parts):
        at = first + p * part
        for i, (source, target) in enumerate(zip(sources, targets)):
            copies.append(
                pltpu.make_async_copy(
                    source.at[pl.ds(pl.multiple_of(own_side() * half + at, 16), part), :],
                    target.at[pl.ds(at, part), pl.ds(0, units)], sems.at[i, p],
                )
            )
    return copies


def chunk_at(n, chunk):
    return pl.ds(n * chunk if isinstance(n, int) else pl.multiple_of(n * chunk, LANES), chunk)


def other_copy(source, held, spare, i, c, chunk, sem, part=0, parts=1):
    half = source.shape[0] // 2
    size = half // parts
    first = pl.multiple_of((1 - own_side()) * half + part * size, 16)
    rows = pl.ds(part * size, size)
    count = spare.shape[0]
    target = spare.at[c, i, rows] if c < count else held.at[rows, chunk_at(c - count, chunk)]
    return pltpu.make_async_copy(source.at[pl.ds(first, size), chunk_at(c, chunk)], target, sem)


def load_kernel(first, rows, ahead, dep_ref, g_hbm, u_hbm, *refs):
    g_vmem, u_vmem, spare, token_ref, sems, sem = refs[3:]
    copies = row_copies((g_hbm, u_hbm), (g_vmem, u_vmem), first, rows, sems)
    if ahead:
        for i, source in enumerate((g_hbm, u_hbm)):
            for p in range(sem.shape[1]):
                copies.append(other_copy(
                    source, None, spare, i, 0, spare.shape[3], sem.at[i, p], p, sem.shape[1]
                ))
    for copy in copies:
        copy.start()
    token_ref[...] = jnp.zeros_like(token_ref)
    for copy in copies:
        copy.wait()


def load_rows(first, rows, ahead, after, gate_weight, up_weight, held):
    hidden = gate_weight.shape[1]
    return pl.pallas_call(
        functools.partial(load_kernel, first, rows, ahead),
        out_shape=tuple(pltpu.VMEM(h.shape, BF16) for h in held) + (pltpu.VMEM((8, LANES), F32),),
        in_specs=[pl.BlockSpec(memory_space=pl.ANY), HBM_SPEC, HBM_SPEC] + [VMEM_SPEC] * 3,
        out_specs=(VMEM_SPEC,) * 4,
        scratch_shapes=[pltpu.SemaphoreType.DMA((2, 4)), pltpu.SemaphoreType.DMA((2, 4))],
        input_output_aliases={3: 0, 4: 1, 5: 2},
        compiler_params=pltpu.CompilerParams(vmem_limit_bytes=LOADED_BELOW),
        cost_estimate=pl.CostEstimate(flops=0, bytes_accessed=4 * rows * hidden, transcendentals=0),
        name="load_weights",
    )(*in_vmem(after), *in_hbm(gate_weight, up_weight), *in_vmem_always(held))


def unfold_kernel(tok, *refs):
    *arrays, _, out_ref, scr = refs
    fold_width = arrays[0].shape[1] - LANES
    for i, array in enumerate([arrays[0], *reversed(arrays[1:])]):
        rows = array[...].astype(F32)
        to = slice(i * tok, (i + 1) * tok)
        for f in range(FOLD):
            scr[to, f * fold_width:(f + 1) * fold_width] = rows[f * tok:(f + 1) * tok, :fold_width]
        scr[to, FOLD * fold_width:] = rows[:tok, fold_width:]
    out_ref[...] = scr[...].astype(BF16)


def unfold(tok, arrays, token):
    shape = (len(arrays) * tok, FOLD * (arrays[0].shape[1] - LANES) + LANES)
    return pl.pallas_call(
        functools.partial(unfold_kernel, tok),
        out_shape=pltpu.VMEM(shape, BF16),
        in_specs=[VMEM_SPEC] * (len(arrays) + 1),
        out_specs=VMEM_SPEC,
        scratch_shapes=[pltpu.VMEM(shape, F32)],
        compiler_params=pltpu.CompilerParams(vmem_limit_bytes=3 * MIB),
        name="unfold",
    )(*in_vmem_always([*arrays, token]))


def join_kernel(a_ref, b_ref, token_ref, out_ref):
    rows = a_ref.shape[0]
    out_ref[:rows, :] = a_ref[...]
    out_ref[rows:, :] = b_ref[...]


def join(a, b, token):
    return pl.pallas_call(
        join_kernel,
        out_shape=vmem_array((a.shape[0] + b.shape[0], a.shape[1]), BF16),
        in_specs=[VMEM_SPEC] * 3,
        out_specs=VMEM_SPEC,
        compiler_params=pltpu.CompilerParams(vmem_limit_bytes=HELD_BELOW),
        name="join",
    )(*in_vmem(a, b, token))


def split_three(value):
    first = value.astype(BF16).astype(F32)
    second = (value - first).astype(BF16).astype(F32)
    return first, second, value - first - second


def attend_kernel(
    ahead, len_hbm, routes_hbm, q_hbm, k_hbm, v_hbm, nk_hbm, nv_hbm, res_hbm, gain_hbm, rt_hbm,
    g_hbm, u_hbm, carried_ref, pay_ref, g_vmem, u_vmem, spare_ref,
    q_ref, k_ref, v_ref, nk_ref, nv_ref, res_ref, gain_ref, rt_ref,
    q_scr, o_scr, nk_scr, nv_scr, pay_scr, len_ref, routes_ref, sems, w_sems,
):
    tok, width = q_ref.shape
    cache_len, kv_width = k_ref.shape[1], k_ref.shape[2]
    heads = width // HEAD_DIM
    groups = kv_width // HEAD_DIM
    fold_width = width // FOLD
    scaling = 1.0 / math.sqrt(HEAD_DIM)
    columns = pl.ds(pl.multiple_of(own_side() * width, LANES), width)
    moves = [
        (q_hbm, q_ref), (k_hbm, k_ref), (nk_hbm, nk_ref), (len_hbm, len_ref), (v_hbm, v_ref),
        (nv_hbm, nv_ref), (res_hbm, res_ref),
        (gain_hbm.at[:, columns], gain_ref), (rt_hbm.at[:, columns], rt_ref),
        (routes_hbm, routes_ref),
    ]
    copies = [pltpu.make_async_copy(a, b, sems.at[i]) for i, (a, b) in enumerate(moves)]
    weights = row_copies((g_hbm, u_hbm), (g_vmem, u_vmem), 0, ahead, w_sems)
    for copy in copies[:5] + weights + copies[5:]:
        copy.start()
    copies[0].wait()
    for h in range(heads):
        q_scr[h * tok:(h + 1) * tok, :] = q_ref[:, h * HEAD_DIM:(h + 1) * HEAD_DIM].astype(F32)
    copies[2].wait()
    nk_scr[...] = nk_ref[...].astype(F32)
    row_group = lax.broadcasted_iota(jnp.int32, (heads, HEAD_DIM), 0) // GROUP
    position = lax.broadcasted_iota(jnp.int32, (heads, cache_len), 1)
    scores, fresh = [], []
    for t in range(tok):
        if t == 0:
            copies[1].wait()
        q_rows = q_scr[pl.ds(t, heads, stride=tok), :]
        q_wide = jnp.concatenate(
            [jnp.where(row_group == g, q_rows, 0.0) for g in range(groups)], axis=1
        )
        scores.append(
            lax.dot_general(
                q_wide.astype(BF16), k_ref[t], (((1,), (1,)), ((), ())),
                preferred_element_type=F32,
            ) * scaling
        )
        fresh.append(
            jnp.sum(q_wide * nk_scr[pl.ds(t, 1), :], axis=1, keepdims=True) * scaling
        )
    copies[3].wait()
    terms, fresh_terms, totals = [], [], []
    for t in range(tok):
        score = jnp.where(position < len_ref[t], scores[t], -1e30)
        largest = jnp.maximum(jnp.max(score, axis=1, keepdims=True), fresh[t])
        term = jnp.exp(score - largest)
        fresh_term = jnp.exp(fresh[t] - largest)
        totals.append(jnp.sum(term, axis=1, keepdims=True) + fresh_term)
        terms.append(term.astype(BF16))
        fresh_terms.append(fresh_term.astype(BF16).astype(F32))
    copies[5].wait()
    nv_scr[...] = nv_ref[...].astype(F32)
    for t in range(tok):
        if t == 0:
            copies[4].wait()
        wide = jnp.dot(terms[t], v_ref[t], preferred_element_type=F32)
        wide = wide + fresh_terms[t] * nv_scr[pl.ds(t, 1), :]
        picked = wide[:, :HEAD_DIM]
        for g in range(1, groups):
            picked = jnp.where(
                row_group == g, wide[:, g * HEAD_DIM:(g + 1) * HEAD_DIM], picked
            )
        o_scr[pl.ds(t, heads, stride=tok), :] = picked / totals[t]
    for copy in copies[6:]:
        copy.wait()
    for h in range(heads):
        cols = slice(h * HEAD_DIM, (h + 1) * HEAD_DIM)
        carried_ref[:, cols] = res_ref[:, cols].astype(F32) + o_scr[h * tok:(h + 1) * tok, :]
    carried = carried_ref[...]
    scaled = carried * gain_ref[...]
    rounded = scaled.astype(BF16).astype(F32)
    router = rt_ref[...].astype(F32)
    for f in range(FOLD):
        pay_scr[f * tok:(f + 1) * tok, :fold_width] = scaled[:, f * fold_width:(f + 1) * fold_width]
    lane = lax.broadcasted_iota(jnp.int32, (tok, LANES), 1)
    row = lax.broadcasted_iota(jnp.int32, (tok, LANES), 0)
    sums = [jnp.sum(carried * carried, axis=1, keepdims=True)]
    for e in range(EXPERTS):
        sums.append(jnp.sum(rounded * router[e:e + 1, :], axis=1, keepdims=True))
    extra = jnp.zeros((tok, LANES), F32)
    for i, total in enumerate(sums):
        for j, term in enumerate(split_three(total)):
            extra = jnp.where(lane == 3 * i + j, term, extra)
    for t in range(tok):
        for i in range(2):
            extra = jnp.where(
                jnp.logical_and(row == t, lane == ROUTE_LANE + i),
                routes_ref[i, t].astype(F32), extra,
            )
    for f in range(FOLD):
        pay_scr[f * tok:(f + 1) * tok, fold_width:] = extra
    pay_ref[...] = pay_scr[...].astype(BF16)
    for copy in weights:
        copy.wait()


def attend(
    ahead, lengths, routes_t, queries, key_cache, value_cache, new_key, new_value,
    residual, gain, router_t, gate_weight, up_weight,
):
    tok, width = queries.shape
    kv_width = new_key.shape[1]
    heads = width // HEAD_DIM
    wide = width // FOLD + LANES
    here = [
        pltpu.VMEM(a.shape, a.dtype)
        for a in (queries, key_cache, value_cache, new_key, new_value, residual)
    ]
    return pl.pallas_call(
        functools.partial(attend_kernel, ahead),
        out_shape=(
            pltpu.VMEM((tok, width), F32),
            pltpu.VMEM((FOLD * tok, wide), BF16),
            pltpu.VMEM(held_shape(gate_weight), BF16),
            pltpu.VMEM(held_shape(gate_weight), BF16),
            pltpu.VMEM(spare_shape(gate_weight), BF16),
        ),
        in_specs=[HBM_SPEC] * 12,
        out_specs=(VMEM_SPEC,) * 5,
        scratch_shapes=here + [
            pltpu.VMEM((1, width), F32),
            pltpu.VMEM((EXPERTS, width), BF16),
            pltpu.VMEM((heads * tok + 16, HEAD_DIM), F32),
            pltpu.VMEM((heads * tok + 16, HEAD_DIM), F32),
            pltpu.VMEM((tok, kv_width), F32),
            pltpu.VMEM((tok, kv_width), F32),
            pltpu.VMEM((FOLD * tok, wide), F32),
            pltpu.SMEM(lengths.shape, jnp.int32),
            pltpu.SMEM(routes_t.shape, jnp.int32),
            pltpu.SemaphoreType.DMA((10,)),
            pltpu.SemaphoreType.DMA((2, 1)),
        ],
        compiler_params=pltpu.CompilerParams(vmem_limit_bytes=LOADED_BELOW),
        cost_estimate=pl.CostEstimate(flops=10**8, bytes_accessed=8 * 10**6, transcendentals=10**5),
        name="attend",
    )(
        *in_hbm(
            lengths, routes_t, queries, key_cache, value_cache, new_key, new_value, residual, gain, router_t,
            gate_weight, up_weight,
        ),
    )


def ready_parts(count, chunks):
    parts = [(i, c) for c in range(1, chunks) for i in range(2)]
    return parts[:2 * count + 1]


def first_half_kernel(
    x_ref, g_hbm, u_hbm, g_in, u_in, spare_in, gate_ref, up_ref, g_ref, u_ref, spare_ref, sems
):
    del g_in, u_in, spare_in
    half, units = g_ref.shape[0], gate_ref.shape[1]
    chunk = chunk_of(units)
    chunks = units // chunk
    count = spare_ref.shape[0]
    ready = ready_parts(count, chunks)

    def copy(i, c):
        return [
            other_copy(
                (g_hbm, u_hbm)[i], (g_ref, u_ref)[i], spare_ref, i, c, chunk, sems.at[i, c, p], p,
                sems.shape[2],
            )
            for p in range(sems.shape[2])
        ]

    for i, c in ready:
        if c < count:
            for item in copy(i, c):
                item.start()

    def step(n, _):
        at = chunk_at(n, chunk)
        rows = x_ref[:, :half]
        gate_ref[:, at] = jnp.dot(rows, g_ref[:, at], preferred_element_type=F32)
        up_ref[:, at] = jnp.dot(rows, u_ref[:, at], preferred_element_type=F32)
        for i, c in ready:
            if c >= count:
                @pl.when(n == c - count)
                def _(i=i, c=c):
                    for item in copy(i, c):
                        item.start()

        return 0

    lax.fori_loop(0, chunks, step, 0)
    for i, c in ready:
        for item in copy(i, c):
            item.wait()


def first_half(mine, held, gate_weight, up_weight):
    rows = mine.shape[0]
    width, units = gate_weight.shape
    acc = pltpu.VMEM((rows, units), F32)
    return pl.pallas_call(
        first_half_kernel,
        out_shape=(acc, acc) + tuple(pltpu.VMEM(h.shape, BF16) for h in held),
        in_specs=[VMEM_SPEC] + [HBM_SPEC] * 2 + [VMEM_SPEC] * 3,
        out_specs=(VMEM_SPEC,) * 5,
        scratch_shapes=[pltpu.SemaphoreType.DMA((2, units // chunk_of(units), 2))],
        input_output_aliases={3: 2, 4: 3, 5: 4},
        compiler_params=pltpu.CompilerParams(vmem_limit_bytes=HELD_BELOW),
        cost_estimate=pl.CostEstimate(
            flops=2 * rows * width * units, bytes_accessed=width * units, transcendentals=0
        ),
        name="first_half",
    )(*in_vmem_always([mine]), *in_hbm(gate_weight, up_weight), *in_vmem_always(held))


def down_tools(d_hbm, g_ref, u_ref, spare_ref, h_ref, sems, width):
    units = h_ref.shape[1]
    chunk = chunk_of(units)
    chunks, count = units // chunk, spare_ref.shape[0]
    per_side = width // chunk
    places = count + chunks
    side = own_side()

    def place(i, part, r):
        if part == 1:
            return spare_ref.at[r - count, i, pl.ds(0, units)]
        start = r + chunks - count if part == 0 else r - 2 * count
        return (g_ref, u_ref)[i].at[pl.ds(0, units), chunk_at(start, chunk)]

    def copy(i, p, part, r):
        n = 2 * p + i
        column = jnp.where(n < per_side, 1 - side, side) * width + lax.rem(n, per_side) * chunk
        return pltpu.make_async_copy(
            d_hbm.at[:, pl.ds(pl.multiple_of(column, LANES), chunk)], place(i, part, r), sems.at[i, p]
        )

    def copies(p):
        r = p % places
        part = 0 if r < count else 1 if r < 2 * count else 2
        return [copy(i, p, part, r) for i in range(2)]

    def run(low, high, limit, put, ready=0):
        def step(turn, part, r, _):
            p = turn * places + r
            for i in range(2):
                @pl.when(p >= ready)
                def _(i=i):
                    copy(i, p, part, r).wait()

                value = jnp.dot(h_ref[...], place(i, part, r)[...], preferred_element_type=F32)
                put(chunk_at(lax.rem(2 * p + i, per_side), chunk), value)
            return 0

        for turn in range(low // places, -(-high // places)):
            for part, (start, end) in enumerate(((0, count), (count, 2 * count), (2 * count, places))):
                start = max(start, low - turn * places)
                end = min(end, high - turn * places)
                if start < end:
                    lax.fori_loop(start, end, functools.partial(step, turn, part), 0)
                for r in range(start, end):
                    if (turn + 1) * places + r < limit:
                        for item in copies((turn + 1) * places + r):
                            item.start()

    return copies, run, places


def pairs_ahead(places, leaving):
    return max(0, min(2, places - leaving))


def second_half_kernel(
    per_plane, x_ref, ox_ref, gate_ref, up_ref, g_hbm, u_hbm, d_hbm, g_in, u_in, spare_in,
    leaving_ref, h_scr, weight_ref, g_ref, u_ref, spare_ref, gu_sems, sems,
):
    del g_in, u_in, spare_in
    rows, units = h_scr.shape
    width = leaving_ref.shape[1]
    chunk = chunk_of(units)
    chunks = units // chunk
    count = spare_ref.shape[0]
    leaving = width // chunk // 2
    copies, run, places = down_tools(d_hbm, g_ref, u_ref, spare_ref, h_scr, sems, width)
    ahead = pairs_ahead(places, leaving)

    def gu_copy(i, c):
        return other_copy(
            (g_hbm, u_hbm)[i], (g_ref, u_ref)[i], spare_ref, i, c, chunk, gu_sems.at[i, c]
        )

    def start_down(p):
        for item in copies(p):
            item.start()

    def in_order(values):
        quarter = rows // 4
        return jnp.concatenate(
            [values[q * quarter:(q + 1) * quarter, :] for q in (0, 2, 1, 3)], axis=0
        )

    there = ready_parts(count, chunks)
    later = [(i, c) for c in range(1, chunks) for i in range(2) if (i, c) not in there]
    for i, c in later:
        gu_copy(i, c).start()
    for p in range(min(count, leaving + ahead)):
        start_down(p)

    own = x_ref[:, width:].astype(F32)
    both = own + in_order(ox_ref[:, width:].astype(F32))
    lane = lax.broadcasted_iota(jnp.int32, (rows, LANES), 1)

    def pick(values, mask):
        return jnp.sum(jnp.where(mask, values, 0.0), axis=1, keepdims=True)

    scale = lax.rsqrt(pick(both, lane < 3) * (1.0 / (2 * width)) + 1e-05)
    first, second = pick(own, lane == ROUTE_LANE), pick(own, lane == ROUTE_LANE + 1)
    expert_of = (lane - 3) // 3
    logit_lane = jnp.logical_and(lane >= 3, lane < ROUTE_LANE)

    def logit_at(route):
        return pick(both, jnp.logical_and(logit_lane, expert_of == route.astype(jnp.int32))) * scale

    share = 1.0 / (1.0 + jnp.exp(logit_at(second) - logit_at(first)))
    here = (lax.axis_index("node") // per_plane).astype(F32)
    weight = jnp.where(first == here, share, 0.0) + jnp.where(second == here, 1.0 - share, 0.0)

    def hidden_chunk(c, g_part, u_part):
        at = chunk_at(c, chunk)
        rows_in = ox_ref[:, :width]
        gate = gate_ref[:, at] + in_order(jnp.dot(rows_in, g_part, preferred_element_type=F32))
        up = up_ref[:, at] + in_order(jnp.dot(rows_in, u_part, preferred_element_type=F32))
        gate = gate * scale
        h_scr[:, at] = (gate / (1.0 + jnp.exp(-gate)) * (up * scale)).astype(BF16)
        for late in range(chunks):
            if count + late < leaving + ahead:
                @pl.when(c == late)
                def _(late=late):
                    start_down(count + late)

    def spare_step(c, _):
        hidden_chunk(c, spare_ref[c, 0], spare_ref[c, 1])
        return 0

    def held_step(c, _):
        for i, late in later:
            @pl.when(c == late)
            def _(i=i, late=late):
                gu_copy(i, late).wait()

        slot = chunk_at(c - count, chunk)
        hidden_chunk(c, g_ref[:, slot], u_ref[:, slot])
        return 0

    lax.fori_loop(0, count, spare_step, 0)
    lax.fori_loop(count, chunks, held_step, 0)

    def leave(to, value):
        leaving_ref[:, to] = in_order(value * weight).astype(BF16)

    run(0, leaving, leaving + ahead, leave)
    weight_ref[...] = jnp.broadcast_to(weight, weight_ref.shape)
    for p in range(leaving, leaving + ahead):
        for item in copies(p):
            item.wait()


def second_half(per_plane, mine, other, sums, held, gate_weight, up_weight, down_weight):
    rows, units = sums[0].shape
    width = down_weight.shape[1] // 2
    chunk = chunk_of(units)
    return pl.pallas_call(
        functools.partial(second_half_kernel, per_plane),
        out_shape=(vmem_array((rows, width), BF16), pltpu.VMEM((rows, units), BF16))
        + (pltpu.VMEM((rows, LANES), F32),) + tuple(pltpu.VMEM(h.shape, BF16) for h in held),
        in_specs=[VMEM_SPEC] * 4 + [HBM_SPEC] * 3 + [VMEM_SPEC] * 3,
        out_specs=(VMEM_SPEC,) * 6,
        scratch_shapes=[
            pltpu.SemaphoreType.DMA((2, units // chunk)),
            pltpu.SemaphoreType.DMA((2, width // chunk)),
        ],
        input_output_aliases={7: 3, 8: 4, 9: 5},
        compiler_params=pltpu.CompilerParams(
            vmem_limit_bytes=HELD_BELOW if rows < 256 else 40 * MIB
        ),
        cost_estimate=pl.CostEstimate(
            flops=6 * rows * width * units, bytes_accessed=4 * width * units, transcendentals=0
        ),
        name="second_half",
    )(
        *in_vmem_always([mine, other]), *in_vmem(*sums),
        *in_hbm(gate_weight, up_weight, down_weight), *in_vmem_always(held),
    )


def staying_kernel(
    h_ref, weight_ref, d_hbm, g_in, u_in, spare_in, out_ref, g_ref, u_ref, spare_ref, sems
):
    del g_in, u_in, spare_in
    width = out_ref.shape[1]
    pairs = sems.shape[1]
    leaving = pairs // 2
    copies, run, places = down_tools(d_hbm, g_ref, u_ref, spare_ref, h_ref, sems, width)
    ahead = pairs_ahead(places, leaving)
    for p in range(leaving + ahead, min(leaving + places, pairs)):
        for item in copies(p):
            item.start()
    weight = weight_ref[:, 0:1]

    def stay(to, value):
        out_ref[:, to] = value * weight

    run(leaving, pairs, pairs, stay, leaving + ahead)


def staying_half(hidden, weight, held, down_weight):
    rows, units = hidden.shape
    width = down_weight.shape[1] // 2
    return pl.pallas_call(
        staying_kernel,
        out_shape=(vmem_array((rows, width), F32),)
        + tuple(pltpu.VMEM(h.shape, BF16) for h in held),
        in_specs=[VMEM_SPEC] * 2 + [HBM_SPEC] + [VMEM_SPEC] * 3,
        out_specs=(VMEM_SPEC,) * 4,
        scratch_shapes=[pltpu.SemaphoreType.DMA((2, width // chunk_of(units)))],
        input_output_aliases={3: 1, 4: 2, 5: 3},
        compiler_params=pltpu.CompilerParams(
            vmem_limit_bytes=HELD_BELOW if rows < 256 else 40 * MIB
        ),
        cost_estimate=pl.CostEstimate(
            flops=2 * rows * width * units, bytes_accessed=width * units, transcendentals=0
        ),
        name="staying_half",
    )(*in_vmem_always([hidden, weight]), *in_hbm(down_weight), *in_vmem_always(held))[0]


def split_kernel(own_ref, got_ref, keep_ref, send_ref):
    size = keep_ref.shape[0]
    keep_ref[...] = own_ref[:size, :] + got_ref[:size, :].astype(F32)
    send_ref[...] = (own_ref[size:, :] + got_ref[size:, :].astype(F32)).astype(BF16)


def split_rows(own, got):
    rows, width = own.shape
    size = rows // 2
    return pl.pallas_call(
        split_kernel,
        out_shape=(vmem_array((size, width), F32), vmem_array((size, width), BF16)),
        in_specs=[VMEM_SPEC] * 2,
        out_specs=(VMEM_SPEC,) * 2,
        compiler_params=pltpu.CompilerParams(vmem_limit_bytes=(8 if rows < 256 else 32) * MIB),
        name="split_rows",
    )(*in_vmem(own, got))


def split_last_kernel(own_ref, got_ref, keep_ref, *refs):
    *sends, total = refs
    total[...] = own_ref[...] + got_ref[...].astype(F32)
    tok, width = keep_ref.shape
    fold_width = width // FOLD
    keep_ref[...] = total[:tok, :]
    for i, send in enumerate(sends, 1):
        rows = total[i * tok:(i + 1) * tok, :]
        send[...] = jnp.concatenate(
            [rows[:, f * fold_width:(f + 1) * fold_width] for f in range(FOLD)], axis=0
        ).astype(BF16)


def split_last(own, got, parts):
    rows, width = own.shape
    tok = rows // parts
    return pl.pallas_call(
        split_last_kernel,
        out_shape=(pltpu.VMEM((tok, width), F32),)
        + (pltpu.VMEM((FOLD * tok, width // FOLD), BF16),) * (parts - 1),
        in_specs=[VMEM_SPEC] * 2,
        out_specs=(VMEM_SPEC,) * parts,
        scratch_shapes=[pltpu.VMEM((rows, width), F32)],
        compiler_params=pltpu.CompilerParams(vmem_limit_bytes=4 * MIB),
        name="split_last",
    )(*in_vmem(own, got))


def finish_kernel(carried_ref, own_ref, *refs):
    *got, out_ref, folded = refs
    tok, width = carried_ref.shape
    fold_width = width // FOLD
    total = got[0][...].astype(F32)
    for ref in got[1:]:
        total = total + ref[...].astype(F32)
    folded[...] = total
    for f in range(FOLD):
        at = slice(f * fold_width, (f + 1) * fold_width)
        value = carried_ref[:, at] + own_ref[:, at] + folded[f * tok:(f + 1) * tok, :]
        out_ref[:, at] = value.astype(BF16)


def finish(carried, own, got):
    tok, width = carried.shape
    return pl.pallas_call(
        finish_kernel,
        out_shape=jax.ShapeDtypeStruct((tok, width), BF16),
        in_specs=[VMEM_SPEC] * (2 + len(got)),
        out_specs=VMEM_SPEC,
        scratch_shapes=[pltpu.VMEM((FOLD * tok, width // FOLD), F32)],
        compiler_params=pltpu.CompilerParams(vmem_limit_bytes=8 * MIB),
        name="finish",
    )(*in_vmem(carried, own, *got))


def on_device(
    residual, queries, key_cache, value_cache, new_key, new_value, cache_lengths,
    norm_gain, router, routes, gate_weight, up_weight, down_weight,
):
    nodes = lax.axis_size("node")
    per_plane = nodes // EXPERTS
    stages = nodes.bit_length() - 1
    masks = [nodes >> (s + 1) for s in range(stages)]
    routes_of = (masks, masks[:-2] + masks[:-3:-1])

    def exchange(array, *flips):
        masks = [sum(side[s] for s in flips) for side in routes_of]
        perm = [(2 * n + c, 2 * (n ^ masks[c]) + c) for n in range(nodes) for c in range(2)]
        return lax.ppermute(array, ("node", "shard"), perm)

    def to_core(array):
        return lax.ppermute(array, "shard", [(0, 1), (1, 0)])

    tok = residual.shape[0]
    half = gate_weight.shape[0] // 2
    heights = [half // 6, half // 2, half // 3]
    carried, payload, *held = attend(
        heights[0], cache_lengths, routes.T, queries, key_cache, value_cache, new_key, new_value,
        residual, norm_gain.reshape(1, -1), router.T, gate_weight, up_weight,
    )
    near = ((0,), (1,), (0, 1))
    got = [exchange(payload, *flips) for flips in near]
    *held, token = load_rows(
        heights[0], heights[1], False, payload, gate_weight, up_weight, held
    )
    payload = unfold(tok, [payload, *reversed(got)], token)
    for stage in range(2, stages):
        got = exchange(payload, stage)
        if stage == 2:
            *held, token = load_rows(
                heights[0] + heights[1], heights[2], True, payload, gate_weight, up_weight, held
            )
        payload = join(payload, got, token)
    mine = payload
    other = to_core(mine)
    gate, up, *held = first_half(mine, held, gate_weight, up_weight)
    leaving, hidden, weight, *held = second_half(
        per_plane, mine, other, (gate, up), held, gate_weight, up_weight, down_weight
    )
    got = to_core(leaving)
    keep = staying_half(hidden, weight, held, down_weight)
    for stage in range(stages - 1, 1, -1):
        keep, send = split_rows(keep, got)
        got = exchange(send, stage)
    keep, *sends = split_last(keep, got, 1 + len(near))
    return finish(carried, keep, [exchange(send, *flips) for send, flips in zip(sends, near)])


def solution(mesh):
    rows = ("replica", "node")
    in_specs = (
        P(rows, "shard"),
        P(rows, "shard"),
        P(rows, None, "shard"),
        P(rows, None, "shard"),
        P(rows, "shard"),
        P(rows, "shard"),
        P(rows),
        P(),
        P(),
        P(rows, None),
        P(None, ("node", "shard")),
        P(None, ("node", "shard")),
        P(("node", "shard"), None),
    )
    return jax.shard_map(
        on_device,
        mesh=mesh,
        in_specs=in_specs,
        out_specs=P(rows, "shard"),
        check_vma=False,
    )
```
